32 devices in a mesh: dp: 8 (over y, x, core), seq: 4 (over z).
Axes of the slice: x: 2, y: 2, z: 4, core: 2. Of those that a mesh axis runs over, the one named last changes fastest.
Arguments:
- tokens: bfloat16 [32768, 512], P(('dp', 'seq')), may hold values from -6 to 6
- routes: int32 [32768, 2], P(('dp', 'seq')), may hold values from 0 to 7, all different within a row
- lengths: int32 [8, 13], P('dp'), may hold values from 1 to 4084, as said below
- cotangent: bfloat16 [32768, 512], P(('dp', 'seq')), may hold values from -6 to 6
- first_gain: float32 [512], P(('dp', 'seq')), may hold values from 0.5 to 1.5
- first_shift: float32 [512], P(('dp', 'seq')), may hold values from -1.25 to 1.25
- router: float32 [512, 8], P(('dp', 'seq')), may hold values from -0.21875 to 0.21875
- query_map: float32 [512, 512], P(('dp', 'seq')), may hold values from -0.375 to 0.375
- keyval: float32 [512, 128], P(('dp', 'seq')), may hold values from -0.375 to 0.375
- output_map: float32 [512, 512], P(('dp', 'seq')), may hold values from -2 to 2
- second_gain: float32 [512], P(('dp', 'seq')), may hold values from 0.5 to 1.5
- second_shift: float32 [512], P(('dp', 'seq')), may hold values from -1.25 to 1.25
- expand: float32 [512, 2048], P(('dp', 'seq')), may hold values from -0.25 to 0.25
- expand_bias: float32 [2048], P(('dp', 'seq')), may hold values from -1.75 to 1.75
- contract: float32 [2048, 512], P(('dp', 'seq')), may hold values from -0.125 to 0.125
- contract_bias: float32 [512], P(('dp', 'seq')), may hold values from -1.75 to 1.75
Outputs:
- layer_out: bfloat16 [32768, 512], P(('dp', 'seq'))
- grad_tokens: bfloat16 [32768, 512], P(('dp', 'seq'))
- grad_first_gain: float32 [512], P(('dp', 'seq'))
- grad_first_shift: float32 [512], P(('dp', 'seq'))
- grad_router: float32 [512, 8], P(('dp', 'seq'))
- grad_query_map: float32 [512, 512], P(('dp', 'seq'))
- grad_keyval: float32 [512, 128], P(('dp', 'seq'))
- grad_output_map: float32 [512, 512], P(('dp', 'seq'))
- grad_second_gain: float32 [512], P(('dp', 'seq'))
- grad_second_shift: float32 [512], P(('dp', 'seq'))
- grad_expand: float32 [512, 2048], P(('dp', 'seq'))
- grad_expand_bias: float32 [2048], P(('dp', 'seq'))
- grad_contract: float32 [2048, 512], P(('dp', 'seq'))
- grad_contract_bias: float32 [512], P(('dp', 'seq'))
The draws below stay inside these ranges and needn't reach their ends.
Inputs may be any that keep to these rules, and one draw needn't show every extreme that they name: `routes`: the 2 experts of a token differ. `lengths`: each row sums to 4096; one entry of each row is larger than 3072, every other entry is at most 64.
All inputs are finite; a program needn't handle non-finite values.
Results may differ from the reference program's by a relative error of at most 0.024.
Values may be sent and summed in bfloat16 or wider, within the bound.
No kernel may reach another device: no remote copies, remote signals or barrier semaphores. Data moves between devices by JAX's collectives and lax.ppermute only.
A program may use at most 128 MiB of HBM per device.

```python
import jax
import jax.numpy as jnp
from jax import lax

D = 512
FF = 2048
EXPERTS = 8
HEAD = 64
TOP = 2
SHORT = 12
TOK_DEV = 1024
LENGTH = 4096
SEQS = 8
TOKENS = 32768


def draw_lengths(key, part):
    key = jax.random.fold_in(key, 7)
    piece_key, place_key = jax.random.split(key)
    pieces = jax.random.randint(piece_key, (SEQS, SHORT), 1, TOK_DEV // 16 + 1)
    row_ids = jnp.arange(SEQS)[:, None] * jnp.ones_like(pieces)
    pieces = jnp.where(row_ids == 0, 1, pieces)
    longest = LENGTH - jnp.sum(pieces, axis=1, keepdims=True)
    long_place = jax.random.randint(place_key, (SEQS, 1), 0, SHORT + 1)
    slot_ids = jnp.arange(SHORT + 1)[None, :] * jnp.ones_like(long_place)
    earlier = jnp.take_along_axis(pieces, jnp.clip(slot_ids, 0, SHORT - 1), axis=1)
    latter = jnp.take_along_axis(pieces, jnp.clip(slot_ids - 1, 0, SHORT - 1), axis=1)
    return jnp.where(slot_ids < long_place, earlier, jnp.where(slot_ids == long_place, longest, latter)).astype(jnp.int32)


def levels(key, dims, cuts, smallest, high):
    factor_of = 1.0
    for position, parts in cuts:
        draws = jax.random.uniform(jax.random.fold_in(jax.random.fold_in(key, 6), position), (parts,), jnp.float32, smallest / len(cuts), high / len(cuts))
        factor_of = factor_of * jnp.repeat(jnp.exp(draws), dims[position] // parts).reshape((-1,) + (1,) * (len(dims) - 1 - position))
    return factor_of


def picks_of(key, rows, number_of, top, lift):
    order = jax.random.permutation(jax.random.fold_in(key, 1), number_of)
    boost = order
    for power in range(3):
        boost = boost * boost // number_of
    boost = boost * lift // number_of
    tickets = jax.random.randint(jax.random.fold_in(key, 2), (rows, number_of), 0, 4096) + boost
    sure = jax.random.permutation(jax.random.fold_in(key, 3), rows)[jnp.arange(number_of) % rows]
    tickets = jnp.where(jnp.arange(rows)[:, None] == sure[None, :], 1 << 14, tickets)
    score = tickets * number_of + jnp.arange(number_of)
    return lax.top_k(score.astype(jnp.int32), top)[1].astype(jnp.int32)


def centred(stream_key, dims, scale, reach, cuts=(), kind=jnp.bfloat16):
    loudness = levels(stream_key, dims, cuts, -0.22, 0.18) if cuts else 1.0
    entries = jax.random.normal(stream_key, dims, jnp.float32) * scale * loudness
    return jnp.minimum(jnp.maximum(entries, -reach), reach).astype(kind)


def setup_inputs(seed: int = 0) -> dict:
    streams_of = jax.random.split(jax.random.key(seed), 17)
    return {
        "tokens": centred(streams_of[0], (TOKENS, D), 1.0, 6.0, ((0, 32),)),
        "routes": picks_of(streams_of[1], TOKENS, EXPERTS, TOP, 2048),
        "lengths": draw_lengths(jax.random.fold_in(streams_of[16], 71), 0),
        "cotangent": centred(streams_of[3], (TOKENS, D), 1.0, 6.0, ((0, 32),)),
        "first_gain": jnp.clip(1.0 + 0.1 * jax.random.normal(streams_of[4], (D,), jnp.float32), 0.5, 1.5),
        "first_shift": centred(streams_of[5], (D,), 0.2, 1.25, ((0, 32),), jnp.float32),
        "router": centred(streams_of[6], (D, EXPERTS), (0.8 * D ** -0.5), 0.21875, ((0, 32),), jnp.float32),
        "query_map": centred(streams_of[7], (D, EXPERTS * HEAD), (1.4 * D ** -0.5), 0.375, ((0, 32),), jnp.float32),
        "keyval": centred(streams_of[8], (D, 2 * HEAD), (1.4 * D ** -0.5), 0.375, ((0, 32),), jnp.float32),
        "output_map": centred(streams_of[9], (EXPERTS * HEAD, D), (max(LENGTH // 512, 1) ** 0.5 * HEAD ** -0.5), 2.0, ((0, 32),), jnp.float32),
        "second_gain": jnp.clip(1.0 + 0.1 * jax.random.normal(streams_of[10], (D,), jnp.float32), 0.5, 1.5),
        "second_shift": centred(streams_of[11], (D,), 0.2, 1.25, ((0, 32),), jnp.float32),
        "expand": centred(streams_of[12], (D, FF), D ** -0.5, 0.25, ((0, 32),), jnp.float32),
        "expand_bias": centred(streams_of[13], (FF,), 0.3, 1.75, ((0, 32),), jnp.float32),
        "contract": centred(streams_of[14], (FF, D), FF ** -0.5, 0.125, ((0, 32),), jnp.float32),
        "contract_bias": centred(streams_of[15], (D,), 0.3, 1.75, ((0, 32),), jnp.float32),
    }


highest = lax.Precision.HIGHEST

@jax.custom_vjp
def low(v):
    return lax.optimization_barrier(v.astype(jnp.bfloat16)).astype(jnp.float32)

@jax.custom_vjp
def low_back(v):
    return v

def low_keep(v):
    return (low(v), None)

def low_pass(kept, grad):
    return (grad,)

def back_keep(v):
    return (v, None)

def back_low(kept, grad):
    return (low(grad),)
low.defvjp(low_keep, low_pass)
low_back.defvjp(back_keep, back_low)

def matmul(left_side, right_side):
    return jnp.dot(left_side, right_side, precision=highest, preferred_element_type=jnp.float32)

def norm_rows(matrix, scale_row, shift_row):
    center = matrix - lax.optimization_barrier(jnp.mean(matrix, axis=-1, keepdims=True))
    spread = lax.optimization_barrier(jnp.mean(center * center, axis=-1, keepdims=True))
    return center * lax.rsqrt(spread + 1e-05) * scale_row + shift_row

def pick_rows(per_expert, onehot):
    return lax.optimization_barrier(jnp.sum(per_expert[:, None, :, :] * onehot[:, :, :, None], axis=2))

def spread_rows(per_choice, onehot):
    return lax.optimization_barrier(jnp.sum(per_choice[:, :, None, :] * onehot[:, :, :, None], axis=1))

def document_ids(row_lengths):
    doc_ends = jnp.cumsum(row_lengths).astype(jnp.int32)
    positions = jnp.arange(LENGTH, dtype=jnp.int32)
    return lax.optimization_barrier(jnp.sum((positions[:, None] >= doc_ends[None, :]).astype(jnp.int32), axis=1)).astype(jnp.int32)

def sequence_layer(params, inputs, route_rows, doc_ids):
    first_gain, first_shift, router, query_map, keyval, output_map, second_gain, second_shift, expand, expand_bias, contract, contract_bias = params
    hidden = low(norm_rows(inputs, first_gain, first_shift))
    logits = low_back(matmul(hidden, router))
    onehot = (route_rows[:, :, None] == jnp.arange(EXPERTS, dtype=jnp.int32)[None, None, :]).astype(jnp.float32)
    picked = lax.optimization_barrier(jnp.sum(logits[:, None, :] * onehot, axis=2))
    gate_weights = jax.nn.softmax(picked, axis=-1)
    query_all = matmul(hidden, query_map).reshape(LENGTH, EXPERTS, HEAD)
    queries = low(low_back(pick_rows(query_all, onehot))).reshape(LENGTH * TOP, HEAD)
    kv_rows = low(low_back(matmul(hidden, keyval)))
    key_part = kv_rows[:, :HEAD]
    value_part = kv_rows[:, HEAD:]
    doc_rows = jnp.repeat(doc_ids, TOP)
    score_scale = HEAD ** (-0.5)
    block_rows = min(1024, LENGTH * TOP)

    def attend(block_pair):
        query_block, doc_block = block_pair
        scores = low_back(matmul(query_block, key_part.T) * score_scale)
        same_doc = doc_block[:, None] == doc_ids[None, :]
        probs = jax.nn.softmax(jnp.where(same_doc, scores, -1e+30), axis=-1)
        return low_back(matmul(low(probs), value_part))
    blocks = (queries.reshape(-1, block_rows, HEAD), doc_rows.reshape(-1, block_rows))
    attn = lax.map(jax.checkpoint(attend), blocks).reshape(LENGTH, TOP, HEAD)
    mixed = low(spread_rows(attn * gate_weights[:, :, None], onehot).reshape(LENGTH, EXPERTS * HEAD))
    middle = inputs + low_back(matmul(mixed, output_map))
    hidden_two = low(norm_rows(middle, second_gain, second_shift))
    inner = low_back(matmul(hidden_two, expand) + expand_bias)
    active = low(jax.nn.gelu(inner, approximate=True))
    return middle + matmul(active, contract) + contract_bias

def reference(tokens, routes, lengths, cotangent, first_gain, first_shift, router, query_map, keyval, output_map, second_gain, second_shift, expand, expand_bias, contract, contract_bias):
    masters = (first_gain, first_shift, router, query_map, keyval, output_map, second_gain, second_shift, expand, expand_bias, contract, contract_bias)
    doc_all = jax.vmap(document_ids)(lengths)
    route_all = routes.reshape(SEQS, LENGTH, TOP)

    def forward(inputs, weights):
        lowered = tuple((low(weight) for weight in weights))

        def one_sequence(packed):
            seq_inputs, seq_routes, seq_docs = packed
            return sequence_layer(lowered, seq_inputs, seq_routes, seq_docs)
        outputs = lax.map(jax.checkpoint(one_sequence), (inputs.reshape(SEQS, LENGTH, D), route_all, doc_all))
        return outputs.reshape(TOKENS, D)
    result, pullback = jax.vjp(forward, tokens.astype(jnp.float32), masters)
    grad_inputs, grads = pullback(cotangent.astype(jnp.float32))
    return (result.astype(jnp.bfloat16), grad_inputs.astype(jnp.bfloat16), grads[0], grads[1], grads[2], grads[3], grads[4], grads[5], grads[6], grads[7], grads[8], grads[9], grads[10], grads[11])
```

```python
import jax
import jax.numpy as jnp
from jax import lax
from jax.sharding import PartitionSpec as P


def to_low(matrix):
    return matrix.astype(jnp.bfloat16)


def dot_plain(left_side, right_side):
    return jnp.dot(left_side, right_side, preferred_element_type=jnp.float32)


def dot_last(left_side, right_side):
    return lax.dot_general(
        left_side, right_side, (((1,), (1,)), ((), ())), preferred_element_type=jnp.float32
    )


def dot_first(left_side, right_side):
    return lax.dot_general(
        left_side, right_side, (((0,), (0,)), ((), ())), preferred_element_type=jnp.float32
    )


def norm_rows(matrix, scale_row, shift_row):
    center = matrix - jnp.mean(matrix, axis=-1, keepdims=True)
    spread = jnp.mean(center * center, axis=-1, keepdims=True)
    return center * lax.rsqrt(spread + 1e-05) * scale_row + shift_row


def smooth_gate(matrix):
    return jax.nn.gelu(matrix, approximate=True)


def pick_rows(per_expert, onehot):
    return jnp.sum(per_expert[:, None, :, :] * onehot[:, :, :, None], axis=2)


def spread_rows(per_choice, onehot):
    return jnp.sum(per_choice[:, :, None, :] * onehot[:, :, :, None], axis=1)


def block_scores(query_block, doc_block, key_value, doc_keys, score_scale):
    head_size = query_block.shape[1]
    scores = dot_last(query_block, key_value[:, :head_size]) * score_scale
    same_doc = doc_block[:, None] == doc_keys[None, :]
    return (scores, same_doc)


def attention_forward(query_block, doc_block, keyval_all, doc_all, key_rows, score_scale):
    head_size = query_block.shape[1]

    def advance(block_index, partial_value):
        running_max, running_sum, running_acc = partial_value
        key_value = lax.dynamic_slice_in_dim(keyval_all, block_index * key_rows, key_rows, 0)
        doc_keys = lax.dynamic_slice_in_dim(doc_all, block_index * key_rows, key_rows, 0)
        scores, same_doc = block_scores(query_block, doc_block, key_value, doc_keys, score_scale)
        masked = jnp.where(same_doc, scores, -1e30)
        new_max = jnp.maximum(running_max, jnp.max(masked, axis=1))
        factor = jnp.exp(running_max - new_max)
        weights = jnp.where(same_doc, jnp.exp(masked - new_max[:, None]), 0.0)
        running_sum = running_sum * factor + jnp.sum(weights, axis=1)
        running_acc = running_acc * factor[:, None] + dot_plain(
            to_low(weights), key_value[:, head_size:]
        )
        return (new_max, running_sum, running_acc)

    row_count = query_block.shape[0]
    initial = (
        jnp.full((row_count,), -1e30, jnp.float32),
        jnp.zeros((row_count,), jnp.float32),
        jnp.zeros(query_block.shape, jnp.float32),
    )
    running_max, running_sum, running_acc = lax.fori_loop(
        0, keyval_all.shape[0] // key_rows, advance, initial
    )
    return (running_acc / running_sum[:, None], running_max + jnp.log(running_sum))


def block_backward(
    query_block, doc_block, log_total, delta_rows, grad_attn, key_value, doc_keys, score_scale
):
    head_size = query_block.shape[1]
    scores, same_doc = block_scores(query_block, doc_block, key_value, doc_keys, score_scale)
    probs = jnp.where(
        same_doc, jnp.exp(jnp.where(same_doc, scores, -1e30) - log_total[:, None]), 0.0
    )
    probs_low = to_low(probs)
    grad_probs = dot_last(grad_attn, key_value[:, head_size:])
    grad_scores = to_low(probs * (grad_probs - delta_rows[:, None]))
    grad_query = dot_plain(grad_scores, key_value[:, :head_size])
    grad_keys = dot_first(grad_scores, query_block) * score_scale
    grad_values = dot_first(probs_low, grad_attn)
    return (grad_query, jnp.concatenate([grad_keys, grad_values], axis=1))


def index_bits(axis):
    size = lax.axis_size(axis)
    return [(axis, 1 << b) for b in range(size.bit_length() - 1)]


def bit_of(stage):
    axis, mask = stage
    return (lax.axis_index(axis) & mask) // mask


def exchange(block, stage):
    axis, mask = stage
    pairs = [(i, i ^ mask) for i in range(lax.axis_size(axis))]
    return lax.ppermute(block, axis, pairs)


def device_bits():
    return index_bits("dp")[::-1] + index_bits("seq")[::-1]


def gather_blocks(block, stages):
    order = device_bits()
    have = []
    for stage in stages:
        other = exchange(block, stage)
        position = sum(1 for s in have if order.index(s) < order.index(stage))
        swap = bit_of(stage) == 1
        first = jnp.where(swap, other, block)
        second = jnp.where(swap, block, other)
        block = jnp.stack([first, second], axis=position)
        have.append(stage)
    return block.reshape((-1,) + block.shape[len(have):])


def scatter_sum(blocks, stages):
    order = device_bits()
    left = list(order)
    value = blocks.reshape((2,) * len(order) + blocks.shape[1:])
    for stage in stages:
        position = left.index(stage)
        bit = bit_of(stage)
        keep = lax.dynamic_index_in_dim(value, bit, position, keepdims=False)
        send = lax.dynamic_index_in_dim(value, 1 - bit, position, keepdims=False)
        value = keep.astype(jnp.float32) + exchange(to_low(send), stage).astype(jnp.float32)
        left.remove(stage)
    return value


def stage_orders():
    dp_bits, seq_bits = index_bits("dp"), index_bits("seq")
    core, plane = dp_bits[:1], dp_bits[1:]
    return (seq_bits + plane + core, seq_bits + plane[::-1] + core)


def per_device(
    tokens,
    routes,
    lengths,
    cotangent,
    first_gain,
    first_shift,
    router,
    query_map,
    keyval,
    output_map,
    second_gain,
    second_shift,
    expand,
    expand_bias,
    contract,
    contract_bias,
):
    order_a, order_b = stage_orders()
    device_count = lax.axis_size("dp") * lax.axis_size("seq")
    rows = first_gain.shape[0]
    width = rows * device_count
    misc = jnp.concatenate(
        [
            router,
            first_gain[:, None],
            first_shift[:, None],
            second_gain[:, None],
            second_shift[:, None],
            contract_bias[:, None],
            expand_bias.reshape(rows, -1),
        ],
        axis=1,
    )
    misc_width = misc.shape[1]
    misc = jnp.pad(misc, ((0, 0), (0, 128 - misc_width)))
    small = to_low(jnp.concatenate([query_map, keyval, misc], axis=1))
    small_all = gather_blocks(small, order_a).reshape(width, -1)
    query_cols = query_map.shape[1]
    keyval_cols = keyval.shape[1]
    query_weight = small_all[:, :query_cols]
    keyval_weight = small_all[:, query_cols : query_cols + keyval_cols]
    misc_all = small_all[:, query_cols + keyval_cols :]
    experts = router.shape[1]
    router_weight = misc_all[:, :experts]
    gain_one, shift_one, gain_two, shift_two, contract_shift = (
        misc_all[:, experts + i] for i in range(5)
    )
    expand_shift = misc_all[:, experts + 5 : misc_width].reshape(-1)
    output_expand = gather_blocks(
        to_low(jnp.concatenate([output_map, expand], axis=1)), order_a
    ).reshape(width, -1)
    output_weight = output_expand[:, : output_map.shape[1]]
    expand_weight = output_expand[:, output_map.shape[1] :]
    contract_weight = gather_blocks(to_low(contract), order_b).reshape(-1, contract.shape[1])
    gain_one_f = gain_one.astype(jnp.float32)
    shift_one_f = shift_one.astype(jnp.float32)
    gain_two_f = gain_two.astype(jnp.float32)
    shift_two_f = shift_two.astype(jnp.float32)
    token_count = tokens.shape[0]
    expert_count = router_weight.shape[1]
    head_size = keyval_weight.shape[1] // 2
    choice_count = routes.shape[1]
    seq_count = lax.axis_size("seq")
    seq_length = token_count * seq_count
    score_scale = head_size ** (-0.5)
    key_rows = min(1024, seq_length)
    query_rows = token_count * choice_count
    block_rows = min(1024, query_rows)
    doc_ends = jnp.cumsum(lengths[0])
    positions = jnp.arange(seq_length, dtype=jnp.int32)
    doc_all = jnp.sum((positions[:, None] >= doc_ends[None, :]).astype(jnp.int32), axis=1)
    my_index = lax.axis_index("seq")
    doc_shards = doc_all.reshape(seq_count, token_count)
    doc_mine = doc_shards[my_index]
    doc_all = doc_shards[my_index ^ jnp.arange(seq_count)].reshape(-1)
    doc_rows = jnp.repeat(doc_mine, choice_count)
    inputs = tokens.astype(jnp.float32)
    hidden = to_low(norm_rows(inputs, gain_one_f, shift_one_f))
    logits = dot_plain(hidden, router_weight)
    onehot = (
        routes[:, :, None] == jnp.arange(expert_count, dtype=jnp.int32)[None, None, :]
    ).astype(jnp.float32)
    picked = jnp.sum(logits[:, None, :] * onehot, axis=2)
    gate_weights = jax.nn.softmax(picked, axis=-1)
    query_all = dot_plain(hidden, query_weight).reshape(token_count, expert_count, head_size)
    queries = to_low(pick_rows(query_all, onehot)).reshape(query_rows, head_size)
    keyval_mine = to_low(dot_plain(hidden, keyval_weight))
    shards = [keyval_mine]
    for mask in range(1, seq_count):
        shards.append(exchange(keyval_mine, ("seq", mask)))
    keyval_all = jnp.concatenate(shards, axis=0)
    totals = []
    attn_parts = []
    for row_start in range(0, query_rows, block_rows):
        query_block = queries[row_start : row_start + block_rows]
        doc_block = doc_rows[row_start : row_start + block_rows]
        attn_block, log_total = attention_forward(
            query_block, doc_block, keyval_all, doc_all, key_rows, score_scale
        )
        totals.append(log_total)
        attn_parts.append(attn_block)
    log_totals = jnp.concatenate(totals, axis=0)
    attn_rows = jnp.concatenate(attn_parts, axis=0)
    attn_three = attn_rows.reshape(token_count, choice_count, head_size)
    mixed_heads = to_low(
        spread_rows(attn_three * gate_weights[:, :, None], onehot).reshape(
            token_count, expert_count * head_size
        )
    )
    middle = inputs + dot_plain(mixed_heads, output_weight)
    hidden_two = to_low(norm_rows(middle, gain_two_f, shift_two_f))
    inner_pre = dot_plain(hidden_two, expand_weight) + expand_shift.astype(jnp.float32)
    active = to_low(smooth_gate(inner_pre))
    result = middle + dot_plain(active, contract_weight) + contract_shift.astype(jnp.float32)
    layer_out = result.astype(jnp.bfloat16)
    grad_contract = dot_first(active, cotangent)
    grad_contract_bias = jnp.sum(cotangent.astype(jnp.float32), axis=0)
    grad_active = dot_last(cotangent, contract_weight)
    unused_gate, gate_back = jax.vjp(smooth_gate, inner_pre)
    grad_inner = to_low(gate_back(grad_active)[0])
    grad_expand = dot_first(hidden_two, grad_inner)
    grad_expand_bias = jnp.sum(grad_inner.astype(jnp.float32), axis=0)
    grad_hidden_two = dot_last(grad_inner, expand_weight)
    unused_norm, norm_back = jax.vjp(norm_rows, middle, gain_two_f, shift_two_f)
    grad_mid_norm, grad_second_gain, grad_second_shift = norm_back(grad_hidden_two)
    grad_middle = cotangent.astype(jnp.float32) + grad_mid_norm
    grad_branch = to_low(grad_middle)
    grad_output_map = dot_first(mixed_heads, grad_branch)
    grad_mixed = dot_last(grad_branch, output_weight).reshape(token_count, expert_count, head_size)
    grad_weighted = pick_rows(grad_mixed, onehot)
    grad_gates = jnp.sum(grad_weighted * attn_three, axis=-1)
    grad_attn = to_low(grad_weighted * gate_weights[:, :, None]).reshape(query_rows, head_size)
    grad_picked = gate_weights * (
        grad_gates - jnp.sum(gate_weights * grad_gates, axis=-1, keepdims=True)
    )
    grad_logits = to_low(jnp.sum(grad_picked[:, :, None] * onehot, axis=1))
    grad_router = dot_first(hidden, grad_logits)
    grad_hidden = dot_last(grad_logits, router_weight)
    delta_rows = jnp.sum(grad_attn.astype(jnp.float32) * attn_rows, axis=-1)
    block_starts = list(range(0, query_rows, block_rows))

    def key_step(block_index, carry):
        grad_kv_all, grad_query_all = carry
        offset = block_index * key_rows
        key_value = lax.dynamic_slice_in_dim(keyval_all, offset, key_rows, 0)
        doc_keys = lax.dynamic_slice_in_dim(doc_all, offset, key_rows, 0)
        query_parts = []
        kv_block = jnp.zeros((key_rows, 2 * head_size), jnp.float32)
        for row_start in block_starts:
            part_rows = slice(row_start, row_start + block_rows)
            grad_query, grad_kv_block = block_backward(
                queries[part_rows],
                doc_rows[part_rows],
                log_totals[part_rows],
                delta_rows[part_rows],
                grad_attn[part_rows],
                key_value,
                doc_keys,
                score_scale,
            )
            kv_block = kv_block + grad_kv_block
            query_parts.append(grad_query)
        grad_kv_all = lax.dynamic_update_slice_in_dim(grad_kv_all, kv_block, offset, 0)
        return (grad_kv_all, grad_query_all + jnp.concatenate(query_parts, axis=0))

    key_start = (
        jnp.zeros((seq_length, 2 * head_size), jnp.float32),
        jnp.zeros((query_rows, head_size), jnp.float32),
    )
    grad_kv_all, query_total = lax.fori_loop(0, seq_length // key_rows, key_step, key_start)
    grad_parts = to_low(grad_kv_all).reshape(seq_count, token_count, -1)
    grad_kv_sum = grad_kv_all[:token_count]
    for mask in range(1, seq_count):
        grad_kv_sum = grad_kv_sum + exchange(grad_parts[mask], ("seq", mask)).astype(jnp.float32)
    grad_kv_mine = to_low(grad_kv_sum)
    grad_queries = to_low(query_total * score_scale).reshape(token_count, choice_count, head_size)
    placed = to_low(
        spread_rows(grad_queries.astype(jnp.float32), onehot).reshape(
            token_count, expert_count * head_size
        )
    )
    grad_query_map = dot_first(hidden, placed)
    grad_keyval = dot_first(hidden, grad_kv_mine)
    grad_hidden = (
        grad_hidden + dot_last(placed, query_weight) + dot_last(grad_kv_mine, keyval_weight)
    )
    unused_first, first_back = jax.vjp(norm_rows, inputs, gain_one_f, shift_one_f)
    grad_in_norm, grad_first_gain, grad_first_shift = first_back(grad_hidden)
    grad_tokens = (grad_middle + grad_in_norm).astype(jnp.bfloat16)
    grad_misc = jnp.concatenate(
        [
            grad_router,
            grad_first_gain[:, None],
            grad_first_shift[:, None],
            grad_second_gain[:, None],
            grad_second_shift[:, None],
            grad_contract_bias[:, None],
            grad_expand_bias.reshape(width, -1),
        ],
        axis=1,
    )
    grad_misc = jnp.pad(grad_misc, ((0, 0), (0, 128 - misc_width)))
    grad_small = jnp.concatenate([grad_query_map, grad_keyval, grad_misc], axis=1)
    sum_small = scatter_sum(grad_small.reshape(device_count, rows, -1), order_a[::-1])
    sum_misc = sum_small[:, query_cols + keyval_cols :]
    grad_pair = jnp.concatenate([grad_output_map, grad_expand], axis=1)
    sum_pair = scatter_sum(grad_pair.reshape(device_count, rows, -1), order_a[::-1])
    sum_contract = scatter_sum(
        grad_contract.reshape((device_count,) + contract.shape), order_b[::-1]
    )
    every_sum = (
        sum_misc[:, experts],
        sum_misc[:, experts + 1],
        sum_misc[:, :experts],
        sum_small[:, :query_cols],
        sum_small[:, query_cols : query_cols + keyval_cols],
        sum_pair[:, :query_cols],
        sum_misc[:, experts + 2],
        sum_misc[:, experts + 3],
        sum_pair[:, query_cols:],
        sum_misc[:, experts + 5 : misc_width].reshape(-1),
        sum_contract,
        sum_misc[:, experts + 4],
    )
    return (
        layer_out,
        grad_tokens,
        every_sum[0],
        every_sum[1],
        every_sum[2],
        every_sum[3],
        every_sum[4],
        every_sum[5],
        every_sum[6],
        every_sum[7],
        every_sum[8],
        every_sum[9],
        every_sum[10],
        every_sum[11],
    )


def solution(mesh):
    return jax.shard_map(
        per_device,
        mesh=mesh,
        in_specs=(
            P(("dp", "seq"), None),
            P(("dp", "seq"), None),
            P("dp", None),
            P(("dp", "seq"), None),
            P(("dp", "seq")),
            P(("dp", "seq")),
            P(("dp", "seq"), None),
            P(("dp", "seq"), None),
            P(("dp", "seq"), None),
            P(("dp", "seq"), None),
            P(("dp", "seq")),
            P(("dp", "seq")),
            P(("dp", "seq"), None),
            P(("dp", "seq")),
            P(("dp", "seq"), None),
            P(("dp", "seq")),
        ),
        out_specs=(
            P(("dp", "seq"), None),
            P(("dp", "seq"), None),
            P(("dp", "seq")),
            P(("dp", "seq")),
            P(("dp", "seq"), None),
            P(("dp", "seq"), None),
            P(("dp", "seq"), None),
            P(("dp", "seq"), None),
            P(("dp", "seq")),
            P(("dp", "seq")),
            P(("dp", "seq"), None),
            P(("dp", "seq")),
            P(("dp", "seq"), None),
            P(("dp", "seq")),
        ),
        check_vma=False,
    )
```

```python
import functools

import jax
import jax.numpy as jnp
from jax import lax
from jax.experimental import pallas as pl
from jax.experimental.pallas import tpu as pltpu
from jax.sharding import PartitionSpec as P

LOW = jnp.bfloat16
FULL = jnp.float32
FAR = 1e30
EPS = 1e-05
DOC_LANE = 64
LSE_LANE = 96
SUM_LANE = 64
MAX_LANE = 67
LANES = 128
MEGA = 1 << 20


def to_low(matrix):
    return matrix.astype(LOW)


def dot_plain(left, right):
    return lax.dot_general(left, right, (((1,), (0,)), ((), ())), preferred_element_type=FULL)


def dot_last(left, right):
    return lax.dot_general(left, right, (((1,), (1,)), ((), ())), preferred_element_type=FULL)


def dot_first(left, right):
    return lax.dot_general(left, right, (((0,), (0,)), ((), ())), preferred_element_type=FULL)


def index_bits(axis):
    size = lax.axis_size(axis)
    return [(axis, 1 << b) for b in range(size.bit_length() - 1)]


def bit_of(stage):
    axis, mask = stage
    return (lax.axis_index(axis) & mask) // mask


def exchange(block, stage):
    axis, mask = stage
    pairs = [(i, i ^ mask) for i in range(lax.axis_size(axis))]
    return lax.ppermute(block, axis, pairs)


def device_bits():
    return index_bits("dp")[::-1] + index_bits("seq")[::-1]


def stage_orders():
    dp_bits, seq_bits = index_bits("dp"), index_bits("seq")
    core, plane = dp_bits[:1], dp_bits[1:]
    return (seq_bits + plane + core, seq_bits + plane[::-1] + core)


def gather_blocks(block, stages):
    order = device_bits()
    have = []
    lead, tail = block.shape[0], block.shape[1:]
    for stage in stages:
        other = exchange(block, stage)
        position = 1 + sum(1 for s in have if order.index(s) < order.index(stage))
        swap = bit_of(stage) == 1
        first = jnp.where(swap, other, block)
        second = jnp.where(swap, block, other)
        block = jnp.stack([first, second], axis=position)
        have.append(stage)
    return block.reshape(lead, -1, tail[1])


def scatter_sum(blocks, stages):
    order = device_bits()
    left = list(order)
    lead, total, columns = blocks.shape
    value = blocks.reshape((lead,) + (2,) * len(order) + (total >> len(order), columns))
    for stage in stages:
        position = 1 + left.index(stage)
        bit = bit_of(stage)
        keep = lax.dynamic_index_in_dim(value, bit, position, keepdims=False)
        send = lax.dynamic_index_in_dim(value, 1 - bit, position, keepdims=False)
        value = keep.astype(FULL) + exchange(to_low(send), stage).astype(FULL)
        left.remove(stage)
    return value


def lane_ids(shape):
    return lax.broadcasted_iota(jnp.int32, shape, len(shape) - 1)


def row_positions(offset, rows):
    return offset + lax.broadcasted_iota(jnp.int32, (rows, 1), 0)


def in_document(bounds_ref, positions):
    return (positions >= bounds_ref[0:1, :]) & (positions < bounds_ref[1:2, :])


def three_parts(column):
    first = to_low(column).astype(FULL)
    rest = column - first
    second = to_low(rest).astype(FULL)
    return first, second, rest - second


def put_parts(base, lanes, lane, column):
    for step, part in enumerate(three_parts(column)):
        base = jnp.where(lanes == lane + step, part, base)
    return base


def normalize(matrix):
    center = matrix - jnp.mean(matrix, axis=1, keepdims=True)
    spread = jnp.mean(center * center, axis=1, keepdims=True)
    factor = lax.rsqrt(spread + EPS)
    return center * factor, factor


def norm_backward(grad, unit, factor, gain):
    scaled = grad * gain
    mean = jnp.mean(scaled, axis=1, keepdims=True)
    along = jnp.mean(scaled * unit, axis=1, keepdims=True)
    return factor * (scaled - mean - unit * along)


def half_of(route, head):
    return route % (LANES // head)


def choose(wide, route, head):
    per_tile = LANES // head
    tile = route // per_tile
    picked = wide[:, :LANES]
    for index in range(1, wide.shape[1] // LANES):
        picked = jnp.where(tile == index, wide[:, index * LANES : (index + 1) * LANES], picked)
    turned = pltpu.roll(picked, head, 1)
    lanes = lane_ids((1, LANES))
    mine = (lanes // head) == (route % per_tile)
    return jnp.where(mine, picked, turned)


def place(doubled, routes, head, width):
    lanes = lane_ids((1, LANES))
    per_tile = LANES // head
    tiles = []
    for index in range(width // LANES):
        expert = lanes // head + index * per_tile
        tile = jnp.zeros_like(doubled[0])
        for rows, route in zip(doubled, routes):
            tile = jnp.where(expert == route, rows, tile)
        tiles.append(tile)
    return jnp.concatenate(tiles, axis=1)


def doubled_head(rows, head):
    lanes = lane_ids((1, LANES))
    return jnp.where(lanes < head, rows, pltpu.roll(rows, head, 1))


def key_rows_of(kv, hot, head):
    lanes = lane_ids((1, LANES))
    kv = kv.astype(FULL)
    marks = jnp.where((lanes >= LSE_LANE) & (lanes < LSE_LANE + 3), 1.0, 0.0)
    keys = jnp.where(lanes < head, kv, jnp.where(hot, 1.0, marks))
    ones = jnp.where((lanes >= SUM_LANE) & (lanes < SUM_LANE + 3), 1.0, 0.0)
    values = jnp.where(lanes < head, pltpu.roll(kv, head, 1), ones)
    return to_low(keys), to_low(values)


def hidden_kernel(tokens_ref, side_ref, routes_ref, hidden_ref, kv_ref, gates_ref, *, experts):
    side = side_ref[...]
    vectors = side[:, LANES:].astype(FULL).T
    unit, factor = normalize(tokens_ref[...].astype(FULL))
    hidden = to_low(unit * vectors[experts : experts + 1] + vectors[experts + 1 : experts + 2])
    hidden_ref[...] = hidden
    both = dot_plain(hidden, side)
    kv_ref[...] = to_low(both[:, :LANES])
    logits = both[:, LANES:]
    lanes = lane_ids((1, LANES))
    picked = [
        jnp.sum(jnp.where(lanes == routes_ref[:, j : j + 1], logits, 0.0), axis=1, keepdims=True)
        for j in range(2)
    ]
    top = jnp.maximum(picked[0], picked[1])
    raised = [jnp.exp(p - top) for p in picked]
    total = raised[0] + raised[1]
    gates_ref[...] = jnp.where(
        lanes == 0, raised[0] / total, jnp.where(lanes == 1, raised[1] / total, 0.0)
    )


def query_kernel(
    place_ref, hidden_ref, weight_ref, routes_ref, bounds_ref, query_ref, *, head, rows
):
    wide = dot_plain(hidden_ref[...], weight_ref[...])
    lanes = lane_ids((1, LANES))
    hot = in_document(bounds_ref, row_positions(place_ref[0] + pl.program_id(0) * rows, rows))
    documents = (bounds_ref[1:2, :] > 0) & (lanes >= head)
    marks = jnp.where(documents & jnp.logical_not(hot), -FAR, 0.0)
    for j in range(2):
        rows_of = choose(wide, routes_ref[:, j : j + 1], head) * head**-0.5
        query_ref[j] = to_low(jnp.where(lanes < head, rows_of, marks))


def forward_kernel(place_ref, query_ref, kv_ref, bounds_ref, *rest, head, first, last):
    rest = list(rest)
    state_ref = None if first else rest.pop(0)
    if last:
        attn_ref, wide_ref, held = rest
    else:
        held_ref, held = rest
    step = pl.program_id(1)
    query = query_ref[...]
    rows = query.shape[0]
    key_count = kv_ref.shape[0]
    lanes = lane_ids((1, LANES))
    hot = in_document(bounds_ref, row_positions(place_ref[step], key_count))
    keys, values = key_rows_of(kv_ref[...], hot, head)
    scores = dot_last(query, keys)
    top = jnp.max(scores, axis=1, keepdims=True)

    @pl.when(step == 0)
    def _():
        if first:
            held[...] = jnp.where(lanes == MAX_LANE, -FAR, jnp.zeros((rows, LANES), FULL))
        else:
            held[...] = state_ref[...]

    before = held[...]
    old = before[:, MAX_LANE : MAX_LANE + 1]
    new = jnp.maximum(old, top)
    weights = to_low(jnp.exp(scores - new))
    after = before * jnp.exp(old - new) + dot_plain(weights, values)
    held[...] = jnp.where(lanes == MAX_LANE, new, after)

    @pl.when(step == pl.num_programs(1) - 1)
    def _():
        end = held[...]
        if last:
            total = end[:, SUM_LANE : SUM_LANE + 1]
            attn_ref[...] = jnp.where(lanes < head, end / total, 0.0)
            log_total = end[:, MAX_LANE : MAX_LANE + 1] + jnp.log(total)
            wide_ref[...] = to_low(
                put_parts(query_ref[...].astype(FULL), lanes, LSE_LANE, -log_total)
            )
        else:
            held_ref[...] = end


def middle_kernel(
    tokens_ref,
    cotangent_ref,
    attn_ref,
    gates_ref,
    routes_ref,
    vectors_ref,
    bias_ref,
    pair_ref,
    contract_ref,
    out_ref,
    grad_middle_ref,
    grad_attn_ref,
    grad_logits_ref,
    grad_pair_ref,
    grad_contract_ref,
    grad_rows_ref,
    grad_bias_ref,
    pair_sum,
    contract_sum,
    *,
    head,
):
    step = pl.program_id(0)

    @pl.when(step == 0)
    def _():
        pair_sum[...] = jnp.zeros_like(pair_sum)
        contract_sum[...] = jnp.zeros_like(contract_sum)
        grad_rows_ref[...] = jnp.zeros_like(grad_rows_ref)
        grad_bias_ref[...] = jnp.zeros_like(grad_bias_ref)

    width = tokens_ref.shape[1]
    chunks = pair_ref.shape[0] - 1
    part = contract_ref.shape[0] // chunks
    gain, shift, contract_bias = (vectors_ref[i : i + 1, :] for i in range(3))
    lanes = lane_ids((1, LANES))
    routes = [routes_ref[:, j : j + 1] for j in range(2)]
    gates = [gates_ref[:, j : j + 1] for j in range(2)]
    attn = [attn_ref[j] for j in range(2)]
    mixed = to_low(
        place([doubled_head(a, head) * g for a, g in zip(attn, gates)], routes, head, width)
    )
    middle = tokens_ref[...].astype(FULL) + dot_plain(mixed, pair_ref[0])
    unit, factor = normalize(middle)
    hidden = to_low(unit * gain + shift)
    cotangent = cotangent_ref[...]
    cotangent_full = cotangent.astype(FULL)
    out = middle + contract_bias
    grad_hidden = jnp.zeros_like(middle)
    slope = 0.7978845608028654
    cube = 0.044715
    for chunk in range(chunks):
        rows = pl.ds(chunk * part, part)
        expand = pair_ref[chunk + 1]
        contract = contract_ref[rows, :]
        inner = dot_plain(hidden, expand) + bias_ref[:, rows]
        square = inner * inner
        bent = jnp.tanh(slope * inner * (1.0 + cube * square))
        half = 0.5 * (1.0 + bent)
        active = to_low(inner * half)
        out += dot_plain(active, contract)
        steep = half + 0.5 * inner * (1.0 - bent * bent) * (slope + 3.0 * cube * slope * square)
        grad_inner_full = steep * dot_last(cotangent, contract)
        grad_inner = to_low(grad_inner_full)
        grad_bias_ref[0:1, rows] += jnp.sum(grad_inner.astype(FULL), axis=0, keepdims=True)
        contract_sum[rows, :] += dot_first(active, cotangent)
        pair_sum[chunk + 1] += dot_first(hidden, grad_inner)
        grad_hidden += dot_last(grad_inner, expand)
    out_ref[...] = to_low(out)
    grad_middle = cotangent_full + norm_backward(grad_hidden, unit, factor, gain)
    grad_middle_ref[...] = grad_middle
    grad_rows_ref[0:1, :] += jnp.sum(grad_hidden * unit, axis=0, keepdims=True)
    grad_rows_ref[1:2, :] += jnp.sum(grad_hidden, axis=0, keepdims=True)
    grad_rows_ref[2:3, :] += jnp.sum(cotangent_full, axis=0, keepdims=True)
    branch = to_low(grad_middle)
    pair_sum[0] += dot_first(mixed, branch)
    grad_mixed = dot_last(branch, pair_ref[0])
    grad_gates = []
    for j in range(2):
        weighted = jnp.where(lanes < head, choose(grad_mixed, routes[j], head), 0.0)
        grad_gates.append(jnp.sum(weighted * attn[j], axis=1, keepdims=True))
        grad_attn = to_low(weighted * gates[j]).astype(FULL)
        delta = jnp.sum(grad_attn * attn[j], axis=1, keepdims=True)
        grad_attn_ref[j] = to_low(put_parts(grad_attn, lanes, SUM_LANE, -delta))
    mean = gates[0] * grad_gates[0] + gates[1] * grad_gates[1]
    grad_logits = jnp.zeros(gates_ref.shape, FULL)
    for j in range(2):
        grad_logits = jnp.where(lanes == routes[j], gates[j] * (grad_gates[j] - mean), grad_logits)
    grad_logits_ref[...] = to_low(grad_logits)

    @pl.when(step == pl.num_programs(0) - 1)
    def _():
        grad_pair_ref[...] = to_low(pair_sum[...])
        grad_contract_ref[...] = to_low(contract_sum[...])


def backward_kernel(
    place_ref, query_ref, grad_ref, kv_ref, bounds_ref, *rest, head, first, rows
):
    rest = list(rest)
    before_ref = None if first else rest.pop(0)
    grad_query_ref, grad_kv_ref, total = rest
    block, step = pl.program_id(0), pl.program_id(1)
    lanes = lane_ids((1, LANES))
    key_count = kv_ref.shape[0]
    hot = in_document(bounds_ref, row_positions(place_ref[block], key_count))
    keys, values = key_rows_of(kv_ref[...], hot, head)
    query = query_ref[...]
    grad = grad_ref[...]
    probs = jnp.exp(dot_last(keys, query))
    grad_scores = to_low(probs * dot_last(values, grad))
    only_query = to_low(jnp.where(lanes < head, query.astype(FULL), 0.0))
    turned = pltpu.roll(grad.astype(FULL), head, 1)
    only_grad = to_low(jnp.where(lanes < head, 0.0, turned))
    update = dot_plain(grad_scores, only_query) + dot_plain(to_low(probs), only_grad)

    @pl.when(step == 0)
    def _():
        total[...] = update

    @pl.when(step > 0)
    def _():
        total[...] += update

    @pl.when(step == pl.num_programs(1) - 1)
    def _():
        grad_kv_ref[...] = to_low(total[...])

    here = pl.ds(pl.multiple_of(step * rows, rows), rows)
    grad_query = dot_first(grad_scores, keys)

    @pl.when(block == 0)
    def _():
        if first:
            grad_query_ref[here, :] = grad_query
        else:
            grad_query_ref[here, :] = before_ref[here, :] + grad_query

    @pl.when(block > 0)
    def _():
        grad_query_ref[here, :] += grad_query


def placed_kernel(
    grad_query_ref, hidden_ref, routes_ref, grad_logits_ref, weight_ref, side_ref,
    grad_hidden_ref, grad_weight_ref, grad_router_ref, total, router_total, *, head
):
    step = pl.program_id(0)

    @pl.when(step == 0)
    def _():
        total[...] = jnp.zeros_like(total)
        router_total[...] = jnp.zeros_like(router_total)

    width = hidden_ref.shape[1]
    lanes = lane_ids((1, LANES))
    rows = [
        doubled_head(to_low(grad_query_ref[j] * head**-0.5).astype(FULL), head) for j in range(2)
    ]
    placed = to_low(place(rows, [routes_ref[:, j : j + 1] for j in range(2)], head, width))
    hidden = hidden_ref[...]
    grad_logits = grad_logits_ref[...]
    total[...] += dot_first(hidden, placed)
    router_total[...] += dot_first(hidden, grad_logits)
    grad_hidden_ref[...] = dot_last(placed, weight_ref[...]) + dot_last(
        grad_logits, side_ref[:, LANES:]
    )

    @pl.when(step == pl.num_programs(0) - 1)
    def _():
        grad_weight_ref[...] = to_low(total[...])
        grad_router_ref[...] = router_total[...]


def last_kernel(
    tokens_ref, hidden_ref, grad_hidden_ref, grad_middle_ref, side_ref, rows_ref, grad_router_ref,
    own_ref, *rest, experts, others
):
    other_refs = rest[:others]
    grad_tokens_ref, grad_side_ref, total, sums = rest[others:]
    step = pl.program_id(0)

    @pl.when(step == 0)
    def _():
        total[...] = jnp.zeros_like(total)
        sums[...] = jnp.zeros_like(sums)

    side = side_ref[...]
    gain = side[:, LANES:].astype(FULL).T[experts : experts + 1]
    grad_kv = own_ref[...].astype(FULL)
    for ref in other_refs:
        grad_kv += ref[...].astype(FULL)
    grad_kv = to_low(grad_kv)
    total[...] += dot_first(hidden_ref[...], grad_kv)
    grad_hidden = grad_hidden_ref[...] + dot_last(grad_kv, side[:, :LANES])
    unit, factor = normalize(tokens_ref[...].astype(FULL))
    grad_tokens_ref[...] = to_low(
        grad_middle_ref[...] + norm_backward(grad_hidden, unit, factor, gain)
    )
    sums[0:1, :] += jnp.sum(grad_hidden * unit, axis=0, keepdims=True)
    sums[1:2, :] += jnp.sum(grad_hidden, axis=0, keepdims=True)

    @pl.when(step == pl.num_programs(0) - 1)
    def _():
        width = sums.shape[1]
        ahead = jnp.zeros((experts, width), FULL)
        behind = jnp.zeros((LANES - experts - 8, width), FULL)
        rows = lax.broadcasted_iota(jnp.int32, (8, 1), 0)
        vectors = jnp.where(rows < 2, sums[...], rows_ref[...])
        columns = jnp.concatenate([ahead, vectors, behind], axis=0).T
        grad_side_ref[:, :LANES] = to_low(total[...])
        grad_side_ref[:, LANES:] = to_low(columns + grad_router_ref[...])


def whole_spec(shape):
    return pl.BlockSpec(tuple(shape), lambda *ids: (0,) * len(shape))


def smem_spec():
    return pl.BlockSpec(memory_space=pltpu.SMEM)


def call(kernel, name, grid, in_specs, out_specs, out_shape, scratch=(), flops=0, moved=0):
    return pl.pallas_call(
        kernel,
        grid=grid,
        in_specs=in_specs,
        out_specs=out_specs,
        out_shape=out_shape,
        scratch_shapes=list(scratch),
        compiler_params=pltpu.CompilerParams(
            dimension_semantics=("arbitrary",) * len(grid), vmem_limit_bytes=48 * MEGA
        ),
        cost_estimate=pl.CostEstimate(flops=flops, bytes_accessed=moved, transcendentals=0),
        name=name,
    )


def shape_of(shape, dtype):
    return jax.ShapeDtypeStruct(tuple(shape), dtype)


def mask_groups(seq_count, first_masks):
    rest = [m for m in range(1, seq_count) if m not in first_masks]
    order = [m for m in first_masks if m < seq_count] + rest
    size = max(1, -(-len(order) // 3))
    return [order[i : i + size] for i in range(0, len(order), size)]


def per_device(
    tokens, routes, lengths, cotangent, first_gain, first_shift, router, query_map, keyval,
    output_map, second_gain, second_shift, expand, expand_bias, contract, contract_bias
):
    order_a, order_b = stage_orders()
    token_count, width = tokens.shape
    rows = first_gain.shape[0]
    experts = router.shape[1]
    head = keyval.shape[1] // 2
    inner_width = expand.shape[1]
    chunks = inner_width // width
    seq_count = lax.axis_size("seq")
    my_index = lax.axis_index("seq")

    columns = [first_gain, first_shift, second_gain, second_shift, contract_bias]
    extra = expand_bias.shape[0] // rows
    used = experts + len(columns) + extra
    side_mine = jnp.concatenate(
        [keyval, router]
        + [c[:, None] for c in columns]
        + [expand_bias.reshape(rows, extra), jnp.zeros((rows, LANES - used), FULL)],
        axis=1,
    )
    small_mine = to_low(jnp.concatenate([query_map, side_mine], axis=1))
    small_all = gather_blocks(small_mine[None], order_a)[0]
    query_weight = small_all[:, :width]
    side = small_all[:, width:]
    pair_mine = to_low(
        jnp.stack([output_map] + [expand[:, c * width : (c + 1) * width] for c in range(chunks)])
    )
    pair = gather_blocks(pair_mine, order_a)
    contract_all = gather_blocks(to_low(contract)[None], order_b)[0]
    vector_columns = side[:, LANES + experts + 2 : LANES + used].astype(FULL)
    vectors = jnp.pad(vector_columns[:, :3].T, ((0, 5), (0, 0)))
    bias = vector_columns[:, 3:].reshape(1, inner_width)

    ends = jnp.cumsum(lengths[0])
    starts = ends - lengths[0]
    count = ends.shape[0]
    fill = (DOC_LANE, LANES - DOC_LANE - count)
    bounds = jnp.pad(
        jnp.stack([jnp.pad(starts, fill, constant_values=1 << 30), jnp.pad(ends, fill)]),
        ((0, 6), (0, 0)),
    ).astype(jnp.int32)

    block = min(256, token_count)
    steps = token_count // block
    row_block = lambda n: pl.BlockSpec((block, n), lambda i: (i, 0))
    two_block = pl.BlockSpec((2, block, LANES), lambda i: (0, i, 0))
    side_width = side.shape[1]
    hidden, kv_mine, gates = call(
        functools.partial(hidden_kernel, experts=experts),
        "hidden",
        (steps,),
        [row_block(width), whole_spec(side.shape), row_block(2)],
        [row_block(width), row_block(LANES), row_block(LANES)],
        [
            shape_of((token_count, width), LOW),
            shape_of((token_count, LANES), LOW),
            shape_of((token_count, LANES), FULL),
        ],
        flops=2 * token_count * width * side_width,
        moved=4 * token_count * width,
    )(tokens, side, routes)

    def place_of(masks):
        return jnp.stack([(my_index ^ m) * token_count for m in masks]).astype(jnp.int32)

    shards = {0: kv_mine}
    for mask in list(range(2, seq_count)) + [1]:
        if mask < seq_count:
            shards[mask] = exchange(kv_mine, ("seq", mask))
    queries = call(
        functools.partial(query_kernel, head=head, rows=block),
        "queries",
        (steps,),
        [smem_spec(), row_block(width), whole_spec(query_weight.shape), row_block(2), whole_spec(bounds.shape)],
        two_block,
        shape_of((2, token_count, LANES), LOW),
        flops=2 * token_count * width * width,
        moved=4 * token_count * width,
    )(place_of([0]), hidden, query_weight, routes, bounds)
    query_rows = queries.reshape(2 * token_count, LANES)
    row_count = 2 * token_count
    part = min(1024, row_count)
    parts = row_count // part

    def keys_of(masks):
        return jnp.concatenate([shards[m] for m in masks], axis=0) if len(masks) > 1 else shards[masks[0]]

    groups = [[0]] + mask_groups(seq_count, [1, 2, 3])
    state = None
    for index, masks in enumerate(groups):
        last = index == len(groups) - 1
        q_spec = pl.BlockSpec((part, LANES), lambda i, g: (i, 0))
        outs = (
            [shape_of((row_count, LANES), FULL), shape_of((row_count, LANES), LOW)]
            if last
            else shape_of((row_count, LANES), FULL)
        )
        state = call(
            functools.partial(forward_kernel, head=head, first=state is None, last=last),
            "attention_forward",
            (parts, len(masks)),
            [
                smem_spec(),
                q_spec,
                pl.BlockSpec((token_count, LANES), lambda i, g: (g, 0)),
                whole_spec(bounds.shape),
            ]
            + ([] if state is None else [q_spec]),
            [q_spec, q_spec] if last else q_spec,
            outs,
            [pltpu.VMEM((part, LANES), FULL)],
            flops=4 * row_count * token_count * len(masks) * 4 * head,
            moved=4 * row_count * LANES,
        )(place_of(masks), query_rows, keys_of(masks), bounds, *([] if state is None else [state]))
    attn, wide_queries = state

    out, grad_middle, grad_attn, grad_logits, grad_pair, grad_contract, grad_rows, grad_bias = call(
        functools.partial(middle_kernel, head=head),
        "feed_forward",
        (steps,),
        [
            row_block(width),
            row_block(width),
            two_block,
            row_block(LANES),
            row_block(2),
            whole_spec(vectors.shape),
            whole_spec(bias.shape),
            whole_spec(pair.shape),
            whole_spec(contract_all.shape),
        ],
        [
            row_block(width),
            row_block(width),
            two_block,
            row_block(LANES),
            whole_spec(pair.shape),
            whole_spec(contract_all.shape),
            whole_spec((8, width)),
            whole_spec((8, inner_width)),
        ],
        [
            shape_of((token_count, width), LOW),
            shape_of((token_count, width), FULL),
            shape_of((2, token_count, LANES), LOW),
            shape_of((token_count, LANES), LOW),
            shape_of(pair.shape, LOW),
            shape_of(contract_all.shape, LOW),
            shape_of((8, width), FULL),
            shape_of((8, inner_width), FULL),
        ],
        [pltpu.VMEM(pair.shape, FULL), pltpu.VMEM(contract_all.shape, FULL)],
        flops=2 * token_count * width * (3 * width + 6 * inner_width),
        moved=12 * width * inner_width,
    )(
        tokens, cotangent, attn.reshape(2, token_count, LANES), gates, routes, vectors, bias,
        pair, contract_all
    )

    grad_rows_in = grad_attn.reshape(row_count, LANES)
    grad_query = None
    kv_parts = {}
    for masks in mask_groups(seq_count, [2, 3, 1]) + [[0]]:
        q_spec = pl.BlockSpec((part, LANES), lambda g, i: (i, 0))
        k_spec = pl.BlockSpec((token_count, LANES), lambda g, i: (g, 0))
        full = whole_spec((row_count, LANES))
        grad_query, grad_keys = call(
            functools.partial(backward_kernel, head=head, first=grad_query is None, rows=part),
            "attention_backward",
            (len(masks), parts),
            [smem_spec(), q_spec, q_spec, k_spec, whole_spec(bounds.shape)]
            + ([] if grad_query is None else [full]),
            [full, k_spec],
            [
                shape_of((row_count, LANES), FULL),
                shape_of((token_count * len(masks), LANES), LOW),
            ],
            [pltpu.VMEM((token_count, LANES), FULL)],
            flops=10 * row_count * token_count * len(masks) * 4 * head,
            moved=8 * row_count * LANES,
        )(
            place_of(masks), wide_queries, grad_rows_in, keys_of(masks), bounds,
            *([] if grad_query is None else [grad_query])
        )
        for index, mask in enumerate(masks):
            piece = grad_keys[index * token_count : (index + 1) * token_count]
            kv_parts[mask] = piece if mask == 0 else exchange(piece, ("seq", mask))

    grad_hidden, grad_query_map, grad_router = call(
        functools.partial(placed_kernel, head=head),
        "query_gradient",
        (steps,),
        [
            two_block,
            row_block(width),
            row_block(2),
            row_block(LANES),
            whole_spec(query_weight.shape),
            whole_spec(side.shape),
        ],
        [row_block(width), whole_spec((width, width)), whole_spec((width, LANES))],
        [
            shape_of((token_count, width), FULL),
            shape_of((width, width), LOW),
            shape_of((width, LANES), FULL),
        ],
        [pltpu.VMEM((width, width), FULL), pltpu.VMEM((width, LANES), FULL)],
        flops=4 * token_count * width * width,
        moved=8 * token_count * width,
    )(grad_query.reshape(2, token_count, LANES), hidden, routes, grad_logits, query_weight, side)

    vector_rows = jnp.concatenate(
        [jnp.zeros((2, width), FULL), grad_rows[:3], grad_bias[0].reshape(width, extra).T[:3]]
    )
    spare = grad_bias[0].reshape(width, extra)[:, 3:]
    others = [kv_parts[m] for m in range(1, seq_count)]
    grad_tokens, grad_side = call(
        functools.partial(last_kernel, experts=experts, others=len(others)),
        "key_gradient",
        (steps,),
        [
            row_block(width),
            row_block(width),
            row_block(width),
            row_block(width),
            whole_spec(side.shape),
            whole_spec((8, width)),
            whole_spec((width, LANES)),
        ]
        + [row_block(LANES)] * (1 + len(others)),
        [row_block(width), whole_spec(side.shape)],
        [shape_of((token_count, width), LOW), shape_of(side.shape, LOW)],
        [pltpu.VMEM((width, LANES), FULL), pltpu.VMEM((8, width), FULL)],
        flops=4 * token_count * width * LANES,
        moved=12 * token_count * width,
    )(
        tokens, hidden, grad_hidden, grad_middle, side, vector_rows,
        grad_router + jnp.pad(spare, ((0, 0), (experts + 8, LANES - experts - 8 - spare.shape[1]))),
        kv_parts[0], *others
    )

    sum_pair = scatter_sum(grad_pair, order_a[::-1])
    sum_contract = scatter_sum(grad_contract[None], order_b[::-1])[0]
    sum_query = scatter_sum(grad_query_map[None], order_a[::-1])[0]
    sum_side = scatter_sum(grad_side[None], order_a[::-1])[0]
    sum_misc = sum_side[:, LANES:]
    sum_expand = jnp.concatenate([sum_pair[c + 1] for c in range(chunks)], axis=1)
    return (
        out,
        grad_tokens,
        sum_misc[:, experts],
        sum_misc[:, experts + 1],
        sum_misc[:, :experts],
        sum_query,
        sum_side[:, :LANES],
        sum_pair[0],
        sum_misc[:, experts + 2],
        sum_misc[:, experts + 3],
        sum_expand,
        sum_misc[:, experts + 5 : used].reshape(-1),
        sum_contract,
        sum_misc[:, experts + 4],
    )


def solution(mesh):
    both = ("dp", "seq")
    rows, vector = P(both, None), P(both)
    return jax.shard_map(
        per_device,
        mesh=mesh,
        in_specs=(
            rows, rows, P("dp", None), rows, vector, vector, rows, rows, rows, rows, vector, vector,
            rows, vector, rows, vector
        ),
        out_specs=(
            rows, rows, vector, vector, rows, rows, rows, rows, vector, vector, rows, vector, rows,
            vector
        ),
        check_vma=False,
    )
```

```python
import functools

import jax
import jax.numpy as jnp
from jax import lax
from jax.experimental import pallas as pl
from jax.experimental.pallas import tpu as pltpu
from jax.sharding import PartitionSpec as P

LOW = jnp.bfloat16
FULL = jnp.float32
FAR = 1e30
EPS = 1e-05
DOC_LANE = 64
LSE_LANE = 96
SUM_LANE = 64
MAX_LANE = 67
BIAS_LANE = 64
LANES = 128
MEGA = 1 << 20
FORWARD_COST = 2.0
BACKWARD_COST = 3.0
FEED_COST = 8.0
FEED_LIMIT = 24


def to_low(matrix):
    return matrix.astype(LOW)


def dot_plain(left, right):
    return lax.dot_general(left, right, (((1,), (0,)), ((), ())), preferred_element_type=FULL)


def dot_last(left, right):
    return lax.dot_general(left, right, (((1,), (1,)), ((), ())), preferred_element_type=FULL)


def dot_first(left, right):
    return lax.dot_general(left, right, (((0,), (0,)), ((), ())), preferred_element_type=FULL)


class Group:
    def __init__(self, axis, shift, size):
        self.axis, self.shift, self.size = axis, shift, size

    def index(self):
        return (lax.axis_index(self.axis) >> self.shift) & (self.size - 1)

    def exchange(self, block, mask):
        step = mask << self.shift
        pairs = [(i, i ^ step) for i in range(lax.axis_size(self.axis))]
        return lax.ppermute(block, self.axis, pairs)


def scalar(value):
    return value.astype(jnp.int32).reshape(1)


def by_place(blocks, index):
    blocks = list(blocks)
    for bit in range(len(blocks).bit_length() - 1):
        swap = (index >> bit) & 1 == 1
        blocks = [jnp.where(swap, blocks[i ^ (1 << bit)], blocks[i]) for i in range(len(blocks))]
    return blocks


def merge_kernel(index_ref, *refs, count):
    out_ref = refs[count]
    rows = refs[0].shape[1]
    for mask in range(count):
        start = pl.multiple_of((index_ref[0] ^ mask) * rows, rows)
        out_ref[:, pl.ds(start, rows), :] = refs[mask][...]


def merge(blocks, group):
    lead, rows, columns = blocks[0].shape
    if rows % 16:
        return jnp.concatenate(by_place(blocks, group.index()), axis=1)
    return call(
        functools.partial(merge_kernel, count=len(blocks)),
        "merge",
        shape_of((lead, rows * len(blocks), columns), blocks[0].dtype),
        0.1,
        scalars=1,
    )(scalar(group.index()), *blocks)


def cut_kernel(index_ref, *refs, sizes, count):
    outs = refs[len(refs) - count :]
    refs = list(refs[: len(refs) - count])
    sets = [[refs.pop(0) for _ in range(size)] for size in sizes]
    width = outs[0].shape[1]
    for mask in range(count):
        row = column = 0
        for terms in sets:
            lead, total, columns = terms[0].shape
            rows = total // count
            start = pl.multiple_of((index_ref[0] ^ mask) * rows, rows)
            for at in range(lead):
                value = sum(term[at, pl.ds(start, rows), :].astype(FULL) for term in terms)
                outs[mask][row : row + rows, column : column + columns] = to_low(value)
                column = (column + columns) % width
                row += 0 if column else rows


def cut(sets, group, width):
    count = group.size
    sets = [[t.reshape((-1,) + t.shape[-2:]) for t in terms] for terms in sets]
    rows = [terms[0].shape[1] // count for terms in sets]
    total = sum(t[0].shape[0] * r * t[0].shape[2] for t, r in zip(sets, rows)) // width
    if any(r % 16 for r in rows):
        index = group.index()
        results = []
        for mask in range(count):
            parts = []
            for terms, r in zip(sets, rows):
                value = sum(t.astype(FULL) for t in terms)
                value = lax.dynamic_slice_in_dim(value, (index ^ mask) * r, r, 1)
                parts += [value[at] for at in range(value.shape[0])]
            axis = 1 if parts[0].shape[1] < width else 0
            results.append(to_low(jnp.concatenate(parts, axis=axis)))
        return results
    return call(
        functools.partial(cut_kernel, sizes=[len(t) for t in sets], count=count),
        "cut",
        [shape_of((total, width), LOW)] * count,
        0.1,
        scalars=1,
    )(scalar(group.index()), *[t for terms in sets for t in terms])


def together(*values):
    return lax.optimization_barrier(values)


class Move:
    def __init__(self, group, blocks, masks=None):
        self.group = group
        self.masks = list(range(1, group.size)) if masks is None else masks
        self.blocks = blocks if isinstance(blocks, dict) else {m: blocks for m in self.masks}

    def start(self):
        return [self.group.exchange(self.blocks[m], m) for m in self.masks]

    def end(self, got):
        self.got = dict(zip(self.masks, got))


def phase(moves, work=lambda: ()):
    moved = [m.start() for m in moves]
    done = work()
    ended = list(together(*[x for xs in moved for x in xs], *done))
    for move in moves:
        move.end([ended.pop(0) for _ in move.masks])
    return ended


def lane_ids(shape):
    return lax.broadcasted_iota(jnp.int32, shape, len(shape) - 1)


def row_positions(offset, rows):
    return offset + lax.broadcasted_iota(jnp.int32, (rows, 1), 0)


def in_document(bounds_ref, positions):
    return (positions >= bounds_ref[0:1, :]) & (positions < bounds_ref[1:2, :])


def three_parts(column):
    first = to_low(column).astype(FULL)
    rest = column - first
    second = to_low(rest).astype(FULL)
    return first, second, rest - second


def put_parts(base, lanes, lane, column):
    for step, part in enumerate(three_parts(column)):
        base = jnp.where(lanes == lane + step, part, base)
    return base


def normalize(matrix):
    center = matrix - jnp.mean(matrix, axis=1, keepdims=True)
    spread = jnp.mean(center * center, axis=1, keepdims=True)
    factor = lax.rsqrt(spread + EPS)
    return center * factor, factor


def norm_backward(grad, unit, factor, gain):
    scaled = grad * gain
    mean = jnp.mean(scaled, axis=1, keepdims=True)
    along = jnp.mean(scaled * unit, axis=1, keepdims=True)
    return factor * (scaled - mean - unit * along)


def half_of(route, head):
    return route % (LANES // head)


def choose(wide, route, head):
    per_tile = LANES // head
    tile = route // per_tile
    picked = wide[:, :LANES]
    for index in range(1, wide.shape[1] // LANES):
        picked = jnp.where(tile == index, wide[:, index * LANES : (index + 1) * LANES], picked)
    turned = pltpu.roll(picked, head, 1)
    lanes = lane_ids((1, LANES))
    mine = (lanes // head) == (route % per_tile)
    return jnp.where(mine, picked, turned)


def place(doubled, routes, head, width):
    lanes = lane_ids((1, LANES))
    per_tile = LANES // head
    tiles = []
    for index in range(width // LANES):
        expert = lanes // head + index * per_tile
        tile = jnp.zeros_like(doubled[0])
        for rows, route in zip(doubled, routes):
            tile = jnp.where(expert == route, rows, tile)
        tiles.append(tile)
    return jnp.concatenate(tiles, axis=1)


def doubled_head(rows, head):
    lanes = lane_ids((1, LANES))
    return jnp.where(lanes < head, rows, pltpu.roll(rows, head, 1))


def key_rows_of(kv, hot, head):
    lanes = lane_ids((1, LANES))
    kv = kv.astype(FULL)
    marks = jnp.where((lanes >= LSE_LANE) & (lanes < LSE_LANE + 3), 1.0, 0.0)
    keys = jnp.where(lanes < head, kv, jnp.where(hot, 1.0, marks))
    ones = jnp.where((lanes >= SUM_LANE) & (lanes < SUM_LANE + 3), 1.0, 0.0)
    values = jnp.where(lanes < head, pltpu.roll(kv, head, 1), ones)
    return to_low(keys), to_low(values)


def as_column(row):
    rows = row.shape[1]
    lanes = lax.broadcasted_iota(jnp.int32, (rows, rows), 1)
    here = lax.broadcasted_iota(jnp.int32, (rows, rows), 0)
    return jnp.sum(jnp.where(lanes == here, row, 0.0), axis=1, keepdims=True)


def as_row(column):
    rows = column.shape[0]
    lanes = lax.broadcasted_iota(jnp.int32, (rows, rows), 1)
    here = lax.broadcasted_iota(jnp.int32, (rows, rows), 0)
    return jnp.sum(jnp.where(lanes == here, column, 0.0), axis=0, keepdims=True)


def pack_kernel(
    *refs, count
):
    small_ref, large_ref = refs[count : count + 2]
    held, semaphores = refs[count + 2 : -1], refs[-1]
    copies = [
        pltpu.make_async_copy(refs[i], held[i], semaphores.at[i]) for i in range(count)
    ]
    for copy in copies:
        copy.start()
    for copy in copies:
        copy.wait()
    (
        query_ref, keyval_ref, router_ref, gain_ref, shift_ref, gain_two_ref, shift_two_ref,
        contract_bias_ref, expand_bias_ref, output_ref, expand_ref, contract_ref
    ) = held
    rows, width = query_ref.shape
    experts = router_ref.shape[1]
    keyval_width = keyval_ref.shape[1]
    small_ref[:, :width] = to_low(query_ref[...])
    small_ref[:, width : width + keyval_width] = to_low(keyval_ref[...])
    lanes = lane_ids((1, LANES))
    side = jnp.concatenate([router_ref[...], jnp.zeros((rows, LANES - experts), FULL)], axis=1)
    vectors = [gain_ref, shift_ref, gain_two_ref, shift_two_ref, contract_bias_ref]
    for index, ref in enumerate(vectors):
        side = jnp.where(lanes == experts + index, as_column(ref[...]), side)
    extra = expand_bias_ref.shape[1]
    bias = jnp.pad(expand_bias_ref[...], ((0, 0), (BIAS_LANE, LANES - BIAS_LANE - extra)))
    first = lax.broadcasted_iota(jnp.int32, (rows, 1), 0) == 0
    side = side + jnp.where(first, bias, 0.0)
    small_ref[:, width + keyval_width :] = to_low(side)
    large = [output_ref[...]]
    large += [
        expand_ref[:, c * width : (c + 1) * width] for c in range(expand_ref.shape[1] // width)
    ]
    large_ref[...] = to_low(jnp.concatenate(large + [contract_ref[...]], axis=0))


def vectors_kernel(small_ref, vectors_ref, bias_ref, *, experts, rows):
    misc = small_ref[:, small_ref.shape[1] - LANES :].astype(FULL)
    turned = misc.T
    vectors_ref[...] = turned[experts + 2 : experts + 10]
    count = misc.shape[0] // rows
    each = bias_ref.shape[1] // count
    per_tile = LANES // each
    firsts = misc.reshape(count, rows, LANES)[:, 0, :].reshape(count // per_tile, per_tile, LANES)
    lanes = lane_ids((1, LANES))
    tiles = jnp.zeros((count // per_tile, LANES), FULL)
    for k in range(per_tile):
        moved = pltpu.roll(firsts[:, k, :], (k * each - BIAS_LANE) % LANES, 1)
        tiles = jnp.where(lanes // each == k, moved, tiles)
    for index in range(count // per_tile):
        bias_ref[:, index * LANES : (index + 1) * LANES] = tiles[index : index + 1]


def bias_rows(bias, count, rows):
    each = bias.shape[1] // count
    per_tile = LANES // each
    tiles = jnp.concatenate(
        [bias[:, i : i + LANES] for i in range(0, bias.shape[1], LANES)], axis=0
    )
    lanes = lane_ids((1, LANES))
    mine = (lanes >= BIAS_LANE) & (lanes < BIAS_LANE + each)
    parts = [
        jnp.where(mine, pltpu.roll(tiles, (BIAS_LANE - k * each) % LANES, 1), 0.0)
        for k in range(per_tile)
    ]
    firsts = jnp.stack(parts, axis=1).reshape(count, 1, LANES)
    here = lax.broadcasted_iota(jnp.int32, (1, rows, 1), 1) == 0
    return jnp.where(here, firsts, 0.0).reshape(count * rows, LANES)


def first_kernel(tokens_ref, routes_ref, lengths_ref, unit_ref, columns_ref, bounds_ref):
    unit_ref[...] = normalize(tokens_ref[...].astype(FULL))[0]
    routes = routes_ref[...].astype(FULL)
    rows = jnp.concatenate([routes, jnp.zeros((8 - routes.shape[0], routes.shape[1]), FULL)], axis=0)
    columns_ref[:, :8] = rows.T.astype(jnp.int32)
    count = lengths_ref.shape[1]
    lanes = lane_ids((1, LANES))
    rest = jnp.zeros((1, LANES - DOC_LANE - count), jnp.int32)
    lengths = jnp.concatenate(
        [jnp.zeros((1, DOC_LANE), jnp.int32), lengths_ref[...], rest], axis=1
    )
    ends = lengths
    step = 1
    while step < count:
        ends = ends + jnp.where(lanes >= DOC_LANE + step, pltpu.roll(ends, step, 1), 0)
        step *= 2
    here = (lanes >= DOC_LANE) & (lanes < DOC_LANE + count)
    starts = jnp.where(here, ends - lengths, 1 << 30)
    ends = jnp.where(here, ends, 0)
    index = lax.broadcasted_iota(jnp.int32, (8, 1), 0)
    bounds_ref[...] = jnp.where(index == 0, starts, jnp.where(index == 1, ends, 0))


def spread_kernel(index_ref, *refs, count, slots, rows):
    pair_ref, half_ref = refs[count:]
    more = refs[0].shape[0] - slots * rows
    for mask in range(count):
        place = index_ref[0] ^ mask
        start = pl.multiple_of(place * rows, rows)
        for slot in range(slots):
            pair_ref[slot, pl.ds(start, rows), :] = refs[mask][slot * rows : (slot + 1) * rows, :]
        half_ref[pl.ds(pl.multiple_of(place * more, more), more), :] = refs[mask][slots * rows :, :]


def hidden_kernel(
    bit_ref, unit_ref, mine_ref, other_ref, routes_ref, hidden_ref, kv_ref, gates_ref, small_ref, *, experts
):
    small = merged(mine_ref[...], other_ref[...], bit_ref[0])
    small_ref[...] = small
    side = small[:, small.shape[1] - 2 * LANES :]
    vectors = side[:, LANES:].astype(FULL).T
    hidden = to_low(
        unit_ref[...] * vectors[experts : experts + 1] + vectors[experts + 1 : experts + 2]
    )
    hidden_ref[...] = hidden
    both = dot_plain(hidden, side)
    kv_ref[...] = to_low(both[:, :LANES])
    logits = both[:, LANES:]
    lanes = lane_ids((1, LANES))
    picked = [
        jnp.sum(jnp.where(lanes == routes_ref[:, j : j + 1], logits, 0.0), axis=1, keepdims=True)
        for j in range(2)
    ]
    top = jnp.maximum(picked[0], picked[1])
    raised = [jnp.exp(p - top) for p in picked]
    total = raised[0] + raised[1]
    gates_ref[...] = jnp.where(
        lanes == 0, raised[0] / total, jnp.where(lanes == 1, raised[1] / total, 0.0)
    )


def query_kernel(place_ref, hidden_ref, small_ref, routes_ref, bounds_ref, query_ref, *, head):
    rows, width = hidden_ref.shape
    wide = dot_plain(hidden_ref[...], small_ref[:, :width])
    lanes = lane_ids((1, LANES))
    hot = in_document(bounds_ref, row_positions(place_ref[0], rows))
    documents = (bounds_ref[1:2, :] > 0) & (lanes >= head)
    marks = jnp.where(documents & jnp.logical_not(hot), -FAR, 0.0)
    for j in range(2):
        rows_of = choose(wide, routes_ref[:, j : j + 1], head) * head**-0.5
        query_ref[j * rows : (j + 1) * rows, :] = to_low(jnp.where(lanes < head, rows_of, marks))


def forward_kernel(place_ref, query_ref, bounds_ref, *rest, head, first, last, count, part):
    kv_refs, rest = rest[:count], list(rest[count:])
    state_ref = None if first else rest.pop(0)
    lanes = lane_ids((1, LANES))
    blocks = []
    for index, ref in enumerate(kv_refs):
        hot = in_document(bounds_ref, row_positions(place_ref[index], ref.shape[0]))
        blocks.append(key_rows_of(ref[...], hot, head))
    for start in range(0, query_ref.shape[0], part):
        rows = slice(start, start + part)
        query = query_ref[rows, :]
        state = None if first else state_ref[rows, :]
        for keys, values in blocks:
            scores = dot_last(query, keys)
            top = jnp.max(scores, axis=1, keepdims=True)
            if state is None:
                new = top
                state = dot_plain(to_low(jnp.exp(scores - new)), values)
            else:
                old = state[:, MAX_LANE : MAX_LANE + 1]
                new = jnp.maximum(old, top)
                weights = to_low(jnp.exp(scores - new))
                state = state * jnp.exp(old - new) + dot_plain(weights, values)
            state = jnp.where(lanes == MAX_LANE, new, state)
        if last:
            attn_ref, wide_ref = rest
            total = state[:, SUM_LANE : SUM_LANE + 1]
            attn_ref[rows, :] = jnp.where(lanes < head, state / total, 0.0)
            log_total = state[:, MAX_LANE : MAX_LANE + 1] + jnp.log(total)
            wide_ref[rows, :] = to_low(
                put_parts(query.astype(FULL), lanes, LSE_LANE, -log_total)
            )
        else:
            rest[0][rows, :] = state


def merged(mine, other, bit):
    low = bit == 0
    both = jnp.stack([jnp.where(low, mine, other), jnp.where(low, other, mine)], axis=1)
    return both.reshape(-1, mine.shape[-1])


def parted(whole, bit, shape):
    both = whole.reshape(shape[0], 2, shape[1], shape[2])
    low = bit == 0
    first, second = both[:, 0], both[:, 1]
    return jnp.where(low, first, second), jnp.where(low, second, first)


def weights(refs, bit):
    mine, other = refs[0][...], refs[1][...]
    shape = mine.shape[-3:]
    return merged(mine.reshape(shape), other.reshape(shape), bit)


def up_kernel(
    bit_ref, tokens_ref, cotangent_ref, attn_ref, gates_ref, routes_ref, vectors_ref, bias_ref, *rest,
    head
):
    output_refs, expand_refs = rest[:2], rest[2:4]
    mixed_ref, hidden_ref, active_ref, steep_ref, keep_ref, send_ref = rest[4:]
    step = pl.program_id(0)
    bit = bit_ref[0]
    width = tokens_ref.shape[1]

    @pl.when(step == 0)
    def _():
        wide = [doubled_head(attn_ref[j], head) * gates_ref[:, j : j + 1] for j in range(2)]
        mixed = to_low(place(wide, [routes_ref[:, j : j + 1] for j in range(2)], head, width))
        mixed_ref[...] = mixed
        middle = tokens_ref[...].astype(FULL) + dot_plain(mixed, weights(output_refs, bit))
        unit, factor = normalize(middle)
        hidden_ref[...] = to_low(unit * vectors_ref[0:1, :] + vectors_ref[1:2, :])

    slope = 0.7978845608028654
    cube = 0.044715
    inner = dot_plain(hidden_ref[...], weights(expand_refs, bit)) + bias_ref[...]
    square = inner * inner
    bent = jnp.tanh(slope * inner * (1.0 + cube * square))
    half = 0.5 * (1.0 + bent)
    active = to_low(inner * half)
    active_ref[0] = active
    steep = half + 0.5 * inner * (1.0 - bent * bent) * (slope + 3.0 * cube * slope * square)
    steep_ref[0] = to_low(steep)
    keep, send = parted(to_low(dot_first(active, cotangent_ref[...])), bit, keep_ref.shape)
    keep_ref[...] = keep
    send_ref[...] = send


def down_kernel(
    bit_ref, hidden_ref, cotangent_ref, active_ref, steep_ref, *rest, head, last
):
    rest = list(rest)
    take = lambda n: [rest.pop(0) for _ in range(n)]
    expand_refs, contract_refs = take(2), take(2)
    if last:
        out_before, grad_before, tokens_ref, mixed_ref, attn_ref, gates_ref, routes_ref, vectors_ref = (
            take(8)
        )
        output_refs = take(2)
        out_ref, branch_ref, grad_attn_ref, grad_logits_ref, grad_rows_ref = take(5)
    else:
        out_held, grad_held = take(2)
    keep_ref, send_ref, grad_bias_ref = take(3)
    if last:
        out_held, grad_held = take(2)
    step = pl.program_id(0)
    bit = bit_ref[0]

    @pl.when(step == 0)
    def _():
        out_held[...] = out_before[...] if last else jnp.zeros(out_held.shape, FULL)
        grad_held[...] = grad_before[...] if last else jnp.zeros(grad_held.shape, FULL)

    def chunk():
        expand, contract = weights(expand_refs, bit), weights(contract_refs, bit)
        out_held[...] += dot_plain(active_ref[0], contract)
        grad_active = dot_last(cotangent_ref[...], contract)
        grad_inner = to_low(steep_ref[0].astype(FULL) * grad_active)
        grad_bias_ref[...] = jnp.sum(grad_inner.astype(FULL), axis=0, keepdims=True)
        grad_held[...] += dot_last(grad_inner, expand)
        keep, send = parted(to_low(dot_first(hidden_ref[...], grad_inner)), bit, keep_ref.shape[1:])
        keep_ref[0] = keep
        send_ref[0] = send

    if not last:
        chunk()
        return
    pl.when(step < pl.num_programs(0) - 1)(chunk)

    @pl.when(step == pl.num_programs(0) - 1)
    def _():
        lanes = lane_ids((1, LANES))
        gain, contract_bias = vectors_ref[0:1, :], vectors_ref[2:3, :]
        output_weight = weights(output_refs, bit)
        mixed = mixed_ref[...]
        middle = tokens_ref[...].astype(FULL) + dot_plain(mixed, output_weight)
        out_ref[...] = to_low(out_held[...] + middle + contract_bias)
        unit, factor = normalize(middle)
        grad_hidden = grad_held[...]
        cotangent = cotangent_ref[...].astype(FULL)
        branch = to_low(cotangent + norm_backward(grad_hidden, unit, factor, gain))
        branch_ref[...] = branch
        grad_rows_ref[...] = jnp.zeros_like(grad_rows_ref)
        grad_rows_ref[0:1, :] = jnp.sum(grad_hidden * unit, axis=0, keepdims=True)
        grad_rows_ref[1:2, :] = jnp.sum(grad_hidden, axis=0, keepdims=True)
        grad_rows_ref[2:3, :] = jnp.sum(cotangent, axis=0, keepdims=True)
        keep, send = parted(to_low(dot_first(mixed, branch)), bit, keep_ref.shape[1:])
        keep_ref[0] = keep
        send_ref[0] = send
        grad_mixed = dot_last(branch, output_weight)
        gates = [gates_ref[:, j : j + 1] for j in range(2)]
        routes = [routes_ref[:, j : j + 1] for j in range(2)]
        grad_gates = []
        for j in range(2):
            attn = attn_ref[j]
            weighted = jnp.where(lanes < head, choose(grad_mixed, routes[j], head), 0.0)
            grad_gates.append(jnp.sum(weighted * attn, axis=1, keepdims=True))
            grad_attn = to_low(weighted * gates[j]).astype(FULL)
            delta = jnp.sum(grad_attn * attn, axis=1, keepdims=True)
            grad_attn_ref[j] = to_low(put_parts(grad_attn, lanes, SUM_LANE, -delta))
        mean = gates[0] * grad_gates[0] + gates[1] * grad_gates[1]
        grad_logits = jnp.zeros(gates_ref.shape, FULL)
        for j in range(2):
            grad_logits = jnp.where(
                lanes == routes[j], gates[j] * (grad_gates[j] - mean), grad_logits
            )
        grad_logits_ref[...] = to_low(grad_logits)


def backward_kernel(place_ref, query_ref, grad_ref, bounds_ref, *rest, head, first, count, part):
    kv_refs, rest = rest[:count], list(rest[count:])
    before_ref = None if first else rest.pop(0)
    grad_query_ref, grad_kv_refs = rest[0], rest[1:]
    lanes = lane_ids((1, LANES))
    key_count = kv_refs[0].shape[0]
    blocks = []
    for index, ref in enumerate(kv_refs):
        hot = in_document(bounds_ref, row_positions(place_ref[index], key_count))
        blocks.append(key_rows_of(ref[...], hot, head))
    totals = [None] * count
    for start in range(0, query_ref.shape[0], part):
        rows = slice(start, start + part)
        query = query_ref[rows, :]
        grad = grad_ref[rows, :]
        only_query = to_low(jnp.where(lanes < head, query.astype(FULL), 0.0))
        turned = pltpu.roll(grad.astype(FULL), head, 1)
        only_grad = to_low(jnp.where(lanes < head, 0.0, turned))
        grad_query = None if first else before_ref[rows, :]
        for index, (keys, values) in enumerate(blocks):
            probs = jnp.exp(dot_last(keys, query))
            grad_scores = to_low(probs * dot_last(values, grad))
            update = dot_plain(grad_scores, only_query) + dot_plain(to_low(probs), only_grad)
            totals[index] = update if totals[index] is None else totals[index] + update
            step = dot_first(grad_scores, keys)
            grad_query = step if grad_query is None else grad_query + step
        grad_query_ref[rows, :] = grad_query
    for index in range(count):
        grad_kv_refs[index][...] = to_low(totals[index])


def placed_kernel(
    bit_ref, grad_query_ref, hidden_ref, routes_ref, grad_logits_ref, small_ref, grad_hidden_ref,
    keep_ref, send_ref, grad_router_ref, *, head
):
    count, width = hidden_ref.shape
    rows = [
        doubled_head(
            to_low(grad_query_ref[j * count : (j + 1) * count, :] * head**-0.5).astype(FULL), head
        )
        for j in range(2)
    ]
    placed = to_low(place(rows, [routes_ref[:, j : j + 1] for j in range(2)], head, width))
    hidden = hidden_ref[...]
    grad_logits = grad_logits_ref[...]
    keep, send = parted(to_low(dot_first(hidden, placed)), bit_ref[0], keep_ref.shape)
    keep_ref[...] = keep
    send_ref[...] = send
    grad_router_ref[...] = dot_first(hidden, grad_logits)
    grad_hidden_ref[...] = dot_last(placed, small_ref[:, :width]) + dot_last(
        grad_logits, small_ref[:, small_ref.shape[1] - LANES :]
    )


def last_kernel(
    bit_ref, tokens_ref, hidden_ref, grad_hidden_ref, grad_middle_ref, small_ref, rows_ref, bias_ref,
    bias_two_ref, grad_router_ref, own_ref, *rest, experts, others, rows
):
    other_refs = rest[:others]
    grad_tokens_ref, keep_ref, send_ref = rest[-3:]
    side = small_ref[:, small_ref.shape[1] - 2 * LANES :]
    gain = side[:, LANES:].astype(FULL).T[experts : experts + 1]
    grad_kv = own_ref[...].astype(FULL)
    for ref in other_refs:
        grad_kv += ref[...].astype(FULL)
    grad_kv = to_low(grad_kv)
    grad_keyval = dot_first(hidden_ref[...], grad_kv)
    grad_hidden = grad_hidden_ref[...] + dot_last(grad_kv, side[:, :LANES])
    unit, factor = normalize(tokens_ref[...].astype(FULL))
    grad_tokens_ref[...] = to_low(
        grad_middle_ref[...].astype(FULL) + norm_backward(grad_hidden, unit, factor, gain)
    )
    width = tokens_ref.shape[1]
    gain_grad = jnp.sum(grad_hidden * unit, axis=0, keepdims=True)
    shift_grad = jnp.sum(grad_hidden, axis=0, keepdims=True)
    index = lax.broadcasted_iota(jnp.int32, (8, 1), 0)
    later = pltpu.roll(rows_ref[...], 2, 0)
    vectors = jnp.where(index == 0, gain_grad, jnp.where(index == 1, shift_grad, later))
    ahead = jnp.zeros((experts, width), FULL)
    behind = jnp.zeros((LANES - experts - 8, width), FULL)
    columns = jnp.concatenate([ahead, vectors, behind], axis=0).T
    bias = jnp.concatenate([bias_ref[...], bias_two_ref[...]], axis=1)
    spread = bias_rows(bias, width // rows, rows)
    grad_side = jnp.concatenate([grad_keyval, columns + grad_router_ref[...] + spread], axis=1)
    keep, send = parted(to_low(grad_side), bit_ref[0], keep_ref.shape)
    keep_ref[...] = keep
    send_ref[...] = send


def finish_kernel(*refs, terms):
    total = sum(ref[...].astype(FULL) for ref in refs[:terms])
    query_ref, router_ref, keyval_ref, *vector_refs, bias_ref = refs[terms:]
    width = query_ref.shape[1]
    query_ref[...] = total[:, :width]
    side = total[:, width:]
    experts = router_ref.shape[1]
    keyval_ref[...] = side[:, :LANES]
    router_ref[...] = side[:, LANES : LANES + experts]
    for index, ref in enumerate(vector_refs):
        lane = LANES + experts + index
        ref[...] = as_row(side[:, lane : lane + 1])
    start = LANES + BIAS_LANE
    bias_ref[...] = side[0:1, start : start + bias_ref.shape[1]]


def finish_large_kernel(*refs, terms, slots):
    total = sum(ref[...].astype(FULL) for ref in refs[:terms])
    expand_ref, output_ref, contract_ref = refs[terms:]
    rows, width = output_ref.shape
    for slot in range(slots):
        expand_ref[:, slot * width : (slot + 1) * width] = total[slot * rows : (slot + 1) * rows]
    output_ref[...] = total[slots * rows : (slots + 1) * rows]
    contract_ref[...] = total[(slots + 1) * rows :]


def in_hbm(array):
    return pltpu.with_memory_space_constraint(array, pltpu.HBM)


def smem_spec():
    return pl.BlockSpec(memory_space=pltpu.SMEM)


def vmem_spec():
    return pl.BlockSpec(memory_space=pltpu.VMEM)


def shape_of(shape, dtype):
    return jax.ShapeDtypeStruct(tuple(shape), dtype)


def estimate(cost):
    return pl.CostEstimate(flops=int(cost * 1e9), bytes_accessed=0, transcendentals=0)


def call(kernel, name, outs, cost, limit=24, scalars=0):
    def run(*operands):
        return pl.pallas_call(
            kernel,
            in_specs=[smem_spec()] * scalars + [vmem_spec()] * (len(operands) - scalars),
            out_specs=[vmem_spec()] * len(outs) if isinstance(outs, list) else vmem_spec(),
            out_shape=outs,
            compiler_params=pltpu.CompilerParams(vmem_limit_bytes=limit * MEGA),
            cost_estimate=estimate(cost),
            name=name,
        )(*operands)

    return run


def generations(seq_count):
    masks = range(1, seq_count)
    most = seq_count.bit_length() - 1
    return [[m for m in masks if bin(m).count("1") == n] for n in range(1, most + 1)]


def feed_call(kernel, name, grid, cost, operands, outs, scratch=()):
    return pl.pallas_call(
        kernel,
        grid=grid,
        in_specs=[spec for _, spec in operands],
        out_specs=[spec for _, spec in outs],
        out_shape=[shape for shape, _ in outs],
        scratch_shapes=list(scratch),
        compiler_params=pltpu.CompilerParams(
            dimension_semantics=("arbitrary",), vmem_limit_bytes=FEED_LIMIT * MEGA
        ),
        cost_estimate=estimate(cost),
        name=name,
    )(*[array for array, _ in operands])


def first_block(shape, slot):
    rest = (0,) * (len(shape) - 1)
    return pl.BlockSpec((1,) + tuple(shape[1:]), lambda c: (slot(c),) + rest)


def feed_up(bit, tokens, cotangent, attn, gates, routes, vectors, bias, pairs, plain, head):
    token_count, width = tokens.shape
    chunks = pairs[0].shape[0] - 1
    inner = bias.shape[1] // chunks
    whole = vmem_spec()
    plain_spec = pl.BlockSpec((plain[0] // chunks,) + tuple(plain[1:]), lambda c: (c, 0, 0))
    operands = [(bit, smem_spec())]
    operands += [(a, whole) for a in (tokens, cotangent, attn, gates, routes, vectors)]
    operands += [(bias, pl.BlockSpec((1, inner), lambda c: (0, c)))]
    operands += [(p, first_block(p.shape, lambda c: 0)) for p in pairs]
    operands += [(p, first_block(p.shape, lambda c: c + 1)) for p in pairs]
    rows = (token_count, width)
    held = (chunks, token_count, inner)
    outs = [(shape_of(rows, LOW), whole)] * 2
    outs += [(pltpu.HBM(held, LOW), first_block(held, lambda c: c))] * 2
    outs += [(shape_of(plain, LOW), plain_spec)] * 2
    return feed_call(
        functools.partial(up_kernel, head=head), "feed_up", (chunks,), FEED_COST / 2,
        operands, outs
    )


def feed_down(
    bit, hidden, cotangent, active, steep, pairs, contracts, first, count, head, end=None
):
    token_count, width = hidden.shape
    chunks = active.shape[0]
    whole = vmem_spec()
    last = end is not None
    at = lambda c: first + jnp.minimum(c, count - 1)
    operands = [(bit, smem_spec()), (hidden, whole), (cotangent, whole)]
    operands += [(in_hbm(a), first_block(a.shape, at)) for a in (active, steep)]
    operands += [(p, first_block(p.shape, lambda c: at(c) + 1)) for p in pairs]
    for part in contracts:
        block = (part.shape[0] // chunks,) + part.shape[1:]
        operands.append((part, pl.BlockSpec(block, lambda c: (at(c), 0, 0))))
    rows = (token_count, width)
    grads = (count + (1 if last else 0),) + pairs[0].shape[1:]
    inner = active.shape[2]
    after = [
        (shape_of(grads, LOW), first_block(grads, lambda c: c)),
        (shape_of(grads, LOW), first_block(grads, lambda c: c)),
        (
            shape_of((1, count * inner), FULL),
            pl.BlockSpec((1, inner), lambda c: (0, jnp.minimum(c, count - 1))),
        ),
    ]
    if last:
        operands += [(a, whole) for a in end]
        operands += [(p, first_block(p.shape, lambda c: 0)) for p in pairs]
        in_rows = pl.BlockSpec(rows, lambda c: (0, 0))
        outs = [
            (shape_of(rows, LOW), in_rows),
            (shape_of(rows, LOW), whole),
            (shape_of((2, token_count, LANES), LOW), whole),
            (shape_of((token_count, LANES), LOW), whole),
            (shape_of((8, width), FULL), whole),
        ] + after
        scratch = [pltpu.VMEM(rows, FULL)] * 2
    else:
        outs = [(shape_of(rows, FULL), whole)] * 2 + after
        scratch = []
    return feed_call(
        functools.partial(down_kernel, head=head, last=last),
        "feed_down", (count + (1 if last else 0),), FEED_COST / 2, operands, outs, scratch
    )


def per_device(
    tokens, routes, lengths, cotangent, first_gain, first_shift, router, query_map, keyval,
    output_map, second_gain, second_shift, expand, expand_bias, contract, contract_bias
):
    seq_count, plane_count = lax.axis_size("seq"), lax.axis_size("dp") // 2
    along = Group("seq", 0, seq_count)
    plane = Group("dp", 1, plane_count)
    core = Group("dp", 0, 2)
    token_count, width = tokens.shape
    rows = first_gain.shape[0]
    contract_rows = contract.shape[0]
    experts = router.shape[1]
    head = keyval.shape[1] // 2
    inner_width = expand.shape[1]
    chunks = inner_width // width
    slots = 1 + chunks
    my_index = along.index()
    bit = scalar(core.index())
    side_width = 2 * LANES
    row_count = 2 * token_count
    part = min(1024, row_count)

    params = [
        query_map, keyval, router, first_gain[None], first_shift[None], second_gain[None],
        second_shift[None], contract_bias[None], expand_bias[None], output_map, expand, contract
    ]
    small_mine, large_mine = pl.pallas_call(
        functools.partial(pack_kernel, count=len(params)),
        in_specs=[pl.BlockSpec(memory_space=pltpu.HBM)] * len(params),
        out_specs=[vmem_spec()] * 2,
        out_shape=[
            shape_of((rows, width + side_width), LOW),
            shape_of((slots * rows + contract_rows, width), LOW),
        ],
        scratch_shapes=[pltpu.VMEM(p.shape, FULL) for p in params]
        + [pltpu.SemaphoreType.DMA((len(params),))],
        compiler_params=pltpu.CompilerParams(vmem_limit_bytes=16 * MEGA),
        cost_estimate=estimate(0.1),
        name="pack",
    )(*[in_hbm(p) for p in params])

    def place_of(masks):
        return jnp.stack([(my_index ^ m) * token_count for m in masks]).astype(jnp.int32)

    small_move, large_move = Move(along, small_mine[None]), Move(along, large_mine)
    unit, route_columns, bounds = phase(
        [small_move],
        lambda: call(
            first_kernel,
            "first",
            [
                shape_of(tokens.shape, FULL),
                shape_of((token_count, LANES), jnp.int32),
                shape_of((8, LANES), jnp.int32),
            ],
            0.1,
        )(tokens, routes.T, lengths),
    )
    small = merge([small_mine[None]] + [small_move.got[m] for m in range(1, seq_count)], along)
    small_move = Move(plane, small)
    phase([small_move, large_move])
    small = merge([small] + [small_move.got[m] for m in range(1, plane_count)], plane)[0]
    small_move = Move(core, small)
    phase([small_move])
    small_shape = (plane_count, seq_count * rows, width + side_width)
    smalls = [small.reshape(small_shape), small_move.got[1].reshape(small_shape)]
    hidden, kv_mine, gates, small = call(
        functools.partial(hidden_kernel, experts=experts),
        "hidden",
        [
            shape_of((token_count, width), LOW),
            shape_of((token_count, LANES), LOW),
            shape_of((token_count, LANES), FULL),
            shape_of((width, width + side_width), LOW),
        ],
        0.5,
        scalars=1,
    )(bit, unit, *smalls, route_columns)
    ended = together(hidden, kv_mine, gates, small, large_mine, *large_move.got.values())
    hidden, kv_mine, gates, small, *blocks = ended

    if rows % 16:
        lines = jnp.stack(by_place(blocks, my_index))
        pair = lines[:, : slots * rows].reshape(seq_count, slots, rows, width)
        pair = pair.transpose(1, 0, 2, 3).reshape(slots, seq_count * rows, width)
        half = lines[:, slots * rows :].reshape(1, seq_count * contract_rows, width)
    else:
        pair, half = call(
            functools.partial(spread_kernel, count=seq_count, slots=slots, rows=rows),
            "spread",
            [
                shape_of((slots, seq_count * rows, width), LOW),
                shape_of((seq_count * contract_rows, width), LOW),
            ],
            0.1,
            scalars=1,
        )(scalar(my_index), *blocks)
        half = half[None]
    shards = {0: kv_mine}
    coming = generations(seq_count) + [[]]
    ready = [0]
    state = []
    for step, sent in enumerate(coming):
        last = step == len(coming) - 1
        keys = [Move(along, shards[m & (m - 1)], [m & -m]) for m in sent]
        moves = []
        if step == 0:
            pair_move = Move(plane, pair)
            moves = [pair_move]
        if step == 1:
            pair = merge([pair] + [pair_move.got[m] for m in range(1, plane_count)], plane)
            pair = pair.reshape(slots, plane_count, -1, width)
            pair_core, half_move = Move(core, pair), Move(plane, half)
            moves = [pair_core, half_move]
        if step == 2:
            half = merge([half] + [half_move.got[m] for m in range(1, plane_count)], plane)
            half = half.reshape(plane_count, -1, width)
            half_core = Move(core, half)
            moves = [half_core]

        def attend():
            query = queries
            if not state:
                query = call(
                    functools.partial(query_kernel, head=head),
                    "queries",
                    shape_of((row_count, LANES), LOW),
                    0.5,
                    scalars=1,
                )(place_of([0]), hidden, small, route_columns, bounds)
            result = call(
                functools.partial(
                    forward_kernel, head=head, first=not state, last=last, count=len(ready), part=part
                ),
                "attention_forward",
                [shape_of((row_count, LANES), t) for t in ((FULL, LOW) if last else (FULL,))],
                FORWARD_COST * len(ready),
                scalars=1,
            )(place_of(ready), query, bounds, *[shards[m] for m in ready], *state)
            if state:
                return result
            rows_of = call(
                functools.partial(vectors_kernel, experts=experts, rows=rows),
                "vectors",
                [shape_of((8, width), FULL), shape_of((1, inner_width), FULL)],
                0.1,
            )(small)
            return [*result, query, *rows_of]

        queries = queries if state else None
        if state:
            state = phase(keys + moves, attend)
        else:
            *state, queries, vectors, bias = phase(keys + moves, attend)
        for mask, move in zip(sent, keys):
            shards[mask] = move.got[mask & -mask]
        ready = sent
    attn, wide_queries = state
    attn = attn.reshape(2, token_count, LANES)
    pairs, halves = [pair, pair_core.got[1]], [half, half_core.got[1]]

    plain = (plane_count, seq_count * contract_rows, width)
    mixed, hidden_two, active, steep, keep_half, send_half = feed_up(
        bit, tokens, cotangent, attn, gates, route_columns, vectors, bias, pairs, plain, head
    )
    half_move = Move(core, send_half)
    middle_chunk = chunks // 2
    out_held, grad_held, keep_expand, send_expand, grad_bias = phase(
        [half_move],
        lambda: feed_down(
            bit, hidden_two, cotangent, active, steep, pairs, halves, 0, middle_chunk, head
        ),
    )
    flat = lambda lead, *terms: [t.reshape(lead, -1, width) for t in terms]
    half_sent = cut([flat(1, keep_half, half_move.got[1])], plane, width)
    half_move, expand_move = Move(plane, dict(enumerate(half_sent))), Move(core, send_expand)
    (
        out, branch, grad_attn, grad_logits, grad_rows, keep_pair, send_pair, grad_bias_two
    ) = phase(
        [half_move, expand_move],
        lambda: feed_down(
            bit, hidden_two, cotangent, active, steep, pairs, halves, middle_chunk,
            chunks - middle_chunk, head,
            (out_held, grad_held, tokens, mixed, attn, gates, route_columns, vectors),
        ),
    )

    grad_rows_in = grad_attn.reshape(row_count, LANES)
    masks = list(range(seq_count - 1, 0, -1))
    if seq_count > 2:
        masks = [2] + [m for m in masks if m != 2]
    third = max(1, len(masks) // 3)
    groups = [masks[:third], masks[third:], [0]]

    def backward(masks, before):
        return call(
            functools.partial(
                backward_kernel, head=head, first=before is None, count=len(masks), part=part
            ),
            "attention_backward",
            [shape_of((row_count, LANES), FULL)]
            + [shape_of((token_count, LANES), LOW)] * len(masks),
            BACKWARD_COST * len(masks),
            scalars=1,
        )(
            place_of(masks), wide_queries, grad_rows_in, bounds, *[shards[m] for m in masks],
            *([] if before is None else [before])
        )

    expand_sent = cut([flat(middle_chunk, keep_expand, expand_move.got[1])], plane, width)
    expand_move, pair_move = Move(plane, dict(enumerate(expand_sent))), Move(core, send_pair)
    first_query, *leaving = phase([expand_move, pair_move], lambda: backward(groups[0], None))
    lead = chunks - middle_chunk + 1
    pair_sent = cut([flat(lead, keep_pair, pair_move.got[1])], plane, width)
    pair_move = Move(plane, dict(enumerate(pair_sent)))
    keys_first = Move(along, dict(zip(groups[0], leaving)), groups[0])
    second_query, *leaving = phase([keys_first, pair_move], lambda: backward(groups[1], first_query))
    keys_second = Move(along, dict(zip(groups[1], leaving)), groups[1])

    def work():
        grad_query, own = backward(groups[2], second_query)
        shape = (plane_count, seq_count * rows, width)
        return own, *call(
            functools.partial(placed_kernel, head=head),
            "query_gradient",
            [
                shape_of((token_count, width), FULL),
                shape_of(shape, LOW),
                shape_of(shape, LOW),
                shape_of((width, LANES), FULL),
            ],
            1.0,
            scalars=1,
        )(bit, grad_query, hidden, route_columns, grad_logits, small)

    grad_kv, grad_hidden, keep_query, send_query, grad_router = phase([keys_second], work)
    query_move = Move(core, send_query)
    others = list(keys_first.got.values()) + list(keys_second.got.values())
    shape = (plane_count, seq_count * rows, side_width)
    grad_tokens, keep_side, send_side = phase(
        [query_move],
        lambda: call(
            functools.partial(last_kernel, experts=experts, others=len(others), rows=rows),
            "key_gradient",
            [shape_of((token_count, width), LOW), shape_of(shape, LOW), shape_of(shape, LOW)],
            1.0,
            scalars=1,
        )(
            bit, tokens, hidden, grad_hidden, branch, small, grad_rows, grad_bias, grad_bias_two,
            grad_router, grad_kv, *others
        ),
    )

    own = lambda sent, move, lead: [
        t.reshape(lead, -1, width) for t in [sent[0]] + list(move.got.values())
    ]
    large_sent = cut(
        [
            own(expand_sent, expand_move, middle_chunk),
            own(pair_sent, pair_move, lead),
            own(half_sent, half_move, 1),
        ],
        along,
        width,
    )
    large_move = Move(along, dict(enumerate(large_sent)))
    side_move = Move(core, send_side)
    phase([side_move])
    line = lambda *terms: [t.reshape(1, -1, t.shape[-1]) for t in terms]
    small_sent = cut(
        [line(keep_query, query_move.got[1]), line(keep_side, side_move.got[1])],
        plane,
        width + side_width,
    )
    small_move = Move(plane, dict(enumerate(small_sent)))
    phase([small_move, large_move])
    small_sent = cut(
        [line(small_sent[0], *small_move.got.values())], along, width + side_width
    )
    small_move = Move(along, dict(enumerate(small_sent)))
    terms = [large_sent[0]] + list(large_move.got.values())
    grad_expand, grad_output, grad_contract = phase(
        [small_move],
        lambda: call(
            functools.partial(finish_large_kernel, terms=len(terms), slots=chunks),
            "finish_large",
            [
                shape_of(expand.shape, FULL),
                shape_of(output_map.shape, FULL),
                shape_of(contract.shape, FULL),
            ],
            0.1,
        )(*terms),
    )
    terms = [small_sent[0]] + list(small_move.got.values())
    vector_shape = shape_of((1, rows), FULL)
    grad_query_map, grad_router, grad_keyval, *vector_sums, grad_spread = call(
        functools.partial(finish_kernel, terms=len(terms)),
        "finish",
        [shape_of(query_map.shape, FULL), shape_of(router.shape, FULL)]
        + [shape_of(keyval.shape, FULL)]
        + [vector_shape] * 5
        + [shape_of((1, expand_bias.shape[0]), FULL)],
        0.1,
    )(*terms)
    grad_gain, grad_shift, grad_gain_two, grad_shift_two, grad_contract_bias = (
        v.reshape(rows) for v in vector_sums
    )
    return (
        out, grad_tokens, grad_gain, grad_shift, grad_router, grad_query_map, grad_keyval,
        grad_output, grad_gain_two, grad_shift_two, grad_expand, grad_spread.reshape(-1),
        grad_contract, grad_contract_bias
    )


def solution(mesh):
    both = ("dp", "seq")
    rows, vector = P(both, None), P(both)
    return jax.shard_map(
        per_device,
        mesh=mesh,
        in_specs=(
            rows, rows, P("dp", None), rows, vector, vector, rows, rows, rows, rows, vector, vector,
            rows, vector, rows, vector
        ),
        out_specs=(
            rows, rows, vector, vector, rows, rows, rows, rows, vector, vector, rows, vector, rows,
            vector
        ),
        check_vma=False,
    )
```

```python
import functools

import jax
import jax.numpy as jnp
from jax import lax
from jax.experimental import pallas as pl
from jax.experimental.pallas import tpu as pltpu
from jax.sharding import PartitionSpec as P

LOW = jnp.bfloat16
FULL = jnp.float32
FAR = 1e30
EPS = 1e-05
DOC_LANE = 64
LSE_LANE = 96
SUM_LANE = 64
MAX_LANE = 67
BIAS_LANE = 64
SEQ_SLOT, PLANE_SLOT, CORE_SLOT = range(3)
LANES = 128
MEGA = 1 << 20
FORWARD_COST = 0.1
QUERY_COST = 0.05
BACKWARD_COST = 3.0
FEED_COST = 8.0
LIMITS = {
    "pack": 4, "first": 4, "hidden": 6, "vectors": 2, "queries": 6, "attention_forward": 8,
    "attention_backward": 8, "query_gradient": 6, "key_gradient": 12, "merge": 2, "spread": 2,
    "cut": 3, "finish": 2, "feed_up": 24,
    "feed_down": 24, "feed_down_last": 24,
}


def to_low(matrix):
    return matrix.astype(LOW)


def dot_plain(left, right):
    return lax.dot_general(left, right, (((1,), (0,)), ((), ())), preferred_element_type=FULL)


def dot_last(left, right):
    return lax.dot_general(left, right, (((1,), (1,)), ((), ())), preferred_element_type=FULL)


def dot_first(left, right):
    return lax.dot_general(left, right, (((0,), (0,)), ((), ())), preferred_element_type=FULL)


class Group:
    def __init__(self, axis, shift, size, slot):
        self.axis, self.shift, self.size, self.slot = axis, shift, size, slot
        self.ids = None

    def index(self):
        return (lax.axis_index(self.axis) >> self.shift) & (self.size - 1)

    def exchange(self, block, mask):
        step = mask << self.shift
        pairs = [(i, i ^ step) for i in range(lax.axis_size(self.axis))]
        return lax.ppermute(block, self.axis, pairs)


def by_place(blocks, index):
    blocks = list(blocks)
    for bit in range(len(blocks).bit_length() - 1):
        swap = (index >> bit) & 1 == 1
        blocks = [jnp.where(swap, blocks[i ^ (1 << bit)], blocks[i]) for i in range(len(blocks))]
    return blocks


def merge_kernel(ids_ref, *refs, count, slot):
    out_ref = refs[count]
    rows = refs[0].shape[1]
    for mask in range(count):
        start = pl.multiple_of((ids_ref[slot] ^ mask) * rows, rows)
        out_ref[:, pl.ds(start, rows), :] = refs[mask][...]


def merge(blocks, group):
    lead, rows, columns = blocks[0].shape
    if rows % 16:
        return jnp.concatenate(by_place(blocks, group.index()), axis=1)
    return call(
        functools.partial(merge_kernel, count=len(blocks), slot=group.slot),
        "merge",
        shape_of((lead, rows * len(blocks), columns), blocks[0].dtype),
        0.1,
        scalars=1,
    )(group.ids, *blocks)


def columns_of(columns, width):
    return [slice(i, min(i + width, columns)) for i in range(0, columns, width)]


def cut_kernel(ids_ref, *refs, sizes, count, slot):
    outs = refs[len(refs) - count :]
    refs = list(refs[: len(refs) - count])
    sets = [[refs.pop(0) for _ in range(size)] for size in sizes]
    width = outs[0].shape[1]
    for mask in range(count):
        row = column = 0
        for terms in sets:
            lead, total, columns = terms[0].shape
            rows = total // count
            start = pl.multiple_of((ids_ref[slot] ^ mask) * rows, rows)
            for at in range(lead):
                for piece in columns_of(columns, width):
                    value = sum(term[at, pl.ds(start, rows), piece].astype(FULL) for term in terms)
                    end = column + value.shape[1]
                    outs[mask][row : row + rows, column:end] = to_low(value)
                    column = end % width
                    row += 0 if column else rows
        if column:
            rest = outs[mask].shape[0] - row
            outs[mask][row:, column:] = jnp.zeros((rest, width - column), LOW)


def cut(sets, group, width):
    count = group.size
    sets = [[t.reshape((-1,) + t.shape[-2:]) for t in terms] for terms in sets]
    rows = [terms[0].shape[1] // count for terms in sets]
    total = sum(t[0].shape[0] * r * t[0].shape[2] for t, r in zip(sets, rows))
    total = -(-total // (width * rows[-1])) * rows[-1]
    if any(r % 16 for r in rows):
        index = group.index()
        results = []
        for mask in range(count):
            bands, band = [], []
            for terms, r in zip(sets, rows):
                value = sum(t.astype(FULL) for t in terms)
                value = lax.dynamic_slice_in_dim(value, (index ^ mask) * r, r, 1)
                for at in range(value.shape[0]):
                    for piece in columns_of(value.shape[2], width):
                        band.append(value[at, :, piece])
                        if sum(b.shape[1] for b in band) == width:
                            bands.append(jnp.concatenate(band, axis=1))
                            band = []
            if band:
                band = jnp.concatenate(band, axis=1)
                bands.append(jnp.pad(band, ((0, 0), (0, width - band.shape[1]))))
            results.append(to_low(jnp.concatenate(bands, axis=0)))
        return results
    return call(
        functools.partial(
            cut_kernel, sizes=[len(t) for t in sets], count=count, slot=group.slot
        ),
        "cut",
        [shape_of((total, width), LOW)] * count,
        0.1,
        scalars=1,
    )(group.ids, *[t for terms in sets for t in terms])


def together(*values):
    return lax.optimization_barrier(values)


class Move:
    def __init__(self, group, blocks, masks=None):
        self.group = group
        self.masks = list(range(1, group.size)) if masks is None else masks
        self.blocks = blocks if isinstance(blocks, dict) else {m: blocks for m in self.masks}

    def begin(self):
        self.moved = [self.group.exchange(self.blocks[m], m) for m in self.masks]
        return self

    def end(self, got):
        self.got = dict(zip(self.masks, got))
        self.moved = None


def phase(moves, work=lambda: (), held=()):
    for move in moves:
        if getattr(move, "moved", None) is None:
            move.begin()
    done = work()
    ended = list(together(*[x for m in moves for x in m.moved], *done, *held))
    for move in moves:
        move.end([ended.pop(0) for _ in move.masks])
    return ended


def lane_ids(shape):
    return lax.broadcasted_iota(jnp.int32, shape, len(shape) - 1)


def row_positions(offset, rows):
    return offset + lax.broadcasted_iota(jnp.int32, (rows, 1), 0)


def in_document(bounds_ref, positions):
    return (positions >= bounds_ref[0:1, :]) & (positions < bounds_ref[1:2, :])


def put_parts(base, lanes, lane, rows, count):
    for step in range(count):
        part = to_low(rows).astype(FULL)
        base = jnp.where(lanes == lane + step, part, base)
        rows = rows - part
    return base


def lane_sum(matrix):
    total = sum(matrix[:, i : i + LANES] for i in range(0, matrix.shape[1], LANES))
    high = to_low(total)
    low = to_low(total - high.astype(FULL))
    ones = jnp.ones((LANES, LANES), LOW)
    return dot_plain(high, ones) + dot_plain(low, ones)


def over(rows, width):
    return jnp.concatenate([rows] * (width // LANES), axis=1)


def normalize(matrix):
    width = matrix.shape[1]
    center = matrix - over(lane_sum(matrix) * (1.0 / width), width)
    factor = lax.rsqrt(lane_sum(center * center) * (1.0 / width) + EPS)
    return center * over(factor, width), factor


def norm_backward(grad, unit, factor, gain):
    width = grad.shape[1]
    scaled = grad * gain
    mean = over(lane_sum(scaled) * (1.0 / width), width)
    along = over(lane_sum(scaled * unit) * (1.0 / width), width)
    return over(factor, width) * (scaled - mean - unit * along)


def choose(wide, route, head):
    shift = (LANES // head).bit_length() - 1
    tile = lax.shift_right_logical(route, shift)
    picked = wide[:, :LANES]
    for index in range(1, wide.shape[1] // LANES):
        picked = jnp.where(tile == index, wide[:, index * LANES : (index + 1) * LANES], picked)
    turned = pltpu.roll(picked, head, 1)
    lanes = lane_ids((1, LANES))
    mine = (lanes // head) == (route & ((1 << shift) - 1))
    return jnp.where(mine, picked, turned)


def place(doubled, routes, head, width):
    lanes = lane_ids((1, LANES))
    per_tile = LANES // head
    tiles = []
    for index in range(width // LANES):
        expert = lanes // head + index * per_tile
        tile = jnp.zeros_like(doubled[0])
        for rows, route in zip(doubled, routes):
            tile = jnp.where(route == expert, rows, tile)
        tiles.append(tile)
    return jnp.concatenate(tiles, axis=1)


def doubled_head(rows, head):
    lanes = lane_ids((1, LANES))
    return jnp.where(lanes < head, rows, pltpu.roll(rows, head, 1))


def key_rows_of(kv, hot, head):
    lanes = lane_ids((1, LANES))
    kv = kv.astype(FULL)
    marks = jnp.where((lanes >= LSE_LANE) & (lanes < LSE_LANE + 3), 1.0, 0.0)
    keys = jnp.where(lanes < head, kv, jnp.where(hot, 1.0, marks))
    ones = jnp.where((lanes >= SUM_LANE) & (lanes < SUM_LANE + 3), 1.0, 0.0)
    values = jnp.where(lanes < head, pltpu.roll(kv, head, 1), ones)
    return to_low(keys), to_low(values)


def as_column(row):
    rows = row.shape[1]
    lanes = lax.broadcasted_iota(jnp.int32, (rows, rows), 1)
    here = lax.broadcasted_iota(jnp.int32, (rows, rows), 0)
    return jnp.sum(jnp.where(lanes == here, row, 0.0), axis=1, keepdims=True)


def as_row(column):
    rows = column.shape[0]
    lanes = lax.broadcasted_iota(jnp.int32, (rows, rows), 1)
    here = lax.broadcasted_iota(jnp.int32, (rows, rows), 0)
    return jnp.sum(jnp.where(lanes == here, column, 0.0), axis=0, keepdims=True)


def fetch(refs, held, semaphores):
    copies = [
        pltpu.make_async_copy(ref, into, semaphores.at[i])
        for i, (ref, into) in enumerate(zip(refs, held))
    ]
    for copy in copies:
        copy.start()
    for copy in copies:
        copy.wait()


def pack_kernel(*refs, count):
    small_ref, large_ref = refs[count : count + 2]
    held = refs[count + 2 : -1]
    fetch(refs[:count], held, refs[-1])
    (
        query_ref, keyval_ref, router_ref, gain_ref, shift_ref, gain_two_ref, shift_two_ref,
        contract_bias_ref, expand_bias_ref, output_ref, expand_ref, contract_ref
    ) = held
    rows, width = query_ref.shape
    experts = router_ref.shape[0]
    keyval_width = keyval_ref.shape[1]
    small_ref[:, :width] = to_low(query_ref[...])
    small_ref[:, width : width + keyval_width] = to_low(keyval_ref[...])
    lanes = lane_ids((1, LANES))
    turned = router_ref[...]
    side = jnp.zeros((rows, LANES), FULL)
    for expert in range(experts):
        side = jnp.where(lanes == expert, as_column(turned[expert : expert + 1]), side)
    vectors = [gain_ref, shift_ref, gain_two_ref, shift_two_ref, contract_bias_ref]
    for index, ref in enumerate(vectors):
        side = jnp.where(lanes == experts + index, as_column(ref[...]), side)
    extra = expand_bias_ref.shape[1]
    bias = jnp.pad(expand_bias_ref[...], ((0, 0), (BIAS_LANE, LANES - BIAS_LANE - extra)))
    first = lax.broadcasted_iota(jnp.int32, (rows, 1), 0) == 0
    side = side + jnp.where(first, bias, 0.0)
    small_ref[:, width + keyval_width :] = to_low(side)
    large = [output_ref[...]]
    large += [
        expand_ref[:, c * width : (c + 1) * width] for c in range(expand_ref.shape[1] // width)
    ]
    large_ref[...] = to_low(jnp.concatenate(large + [contract_ref[...]], axis=0))


def first_kernel(ids_ref, routes_hbm, lengths_hbm, columns_ref, bounds_ref, ids_out, *held):
    for slot in range(ids_ref.shape[0]):
        ids_out[slot] = ids_ref[slot]
    routes_ref, lengths_ref, semaphores = held
    fetch((routes_hbm, lengths_hbm), (routes_ref, lengths_ref), semaphores)
    routes = routes_ref[...].astype(FULL)
    choices = routes.shape[0]
    routes = jnp.concatenate([routes, jnp.zeros((8 - routes.shape[0], routes.shape[1]), FULL)], axis=0)
    turned = routes.T
    for j in range(choices):
        wide = jnp.broadcast_to(turned[:, j : j + 1], columns_ref.shape[1:])
        columns_ref[j] = wide.astype(jnp.int32)
    count = lengths_ref.shape[1]
    lanes = lane_ids((1, LANES))
    rest = jnp.zeros((1, LANES - DOC_LANE - count), jnp.int32)
    lengths = jnp.concatenate(
        [jnp.zeros((1, DOC_LANE), jnp.int32), lengths_ref[...], rest], axis=1
    )
    ends = lengths
    step = 1
    while step < count:
        ends = ends + jnp.where(lanes >= DOC_LANE + step, pltpu.roll(ends, step, 1), 0)
        step *= 2
    here = (lanes >= DOC_LANE) & (lanes < DOC_LANE + count)
    starts = jnp.where(here, ends - lengths, 1 << 30)
    ends = jnp.where(here, ends, 0)
    index = lax.broadcasted_iota(jnp.int32, (8, 1), 0)
    bounds_ref[...] = jnp.where(index == 0, starts, jnp.where(index == 1, ends, 0))


def vectors_kernel(small_ref, vectors_ref, bias_ref, *, experts, rows):
    misc = small_ref[:, small_ref.shape[1] - LANES :].astype(FULL)
    turned = misc.T
    vectors_ref[...] = turned[experts + 2 : experts + 10]
    count = misc.shape[0] // rows
    each = bias_ref.shape[1] // count
    per_tile = LANES // each
    firsts = misc.reshape(count, rows, LANES)[:, 0, :].reshape(count // per_tile, per_tile, LANES)
    lanes = lane_ids((1, LANES))
    tiles = jnp.zeros((count // per_tile, LANES), FULL)
    for k in range(per_tile):
        moved = pltpu.roll(firsts[:, k, :], (k * each - BIAS_LANE) % LANES, 1)
        tiles = jnp.where(lanes // each == k, moved, tiles)
    for index in range(count // per_tile):
        bias_ref[:, index * LANES : (index + 1) * LANES] = tiles[index : index + 1]


def bias_rows(bias, count, rows):
    each = bias.shape[1] // count
    per_tile = LANES // each
    tiles = jnp.concatenate(
        [bias[:, i : i + LANES] for i in range(0, bias.shape[1], LANES)], axis=0
    )
    lanes = lane_ids((1, LANES))
    mine = (lanes >= BIAS_LANE) & (lanes < BIAS_LANE + each)
    parts = [
        jnp.where(mine, pltpu.roll(tiles, (BIAS_LANE - k * each) % LANES, 1), 0.0)
        for k in range(per_tile)
    ]
    firsts = jnp.stack(parts, axis=1).reshape(count, 1, LANES)
    here = lax.broadcasted_iota(jnp.int32, (1, rows, 1), 1) == 0
    return jnp.where(here, firsts, 0.0).reshape(count * rows, LANES)


def spread_kernel(ids_ref, *refs, count, slots, rows):
    pair_ref, half_ref = refs[count:]
    more = refs[0].shape[0] - slots * rows
    for mask in range(count):
        place = ids_ref[SEQ_SLOT] ^ mask
        start = pl.multiple_of(place * rows, rows)
        for slot in range(slots):
            pair_ref[slot, pl.ds(start, rows), :] = refs[mask][slot * rows : (slot + 1) * rows, :]
        half_ref[pl.ds(pl.multiple_of(place * more, more), more), :] = refs[mask][slots * rows :, :]


def hidden_kernel(
    ids_ref, tokens_ref, mine_ref, other_ref, routes_ref, hidden_ref, kv_ref, gates_ref, small_ref, *, experts
):
    small = merged(mine_ref[...], other_ref[...], ids_ref[CORE_SLOT])
    small_ref[...] = small
    side = small[:, small.shape[1] - 2 * LANES :]
    vectors = side[:, LANES:].astype(FULL).T
    unit = normalize(tokens_ref[...].astype(FULL))[0]
    hidden = to_low(
        unit * vectors[experts : experts + 1] + vectors[experts + 1 : experts + 2]
    )
    hidden_ref[...] = hidden
    both = dot_plain(hidden, side)
    kv_ref[...] = to_low(both[:, :LANES])
    logits = both[:, LANES:]
    lanes = lane_ids((1, LANES))
    picked = [lane_sum(jnp.where(lanes == routes_ref[j], logits, 0.0)) for j in range(2)]
    top = jnp.maximum(picked[0], picked[1])
    raised = [jnp.exp(p - top) for p in picked]
    total = raised[0] + raised[1]
    for j in range(2):
        gates_ref[j] = raised[j] / total


def query_kernel(ids_ref, hidden_ref, small_ref, routes_ref, bounds_ref, query_ref, *, head):
    rows, width = hidden_ref.shape
    wide = dot_plain(hidden_ref[...], small_ref[:, :width])
    lanes = lane_ids((1, LANES))
    hot = in_document(bounds_ref, row_positions(ids_ref[SEQ_SLOT] * rows, rows))
    documents = (bounds_ref[1:2, :] > 0) & (lanes >= head)
    marks = jnp.where(documents & jnp.logical_not(hot), -FAR, 0.0)
    for j in range(2):
        rows_of = choose(wide, routes_ref[j], head) * head**-0.5
        query_ref[j * rows : (j + 1) * rows, :] = to_low(jnp.where(lanes < head, rows_of, marks))


def forward_kernel(ids_ref, query_ref, bounds_ref, *rest, head, first, last, masks, part):
    count = len(masks)
    kv_refs, rest = rest[:count], list(rest[count:])
    state_ref = None if first else rest.pop(0)
    lanes = lane_ids((1, LANES))
    blocks = []
    for index, ref in enumerate(kv_refs):
        start = (ids_ref[SEQ_SLOT] ^ masks[index]) * ref.shape[0]
        hot = in_document(bounds_ref, row_positions(start, ref.shape[0]))
        blocks.append(key_rows_of(ref[...], hot, head))
    for start in range(0, query_ref.shape[0], part):
        rows = slice(start, start + part)
        query = query_ref[rows, :]
        state = None if first else state_ref[rows, :]
        for keys, values in blocks:
            scores = dot_last(query, keys)
            top = jnp.max(scores, axis=1, keepdims=True)
            if state is None:
                new = top
                state = dot_plain(to_low(jnp.exp(scores - new)), values)
            else:
                old = state[:, MAX_LANE : MAX_LANE + 1]
                new = jnp.maximum(old, top)
                weights = to_low(jnp.exp(scores - new))
                state = state * jnp.exp(old - new) + dot_plain(weights, values)
            state = jnp.where(lanes == MAX_LANE, new, state)
        if last:
            attn_ref, wide_ref = rest
            total = state[:, SUM_LANE : SUM_LANE + 1]
            attn_ref[rows, :] = jnp.where(lanes < head, state / total, 0.0)
            log_total = state[:, MAX_LANE : MAX_LANE + 1] + jnp.log(total)
            wide_ref[rows, :] = to_low(
                put_parts(query.astype(FULL), lanes, LSE_LANE, -log_total, 3)
            )
        else:
            rest[0][rows, :] = state


def merged(mine, other, bit):
    low = bit == 0
    both = jnp.stack([jnp.where(low, mine, other), jnp.where(low, other, mine)], axis=1)
    return both.reshape(-1, mine.shape[-1])


def parted(whole, bit, shape):
    both = whole.reshape(shape[0], 2, shape[1], shape[2])
    low = bit == 0
    first, second = both[:, 0], both[:, 1]
    return jnp.where(low, first, second), jnp.where(low, second, first)


def weights(refs, bit):
    mine, other = refs[0][...], refs[1][...]
    shape = mine.shape[-3:]
    return merged(mine.reshape(shape), other.reshape(shape), bit)


def weights(mine, other, ids_ref):
    return merged(mine, other, ids_ref[CORE_SLOT])


def chunk_of(refs, chunk, chunks):
    count = refs[0].shape[0] // chunks
    return [ref[chunk * count : (chunk + 1) * count] for ref in refs]


def up_kernel(
    ids_ref, tokens_ref, cotangent_ref, attn_ref, gates_ref, routes_ref, vectors_ref, bias_ref,
    pair_mine, pair_other, mixed_ref, hidden_ref, active_ref, steep_ref, keep_ref, send_ref, *, head
):
    width = tokens_ref.shape[1]
    wide = [doubled_head(attn_ref[j], head) * gates_ref[j] for j in range(2)]
    mixed = to_low(place(wide, [routes_ref[j] for j in range(2)], head, width))
    mixed_ref[...] = mixed
    output_weight = weights(pair_mine[0], pair_other[0], ids_ref)
    middle = tokens_ref[...].astype(FULL) + dot_plain(mixed, output_weight)
    unit, _ = normalize(middle)
    hidden = to_low(unit * vectors_ref[0:1, :] + vectors_ref[1:2, :])
    hidden_ref[...] = hidden
    slope = 0.7978845608028654
    cube = 0.044715
    chunks, _, inner_width = active_ref.shape
    part = min(256, tokens_ref.shape[0])
    groups = keep_ref.shape[0] // chunks
    for chunk in range(chunks):
        expand = weights(pair_mine[chunk + 1], pair_other[chunk + 1], ids_ref)
        columns = slice(chunk * inner_width, (chunk + 1) * inner_width)
        for start in range(0, hidden.shape[0], part):
            here = slice(start, start + part)
            inner = dot_plain(hidden[here], expand) + bias_ref[:, columns]
            square = inner * inner
            half = 0.5 + 0.5 * jnp.tanh(inner * (slope + slope * cube * square))
            whole = inner * half
            active_ref[chunk, here] = to_low(whole)
            steep = half + whole * (1.0 - half) * (2.0 * slope + 6.0 * slope * cube * square)
            steep_ref[chunk, here] = to_low(steep)
        shape = (groups,) + keep_ref.shape[1:]
        grad = to_low(dot_first(active_ref[chunk], cotangent_ref[...]))
        here = slice(chunk * groups, (chunk + 1) * groups)
        keep_ref[here], send_ref[here] = parted(grad, ids_ref[CORE_SLOT], shape)


def down_kernel(
    ids_ref, hidden_ref, cotangent_ref, active_ref, steep_ref, pair_mine, pair_other, contract_mine,
    contract_other, *rest, head, first, count, last
):
    rest = list(rest)
    take = lambda n: [rest.pop(0) for _ in range(n)]
    if last:
        out_before, grad_before, tokens_ref, mixed_ref, attn_ref, gates_ref, routes_ref, vectors_ref = (
            take(8)
        )
        out_ref, branch_ref, grad_attn_ref, grad_logits_ref, grad_rows_ref = take(5)
        out, grad_hidden = out_before[...], grad_before[...]
    else:
        out_held, grad_held = take(2)
        out = grad_hidden = None
    keep_ref, send_ref, grad_bias_ref = take(3)
    chunks, _, inner = active_ref.shape
    add = lambda total, term: term if total is None else total + term
    for at in range(count):
        chunk = first + at
        expand = weights(pair_mine[chunk + 1], pair_other[chunk + 1], ids_ref)
        contract = weights(*chunk_of((contract_mine, contract_other), chunk, chunks), ids_ref)
        out = add(out, dot_plain(active_ref[chunk], contract))
        grad_active = dot_last(cotangent_ref[...], contract)
        grad_inner = to_low(steep_ref[chunk].astype(FULL) * grad_active)
        columns = slice(at * inner, (at + 1) * inner)
        grad_bias_ref[:, columns] = jnp.sum(grad_inner.astype(FULL), axis=0, keepdims=True)
        grad_hidden = add(grad_hidden, dot_last(grad_inner, expand))
        grad = to_low(dot_first(hidden_ref[...], grad_inner))
        keep_ref[at], send_ref[at] = parted(grad, ids_ref[CORE_SLOT], keep_ref.shape[1:])
    if not last:
        out_held[...] = out
        grad_held[...] = grad_hidden
        return
    lanes = lane_ids((1, LANES))
    gain, contract_bias = vectors_ref[0:1, :], vectors_ref[2:3, :]
    output_weight = weights(pair_mine[0], pair_other[0], ids_ref)
    mixed = mixed_ref[...]
    middle = tokens_ref[...].astype(FULL) + dot_plain(mixed, output_weight)
    out_ref[...] = to_low(out + middle + contract_bias)
    unit, factor = normalize(middle)
    cotangent = cotangent_ref[...].astype(FULL)
    branch = to_low(cotangent + norm_backward(grad_hidden, unit, factor, gain))
    branch_ref[...] = branch
    grad_rows_ref[...] = jnp.zeros_like(grad_rows_ref)
    grad_rows_ref[0:1, :] = jnp.sum(grad_hidden * unit, axis=0, keepdims=True)
    grad_rows_ref[1:2, :] = jnp.sum(grad_hidden, axis=0, keepdims=True)
    grad_rows_ref[2:3, :] = jnp.sum(cotangent, axis=0, keepdims=True)
    grad = to_low(dot_first(mixed, branch))
    keep_ref[count], send_ref[count] = parted(grad, ids_ref[CORE_SLOT], keep_ref.shape[1:])
    grad_mixed = dot_last(branch, output_weight)
    scaled = []
    for j in range(2):
        weighted = jnp.where(lanes < head, choose(grad_mixed, routes_ref[j], head), 0.0)
        scaled.append(gates_ref[j] * lane_sum(weighted * attn_ref[j]))
        grad_attn = weighted * gates_ref[j]
        grad_attn_ref[j] = to_low(put_parts(grad_attn, lanes, SUM_LANE, -scaled[j], 3))
    mean = scaled[0] + scaled[1]
    grad_logits = jnp.zeros(gates_ref.shape[1:], FULL)
    for j in range(2):
        grad_picked = scaled[j] - gates_ref[j] * mean
        grad_logits = jnp.where(lanes == routes_ref[j], grad_picked, grad_logits)
    grad_logits_ref[...] = to_low(grad_logits)


def backward_kernel(ids_ref, query_ref, grad_ref, bounds_ref, *rest, head, first, masks, part):
    count = len(masks)
    kv_refs, rest = rest[:count], list(rest[count:])
    before_ref = None if first else rest.pop(0)
    grad_query_ref, grad_kv_refs = rest[0], rest[1:]
    lanes = lane_ids((1, LANES))
    key_count = kv_refs[0].shape[0]
    blocks = []
    for index, ref in enumerate(kv_refs):
        start = (ids_ref[SEQ_SLOT] ^ masks[index]) * key_count
        hot = in_document(bounds_ref, row_positions(start, key_count))
        blocks.append(key_rows_of(ref[...], hot, head))
    totals = [None] * count
    for start in range(0, query_ref.shape[0], part):
        rows = slice(start, start + part)
        query = query_ref[rows, :]
        grad = grad_ref[rows, :]
        only_query = to_low(jnp.where(lanes < head, query.astype(FULL), 0.0))
        turned = pltpu.roll(grad.astype(FULL), head, 1)
        only_grad = to_low(jnp.where(lanes < head, 0.0, turned))
        grad_query = None if first else before_ref[rows, :]
        for index, (keys, values) in enumerate(blocks):
            probs = jnp.exp(dot_last(keys, query))
            grad_scores = to_low(probs * dot_last(values, grad))
            update = dot_plain(grad_scores, only_query) + dot_plain(to_low(probs), only_grad)
            totals[index] = update if totals[index] is None else totals[index] + update
            step = dot_first(grad_scores, keys)
            grad_query = step if grad_query is None else grad_query + step
        grad_query_ref[rows, :] = grad_query
    for index in range(count):
        grad_kv_refs[index][...] = to_low(totals[index])


def placed_kernel(
    ids_ref, grad_query_ref, hidden_ref, routes_ref, grad_logits_ref, small_ref, grad_hidden_ref,
    keep_ref, send_ref, grad_router_ref, *, head
):
    count, width = hidden_ref.shape
    rows = [
        doubled_head(
            to_low(grad_query_ref[j * count : (j + 1) * count, :] * head**-0.5).astype(FULL), head
        )
        for j in range(2)
    ]
    placed = to_low(place(rows, [routes_ref[j] for j in range(2)], head, width))
    hidden = hidden_ref[...]
    grad_logits = grad_logits_ref[...]
    keep, send = parted(to_low(dot_first(hidden, placed)), ids_ref[CORE_SLOT], keep_ref.shape)
    keep_ref[...] = keep
    send_ref[...] = send
    grad_router_ref[...] = dot_first(hidden, grad_logits)
    grad_hidden_ref[...] = dot_last(placed, small_ref[:, :width]) + dot_last(
        grad_logits, small_ref[:, small_ref.shape[1] - LANES :]
    )


def last_kernel(
    ids_ref, tokens_ref, hidden_ref, grad_hidden_ref, grad_middle_ref, small_ref, rows_ref, bias_ref,
    bias_two_ref, grad_router_ref, own_ref, *rest, experts, others, rows
):
    other_refs = rest[:others]
    grad_tokens_ref, keep_ref, send_ref = rest[-3:]
    side = small_ref[:, small_ref.shape[1] - 2 * LANES :]
    gain = side[:, LANES:].astype(FULL).T[experts : experts + 1]
    grad_kv = own_ref[...].astype(FULL)
    for ref in other_refs:
        grad_kv += ref[...].astype(FULL)
    grad_kv = to_low(grad_kv)
    grad_keyval = dot_first(hidden_ref[...], grad_kv)
    grad_hidden = grad_hidden_ref[...] + dot_last(grad_kv, side[:, :LANES])
    unit, factor = normalize(tokens_ref[...].astype(FULL))
    grad_tokens_ref[...] = to_low(
        grad_middle_ref[...].astype(FULL) + norm_backward(grad_hidden, unit, factor, gain)
    )
    width = tokens_ref.shape[1]
    gain_grad = jnp.sum(grad_hidden * unit, axis=0, keepdims=True)
    shift_grad = jnp.sum(grad_hidden, axis=0, keepdims=True)
    index = lax.broadcasted_iota(jnp.int32, (8, 1), 0)
    later = pltpu.roll(rows_ref[...], 2, 0)
    vectors = jnp.where(index == 0, gain_grad, jnp.where(index == 1, shift_grad, later))
    ahead = jnp.zeros((experts, width), FULL)
    behind = jnp.zeros((LANES - experts - 8, width), FULL)
    columns = jnp.concatenate([ahead, vectors, behind], axis=0).T
    bias = jnp.concatenate([bias_ref[...], bias_two_ref[...]], axis=1)
    spread = bias_rows(bias, width // rows, rows)
    grad_side = jnp.concatenate([grad_keyval, columns + grad_router_ref[...] + spread], axis=1)
    keep, send = parted(to_low(grad_side), ids_ref[CORE_SLOT], keep_ref.shape)
    keep_ref[...] = keep
    send_ref[...] = send


def finish_kernel(*refs, terms, slots):
    count = terms // 3
    total, last, rest = (
        sum(ref[...].astype(FULL) for ref in refs[i : i + count]) for i in range(0, terms, count)
    )
    expand_ref, output_ref, contract_ref, query_ref, router_ref, keyval_ref = refs[terms : terms + 6]
    *vector_refs, bias_ref = refs[terms + 6 :]
    rows, width = output_ref.shape
    part = lambda index: total[index * rows : (index + 1) * rows]
    for slot in range(slots):
        expand_ref[:, slot * width : (slot + 1) * width] = part(slot)
    output_ref[...] = part(slots)
    query_ref[...] = last[:rows]
    side = last[rows:]
    contract_ref[...] = rest
    experts = router_ref.shape[0]
    keyval_ref[...] = side[:, :LANES]
    for expert in range(experts):
        lane = LANES + expert
        router_ref[expert : expert + 1, :] = as_row(side[:, lane : lane + 1])
    for index, ref in enumerate(vector_refs):
        lane = LANES + experts + index
        ref[...] = as_row(side[:, lane : lane + 1])
    start = LANES + BIAS_LANE
    bias_ref[...] = side[0:1, start : start + bias_ref.shape[1]]


def in_hbm(array):
    return pltpu.with_memory_space_constraint(array, pltpu.HBM)


def smem_spec():
    return pl.BlockSpec(memory_space=pltpu.SMEM)


def vmem_spec():
    return pl.BlockSpec(memory_space=pltpu.VMEM)


def shape_of(shape, dtype):
    return jax.ShapeDtypeStruct(tuple(shape), dtype)


def limit_of(name):
    return LIMITS[name] * MEGA


def estimate(cost):
    return pl.CostEstimate(flops=int(cost * 1e9), bytes_accessed=0, transcendentals=0)


def call(kernel, name, outs, cost, scalars=0, more=0):
    def run(*operands):
        return pl.pallas_call(
            kernel,
            in_specs=[smem_spec()] * scalars + [vmem_spec()] * (len(operands) - scalars),
            out_specs=[vmem_spec()] * len(outs) if isinstance(outs, list) else vmem_spec(),
            out_shape=outs,
            compiler_params=pltpu.CompilerParams(vmem_limit_bytes=limit_of(name) + more * MEGA),
            cost_estimate=estimate(cost),
            name=name,
        )(*operands)

    return run


def generations(seq_count):
    masks = range(1, seq_count)
    most = seq_count.bit_length() - 1
    return [[m for m in masks if bin(m).count("1") == n] for n in range(1, most + 1)]


def feed_up(ids, tokens, cotangent, attn, gates, routes, vectors, bias, pairs, plain, head):
    token_count, width = tokens.shape
    chunks = pairs[0].shape[0] - 1
    rows = shape_of((token_count, width), LOW)
    held = shape_of((chunks, token_count, bias.shape[1] // chunks), LOW)
    return call(
        functools.partial(up_kernel, head=head), "feed_up", [rows, rows, held, held]
        + [shape_of(plain, LOW)] * 2, FEED_COST / 2, scalars=1
    )(ids, tokens, cotangent, attn, gates, routes, vectors, bias, *pairs)


def feed_down(ids, hidden, cotangent, active, steep, pairs, contracts, first, count, head, end=()):
    token_count, width = hidden.shape
    inner = active.shape[2]
    last = bool(end)
    rows = (token_count, width)
    grads = shape_of((count + (1 if last else 0),) + pairs[0].shape[1:], LOW)
    if last:
        outs = [
            shape_of(rows, LOW),
            shape_of(rows, LOW),
            shape_of((2, token_count, LANES), LOW),
            shape_of((token_count, LANES), LOW),
            shape_of((8, width), FULL),
        ]
    else:
        outs = [shape_of(rows, FULL)] * 2
    return call(
        functools.partial(down_kernel, head=head, first=first, count=count, last=last),
        "feed_down_last" if last else "feed_down",
        outs + [grads, grads, shape_of((1, count * inner), FULL)],
        FEED_COST / 2,
        scalars=1,
    )(ids, hidden, cotangent, active, steep, *pairs, *contracts, *end)


def per_device(
    tokens, routes, lengths, cotangent, first_gain, first_shift, router, query_map, keyval,
    output_map, second_gain, second_shift, expand, expand_bias, contract, contract_bias
):
    seq_count, plane_count = lax.axis_size("seq"), lax.axis_size("dp") // 2
    along = Group("seq", 0, seq_count, SEQ_SLOT)
    plane = Group("dp", 1, plane_count, PLANE_SLOT)
    core = Group("dp", 0, 2, CORE_SLOT)
    token_count, width = tokens.shape
    rows = first_gain.shape[0]
    contract_rows = contract.shape[0]
    experts = router.shape[1]
    head = keyval.shape[1] // 2
    inner_width = expand.shape[1]
    chunks = inner_width // width
    slots = 1 + chunks
    my_index = along.index()
    ids = jnp.stack([g.index() for g in (along, plane, core)]).astype(jnp.int32)
    side_width = 2 * LANES
    row_count = 2 * token_count
    part = min(1024, row_count)

    params = [
        query_map, keyval, router.T, first_gain[None], first_shift[None], second_gain[None],
        second_shift[None], contract_bias[None], expand_bias[None], output_map, expand, contract
    ]
    small_mine, large_mine = pl.pallas_call(
        functools.partial(pack_kernel, count=len(params)),
        in_specs=[pl.BlockSpec(memory_space=pltpu.HBM)] * len(params),
        out_specs=[vmem_spec()] * 2,
        out_shape=[
            shape_of((rows, width + side_width), LOW),
            shape_of((slots * rows + contract_rows, width), LOW),
        ],
        scratch_shapes=[pltpu.VMEM(p.shape, p.dtype) for p in params]
        + [pltpu.SemaphoreType.DMA((len(params),))],
        compiler_params=pltpu.CompilerParams(vmem_limit_bytes=limit_of("pack")),
        cost_estimate=estimate(0.1),
        name="pack",
    )(*[in_hbm(p) for p in params])

    def first_work():
        given = [routes.T, lengths]
        return pl.pallas_call(
            first_kernel,
            in_specs=[smem_spec()] + [pl.BlockSpec(memory_space=pltpu.HBM)] * 2,
            out_specs=[vmem_spec()] * 2 + [smem_spec()],
            out_shape=[
                shape_of((2, token_count, LANES), jnp.int32),
                shape_of((8, LANES), jnp.int32),
                shape_of(ids.shape, jnp.int32),
            ],
            scratch_shapes=[pltpu.VMEM(p.shape, p.dtype) for p in given]
            + [pltpu.SemaphoreType.DMA((2,))],
            compiler_params=pltpu.CompilerParams(vmem_limit_bytes=limit_of("first")),
            cost_estimate=estimate(0.1),
            name="first",
        )(ids, *[in_hbm(p) for p in given])


    small_move = Move(along, small_mine[None])
    masks = list(range(1, seq_count))
    early = len(masks) - max(1, len(masks) // 3)
    large_moves = [Move(along, large_mine, masks[:early]), Move(along, large_mine, masks[early:])]
    route_columns, bounds, ids, large_mine = phase(
        [small_move, large_moves[0]], first_work, held=[large_mine]
    )
    for group in (along, plane, core):
        group.ids = ids
    small = merge([small_mine[None]] + [small_move.got[m] for m in range(1, seq_count)], along)
    large_mine, small = together(large_mine, small)
    large_moves[1].blocks = {m: large_mine for m in masks}
    small_move = Move(plane, small)
    phase([small_move, large_moves[1]])
    small = merge([small] + [small_move.got[m] for m in range(1, plane_count)], plane)[0]
    small_move = Move(core, small)
    phase([small_move])
    small_shape = (plane_count, seq_count * rows, width + side_width)
    smalls = [small.reshape(small_shape), small_move.got[1].reshape(small_shape)]
    hidden, kv_mine, gates, small = call(
        functools.partial(hidden_kernel, experts=experts),
        "hidden",
        [
            shape_of((token_count, width), LOW),
            shape_of((token_count, LANES), LOW),
            shape_of((2, token_count, LANES), FULL),
            shape_of((width, width + side_width), LOW),
        ],
        0.5,
        scalars=1,
    )(ids, tokens, *smalls, route_columns)

    def attend(state, masks, queries, last=False):
        return call(
            functools.partial(
                forward_kernel, head=head, first=not state, last=last, masks=masks, part=part
            ),
            "attention_forward",
            [shape_of((row_count, LANES), t) for t in ((FULL, LOW) if last else (FULL,))],
            FORWARD_COST * len(masks),
            scalars=1,
            more=3 * (len(masks) - 1),
        )(ids, queries, bounds, *[shards[m] for m in masks], *state)

    def keys_of(masks):
        return [Move(along, shards[m & (m - 1)], [m & -m]) for m in masks]

    def come(masks, moves):
        for mask, move in zip(masks, moves):
            shards[mask] = move.got[mask & -mask]

    shards = {0: kv_mine}
    coming = generations(seq_count)
    keys = keys_of(coming[0])

    for move in keys:
        move.begin()
    queries = call(
        functools.partial(query_kernel, head=head),
        "queries",
        shape_of((row_count, LANES), LOW),
        QUERY_COST,
        scalars=1,
    )(ids, hidden, small, route_columns, bounds)
    blocks = [large_mine] + [m.got[x] for m in large_moves for x in m.masks]
    queries, *blocks = together(queries, *blocks)
    if rows % 16:
        lines = jnp.stack(by_place(blocks, my_index))
        pair = lines[:, : slots * rows].reshape(seq_count, slots, rows, width)
        pair = pair.transpose(1, 0, 2, 3).reshape(slots, seq_count * rows, width)
        half = lines[:, slots * rows :].reshape(1, seq_count * contract_rows, width)
    else:
        pair, half = call(
            functools.partial(spread_kernel, count=seq_count, slots=slots, rows=rows),
            "spread",
            [
                shape_of((slots, seq_count * rows, width), LOW),
                shape_of((seq_count * contract_rows, width), LOW),
            ],
            0.1,
            scalars=1,
        )(ids, *blocks)
        half = half[None]
    pair_move = Move(plane, pair).begin()
    [state] = phase(keys, lambda: attend([], [0], queries))
    come(coming[0], keys)
    for before, masks in zip(coming, coming[1:]):
        keys = keys_of(masks)
        moves = keys + [pair_move] if masks is coming[-1] else keys
        [state] = phase(moves, lambda: attend([state], before, queries))
        come(masks, keys)
    pair = merge([pair] + [pair_move.got[m] for m in range(1, plane_count)], plane)
    pair = pair.reshape(slots, plane_count, -1, width)
    pair_move = Move(core, pair)
    half_move = Move(plane, half).begin()
    attn, wide_queries = phase([pair_move], lambda: attend([state], coming[-1], queries, True))
    attn = attn.reshape(2, token_count, LANES)
    pairs = [pair, pair_move.got[1]]
    vectors, bias = call(
        functools.partial(vectors_kernel, experts=experts, rows=rows),
        "vectors",
        [shape_of((8, width), FULL), shape_of((1, inner_width), FULL)],
        0.1,
    )(small)

    plain = (plane_count, seq_count * contract_rows, width)
    mixed, hidden_two, active, steep, keep_half, send_half = phase(
        [half_move],
        lambda: feed_up(
            ids, tokens, cotangent, attn, gates, route_columns, vectors, bias, pairs, plain, head
        ),
    )
    half = merge([half] + [half_move.got[m] for m in range(1, plane_count)], plane)
    half = half.reshape(plane_count, -1, width)
    half_move = Move(core, half)
    phase([half_move])
    halves = [half, half_move.got[1]]
    half_move = Move(core, send_half)
    middle_chunk = chunks // 2
    out_held, grad_held, keep_expand, send_expand, grad_bias = phase(
        [half_move],
        lambda: feed_down(
            ids, hidden_two, cotangent, active, steep, pairs, halves, 0, middle_chunk, head
        ),
    )
    flat = lambda lead, *terms: [t.reshape(lead, -1, width) for t in terms]
    half_sent = cut([flat(1, keep_half, half_move.got[1])], plane, width)
    half_move, expand_move = Move(plane, dict(enumerate(half_sent))), Move(core, send_expand)
    (
        out, branch, grad_attn, grad_logits, grad_rows, keep_pair, send_pair, grad_bias_two
    ) = phase(
        [half_move, expand_move],
        lambda: feed_down(
            ids, hidden_two, cotangent, active, steep, pairs, halves, middle_chunk,
            chunks - middle_chunk, head,
            (out_held, grad_held, tokens, mixed, attn, gates, route_columns, vectors),
        ),
    )

    grad_rows_in = grad_attn.reshape(row_count, LANES)
    masks = list(range(seq_count - 1, 0, -1))
    if seq_count > 2:
        masks = [2] + [m for m in masks if m != 2]
    third = max(1, len(masks) // 3)
    groups = [masks[:third], masks[third:], [0]]

    def backward(masks, before):
        return call(
            functools.partial(
                backward_kernel, head=head, first=before is None, masks=masks, part=part
            ),
            "attention_backward",
            [shape_of((row_count, LANES), FULL)]
            + [shape_of((token_count, LANES), LOW)] * len(masks),
            BACKWARD_COST * len(masks),
            scalars=1,
            more=3 * (len(masks) - 1),
        )(
            ids, wide_queries, grad_rows_in, bounds, *[shards[m] for m in masks],
            *([] if before is None else [before])
        )

    half_terms = [half_sent[0]] + list(half_move.got.values())
    half_sent = cut([flat(1, *half_terms)], along, width)
    half_move, pair_move = Move(along, dict(enumerate(half_sent))), Move(core, send_pair)
    first_query, *leaving = phase([half_move, pair_move], lambda: backward(groups[0], None))
    lead = chunks - middle_chunk + 1
    pair_sent = cut(
        [
            flat(middle_chunk, keep_expand, expand_move.got[1]),
            flat(lead, keep_pair, pair_move.got[1]),
        ],
        plane,
        width,
    )
    pair_move = Move(plane, dict(enumerate(pair_sent)))
    keys_first = Move(along, dict(zip(groups[0], leaving)), groups[0])
    second_query, *leaving = phase([keys_first, pair_move], lambda: backward(groups[1], first_query))
    keys_second = Move(along, dict(zip(groups[1], leaving)), groups[1])

    def work():
        grad_query, own = backward(groups[2], second_query)
        shape = (plane_count, seq_count * rows, width)
        return own, *call(
            functools.partial(placed_kernel, head=head),
            "query_gradient",
            [
                shape_of((token_count, width), FULL),
                shape_of(shape, LOW),
                shape_of(shape, LOW),
                shape_of((width, LANES), FULL),
            ],
            1.0,
            scalars=1,
        )(ids, grad_query, hidden, route_columns, grad_logits, small)

    pair_terms = [pair_sent[0]] + list(pair_move.got.values())
    grad_kv, grad_hidden, keep_query, send_query, grad_router, *pair_terms = phase(
        [keys_second], work, held=pair_terms
    )
    query_move = Move(core, send_query)
    others = list(keys_first.got.values()) + list(keys_second.got.values())
    shape = (plane_count, seq_count * rows, side_width)
    grad_tokens, keep_side, send_side, *pair_terms = phase(
        [query_move],
        lambda: call(
            functools.partial(last_kernel, experts=experts, others=len(others), rows=rows),
            "key_gradient",
            [shape_of((token_count, width), LOW), shape_of(shape, LOW), shape_of(shape, LOW)],
            1.0,
            scalars=1,
        )(
            ids, tokens, hidden, grad_hidden, branch, small, grad_rows, grad_bias, grad_bias_two,
            grad_router, grad_kv, *others
        ),
        held=pair_terms,
    )

    side_move = Move(core, send_side)
    phase([side_move])
    line = lambda *terms: [t.reshape(1, -1, t.shape[-1]) for t in terms]
    small_sent = cut(
        [line(keep_query, query_move.got[1]), line(keep_side, side_move.got[1])],
        plane,
        width + side_width,
    )
    small_move = Move(plane, dict(enumerate(small_sent)))
    pair_sent = dict(enumerate(cut([flat(slots, *pair_terms)], along, width)))
    masks = list(range(1, seq_count))
    pair_moves = [Move(along, pair_sent, masks[:1]), Move(along, pair_sent, masks[1:]).begin()]
    phase([small_move, pair_moves[0]])
    last_sent = cut([line(small_sent[0], *small_move.got.values())], along, width)
    last_move = Move(along, dict(enumerate(last_sent)))
    phase([pair_moves[1], last_move])
    terms = [pair_sent[0]] + [x for m in pair_moves for x in m.got.values()]
    terms += [last_sent[0]] + list(last_move.got.values())
    terms += [half_sent[0]] + list(half_move.got.values())
    vector_shape = shape_of((1, rows), FULL)
    (
        grad_expand, grad_output, grad_contract, grad_query_map, grad_router, grad_keyval,
        *vector_sums, grad_spread
    ) = call(
        functools.partial(finish_kernel, terms=len(terms), slots=chunks),
        "finish",
        [
            shape_of(expand.shape, FULL),
            shape_of(output_map.shape, FULL),
            shape_of(contract.shape, FULL),
            shape_of(query_map.shape, FULL),
            shape_of((experts, rows), FULL),
            shape_of(keyval.shape, FULL),
        ]
        + [vector_shape] * 5
        + [shape_of((1, expand_bias.shape[0]), FULL)],
        0.1,
    )(*terms)
    grad_gain, grad_shift, grad_gain_two, grad_shift_two, grad_contract_bias = (
        v.reshape(rows) for v in vector_sums
    )
    return (
        out, grad_tokens, grad_gain, grad_shift, grad_router.T, grad_query_map, grad_keyval,
        grad_output, grad_gain_two, grad_shift_two, grad_expand, grad_spread.reshape(-1),
        grad_contract, grad_contract_bias
    )


def solution(mesh):
    both = ("dp", "seq")
    rows, vector = P(both, None), P(both)
    return jax.shard_map(
        per_device,
        mesh=mesh,
        in_specs=(
            rows, rows, P("dp", None), rows, vector, vector, rows, rows, rows, rows, vector, vector,
            rows, vector, rows, vector
        ),
        out_specs=(
            rows, rows, vector, vector, rows, rows, rows, rows, vector, vector, rows, vector, rows,
            vector
        ),
        check_vma=False,
    )
```

```python
import functools

import jax
import jax.numpy as jnp
from jax import lax
from jax.experimental import pallas as pl
from jax.experimental.pallas import tpu as pltpu
from jax.sharding import PartitionSpec as P

LOW = jnp.bfloat16
FULL = jnp.float32
FAR = 1e30
EPS = 1e-05
DOC_LANE = 64
LSE_LANE = 96
SUM_LANE = 64
MAX_LANE = 67
BIAS_LANE = 64
SEQ_SLOT, PLANE_SLOT, CORE_SLOT = range(3)
LANES = 128
MEGA = 1 << 20
FORWARD_COST = 0.1
QUERY_COST = 0.05
BACKWARD_COST = 3.0
FEED_COST = 8.0
LIMITS = {
    "pack": 4, "first": 8, "hidden": 6, "vectors": 2, "queries": 6, "attention_forward": 8,
    "attention_backward": 8, "query_gradient": 8, "key_gradient": 12, "token_gradient": 12, "merge": 2, "spread": 2,
    "cut": 3, "fold": 4, "finish": 2, "feed_up": 24,
    "feed_down": 24, "feed_down_last": 24,
}


def to_low(matrix):
    return matrix.astype(LOW)


def dot_plain(left, right):
    return lax.dot_general(left, right, (((1,), (0,)), ((), ())), preferred_element_type=FULL)


def dot_last(left, right):
    return lax.dot_general(left, right, (((1,), (1,)), ((), ())), preferred_element_type=FULL)


def dot_first(left, right):
    return lax.dot_general(left, right, (((0,), (0,)), ((), ())), preferred_element_type=FULL)


class Group:
    def __init__(self, axis, shift, size, slot):
        self.axis, self.shift, self.size, self.slot = axis, shift, size, slot
        self.ids = None

    def index(self):
        return (lax.axis_index(self.axis) >> self.shift) & (self.size - 1)

    def exchange(self, block, mask):
        step = mask << self.shift
        pairs = [(i, i ^ step) for i in range(lax.axis_size(self.axis))]
        return lax.ppermute(block, self.axis, pairs)


def by_place(blocks, index):
    blocks = list(blocks)
    for bit in range(len(blocks).bit_length() - 1):
        swap = (index >> bit) & 1 == 1
        blocks = [jnp.where(swap, blocks[i ^ (1 << bit)], blocks[i]) for i in range(len(blocks))]
    return blocks


def merge_kernel(ids_ref, *refs, count, slot):
    out_ref = refs[count]
    rows = refs[0].shape[1]
    for mask in range(count):
        start = pl.multiple_of((ids_ref[slot] ^ mask) * rows, rows)
        out_ref[:, pl.ds(start, rows), :] = refs[mask][...]


def merge(blocks, group):
    lead, rows, columns = blocks[0].shape
    if rows % 16:
        return jnp.concatenate(by_place(blocks, group.index()), axis=1)
    return call(
        functools.partial(merge_kernel, count=len(blocks), slot=group.slot),
        "merge",
        shape_of((lead, rows * len(blocks), columns), blocks[0].dtype),
        0.1,
        scalars=1,
    )(group.ids, *blocks)


def columns_of(columns, width):
    return [slice(i, min(i + width, columns)) for i in range(0, columns, width)]


def cut_kernel(ids_ref, *refs, sizes, count, slot):
    outs = refs[len(refs) - count :]
    refs = list(refs[: len(refs) - count])
    sets = [[refs.pop(0) for _ in range(size)] for size in sizes]
    width = outs[0].shape[1]
    for mask in range(count):
        row = column = 0
        for terms in sets:
            lead, total, columns = terms[0].shape
            rows = total // count
            start = pl.multiple_of((ids_ref[slot] ^ mask) * rows, rows)
            for at in range(lead):
                for piece in columns_of(columns, width):
                    value = sum(term[at, pl.ds(start, rows), piece].astype(FULL) for term in terms)
                    end = column + value.shape[1]
                    outs[mask][row : row + rows, column:end] = to_low(value)
                    column = end % width
                    row += 0 if column else rows
        if column:
            rest = outs[mask].shape[0] - row
            outs[mask][row:, column:] = jnp.zeros((rest, width - column), LOW)


def cut(sets, group, width):
    count = group.size
    sets = [[t.reshape((-1,) + t.shape[-2:]) for t in terms] for terms in sets]
    rows = [terms[0].shape[1] // count for terms in sets]
    total = sum(t[0].shape[0] * r * t[0].shape[2] for t, r in zip(sets, rows))
    total = -(-total // (width * rows[-1])) * rows[-1]
    if any(r % 16 for r in rows):
        index = group.index()
        results = []
        for mask in range(count):
            bands, band = [], []
            for terms, r in zip(sets, rows):
                value = sum(t.astype(FULL) for t in terms)
                value = lax.dynamic_slice_in_dim(value, (index ^ mask) * r, r, 1)
                for at in range(value.shape[0]):
                    for piece in columns_of(value.shape[2], width):
                        band.append(value[at, :, piece])
                        if sum(b.shape[1] for b in band) == width:
                            bands.append(jnp.concatenate(band, axis=1))
                            band = []
            if band:
                band = jnp.concatenate(band, axis=1)
                bands.append(jnp.pad(band, ((0, 0), (0, width - band.shape[1]))))
            results.append(to_low(jnp.concatenate(bands, axis=0)))
        return results
    return call(
        functools.partial(
            cut_kernel, sizes=[len(t) for t in sets], count=count, slot=group.slot
        ),
        "cut",
        [shape_of((total, width), LOW)] * count,
        0.1,
        scalars=1,
    )(group.ids, *[t for terms in sets for t in terms])


def together(*values):
    return lax.optimization_barrier(values)


class Move:
    def __init__(self, group, blocks, masks=None):
        self.group = group
        self.masks = list(range(1, group.size)) if masks is None else masks
        self.blocks = blocks if isinstance(blocks, dict) else {m: blocks for m in self.masks}

    def begin(self):
        self.moved = [self.group.exchange(self.blocks[m], m) for m in self.masks]
        return self

    def end(self, got):
        self.got = dict(zip(self.masks, got))
        self.moved = None


def phase(moves, work=lambda: (), held=()):
    for move in moves:
        if getattr(move, "moved", None) is None:
            move.begin()
    done = work()
    ended = list(together(*[x for m in moves for x in m.moved], *done, *held))
    for move in moves:
        move.end([ended.pop(0) for _ in move.masks])
    return ended


def fold_kernel(ids_ref, *refs, plan):
    refs = list(refs)
    folds = [(bit, [[refs.pop(0) for _ in range(n)] for n in sizes]) for bit, sizes in plan]
    for (slot, shift), sets in folds:
        keep_ref, send_ref = refs.pop(0), refs.pop(0)
        bit = (ids_ref[slot] >> shift) & 1
        start = 0
        for terms in sets:
            end = start + terms[0].shape[0]
            keep_ref[start:end] = sum(term[:, bit].astype(FULL) for term in terms)
            send_ref[start:end] = to_low(sum(term[:, 1 - bit].astype(FULL) for term in terms))
            start = end


class Fold:
    def __init__(self, sets, groups):
        self.sets = sets
        bits = [(g, b) for g in groups for b in reversed(range(g.size.bit_length() - 1))]
        self.left = bits
        self.stages = [x for x in bits if x[0].axis == "dp"]
        self.stages += [x for x in bits if x[0].axis == "seq"][::-1]

    def shaped(self):
        ahead = 1 << self.left.index(self.stages[0])
        return [
            [t.reshape(t.shape[0] * ahead, 2, t.shape[1] // (2 * ahead), t.shape[2]) for t in terms]
            for terms in self.sets
        ]


def fold(folds):
    folds = [f for f in folds if f.stages]
    if not folds:
        return []
    plan, operands, outs = [], [], []
    for f in folds:
        sets = f.shaped()
        group, bit = f.stages[0]
        plan.append(((group.slot, bit), [len(terms) for terms in sets]))
        operands += [t for terms in sets for t in terms]
        count = sum(terms[0].shape[0] for terms in sets)
        shape = (count,) + sets[0][0].shape[2:]
        outs += [shape_of(shape, FULL), shape_of(shape, LOW)]
    results = call(
        functools.partial(fold_kernel, plan=plan), "fold", outs, 0.1, scalars=1
    )(folds[0].stages[0][0].ids, *operands)
    moves = []
    for at, f in enumerate(folds):
        group, bit = f.stages.pop(0)
        f.lead = sum(terms[0].shape[0] for terms in f.sets)
        f.left.remove((group, bit))
        f.keep = results[2 * at]
        f.move = Move(group, results[2 * at + 1], [1 << bit])
        moves.append(f.move)
    return moves


def folded(folds):
    for f in folds:
        if getattr(f, "move", None) is not None:
            [got] = f.move.got.values()
            columns = got.shape[-1]
            f.sets = [[t.reshape(f.lead, -1, columns) for t in (f.keep, got)]]
            f.move = None


def lane_ids(shape):
    return lax.broadcasted_iota(jnp.int32, shape, len(shape) - 1)


def row_positions(offset, rows):
    return offset + lax.broadcasted_iota(jnp.int32, (rows, 1), 0)


def in_document(bounds_ref, positions):
    return (positions >= bounds_ref[0:1, :]) & (positions < bounds_ref[1:2, :])


def put_parts(base, lanes, lane, rows, count):
    for step in range(count):
        part = to_low(rows).astype(FULL)
        base = jnp.where(lanes == lane + step, part, base)
        rows = rows - part
    return base


def lane_sum(matrix):
    total = sum(matrix[:, i : i + LANES] for i in range(0, matrix.shape[1], LANES))
    high = to_low(total)
    low = to_low(total - high.astype(FULL))
    ones = jnp.ones((LANES, LANES), LOW)
    return dot_plain(high, ones) + dot_plain(low, ones)


def over(rows, width):
    return jnp.concatenate([rows] * (width // LANES), axis=1)


def normalize(matrix):
    width = matrix.shape[1]
    center = matrix - over(lane_sum(matrix) * (1.0 / width), width)
    factor = lax.rsqrt(lane_sum(center * center) * (1.0 / width) + EPS)
    return center * over(factor, width), factor


def norm_backward(grad, unit, factor, gain):
    width = grad.shape[1]
    scaled = grad * gain
    mean = over(lane_sum(scaled) * (1.0 / width), width)
    along = over(lane_sum(scaled * unit) * (1.0 / width), width)
    return over(factor, width) * (scaled - mean - unit * along)


def choose(wide, route, head):
    shift = (LANES // head).bit_length() - 1
    tile = lax.shift_right_logical(route, shift)
    picked = wide[:, :LANES]
    for index in range(1, wide.shape[1] // LANES):
        picked = jnp.where(tile == index, wide[:, index * LANES : (index + 1) * LANES], picked)
    turned = pltpu.roll(picked, head, 1)
    lanes = lane_ids((1, LANES))
    mine = (lanes // head) == (route & ((1 << shift) - 1))
    return jnp.where(mine, picked, turned)


def place(doubled, routes, head, width):
    lanes = lane_ids((1, LANES))
    per_tile = LANES // head
    tiles = []
    for index in range(width // LANES):
        expert = lanes // head + index * per_tile
        tile = jnp.zeros_like(doubled[0])
        for rows, route in zip(doubled, routes):
            tile = jnp.where(route == expert, rows, tile)
        tiles.append(tile)
    return jnp.concatenate(tiles, axis=1)


def doubled_head(rows, head):
    lanes = lane_ids((1, LANES))
    return jnp.where(lanes < head, rows, pltpu.roll(rows, head, 1))


def key_rows_of(kv, hot, head):
    lanes = lane_ids((1, LANES))
    kv = kv.astype(FULL)
    marks = jnp.where((lanes >= LSE_LANE) & (lanes < LSE_LANE + 3), 1.0, 0.0)
    keys = jnp.where(lanes < head, kv, jnp.where(hot, 1.0, marks))
    ones = jnp.where((lanes >= SUM_LANE) & (lanes < SUM_LANE + 3), 1.0, 0.0)
    values = jnp.where(lanes < head, pltpu.roll(kv, head, 1), ones)
    return to_low(keys), to_low(values)


def as_column(row):
    rows = row.shape[1]
    lanes = lax.broadcasted_iota(jnp.int32, (rows, rows), 1)
    here = lax.broadcasted_iota(jnp.int32, (rows, rows), 0)
    return jnp.sum(jnp.where(lanes == here, row, 0.0), axis=1, keepdims=True)


def as_row(column):
    rows = column.shape[0]
    lanes = lax.broadcasted_iota(jnp.int32, (rows, rows), 1)
    here = lax.broadcasted_iota(jnp.int32, (rows, rows), 0)
    return jnp.sum(jnp.where(lanes == here, column, 0.0), axis=0, keepdims=True)


def fetch(refs, held, semaphores):
    copies = [
        pltpu.make_async_copy(ref, into, semaphores.at[i])
        for i, (ref, into) in enumerate(zip(refs, held))
    ]
    for copy in copies:
        copy.start()
    for copy in copies:
        copy.wait()


def pack_kernel(*refs, count):
    small_ref, large_ref = refs[count : count + 2]
    held = refs[count + 2 : -1]
    fetch(refs[:count], held, refs[-1])
    (
        query_ref, keyval_ref, router_ref, gain_ref, shift_ref, gain_two_ref, shift_two_ref,
        contract_bias_ref, expand_bias_ref, output_ref, expand_ref, contract_ref
    ) = held
    rows, width = query_ref.shape
    experts = router_ref.shape[0]
    keyval_width = keyval_ref.shape[1]
    small_ref[:, :width] = to_low(query_ref[...])
    small_ref[:, width : width + keyval_width] = to_low(keyval_ref[...])
    lanes = lane_ids((1, LANES))
    turned = router_ref[...]
    side = jnp.zeros((rows, LANES), FULL)
    for expert in range(experts):
        side = jnp.where(lanes == expert, as_column(turned[expert : expert + 1]), side)
    vectors = [gain_ref, shift_ref, gain_two_ref, shift_two_ref, contract_bias_ref]
    for index, ref in enumerate(vectors):
        side = jnp.where(lanes == experts + index, as_column(ref[...]), side)
    extra = expand_bias_ref.shape[1]
    bias = jnp.pad(expand_bias_ref[...], ((0, 0), (BIAS_LANE, LANES - BIAS_LANE - extra)))
    first = lax.broadcasted_iota(jnp.int32, (rows, 1), 0) == 0
    side = side + jnp.where(first, bias, 0.0)
    small_ref[:, width + keyval_width :] = to_low(side)
    large = [output_ref[...]]
    large += [
        expand_ref[:, c * width : (c + 1) * width] for c in range(expand_ref.shape[1] // width)
    ]
    large_ref[...] = to_low(jnp.concatenate(large + [contract_ref[...]], axis=0))


def first_kernel(
    ids_ref, routes_hbm, lengths_hbm, tokens_ref, columns_ref, bounds_ref, unit_ref, ids_out, *held
):
    unit_ref[...] = normalize(tokens_ref[...].astype(FULL))[0]
    for slot in range(ids_ref.shape[0]):
        ids_out[slot] = ids_ref[slot]
    routes_ref, lengths_ref, semaphores = held
    fetch((routes_hbm, lengths_hbm), (routes_ref, lengths_ref), semaphores)
    routes = routes_ref[...].astype(FULL)
    choices = routes.shape[0]
    routes = jnp.concatenate([routes, jnp.zeros((8 - routes.shape[0], routes.shape[1]), FULL)], axis=0)
    turned = routes.T
    for j in range(choices):
        wide = jnp.broadcast_to(turned[:, j : j + 1], columns_ref.shape[1:])
        columns_ref[j] = wide.astype(jnp.int32)
    count = lengths_ref.shape[1]
    lanes = lane_ids((1, LANES))
    rest = jnp.zeros((1, LANES - DOC_LANE - count), jnp.int32)
    lengths = jnp.concatenate(
        [jnp.zeros((1, DOC_LANE), jnp.int32), lengths_ref[...], rest], axis=1
    )
    ends = lengths
    step = 1
    while step < count:
        ends = ends + jnp.where(lanes >= DOC_LANE + step, pltpu.roll(ends, step, 1), 0)
        step *= 2
    here = (lanes >= DOC_LANE) & (lanes < DOC_LANE + count)
    starts = jnp.where(here, ends - lengths, 1 << 30)
    ends = jnp.where(here, ends, 0)
    index = lax.broadcasted_iota(jnp.int32, (8, 1), 0)
    bounds_ref[...] = jnp.where(index == 0, starts, jnp.where(index == 1, ends, 0))


def vectors_kernel(small_ref, vectors_ref, bias_ref, *, experts, rows):
    misc = small_ref[:, small_ref.shape[1] - LANES :].astype(FULL)
    turned = misc.T
    vectors_ref[...] = turned[experts + 2 : experts + 10]
    count = misc.shape[0] // rows
    each = bias_ref.shape[1] // count
    per_tile = LANES // each
    firsts = misc.reshape(count, rows, LANES)[:, 0, :].reshape(count // per_tile, per_tile, LANES)
    lanes = lane_ids((1, LANES))
    tiles = jnp.zeros((count // per_tile, LANES), FULL)
    for k in range(per_tile):
        moved = pltpu.roll(firsts[:, k, :], (k * each - BIAS_LANE) % LANES, 1)
        tiles = jnp.where(lanes // each == k, moved, tiles)
    for index in range(count // per_tile):
        bias_ref[:, index * LANES : (index + 1) * LANES] = tiles[index : index + 1]


def bias_rows(bias, count, rows):
    each = bias.shape[1] // count
    per_tile = LANES // each
    tiles = jnp.concatenate(
        [bias[:, i : i + LANES] for i in range(0, bias.shape[1], LANES)], axis=0
    )
    lanes = lane_ids((1, LANES))
    mine = (lanes >= BIAS_LANE) & (lanes < BIAS_LANE + each)
    parts = [
        jnp.where(mine, pltpu.roll(tiles, (BIAS_LANE - k * each) % LANES, 1), 0.0)
        for k in range(per_tile)
    ]
    firsts = jnp.stack(parts, axis=1).reshape(count, 1, LANES)
    here = lax.broadcasted_iota(jnp.int32, (1, rows, 1), 1) == 0
    return jnp.where(here, firsts, 0.0).reshape(count * rows, LANES)


def spread_kernel(ids_ref, *refs, count, slots, rows):
    pair_ref, half_ref = refs[count:]
    more = refs[0].shape[0] - slots * rows
    for mask in range(count):
        place = ids_ref[SEQ_SLOT] ^ mask
        start = pl.multiple_of(place * rows, rows)
        for slot in range(slots):
            pair_ref[slot, pl.ds(start, rows), :] = refs[mask][slot * rows : (slot + 1) * rows, :]
        half_ref[pl.ds(pl.multiple_of(place * more, more), more), :] = refs[mask][slots * rows :, :]


def hidden_kernel(
    ids_ref, unit_ref, mine_ref, other_ref, routes_ref, hidden_ref, kv_ref, gates_ref, small_ref, *, experts
):
    small = merged(mine_ref[...], other_ref[...], ids_ref[CORE_SLOT])
    small_ref[...] = small
    side = small[:, small.shape[1] - 2 * LANES :]
    vectors = side[:, LANES:].astype(FULL).T
    hidden = to_low(
        unit_ref[...] * vectors[experts : experts + 1] + vectors[experts + 1 : experts + 2]
    )
    hidden_ref[...] = hidden
    both = dot_plain(hidden, side)
    kv_ref[...] = to_low(both[:, :LANES])
    logits = both[:, LANES:]
    lanes = lane_ids((1, LANES))
    picked = [lane_sum(jnp.where(lanes == routes_ref[j], logits, 0.0)) for j in range(2)]
    top = jnp.maximum(picked[0], picked[1])
    raised = [jnp.exp(p - top) for p in picked]
    total = raised[0] + raised[1]
    for j in range(2):
        gates_ref[j] = raised[j] / total


def query_kernel(ids_ref, hidden_ref, small_ref, routes_ref, bounds_ref, query_ref, *, head):
    rows, width = hidden_ref.shape
    wide = dot_plain(hidden_ref[...], small_ref[:, :width])
    lanes = lane_ids((1, LANES))
    hot = in_document(bounds_ref, row_positions(ids_ref[SEQ_SLOT] * rows, rows))
    documents = (bounds_ref[1:2, :] > 0) & (lanes >= head)
    marks = jnp.where(documents & jnp.logical_not(hot), -FAR, 0.0)
    for j in range(2):
        rows_of = choose(wide, routes_ref[j], head) * head**-0.5
        query_ref[j * rows : (j + 1) * rows, :] = to_low(jnp.where(lanes < head, rows_of, marks))


def forward_kernel(ids_ref, query_ref, bounds_ref, *rest, head, first, last, masks, part):
    count = len(masks)
    kv_refs, rest = rest[:count], list(rest[count:])
    state_ref = None if first else rest.pop(0)
    lanes = lane_ids((1, LANES))
    blocks = []
    for index, ref in enumerate(kv_refs):
        start = (ids_ref[SEQ_SLOT] ^ masks[index]) * ref.shape[0]
        hot = in_document(bounds_ref, row_positions(start, ref.shape[0]))
        blocks.append(key_rows_of(ref[...], hot, head))
    for start in range(0, query_ref.shape[0], part):
        rows = slice(start, start + part)
        query = query_ref[rows, :]
        state = None if first else state_ref[rows, :]
        for keys, values in blocks:
            scores = dot_last(query, keys)
            top = jnp.max(scores, axis=1, keepdims=True)
            if state is None:
                new = top
                state = dot_plain(to_low(jnp.exp(scores - new)), values)
            else:
                old = state[:, MAX_LANE : MAX_LANE + 1]
                new = jnp.maximum(old, top)
                weights = to_low(jnp.exp(scores - new))
                state = state * jnp.exp(old - new) + dot_plain(weights, values)
            state = jnp.where(lanes == MAX_LANE, new, state)
        if last:
            attn_ref, wide_ref = rest
            total = state[:, SUM_LANE : SUM_LANE + 1]
            attn_ref[rows, :] = jnp.where(lanes < head, state / total, 0.0)
            log_total = state[:, MAX_LANE : MAX_LANE + 1] + jnp.log(total)
            wide_ref[rows, :] = to_low(
                put_parts(query.astype(FULL), lanes, LSE_LANE, -log_total, 3)
            )
        else:
            rest[0][rows, :] = state


def merged(mine, other, bit):
    low = bit == 0
    both = jnp.stack([jnp.where(low, mine, other), jnp.where(low, other, mine)], axis=1)
    return both.reshape(-1, mine.shape[-1])


def parted(whole, bit, shape):
    both = whole.reshape(shape[0], 2, shape[1], shape[2])
    low = bit == 0
    first, second = both[:, 0], both[:, 1]
    return jnp.where(low, first, second), jnp.where(low, second, first)


def weights(refs, bit):
    mine, other = refs[0][...], refs[1][...]
    shape = mine.shape[-3:]
    return merged(mine.reshape(shape), other.reshape(shape), bit)


def weights(mine, other, ids_ref):
    return merged(mine, other, ids_ref[CORE_SLOT])


def chunk_of(refs, chunk, chunks):
    count = refs[0].shape[0] // chunks
    return [ref[chunk * count : (chunk + 1) * count] for ref in refs]


def up_kernel(
    ids_ref, tokens_ref, cotangent_ref, attn_ref, gates_ref, routes_ref, vectors_ref, bias_ref,
    pair_mine, pair_other, mixed_ref, hidden_ref, active_ref, steep_ref, keep_ref, send_ref, *, head
):
    width = tokens_ref.shape[1]
    wide = [doubled_head(attn_ref[j], head) * gates_ref[j] for j in range(2)]
    mixed = to_low(place(wide, [routes_ref[j] for j in range(2)], head, width))
    mixed_ref[...] = mixed
    output_weight = weights(pair_mine[0], pair_other[0], ids_ref)
    middle = tokens_ref[...].astype(FULL) + dot_plain(mixed, output_weight)
    unit, _ = normalize(middle)
    hidden = to_low(unit * vectors_ref[0:1, :] + vectors_ref[1:2, :])
    hidden_ref[...] = hidden
    slope = 0.7978845608028654
    cube = 0.044715
    chunks, _, inner_width = active_ref.shape
    part = min(256, tokens_ref.shape[0])
    groups = keep_ref.shape[0] // chunks
    for chunk in range(chunks):
        expand = weights(pair_mine[chunk + 1], pair_other[chunk + 1], ids_ref)
        columns = slice(chunk * inner_width, (chunk + 1) * inner_width)
        for start in range(0, hidden.shape[0], part):
            here = slice(start, start + part)
            inner = dot_plain(hidden[here], expand) + bias_ref[:, columns]
            square = inner * inner
            half = 0.5 + 0.5 * jnp.tanh(inner * (slope + slope * cube * square))
            whole = inner * half
            active_ref[chunk, here] = to_low(whole)
            steep = half + whole * (1.0 - half) * (2.0 * slope + 6.0 * slope * cube * square)
            steep_ref[chunk, here] = to_low(steep)
        shape = (groups,) + keep_ref.shape[1:]
        grad = to_low(dot_first(active_ref[chunk], cotangent_ref[...]))
        here = slice(chunk * groups, (chunk + 1) * groups)
        keep_ref[here], send_ref[here] = parted(grad, ids_ref[CORE_SLOT], shape)


def down_kernel(
    ids_ref, hidden_ref, cotangent_ref, active_ref, steep_ref, pair_mine, pair_other, contract_mine,
    contract_other, *rest, head, first, count, last
):
    rest = list(rest)
    take = lambda n: [rest.pop(0) for _ in range(n)]
    if last:
        out_before, grad_before, tokens_ref, mixed_ref, attn_ref, gates_ref, routes_ref, vectors_ref = (
            take(8)
        )
        out_ref, branch_ref, grad_attn_ref, grad_logits_ref, grad_rows_ref = take(5)
        out, grad_hidden = out_before[...], grad_before[...]
    else:
        out_held, grad_held = take(2)
        out = grad_hidden = None
    keep_ref, send_ref, grad_bias_ref = take(3)
    chunks, _, inner = active_ref.shape
    add = lambda total, term: term if total is None else total + term
    for at in range(count):
        chunk = first + at
        expand = weights(pair_mine[chunk + 1], pair_other[chunk + 1], ids_ref)
        contract = weights(*chunk_of((contract_mine, contract_other), chunk, chunks), ids_ref)
        out = add(out, dot_plain(active_ref[chunk], contract))
        grad_active = dot_last(cotangent_ref[...], contract)
        grad_inner = to_low(steep_ref[chunk].astype(FULL) * grad_active)
        columns = slice(at * inner, (at + 1) * inner)
        grad_bias_ref[:, columns] = jnp.sum(grad_inner.astype(FULL), axis=0, keepdims=True)
        grad_hidden = add(grad_hidden, dot_last(grad_inner, expand))
        grad = to_low(dot_first(hidden_ref[...], grad_inner))
        keep_ref[at], send_ref[at] = parted(grad, ids_ref[CORE_SLOT], keep_ref.shape[1:])
    if not last:
        out_held[...] = out
        grad_held[...] = grad_hidden
        return
    lanes = lane_ids((1, LANES))
    gain, contract_bias = vectors_ref[0:1, :], vectors_ref[2:3, :]
    output_weight = weights(pair_mine[0], pair_other[0], ids_ref)
    mixed = mixed_ref[...]
    middle = tokens_ref[...].astype(FULL) + dot_plain(mixed, output_weight)
    out_ref[...] = to_low(out + middle + contract_bias)
    unit, factor = normalize(middle)
    cotangent = cotangent_ref[...].astype(FULL)
    branch = to_low(cotangent + norm_backward(grad_hidden, unit, factor, gain))
    branch_ref[...] = branch
    grad_rows_ref[...] = jnp.zeros_like(grad_rows_ref)
    grad_rows_ref[0:1, :] = jnp.sum(grad_hidden * unit, axis=0, keepdims=True)
    grad_rows_ref[1:2, :] = jnp.sum(grad_hidden, axis=0, keepdims=True)
    grad_rows_ref[2:3, :] = jnp.sum(cotangent, axis=0, keepdims=True)
    grad = to_low(dot_first(mixed, branch))
    keep_ref[count], send_ref[count] = parted(grad, ids_ref[CORE_SLOT], keep_ref.shape[1:])
    grad_mixed = dot_last(branch, output_weight)
    scaled = []
    for j in range(2):
        weighted = jnp.where(lanes < head, choose(grad_mixed, routes_ref[j], head), 0.0)
        scaled.append(gates_ref[j] * lane_sum(weighted * attn_ref[j]))
        grad_attn = weighted * gates_ref[j]
        grad_attn_ref[j] = to_low(put_parts(grad_attn, lanes, SUM_LANE, -scaled[j], 3))
    mean = scaled[0] + scaled[1]
    grad_logits = jnp.zeros(gates_ref.shape[1:], FULL)
    for j in range(2):
        grad_picked = scaled[j] - gates_ref[j] * mean
        grad_logits = jnp.where(lanes == routes_ref[j], grad_picked, grad_logits)
    grad_logits_ref[...] = to_low(grad_logits)


def backward_kernel(ids_ref, query_ref, grad_ref, bounds_ref, *rest, head, first, masks, part):
    count = len(masks)
    kv_refs, rest = rest[:count], list(rest[count:])
    before_ref = None if first else rest.pop(0)
    grad_query_ref, grad_kv_refs = rest[0], rest[1:]
    lanes = lane_ids((1, LANES))
    key_count = kv_refs[0].shape[0]
    blocks = []
    for index, ref in enumerate(kv_refs):
        start = (ids_ref[SEQ_SLOT] ^ masks[index]) * key_count
        hot = in_document(bounds_ref, row_positions(start, key_count))
        blocks.append(key_rows_of(ref[...], hot, head))
    totals = [None] * count
    for start in range(0, query_ref.shape[0], part):
        rows = slice(start, start + part)
        query = query_ref[rows, :]
        grad = grad_ref[rows, :]
        only_query = to_low(jnp.where(lanes < head, query.astype(FULL), 0.0))
        turned = pltpu.roll(grad.astype(FULL), head, 1)
        only_grad = to_low(jnp.where(lanes < head, 0.0, turned))
        grad_query = None if first else before_ref[rows, :]
        for index, (keys, values) in enumerate(blocks):
            probs = jnp.exp(dot_last(keys, query))
            grad_scores = to_low(probs * dot_last(values, grad))
            update = dot_plain(grad_scores, only_query) + dot_plain(to_low(probs), only_grad)
            totals[index] = update if totals[index] is None else totals[index] + update
            step = dot_first(grad_scores, keys)
            grad_query = step if grad_query is None else grad_query + step
        grad_query_ref[rows, :] = grad_query
    for index in range(count):
        grad_kv_refs[index][...] = to_low(totals[index])


def placed_kernel(
    ids_ref, grad_query_ref, hidden_ref, routes_ref, grad_logits_ref, small_ref, tokens_ref,
    grad_hidden_ref, keep_ref, send_ref, grad_router_ref, unit_ref, factor_ref, *, head
):
    unit_ref[...], factor_ref[...] = normalize(tokens_ref[...].astype(FULL))
    count, width = hidden_ref.shape
    rows = [
        doubled_head(
            to_low(grad_query_ref[j * count : (j + 1) * count, :] * head**-0.5).astype(FULL), head
        )
        for j in range(2)
    ]
    placed = to_low(place(rows, [routes_ref[j] for j in range(2)], head, width))
    hidden = hidden_ref[...]
    grad_logits = grad_logits_ref[...]
    keep, send = parted(to_low(dot_first(hidden, placed)), ids_ref[CORE_SLOT], keep_ref.shape)
    keep_ref[...] = keep
    send_ref[...] = send
    grad_router_ref[...] = dot_first(hidden, grad_logits)
    grad_hidden_ref[...] = dot_last(placed, small_ref[:, :width]) + dot_last(
        grad_logits, small_ref[:, small_ref.shape[1] - LANES :]
    )


def side_kernel(
    ids_ref, hidden_ref, grad_before_ref, unit_ref, small_ref, rows_ref, bias_ref, bias_two_ref,
    grad_router_ref, own_ref, *rest, experts, others, rows
):
    other_refs = rest[:others]
    grad_hidden_ref, keep_ref, send_ref = rest[others:]
    side = small_ref[:, small_ref.shape[1] - 2 * LANES :]
    grad_kv = own_ref[...].astype(FULL)
    for ref in other_refs:
        grad_kv += ref[...].astype(FULL)
    grad_kv = to_low(grad_kv)
    grad_keyval = dot_first(hidden_ref[...], grad_kv)
    grad_hidden = grad_before_ref[...] + dot_last(grad_kv, side[:, :LANES])
    grad_hidden_ref[...] = grad_hidden
    gain_grad = jnp.sum(grad_hidden * unit_ref[...], axis=0, keepdims=True)
    shift_grad = jnp.sum(grad_hidden, axis=0, keepdims=True)
    width = hidden_ref.shape[1]
    index = lax.broadcasted_iota(jnp.int32, (8, 1), 0)
    later = pltpu.roll(rows_ref[...], 2, 0)
    vectors = jnp.where(index == 0, gain_grad, jnp.where(index == 1, shift_grad, later))
    ahead = jnp.zeros((experts, width), FULL)
    behind = jnp.zeros((LANES - experts - 8, width), FULL)
    columns = jnp.concatenate([ahead, vectors, behind], axis=0).T
    bias = jnp.concatenate([bias_ref[...], bias_two_ref[...]], axis=1)
    spread = bias_rows(bias, width // rows, rows)
    grad_side = jnp.concatenate([grad_keyval, columns + grad_router_ref[...] + spread], axis=1)
    keep_ref[...], send_ref[...] = parted(to_low(grad_side), ids_ref[CORE_SLOT], keep_ref.shape)


def tokens_kernel(
    grad_hidden_ref, unit_ref, factor_ref, grad_middle_ref, small_ref, grad_tokens_ref, *, experts
):
    misc = small_ref[:, small_ref.shape[1] - LANES :]
    gain = misc.astype(FULL).T[experts : experts + 1]
    grad = norm_backward(grad_hidden_ref[...], unit_ref[...], factor_ref[...], gain)
    grad_tokens_ref[...] = to_low(grad_middle_ref[...].astype(FULL) + grad)


def finish_kernel(*refs, terms, slots):
    total, rest, last = (
        sum(ref[...].astype(FULL) for ref in part) for part in (refs[:2], refs[2:4], refs[4:terms])
    )
    expand_ref, output_ref, contract_ref, query_ref, router_ref, keyval_ref = refs[terms : terms + 6]
    *vector_refs, bias_ref = refs[terms + 6 :]
    rows, width = output_ref.shape
    for slot in range(slots):
        expand_ref[:, slot * width : (slot + 1) * width] = total[slot]
    output_ref[...] = total[slots]
    query_ref[...] = last[:rows]
    side = last[rows:]
    contract_ref[...] = rest[0]
    experts = router_ref.shape[0]
    keyval_ref[...] = side[:, :LANES]
    for expert in range(experts):
        lane = LANES + expert
        router_ref[expert : expert + 1, :] = as_row(side[:, lane : lane + 1])
    for index, ref in enumerate(vector_refs):
        lane = LANES + experts + index
        ref[...] = as_row(side[:, lane : lane + 1])
    start = LANES + BIAS_LANE
    bias_ref[...] = side[0:1, start : start + bias_ref.shape[1]]


def in_hbm(array):
    return pltpu.with_memory_space_constraint(array, pltpu.HBM)


def smem_spec():
    return pl.BlockSpec(memory_space=pltpu.SMEM)


def vmem_spec():
    return pl.BlockSpec(memory_space=pltpu.VMEM)


def shape_of(shape, dtype):
    return jax.ShapeDtypeStruct(tuple(shape), dtype)


def limit_of(name):
    return LIMITS[name] * MEGA


def estimate(cost):
    return pl.CostEstimate(flops=int(cost * 1e9), bytes_accessed=0, transcendentals=0)


def call(kernel, name, outs, cost, scalars=0, more=0):
    def run(*operands):
        return pl.pallas_call(
            kernel,
            in_specs=[smem_spec()] * scalars + [vmem_spec()] * (len(operands) - scalars),
            out_specs=[vmem_spec()] * len(outs) if isinstance(outs, list) else vmem_spec(),
            out_shape=outs,
            compiler_params=pltpu.CompilerParams(vmem_limit_bytes=limit_of(name) + more * MEGA),
            cost_estimate=estimate(cost),
            name=name,
        )(*operands)

    return run


def generations(seq_count):
    masks = range(1, seq_count)
    most = seq_count.bit_length() - 1
    return [[m for m in masks if bin(m).count("1") == n] for n in range(1, most + 1)]


def feed_up(ids, tokens, cotangent, attn, gates, routes, vectors, bias, pairs, plain, head):
    token_count, width = tokens.shape
    chunks = pairs[0].shape[0] - 1
    rows = shape_of((token_count, width), LOW)
    held = shape_of((chunks, token_count, bias.shape[1] // chunks), LOW)
    return call(
        functools.partial(up_kernel, head=head), "feed_up", [rows, rows, held, held]
        + [shape_of(plain, LOW)] * 2, FEED_COST / 2, scalars=1
    )(ids, tokens, cotangent, attn, gates, routes, vectors, bias, *pairs)


def feed_down(ids, hidden, cotangent, active, steep, pairs, contracts, first, count, head, end=()):
    token_count, width = hidden.shape
    inner = active.shape[2]
    last = bool(end)
    rows = (token_count, width)
    grads = shape_of((count + (1 if last else 0),) + pairs[0].shape[1:], LOW)
    if last:
        outs = [
            shape_of(rows, LOW),
            shape_of(rows, LOW),
            shape_of((2, token_count, LANES), LOW),
            shape_of((token_count, LANES), LOW),
            shape_of((8, width), FULL),
        ]
    else:
        outs = [shape_of(rows, FULL)] * 2
    return call(
        functools.partial(down_kernel, head=head, first=first, count=count, last=last),
        "feed_down_last" if last else "feed_down",
        outs + [grads, grads, shape_of((1, count * inner), FULL)],
        FEED_COST / 2,
        scalars=1,
    )(ids, hidden, cotangent, active, steep, *pairs, *contracts, *end)


def per_device(
    tokens, routes, lengths, cotangent, first_gain, first_shift, router, query_map, keyval,
    output_map, second_gain, second_shift, expand, expand_bias, contract, contract_bias
):
    seq_count, plane_count = lax.axis_size("seq"), lax.axis_size("dp") // 2
    along = Group("seq", 0, seq_count, SEQ_SLOT)
    plane = Group("dp", 1, plane_count, PLANE_SLOT)
    core = Group("dp", 0, 2, CORE_SLOT)
    token_count, width = tokens.shape
    rows = first_gain.shape[0]
    contract_rows = contract.shape[0]
    experts = router.shape[1]
    head = keyval.shape[1] // 2
    inner_width = expand.shape[1]
    chunks = inner_width // width
    slots = 1 + chunks
    my_index = along.index()
    ids = jnp.stack([g.index() for g in (along, plane, core)]).astype(jnp.int32)
    side_width = 2 * LANES
    row_count = 2 * token_count
    part = min(1024, row_count)

    params = [
        query_map, keyval, router.T, first_gain[None], first_shift[None], second_gain[None],
        second_shift[None], contract_bias[None], expand_bias[None], output_map, expand, contract
    ]
    small_mine, large_mine = pl.pallas_call(
        functools.partial(pack_kernel, count=len(params)),
        in_specs=[pl.BlockSpec(memory_space=pltpu.HBM)] * len(params),
        out_specs=[vmem_spec()] * 2,
        out_shape=[
            shape_of((rows, width + side_width), LOW),
            shape_of((slots * rows + contract_rows, width), LOW),
        ],
        scratch_shapes=[pltpu.VMEM(p.shape, p.dtype) for p in params]
        + [pltpu.SemaphoreType.DMA((len(params),))],
        compiler_params=pltpu.CompilerParams(vmem_limit_bytes=limit_of("pack")),
        cost_estimate=estimate(0.1),
        name="pack",
    )(*[in_hbm(p) for p in params])

    def first_work():
        given = [routes.T, lengths]
        return pl.pallas_call(
            first_kernel,
            in_specs=[smem_spec()] + [pl.BlockSpec(memory_space=pltpu.HBM)] * 2 + [vmem_spec()],
            out_specs=[vmem_spec()] * 3 + [smem_spec()],
            out_shape=[
                shape_of((2, token_count, LANES), jnp.int32),
                shape_of((8, LANES), jnp.int32),
                shape_of(tokens.shape, FULL),
                shape_of(ids.shape, jnp.int32),
            ],
            scratch_shapes=[pltpu.VMEM(p.shape, p.dtype) for p in given]
            + [pltpu.SemaphoreType.DMA((2,))],
            compiler_params=pltpu.CompilerParams(vmem_limit_bytes=limit_of("first")),
            cost_estimate=estimate(0.1),
            name="first",
        )(ids, *[in_hbm(p) for p in given], tokens)


    small_move = Move(along, small_mine[None])
    large = {0: large_mine}
    coming = generations(seq_count)

    def large_of(masks):
        return [Move(along, large[m & (m - 1)], [m & -m]) for m in masks]

    def large_come(masks, moves):
        for mask, move in zip(masks, moves):
            large[mask] = move.got[mask & -mask]

    first_masks, later_masks = coming[0][:1], coming[0][1:]
    moves = large_of(first_masks)
    route_columns, bounds, unit, ids, large[0] = phase(
        [small_move] + moves, first_work, held=[large[0]]
    )
    large_come(first_masks, moves)
    for group in (along, plane, core):
        group.ids = ids
    small = merge([small_mine[None]] + [small_move.got[m] for m in range(1, seq_count)], along)
    large[0], small = together(large[0], small)
    small_move = Move(plane, small)
    moves = large_of(later_masks)
    phase([small_move] + moves)
    large_come(later_masks, moves)
    small = merge([small] + [small_move.got[m] for m in range(1, plane_count)], plane)[0]
    small_move = Move(core, small)
    phase([small_move])
    small_shape = (plane_count, seq_count * rows, width + side_width)
    smalls = [small.reshape(small_shape), small_move.got[1].reshape(small_shape)]
    moves = large_of(coming[1]) if len(coming) > 1 else []
    hidden_call = call(
        functools.partial(hidden_kernel, experts=experts),
        "hidden",
        [
            shape_of((token_count, width), LOW),
            shape_of((token_count, LANES), LOW),
            shape_of((2, token_count, LANES), FULL),
            shape_of((width, width + side_width), LOW),
        ],
        0.5,
        scalars=1,
    )
    hidden, kv_mine, gates, small = phase(
        moves, lambda: hidden_call(ids, unit, *smalls, route_columns)
    )
    large_come(coming[1] if len(coming) > 1 else [], moves)

    def attend(state, masks, queries, last=False):
        return call(
            functools.partial(
                forward_kernel, head=head, first=not state, last=last, masks=masks, part=part
            ),
            "attention_forward",
            [shape_of((row_count, LANES), t) for t in ((FULL, LOW) if last else (FULL,))],
            FORWARD_COST * len(masks),
            scalars=1,
            more=3 * (len(masks) - 1),
        )(ids, queries, bounds, *[shards[m] for m in masks], *state)

    def keys_of(masks):
        return [Move(along, shards[m & (m - 1)], [m & -m]) for m in masks]

    def come(masks, moves):
        for mask, move in zip(masks, moves):
            shards[mask] = move.got[mask & -mask]

    shards = {0: kv_mine}
    keys = keys_of(coming[0])

    for move in keys:
        move.begin()
    queries = call(
        functools.partial(query_kernel, head=head),
        "queries",
        shape_of((row_count, LANES), LOW),
        QUERY_COST,
        scalars=1,
    )(ids, hidden, small, route_columns, bounds)
    for masks in coming[2:]:
        moves = large_of(masks)
        phase(moves)
        large_come(masks, moves)
    queries, *blocks = together(queries, *[large[m] for m in range(seq_count)])
    if rows % 16:
        lines = jnp.stack(by_place(blocks, my_index))
        pair = lines[:, : slots * rows].reshape(seq_count, slots, rows, width)
        pair = pair.transpose(1, 0, 2, 3).reshape(slots, seq_count * rows, width)
        half = lines[:, slots * rows :].reshape(1, seq_count * contract_rows, width)
    else:
        pair, half = call(
            functools.partial(spread_kernel, count=seq_count, slots=slots, rows=rows),
            "spread",
            [
                shape_of((slots, seq_count * rows, width), LOW),
                shape_of((seq_count * contract_rows, width), LOW),
            ],
            0.1,
            scalars=1,
        )(ids, *blocks)
        half = half[None]
    pair_move = Move(plane, pair).begin()
    state, half = phase(keys, lambda: attend([], [0], queries), held=[half])
    come(coming[0], keys)
    for before, masks in zip(coming, coming[1:]):
        keys = keys_of(masks)
        moves = keys + [pair_move] if masks is coming[-1] else keys
        [state] = phase(moves, lambda: attend([state], before, queries))
        come(masks, keys)
    pair = merge([pair] + [pair_move.got[m] for m in range(1, plane_count)], plane)
    pair = pair.reshape(slots, plane_count, -1, width)
    pair_move = Move(core, pair)
    half_move = Move(plane, half).begin()
    attn, wide_queries = phase([pair_move], lambda: attend([state], coming[-1], queries, True))
    attn = attn.reshape(2, token_count, LANES)
    pairs = [pair, pair_move.got[1]]
    vectors, bias = call(
        functools.partial(vectors_kernel, experts=experts, rows=rows),
        "vectors",
        [shape_of((8, width), FULL), shape_of((1, inner_width), FULL)],
        0.1,
    )(small)

    plain = (plane_count, seq_count * contract_rows, width)
    mixed, hidden_two, active, steep, keep_half, send_half = phase(
        [half_move],
        lambda: feed_up(
            ids, tokens, cotangent, attn, gates, route_columns, vectors, bias, pairs, plain, head
        ),
    )
    half = merge([half] + [half_move.got[m] for m in range(1, plane_count)], plane)
    half = half.reshape(plane_count, -1, width)
    half_move = Move(core, half)
    phase([half_move])
    halves = [half, half_move.got[1]]
    half_move = Move(core, send_half)
    middle_chunk = 1
    out_held, grad_held, keep_expand, send_expand, grad_bias = phase(
        [half_move],
        lambda: feed_down(
            ids, hidden_two, cotangent, active, steep, pairs, halves, 0, middle_chunk, head
        ),
    )
    flat = lambda lead, *terms: [t.reshape(lead, -1, width) for t in terms]
    half_fold = Fold([flat(1, keep_half, half_move.got[1])], [plane, along])
    expand_move = Move(core, send_expand)
    (
        out, branch, grad_attn, grad_logits, grad_rows, keep_pair, send_pair, grad_bias_two
    ) = phase(
        fold([half_fold]) + [expand_move],
        lambda: feed_down(
            ids, hidden_two, cotangent, active, steep, pairs, halves, middle_chunk,
            chunks - middle_chunk, head,
            (out_held, grad_held, tokens, mixed, attn, gates, route_columns, vectors),
        ),
    )
    folded([half_fold])

    grad_rows_in = grad_attn.reshape(row_count, LANES)
    masks = list(range(seq_count - 1, 0, -1))
    if seq_count > 2:
        masks = [2] + [m for m in masks if m != 2]
    third = max(1, len(masks) // 3)
    groups = [masks[:third], masks[third:], [0]]

    def backward(masks, before):
        return call(
            functools.partial(
                backward_kernel, head=head, first=before is None, masks=masks, part=part
            ),
            "attention_backward",
            [shape_of((row_count, LANES), FULL)]
            + [shape_of((token_count, LANES), LOW)] * len(masks),
            BACKWARD_COST * len(masks),
            scalars=1,
            more=3 * (len(masks) - 1),
        )(
            ids, wide_queries, grad_rows_in, bounds, *[shards[m] for m in masks],
            *([] if before is None else [before])
        )

    pair_move = Move(core, send_pair)
    first_query, *leaving = phase([pair_move], lambda: backward(groups[0], None))
    lead = chunks - middle_chunk + 1
    pair_fold = Fold(
        [
            flat(middle_chunk, keep_expand, expand_move.got[1]),
            flat(lead, keep_pair, pair_move.got[1]),
        ],
        [plane, along],
    )
    both = [half_fold, pair_fold]
    keys_first = Move(along, dict(zip(groups[0], leaving)), groups[0])
    second_query, *leaving = phase(
        [keys_first] + fold(both), lambda: backward(groups[1], first_query)
    )
    folded(both)
    keys_second = Move(along, dict(zip(groups[1], leaving)), groups[1])

    def work():
        grad_query, own = backward(groups[2], second_query)
        shape = (plane_count, seq_count * rows, width)
        return own, *call(
            functools.partial(placed_kernel, head=head),
            "query_gradient",
            [
                shape_of((token_count, width), FULL),
                shape_of(shape, LOW),
                shape_of(shape, LOW),
                shape_of((width, LANES), FULL),
                shape_of((token_count, width), FULL),
                shape_of((token_count, LANES), FULL),
            ],
            1.0,
            scalars=1,
        )(ids, grad_query, hidden, route_columns, grad_logits, small, tokens)

    grad_kv, grad_before, keep_query, send_query, grad_router, unit, factor = phase(
        [keys_second] + fold(both), work
    )
    folded(both)
    query_move = Move(core, send_query)
    others = list(keys_first.got.values()) + list(keys_second.got.values())
    shape = (plane_count, seq_count * rows, side_width)
    grad_hidden, keep_side, send_side = phase(
        [query_move],
        lambda: call(
            functools.partial(side_kernel, experts=experts, others=len(others), rows=rows),
            "key_gradient",
            [shape_of((token_count, width), FULL), shape_of(shape, LOW), shape_of(shape, LOW)],
            1.0,
            scalars=1,
        )(
            ids, hidden, grad_before, unit, small, grad_rows, grad_bias, grad_bias_two, grad_router,
            grad_kv, *others
        ),
    )

    side_move = Move(core, send_side)
    phase([side_move])
    moves = fold(both)
    keep_query, *_ = together(keep_query, *[f.keep for f in both if f.move is not None])
    line = lambda *terms: [t.reshape(1, -1, t.shape[-1]) for t in terms]
    small_sent = cut(
        [line(keep_query, query_move.got[1]), line(keep_side, side_move.got[1])],
        plane,
        width + side_width,
    )
    small_move = Move(plane, dict(enumerate(small_sent)))
    phase([small_move] + moves)
    folded(both)
    last_sent = cut([line(small_sent[0], *small_move.got.values())], along, width)
    last_move = Move(along, dict(enumerate(last_sent)))
    moves = fold(both)
    [grad_tokens] = phase(
        [last_move] + moves,
        lambda: [
            call(
                functools.partial(tokens_kernel, experts=experts),
                "token_gradient",
                shape_of((token_count, width), LOW),
                1.0,
            )(grad_hidden, unit, factor, branch, small)
        ],
    )
    folded(both)
    while half_fold.stages or pair_fold.stages:
        phase(fold(both))
        folded(both)
    terms = pair_fold.sets[0] + half_fold.sets[0]
    terms += [last_sent[0]] + list(last_move.got.values())
    vector_shape = shape_of((1, rows), FULL)
    (
        grad_expand, grad_output, grad_contract, grad_query_map, grad_router, grad_keyval,
        *vector_sums, grad_spread
    ) = call(
        functools.partial(finish_kernel, terms=len(terms), slots=chunks),
        "finish",
        [
            shape_of(expand.shape, FULL),
            shape_of(output_map.shape, FULL),
            shape_of(contract.shape, FULL),
            shape_of(query_map.shape, FULL),
            shape_of((experts, rows), FULL),
            shape_of(keyval.shape, FULL),
        ]
        + [vector_shape] * 5
        + [shape_of((1, expand_bias.shape[0]), FULL)],
        0.1,
    )(*terms)
    grad_gain, grad_shift, grad_gain_two, grad_shift_two, grad_contract_bias = (
        v.reshape(rows) for v in vector_sums
    )
    return (
        out, grad_tokens, grad_gain, grad_shift, grad_router.T, grad_query_map, grad_keyval,
        grad_output, grad_gain_two, grad_shift_two, grad_expand, grad_spread.reshape(-1),
        grad_contract, grad_contract_bias
    )


def solution(mesh):
    both = ("dp", "seq")
    rows, vector = P(both, None), P(both)
    return jax.shard_map(
        per_device,
        mesh=mesh,
        in_specs=(
            rows, rows, P("dp", None), rows, vector, vector, rows, rows, rows, rows, vector, vector,
            rows, vector, rows, vector
        ),
        out_specs=(
            rows, rows, vector, vector, rows, rows, rows, rows, vector, vector, rows, vector, rows,
            vector
        ),
        check_vma=False,
    )
```

```python
import functools

import jax
import jax.numpy as jnp
from jax import lax
from jax.experimental import pallas as pl
from jax.experimental.pallas import tpu as pltpu
from jax.sharding import PartitionSpec as P

LOW = jnp.bfloat16
FULL = jnp.float32
FAR = 1e30
EPS = 1e-05
DOC_LANE = 64
LSE_LANE = 96
SUM_LANE = 64
MAX_LANE = 67
BIAS_LANE = 64
SEQ_SLOT, PLANE_SLOT, CORE_SLOT = range(3)
LANES = 128
MEGA = 1 << 20
FORWARD_COST = 0.1
QUERY_COST = 0.05
BACKWARD_COST = 3.0
FEED_COST = 8.0
LIMITS = {
    "pack": 4, "first": 8, "hidden": 6, "vectors": 2, "queries": 6, "attention_forward": 8,
    "attention_backward": 8, "query_gradient": 8, "key_gradient": 12, "token_gradient": 12, "merge": 2, "join": 2, "spread": 2,
    "cut": 3, "fold": 4, "finish": 2, "feed_up": 8,
    "feed_down": 6, "feed_down_last": 17,
}


def to_low(matrix):
    return matrix.astype(LOW)


def dot_plain(left, right):
    return lax.dot_general(left, right, (((1,), (0,)), ((), ())), preferred_element_type=FULL)


def dot_last(left, right):
    return lax.dot_general(left, right, (((1,), (1,)), ((), ())), preferred_element_type=FULL)


def dot_first(left, right):
    return lax.dot_general(left, right, (((0,), (0,)), ((), ())), preferred_element_type=FULL)


class Group:
    def __init__(self, axis, shift, size, slot):
        self.axis, self.shift, self.size, self.slot = axis, shift, size, slot
        self.ids = None

    def index(self):
        return (lax.axis_index(self.axis) >> self.shift) & (self.size - 1)

    def exchange(self, block, mask):
        step = mask << self.shift
        pairs = [(i, i ^ step) for i in range(lax.axis_size(self.axis))]
        return lax.ppermute(block, self.axis, pairs)


def by_place(blocks, index):
    blocks = list(blocks)
    for bit in range(len(blocks).bit_length() - 1):
        swap = (index >> bit) & 1 == 1
        blocks = [jnp.where(swap, blocks[i ^ (1 << bit)], blocks[i]) for i in range(len(blocks))]
    return blocks


def merge_kernel(ids_ref, *refs, count, slot):
    out_ref = refs[count]
    rows = refs[0].shape[1]
    for mask in range(count):
        start = pl.multiple_of((ids_ref[slot] ^ mask) * rows, rows)
        out_ref[:, pl.ds(start, rows), :] = refs[mask][...]


def merge(blocks, group):
    lead, rows, columns = blocks[0].shape
    if rows % 16:
        return jnp.concatenate(by_place(blocks, group.index()), axis=1)
    return call(
        functools.partial(merge_kernel, count=len(blocks), slot=group.slot),
        "merge",
        shape_of((lead, rows * len(blocks), columns), blocks[0].dtype),
        0.1,
        scalars=1,
    )(group.ids, *blocks)


def columns_of(columns, width):
    return [slice(i, min(i + width, columns)) for i in range(0, columns, width)]


def cut_kernel(ids_ref, *refs, sizes, count, slot):
    outs = refs[len(refs) - count :]
    refs = list(refs[: len(refs) - count])
    sets = [[refs.pop(0) for _ in range(size)] for size in sizes]
    width = outs[0].shape[1]
    for mask in range(count):
        row = column = 0
        for terms in sets:
            lead, total, columns = terms[0].shape
            rows = total // count
            start = pl.multiple_of((ids_ref[slot] ^ mask) * rows, rows)
            for at in range(lead):
                for piece in columns_of(columns, width):
                    value = sum(term[at, pl.ds(start, rows), piece].astype(FULL) for term in terms)
                    end = column + value.shape[1]
                    outs[mask][row : row + rows, column:end] = to_low(value)
                    column = end % width
                    row += 0 if column else rows
        if column:
            rest = outs[mask].shape[0] - row
            outs[mask][row:, column:] = jnp.zeros((rest, width - column), LOW)


def cut(sets, group, width):
    count = group.size
    sets = [[t.reshape((-1,) + t.shape[-2:]) for t in terms] for terms in sets]
    rows = [terms[0].shape[1] // count for terms in sets]
    total = sum(t[0].shape[0] * r * t[0].shape[2] for t, r in zip(sets, rows))
    total = -(-total // (width * rows[-1])) * rows[-1]
    if any(r % 16 for r in rows):
        index = group.index()
        results = []
        for mask in range(count):
            bands, band = [], []
            for terms, r in zip(sets, rows):
                value = sum(t.astype(FULL) for t in terms)
                value = lax.dynamic_slice_in_dim(value, (index ^ mask) * r, r, 1)
                for at in range(value.shape[0]):
                    for piece in columns_of(value.shape[2], width):
                        band.append(value[at, :, piece])
                        if sum(b.shape[1] for b in band) == width:
                            bands.append(jnp.concatenate(band, axis=1))
                            band = []
            if band:
                band = jnp.concatenate(band, axis=1)
                bands.append(jnp.pad(band, ((0, 0), (0, width - band.shape[1]))))
            results.append(to_low(jnp.concatenate(bands, axis=0)))
        return results
    return call(
        functools.partial(
            cut_kernel, sizes=[len(t) for t in sets], count=count, slot=group.slot
        ),
        "cut",
        [shape_of((total, width), LOW)] * count,
        0.1,
        scalars=1,
    )(group.ids, *[t for terms in sets for t in terms])


def together(*values):
    return lax.optimization_barrier(values)


class Move:
    def __init__(self, group, blocks, masks=None):
        self.group = group
        self.masks = list(range(1, group.size)) if masks is None else masks
        self.blocks = blocks if isinstance(blocks, dict) else {m: blocks for m in self.masks}

    def begin(self):
        self.moved = [self.group.exchange(self.blocks[m], m) for m in self.masks]
        return self

    def end(self, got):
        self.got = dict(zip(self.masks, got))
        self.moved = None


def phase(moves, work=lambda: (), held=()):
    for move in moves:
        if getattr(move, "moved", None) is None:
            move.begin()
    done = work()
    ended = list(together(*[x for m in moves for x in m.moved], *done, *held))
    for move in moves:
        move.end([ended.pop(0) for _ in move.masks])
    return ended


def fold_kernel(ids_ref, *refs, plan):
    refs = list(refs)
    folds = [
        (bit, [([refs.pop(0) for _ in range(n)], low, high) for n, low, high in sets])
        for bit, sets in plan
    ]
    for (slot, shift), sets in folds:
        keep_ref, send_ref = refs.pop(0), refs.pop(0)
        bit = (ids_ref[slot] >> shift) & 1
        start = 0
        for terms, low, high in sets:
            end = start + high - low
            keep_ref[start:end] = sum(term[low:high, bit].astype(FULL) for term in terms)
            send_ref[start:end] = to_low(
                sum(term[low:high, 1 - bit].astype(FULL) for term in terms)
            )
            start = end


class Fold:
    def __init__(self, sets, groups, upward=False):
        self.sets = sets
        self.left = [(g, b) for g in groups for b in reversed(range(g.size.bit_length() - 1))]
        over = [x for x in self.left if x[0].axis == "dp"]
        self.stages = over[::-1] if upward else over
        self.stages += [x for x in self.left if x[0].axis == "seq"][::-1]
        self.move = None

    def shaped(self):
        ahead = 1 << self.left.index(self.stages[0])
        sets = []
        for terms, low, high in self.sets:
            lead, total, columns = terms[0].shape
            shape = (lead * ahead, 2, total // (2 * ahead), columns)
            sets.append(([t.reshape(shape) for t in terms], low * ahead, high * ahead))
        return sets


def fold(folds):
    folds = [f for f in folds if f.stages]
    if not folds:
        return []
    plan, operands, outs = [], [], []
    for f in folds:
        sets = f.shaped()
        group, bit = f.stages[0]
        plan.append(((group.slot, bit), [(len(terms), low, high) for terms, low, high in sets]))
        operands += [t for terms, _, _ in sets for t in terms]
        count = sum(high - low for _, low, high in sets)
        shape = (count,) + sets[0][0][0].shape[2:]
        outs += [shape_of(shape, FULL), shape_of(shape, LOW)]
    results = call(
        functools.partial(fold_kernel, plan=plan), "fold", outs, 0.1, scalars=1
    )(folds[0].stages[0][0].ids, *operands)
    moves = []
    for at, f in enumerate(folds):
        group, bit = f.stages.pop(0)
        f.lead = sum(high - low for _, low, high in f.sets)
        f.left.remove((group, bit))
        f.keep = results[2 * at]
        f.move = Move(group, results[2 * at + 1], [1 << bit])
        moves.append(f.move)
    return moves


def folded(folds):
    for f in folds:
        if f.move is not None:
            [got] = f.move.got.values()
            columns = got.shape[-1]
            f.sets = [([t.reshape(f.lead, -1, columns) for t in (f.keep, got)], 0, f.lead)]
            f.move = None


def lane_ids(shape):
    return lax.broadcasted_iota(jnp.int32, shape, len(shape) - 1)


def row_positions(offset, rows):
    return offset + lax.broadcasted_iota(jnp.int32, (rows, 1), 0)


def in_document(bounds_ref, positions):
    return (positions >= bounds_ref[0:1, :]) & (positions < bounds_ref[1:2, :])


def put_parts(base, lanes, lane, rows, count):
    for step in range(count):
        part = to_low(rows).astype(FULL)
        base = jnp.where(lanes == lane + step, part, base)
        rows = rows - part
    return base


def lane_sum(matrix):
    total = sum(matrix[:, i : i + LANES] for i in range(0, matrix.shape[1], LANES))
    high = to_low(total)
    low = to_low(total - high.astype(FULL))
    ones = jnp.ones((LANES, LANES), LOW)
    return dot_plain(high, ones) + dot_plain(low, ones)


def over(rows, width):
    return jnp.concatenate([rows] * (width // LANES), axis=1)


def normalize(matrix):
    width = matrix.shape[1]
    center = matrix - over(lane_sum(matrix) * (1.0 / width), width)
    factor = lax.rsqrt(lane_sum(center * center) * (1.0 / width) + EPS)
    return center * over(factor, width), factor


def norm_backward(grad, unit, factor, gain):
    width = grad.shape[1]
    scaled = grad * gain
    mean = over(lane_sum(scaled) * (1.0 / width), width)
    along = over(lane_sum(scaled * unit) * (1.0 / width), width)
    return over(factor, width) * (scaled - mean - unit * along)


def choose(wide, route, head):
    shift = (LANES // head).bit_length() - 1
    tile = lax.shift_right_logical(route, shift)
    picked = wide[:, :LANES]
    for index in range(1, wide.shape[1] // LANES):
        picked = jnp.where(tile == index, wide[:, index * LANES : (index + 1) * LANES], picked)
    turned = pltpu.roll(picked, head, 1)
    lanes = lane_ids((1, LANES))
    mine = (lanes // head) == (route & ((1 << shift) - 1))
    return jnp.where(mine, picked, turned)


def place(doubled, routes, head, width):
    lanes = lane_ids((1, LANES))
    per_tile = LANES // head
    tiles = []
    for index in range(width // LANES):
        expert = lanes // head + index * per_tile
        tile = jnp.zeros_like(doubled[0])
        for rows, route in zip(doubled, routes):
            tile = jnp.where(route == expert, rows, tile)
        tiles.append(tile)
    return jnp.concatenate(tiles, axis=1)


def doubled_head(rows, head):
    lanes = lane_ids((1, LANES))
    return jnp.where(lanes < head, rows, pltpu.roll(rows, head, 1))


def key_rows_of(kv, hot, head):
    lanes = lane_ids((1, LANES))
    kv = kv.astype(FULL)
    marks = jnp.where((lanes >= LSE_LANE) & (lanes < LSE_LANE + 3), 1.0, 0.0)
    keys = jnp.where(lanes < head, kv, jnp.where(hot, 1.0, marks))
    ones = jnp.where((lanes >= SUM_LANE) & (lanes < SUM_LANE + 3), 1.0, 0.0)
    values = jnp.where(lanes < head, pltpu.roll(kv, head, 1), ones)
    return to_low(keys), to_low(values)


def as_column(row):
    rows = row.shape[1]
    lanes = lax.broadcasted_iota(jnp.int32, (rows, rows), 1)
    here = lax.broadcasted_iota(jnp.int32, (rows, rows), 0)
    return jnp.sum(jnp.where(lanes == here, row, 0.0), axis=1, keepdims=True)


def as_row(column):
    rows = column.shape[0]
    lanes = lax.broadcasted_iota(jnp.int32, (rows, rows), 1)
    here = lax.broadcasted_iota(jnp.int32, (rows, rows), 0)
    return jnp.sum(jnp.where(lanes == here, column, 0.0), axis=0, keepdims=True)


def fetch(refs, held, semaphores):
    copies = [
        pltpu.make_async_copy(ref, into, semaphores.at[i])
        for i, (ref, into) in enumerate(zip(refs, held))
    ]
    for copy in copies:
        copy.start()
    for copy in copies:
        copy.wait()


def pack_kernel(*refs, count):
    small_ref, large_ref = refs[count : count + 2]
    held = refs[count + 2 : -1]
    fetch(refs[:count], held, refs[-1])
    (
        query_ref, keyval_ref, router_ref, gain_ref, shift_ref, gain_two_ref, shift_two_ref,
        contract_bias_ref, expand_bias_ref, output_ref, expand_ref, contract_ref
    ) = held
    rows, width = query_ref.shape
    experts = router_ref.shape[0]
    keyval_width = keyval_ref.shape[1]
    small_ref[:, :width] = to_low(query_ref[...])
    small_ref[:, width : width + keyval_width] = to_low(keyval_ref[...])
    lanes = lane_ids((1, LANES))
    turned = router_ref[...]
    side = jnp.zeros((rows, LANES), FULL)
    for expert in range(experts):
        side = jnp.where(lanes == expert, as_column(turned[expert : expert + 1]), side)
    vectors = [gain_ref, shift_ref, gain_two_ref, shift_two_ref, contract_bias_ref]
    for index, ref in enumerate(vectors):
        side = jnp.where(lanes == experts + index, as_column(ref[...]), side)
    extra = expand_bias_ref.shape[1]
    bias = jnp.pad(expand_bias_ref[...], ((0, 0), (BIAS_LANE, LANES - BIAS_LANE - extra)))
    first = lax.broadcasted_iota(jnp.int32, (rows, 1), 0) == 0
    side = side + jnp.where(first, bias, 0.0)
    small_ref[:, width + keyval_width :] = to_low(side)
    large = [output_ref[...]]
    large += [
        expand_ref[:, c * width : (c + 1) * width] for c in range(expand_ref.shape[1] // width)
    ]
    large_ref[...] = to_low(jnp.concatenate(large + [contract_ref[...]], axis=0))


def first_kernel(
    ids_ref, routes_hbm, lengths_hbm, tokens_ref, columns_ref, bounds_ref, unit_ref, ids_out, *held
):
    unit_ref[...] = normalize(tokens_ref[...].astype(FULL))[0]
    for slot in range(ids_ref.shape[0]):
        ids_out[slot] = ids_ref[slot]
    routes_ref, lengths_ref, semaphores = held
    fetch((routes_hbm, lengths_hbm), (routes_ref, lengths_ref), semaphores)
    routes = routes_ref[...].astype(FULL)
    choices = routes.shape[0]
    routes = jnp.concatenate([routes, jnp.zeros((8 - routes.shape[0], routes.shape[1]), FULL)], axis=0)
    turned = routes.T
    for j in range(choices):
        wide = jnp.broadcast_to(turned[:, j : j + 1], columns_ref.shape[1:])
        columns_ref[j] = wide.astype(jnp.int32)
    count = lengths_ref.shape[1]
    lanes = lane_ids((1, LANES))
    rest = jnp.zeros((1, LANES - DOC_LANE - count), jnp.int32)
    lengths = jnp.concatenate(
        [jnp.zeros((1, DOC_LANE), jnp.int32), lengths_ref[...], rest], axis=1
    )
    ends = lengths
    step = 1
    while step < count:
        ends = ends + jnp.where(lanes >= DOC_LANE + step, pltpu.roll(ends, step, 1), 0)
        step *= 2
    here = (lanes >= DOC_LANE) & (lanes < DOC_LANE + count)
    starts = jnp.where(here, ends - lengths, 1 << 30)
    ends = jnp.where(here, ends, 0)
    index = lax.broadcasted_iota(jnp.int32, (8, 1), 0)
    bounds_ref[...] = jnp.where(index == 0, starts, jnp.where(index == 1, ends, 0))


def vectors_kernel(small_ref, vectors_ref, bias_ref, *, experts, rows):
    misc = small_ref[:, small_ref.shape[1] - LANES :].astype(FULL)
    turned = misc.T
    vectors_ref[...] = turned[experts + 2 : experts + 10]
    count = misc.shape[0] // rows
    each = bias_ref.shape[1] // count
    per_tile = LANES // each
    firsts = misc.reshape(count, rows, LANES)[:, 0, :].reshape(count // per_tile, per_tile, LANES)
    lanes = lane_ids((1, LANES))
    tiles = jnp.zeros((count // per_tile, LANES), FULL)
    for k in range(per_tile):
        moved = pltpu.roll(firsts[:, k, :], (k * each - BIAS_LANE) % LANES, 1)
        tiles = jnp.where(lanes // each == k, moved, tiles)
    for index in range(count // per_tile):
        bias_ref[:, index * LANES : (index + 1) * LANES] = tiles[index : index + 1]


def bias_rows(bias, count, rows):
    each = bias.shape[1] // count
    per_tile = LANES // each
    tiles = jnp.concatenate(
        [bias[:, i : i + LANES] for i in range(0, bias.shape[1], LANES)], axis=0
    )
    lanes = lane_ids((1, LANES))
    mine = (lanes >= BIAS_LANE) & (lanes < BIAS_LANE + each)
    parts = [
        jnp.where(mine, pltpu.roll(tiles, (BIAS_LANE - k * each) % LANES, 1), 0.0)
        for k in range(per_tile)
    ]
    firsts = jnp.stack(parts, axis=1).reshape(count, 1, LANES)
    here = lax.broadcasted_iota(jnp.int32, (1, rows, 1), 1) == 0
    return jnp.where(here, firsts, 0.0).reshape(count * rows, LANES)


def stack_kernel(*refs):
    for at, ref in enumerate(refs[:-1]):
        refs[-1][at] = ref[0]


def join_kernel(first_ref, second_ref, out_ref):
    count = first_ref.shape[0]
    out_ref[:count] = first_ref[...]
    out_ref[count:] = second_ref[...]


def spread_kernel(ids_ref, *refs, masks, slots, rows):
    pair_ref, half_ref = refs[len(masks) :]
    more = refs[0].shape[1] - slots * rows
    for ref, masks_of in zip(refs, masks):
        for at, mask in enumerate(masks_of):
            place = ids_ref[SEQ_SLOT] ^ mask
            start = pl.multiple_of(place * rows, rows)
            for slot in range(slots):
                here = slice(slot * rows, (slot + 1) * rows)
                pair_ref[slot, pl.ds(start, rows), :] = ref[at, here, :]
            half_ref[pl.ds(pl.multiple_of(place * more, more), more), :] = ref[at, slots * rows :, :]


def hidden_kernel(
    ids_ref, unit_ref, mine_ref, other_ref, routes_ref, hidden_ref, kv_ref, gates_ref, small_ref, *, experts
):
    small = merged(mine_ref[...], other_ref[...], ids_ref[CORE_SLOT])
    small_ref[...] = small
    side = small[:, small.shape[1] - 2 * LANES :]
    vectors = side[:, LANES:].astype(FULL).T
    hidden = to_low(
        unit_ref[...] * vectors[experts : experts + 1] + vectors[experts + 1 : experts + 2]
    )
    hidden_ref[...] = hidden
    both = dot_plain(hidden, side)
    kv_ref[...] = to_low(both[:, :LANES])
    logits = both[:, LANES:]
    lanes = lane_ids((1, LANES))
    picked = [lane_sum(jnp.where(lanes == routes_ref[j], logits, 0.0)) for j in range(2)]
    top = jnp.maximum(picked[0], picked[1])
    raised = [jnp.exp(p - top) for p in picked]
    total = raised[0] + raised[1]
    for j in range(2):
        gates_ref[j] = raised[j] / total


def query_kernel(ids_ref, hidden_ref, small_ref, routes_ref, bounds_ref, query_ref, *, head):
    rows, width = hidden_ref.shape
    wide = dot_plain(hidden_ref[...], small_ref[:, :width])
    lanes = lane_ids((1, LANES))
    hot = in_document(bounds_ref, row_positions(ids_ref[SEQ_SLOT] * rows, rows))
    documents = (bounds_ref[1:2, :] > 0) & (lanes >= head)
    marks = jnp.where(documents & jnp.logical_not(hot), -FAR, 0.0)
    for j in range(2):
        rows_of = choose(wide, routes_ref[j], head) * head**-0.5
        query_ref[j * rows : (j + 1) * rows, :] = to_low(jnp.where(lanes < head, rows_of, marks))


def forward_kernel(ids_ref, query_ref, bounds_ref, *rest, head, first, last, masks, part):
    count = len(masks)
    kv_refs, rest = rest[:count], list(rest[count:])
    state_ref = None if first else rest.pop(0)
    lanes = lane_ids((1, LANES))
    blocks = []
    for index, ref in enumerate(kv_refs):
        start = (ids_ref[SEQ_SLOT] ^ masks[index]) * ref.shape[0]
        hot = in_document(bounds_ref, row_positions(start, ref.shape[0]))
        blocks.append(key_rows_of(ref[...], hot, head))
    for start in range(0, query_ref.shape[0], part):
        rows = slice(start, start + part)
        query = query_ref[rows, :]
        state = None if first else state_ref[rows, :]
        for keys, values in blocks:
            scores = dot_last(query, keys)
            top = jnp.max(scores, axis=1, keepdims=True)
            if state is None:
                new = top
                state = dot_plain(to_low(jnp.exp(scores - new)), values)
            else:
                old = state[:, MAX_LANE : MAX_LANE + 1]
                new = jnp.maximum(old, top)
                weights = to_low(jnp.exp(scores - new))
                state = state * jnp.exp(old - new) + dot_plain(weights, values)
            state = jnp.where(lanes == MAX_LANE, new, state)
        if last:
            attn_ref, wide_ref = rest
            total = state[:, SUM_LANE : SUM_LANE + 1]
            attn_ref[rows, :] = jnp.where(lanes < head, state / total, 0.0)
            log_total = state[:, MAX_LANE : MAX_LANE + 1] + jnp.log(total)
            wide_ref[rows, :] = to_low(
                put_parts(query.astype(FULL), lanes, LSE_LANE, -log_total, 3)
            )
        else:
            rest[0][rows, :] = state


def merged(mine, other, bit):
    low = bit == 0
    both = jnp.stack([jnp.where(low, mine, other), jnp.where(low, other, mine)], axis=1)
    return both.reshape(-1, mine.shape[-1])


def parted(whole, bit, shape):
    both = whole.reshape(shape[0], 2, shape[1], shape[2])
    low = bit == 0
    first, second = both[:, 0], both[:, 1]
    return jnp.where(low, first, second), jnp.where(low, second, first)


def weights(refs, bit):
    mine, other = refs[0][...], refs[1][...]
    shape = mine.shape[-3:]
    return merged(mine.reshape(shape), other.reshape(shape), bit)


def weights(mine, other, ids_ref):
    return merged(mine, other, ids_ref[CORE_SLOT])


def unit_of(ids_ref, mask, inner, size):
    unit = ids_ref[PLANE_SLOT] ^ mask
    shift = (inner // size).bit_length() - 1
    everywhere = pl.ds(pl.multiple_of(unit * size, size), size)
    if not shift:
        return unit, slice(0, size), everywhere
    start = pl.multiple_of((unit & ((1 << shift) - 1)) * size, size)
    return lax.shift_right_logical(unit, shift), pl.ds(start, size), everywhere


def up_kernel(
    ids_ref, tokens_ref, cotangent_ref, attn_ref, gates_ref, routes_ref, vectors_ref, bias_ref,
    pair_mine, pair_other, mixed_ref, hidden_ref, active_ref, steep_ref, keep_ref, send_ref, *, head
):
    width = tokens_ref.shape[1]
    wide = [doubled_head(attn_ref[j], head) * gates_ref[j] for j in range(2)]
    mixed = to_low(place(wide, [routes_ref[j] for j in range(2)], head, width))
    mixed_ref[...] = mixed
    output_weight = weights(pair_mine[0], pair_other[0], ids_ref)
    middle = tokens_ref[...].astype(FULL) + dot_plain(mixed, output_weight)
    unit, _ = normalize(middle)
    hidden = to_low(unit * vectors_ref[0:1, :] + vectors_ref[1:2, :])
    hidden_ref[...] = hidden
    slope = 0.7978845608028654
    cube = 0.044715
    chunks, _, inner_width = active_ref.shape
    part = min(256, tokens_ref.shape[0])
    groups = keep_ref.shape[0] // chunks
    for chunk in range(chunks):
        expand = weights(pair_mine[chunk + 1], pair_other[chunk + 1], ids_ref)
        columns = slice(chunk * inner_width, (chunk + 1) * inner_width)
        for start in range(0, hidden.shape[0], part):
            here = slice(start, start + part)
            inner = dot_plain(hidden[here], expand) + bias_ref[:, columns]
            square = inner * inner
            half = 0.5 + 0.5 * jnp.tanh(inner * (slope + slope * cube * square))
            whole = inner * half
            active_ref[chunk, here] = to_low(whole)
            steep = half + whole * (1.0 - half) * (2.0 * slope + 6.0 * slope * cube * square)
            steep_ref[chunk, here] = to_low(steep)
        shape = (groups,) + keep_ref.shape[1:]
        grad = to_low(dot_first(active_ref[chunk], cotangent_ref[...]))
        here = slice(chunk * groups, (chunk + 1) * groups)
        keep_ref[here], send_ref[here] = parted(grad, ids_ref[CORE_SLOT], shape)


def down_kernel(
    ids_ref, hidden_ref, cotangent_ref, active_ref, steep_ref, pair_mine, pair_other, contract_mine,
    contract_other, *rest, head, masks, last
):
    rest = list(rest)
    take = lambda n: [rest.pop(0) for _ in range(n)]
    _, _, inner = active_ref.shape
    size = 2 * contract_mine.shape[1]
    if last:
        out_before, grad_before, keep_before, send_before, bias_before = take(5)
        tokens_ref, mixed_ref, attn_ref, gates_ref, routes_ref, vectors_ref = take(6)
        out_ref, branch_ref, grad_attn_ref, grad_logits_ref, grad_rows_ref = take(5)
        keep_ref, send_ref, grad_bias_ref = take(3)
        out, grad_hidden = out_before[...], grad_before[...]
        chunk, columns, everywhere = unit_of(ids_ref, 0, inner, size)
        keep_ref[chunk, :, :, columns] = keep_before[...]
        send_ref[chunk, :, :, columns] = send_before[...]
        grad_bias_ref[:, everywhere] = bias_before[...]
    else:
        out_held, grad_held, keep_ref, send_ref, grad_bias_ref = take(5)
        out = grad_hidden = None
    add = lambda total, term: term if total is None else total + term
    for at, mask in enumerate(masks):
        chunk, columns, everywhere = unit_of(ids_ref, mask, inner, size)
        expand = weights(
            pair_mine[chunk + 1, :, :, columns], pair_other[chunk + 1, :, :, columns], ids_ref
        )
        contract = weights(contract_mine[at : at + 1], contract_other[at : at + 1], ids_ref)
        out = add(out, dot_plain(active_ref[chunk, :, columns], contract))
        grad_active = dot_last(cotangent_ref[...], contract)
        grad_inner = to_low(steep_ref[chunk, :, columns].astype(FULL) * grad_active)
        grad_bias = jnp.sum(grad_inner.astype(FULL), axis=0, keepdims=True)
        grad_hidden = add(grad_hidden, dot_last(grad_inner, expand))
        grad = to_low(dot_first(hidden_ref[...], grad_inner))
        keep, send = parted(grad, ids_ref[CORE_SLOT], pair_mine.shape[1:3] + (size,))
        if last:
            grad_bias_ref[:, everywhere] = grad_bias
            keep_ref[chunk, :, :, columns] = keep
            send_ref[chunk, :, :, columns] = send
        else:
            grad_bias_ref[...] = grad_bias
            keep_ref[...] = keep
            send_ref[...] = send
    if not last:
        out_held[...] = out
        grad_held[...] = grad_hidden
        return
    lanes = lane_ids((1, LANES))
    gain, contract_bias = vectors_ref[0:1, :], vectors_ref[2:3, :]
    output_weight = weights(pair_mine[0], pair_other[0], ids_ref)
    mixed = mixed_ref[...]
    middle = tokens_ref[...].astype(FULL) + dot_plain(mixed, output_weight)
    out_ref[...] = to_low(out + middle + contract_bias)
    unit, factor = normalize(middle)
    cotangent = cotangent_ref[...].astype(FULL)
    branch = to_low(cotangent + norm_backward(grad_hidden, unit, factor, gain))
    branch_ref[...] = branch
    grad_rows_ref[...] = jnp.zeros_like(grad_rows_ref)
    grad_rows_ref[0:1, :] = jnp.sum(grad_hidden * unit, axis=0, keepdims=True)
    grad_rows_ref[1:2, :] = jnp.sum(grad_hidden, axis=0, keepdims=True)
    grad_rows_ref[2:3, :] = jnp.sum(cotangent, axis=0, keepdims=True)
    grad = to_low(dot_first(mixed, branch))
    end = keep_ref.shape[0] - 1
    keep_ref[end], send_ref[end] = parted(grad, ids_ref[CORE_SLOT], keep_ref.shape[1:])
    grad_mixed = dot_last(branch, output_weight)
    scaled = []
    for j in range(2):
        weighted = jnp.where(lanes < head, choose(grad_mixed, routes_ref[j], head), 0.0)
        scaled.append(gates_ref[j] * lane_sum(weighted * attn_ref[j]))
        grad_attn = weighted * gates_ref[j]
        grad_attn_ref[j] = to_low(put_parts(grad_attn, lanes, SUM_LANE, -scaled[j], 3))
    mean = scaled[0] + scaled[1]
    grad_logits = jnp.zeros(gates_ref.shape[1:], FULL)
    for j in range(2):
        grad_picked = scaled[j] - gates_ref[j] * mean
        grad_logits = jnp.where(lanes == routes_ref[j], grad_picked, grad_logits)
    grad_logits_ref[...] = to_low(grad_logits)


def backward_kernel(ids_ref, query_ref, grad_ref, bounds_ref, *rest, head, first, masks, part):
    count = len(masks)
    kv_refs, rest = rest[:count], list(rest[count:])
    before_ref = None if first else rest.pop(0)
    grad_query_ref, grad_kv_refs = rest[0], rest[1:]
    lanes = lane_ids((1, LANES))
    key_count = kv_refs[0].shape[0]
    blocks = []
    for index, ref in enumerate(kv_refs):
        start = (ids_ref[SEQ_SLOT] ^ masks[index]) * key_count
        hot = in_document(bounds_ref, row_positions(start, key_count))
        keys, values = key_rows_of(ref[...], hot, head)
        blocks.append((keys, values, to_low(keys.astype(FULL).T[:head])))
    totals = [None] * count
    for start in range(0, query_ref.shape[0], part):
        rows = slice(start, start + part)
        query = query_ref[rows, :]
        grad = grad_ref[rows, :]
        only_query = to_low(jnp.where(lanes < head, query.astype(FULL), 0.0))
        turned = pltpu.roll(grad.astype(FULL), head, 1)
        only_grad = to_low(jnp.where(lanes < head, 0.0, turned))
        grad_query = None if first else before_ref[:, rows]
        for index, (keys, values, turned_keys) in enumerate(blocks):
            probs = jnp.exp(dot_last(keys, query))
            grad_scores = to_low(probs * dot_last(values, grad))
            update = dot_plain(grad_scores, only_query) + dot_plain(to_low(probs), only_grad)
            totals[index] = update if totals[index] is None else totals[index] + update
            step = dot_plain(turned_keys, grad_scores)
            grad_query = step if grad_query is None else grad_query + step
        grad_query_ref[:, rows] = grad_query
    for index in range(count):
        grad_kv_refs[index][...] = to_low(totals[index])


def placed_kernel(
    ids_ref, grad_query_ref, hidden_ref, routes_ref, grad_logits_ref, small_ref, tokens_ref,
    grad_hidden_ref, keep_ref, send_ref, grad_router_ref, unit_ref, factor_ref, *, head
):
    unit_ref[...], factor_ref[...] = normalize(tokens_ref[...].astype(FULL))
    count, width = hidden_ref.shape
    turned = (grad_query_ref[...] * head**-0.5).T
    rows = []
    for j in range(2):
        half = to_low(turned[j * count : (j + 1) * count]).astype(FULL)
        rows.append(jnp.concatenate([half] * (LANES // head), axis=1))
    placed = to_low(place(rows, [routes_ref[j] for j in range(2)], head, width))
    hidden = hidden_ref[...]
    grad_logits = grad_logits_ref[...]
    keep, send = parted(to_low(dot_first(hidden, placed)), ids_ref[CORE_SLOT], keep_ref.shape)
    keep_ref[...] = keep
    send_ref[...] = send
    grad_router_ref[...] = dot_first(hidden, grad_logits)
    grad_hidden_ref[...] = dot_last(placed, small_ref[:, :width]) + dot_last(
        grad_logits, small_ref[:, small_ref.shape[1] - LANES :]
    )


def side_kernel(
    ids_ref, hidden_ref, grad_before_ref, unit_ref, small_ref, rows_ref, bias_ref,
    grad_router_ref, own_ref, *rest, experts, others, rows
):
    other_refs = rest[:others]
    grad_hidden_ref, keep_ref, send_ref = rest[others:]
    side = small_ref[:, small_ref.shape[1] - 2 * LANES :]
    grad_kv = own_ref[...].astype(FULL)
    for ref in other_refs:
        grad_kv += ref[...].astype(FULL)
    grad_kv = to_low(grad_kv)
    grad_keyval = dot_first(hidden_ref[...], grad_kv)
    grad_hidden = grad_before_ref[...] + dot_last(grad_kv, side[:, :LANES])
    grad_hidden_ref[...] = grad_hidden
    gain_grad = jnp.sum(grad_hidden * unit_ref[...], axis=0, keepdims=True)
    shift_grad = jnp.sum(grad_hidden, axis=0, keepdims=True)
    width = hidden_ref.shape[1]
    index = lax.broadcasted_iota(jnp.int32, (8, 1), 0)
    later = pltpu.roll(rows_ref[...], 2, 0)
    vectors = jnp.where(index == 0, gain_grad, jnp.where(index == 1, shift_grad, later))
    ahead = jnp.zeros((experts, width), FULL)
    behind = jnp.zeros((LANES - experts - 8, width), FULL)
    columns = jnp.concatenate([ahead, vectors, behind], axis=0).T
    spread = bias_rows(bias_ref[...], width // rows, rows)
    grad_side = jnp.concatenate([grad_keyval, columns + grad_router_ref[...] + spread], axis=1)
    keep_ref[...], send_ref[...] = parted(to_low(grad_side), ids_ref[CORE_SLOT], keep_ref.shape)


def tokens_kernel(
    grad_hidden_ref, unit_ref, factor_ref, grad_middle_ref, small_ref, grad_tokens_ref, *, experts
):
    misc = small_ref[:, small_ref.shape[1] - LANES :]
    gain = misc.astype(FULL).T[experts : experts + 1]
    grad = norm_backward(grad_hidden_ref[...], unit_ref[...], factor_ref[...], gain)
    grad_tokens_ref[...] = to_low(grad_middle_ref[...].astype(FULL) + grad)


def finish_kernel(*refs, terms, slots, parts):
    added = lambda part: sum(ref[...].astype(FULL) for ref in part)
    total = jnp.concatenate([added(refs[2 * i : 2 * i + 2]) for i in range(parts)], axis=0)
    rest, last = added(refs[2 * parts : 2 * parts + 2]), added(refs[2 * parts + 2 : terms])
    expand_ref, output_ref, contract_ref, query_ref, router_ref, keyval_ref = refs[terms : terms + 6]
    *vector_refs, bias_ref = refs[terms + 6 :]
    rows, width = output_ref.shape
    for slot in range(slots):
        expand_ref[:, slot * width : (slot + 1) * width] = total[slot]
    output_ref[...] = total[slots]
    query_ref[...] = last[:rows]
    side = last[rows:]
    contract_ref[...] = rest[0]
    experts = router_ref.shape[0]
    keyval_ref[...] = side[:, :LANES]
    for expert in range(experts):
        lane = LANES + expert
        router_ref[expert : expert + 1, :] = as_row(side[:, lane : lane + 1])
    for index, ref in enumerate(vector_refs):
        lane = LANES + experts + index
        ref[...] = as_row(side[:, lane : lane + 1])
    start = LANES + BIAS_LANE
    bias_ref[...] = side[0:1, start : start + bias_ref.shape[1]]


def in_hbm(array):
    return pltpu.with_memory_space_constraint(array, pltpu.HBM)


def smem_spec():
    return pl.BlockSpec(memory_space=pltpu.SMEM)


def vmem_spec():
    return pl.BlockSpec(memory_space=pltpu.VMEM)


def shape_of(shape, dtype):
    return jax.ShapeDtypeStruct(tuple(shape), dtype)


def limit_of(name):
    return LIMITS[name] * MEGA


def estimate(cost):
    return pl.CostEstimate(flops=int(cost * 1e9), bytes_accessed=0, transcendentals=0)


def call(kernel, name, outs, cost, scalars=0, more=0):
    def run(*operands):
        return pl.pallas_call(
            kernel,
            in_specs=[smem_spec()] * scalars + [vmem_spec()] * (len(operands) - scalars),
            out_specs=[vmem_spec()] * len(outs) if isinstance(outs, list) else vmem_spec(),
            out_shape=outs,
            compiler_params=pltpu.CompilerParams(vmem_limit_bytes=limit_of(name) + more * MEGA),
            cost_estimate=estimate(cost),
            name=name,
        )(*operands)

    return run


def generations(seq_count):
    masks = range(1, seq_count)
    most = seq_count.bit_length() - 1
    return [[m for m in masks if bin(m).count("1") == n] for n in range(1, most + 1)]


def feed_up(ids, tokens, cotangent, attn, gates, routes, vectors, bias, pairs, plain, head):
    token_count, width = tokens.shape
    chunks = pairs[0].shape[0] - 1
    rows = shape_of((token_count, width), LOW)
    held = shape_of((chunks, token_count, bias.shape[1] // chunks), LOW)
    return call(
        functools.partial(up_kernel, head=head), "feed_up", [rows, rows, held, held]
        + [shape_of(plain, LOW)] * 2, FEED_COST / 2, scalars=1
    )(ids, tokens, cotangent, attn, gates, routes, vectors, bias, *pairs)


def feed_down(ids, hidden, cotangent, active, steep, pairs, contracts, masks, head, end=()):
    token_count, width = hidden.shape
    last = bool(end)
    rows = (token_count, width)
    size = 2 * contracts[0].shape[1]
    if last:
        grads = shape_of(pairs[0].shape, LOW)
        outs = [
            shape_of(rows, LOW),
            shape_of(rows, LOW),
            shape_of((2, token_count, LANES), LOW),
            shape_of((token_count, LANES), LOW),
            shape_of((8, width), FULL),
            grads,
            grads,
            shape_of((1, active.shape[0] * active.shape[2]), FULL),
        ]
    else:
        grads = shape_of(pairs[0].shape[1:3] + (size,), LOW)
        outs = [shape_of(rows, FULL)] * 2 + [grads, grads, shape_of((1, size), FULL)]
    return call(
        functools.partial(down_kernel, head=head, masks=masks, last=last),
        "feed_down_last" if last else "feed_down",
        outs,
        FEED_COST / 2,
        scalars=1,
    )(ids, hidden, cotangent, active, steep, *pairs, *contracts, *end)


def per_device(
    tokens, routes, lengths, cotangent, first_gain, first_shift, router, query_map, keyval,
    output_map, second_gain, second_shift, expand, expand_bias, contract, contract_bias
):
    seq_count, plane_count = lax.axis_size("seq"), lax.axis_size("dp") // 2
    along = Group("seq", 0, seq_count, SEQ_SLOT)
    plane = Group("dp", 1, plane_count, PLANE_SLOT)
    core = Group("dp", 0, 2, CORE_SLOT)
    token_count, width = tokens.shape
    rows = first_gain.shape[0]
    contract_rows = contract.shape[0]
    experts = router.shape[1]
    head = keyval.shape[1] // 2
    inner_width = expand.shape[1]
    chunks = inner_width // width
    slots = 1 + chunks
    my_index = along.index()
    ids = jnp.stack([g.index() for g in (along, plane, core)]).astype(jnp.int32)
    side_width = 2 * LANES
    row_count = 2 * token_count
    part = min(1024, row_count)

    params = [
        query_map, keyval, router.T, first_gain[None], first_shift[None], second_gain[None],
        second_shift[None], contract_bias[None], expand_bias[None], output_map, expand, contract
    ]
    small_mine, large_mine = pl.pallas_call(
        functools.partial(pack_kernel, count=len(params)),
        in_specs=[pl.BlockSpec(memory_space=pltpu.HBM)] * len(params),
        out_specs=[vmem_spec()] * 2,
        out_shape=[
            shape_of((rows, width + side_width), LOW),
            shape_of((slots * rows + contract_rows, width), LOW),
        ],
        scratch_shapes=[pltpu.VMEM(p.shape, p.dtype) for p in params]
        + [pltpu.SemaphoreType.DMA((len(params),))],
        compiler_params=pltpu.CompilerParams(vmem_limit_bytes=limit_of("pack")),
        cost_estimate=estimate(0.1),
        name="pack",
    )(*[in_hbm(p) for p in params])

    def first_work():
        given = [routes.T, lengths]
        return pl.pallas_call(
            first_kernel,
            in_specs=[smem_spec()] + [pl.BlockSpec(memory_space=pltpu.HBM)] * 2 + [vmem_spec()],
            out_specs=[vmem_spec()] * 3 + [smem_spec()],
            out_shape=[
                shape_of((2, token_count, LANES), jnp.int32),
                shape_of((8, LANES), jnp.int32),
                shape_of(tokens.shape, FULL),
                shape_of(ids.shape, jnp.int32),
            ],
            scratch_shapes=[pltpu.VMEM(p.shape, p.dtype) for p in given]
            + [pltpu.SemaphoreType.DMA((2,))],
            compiler_params=pltpu.CompilerParams(vmem_limit_bytes=limit_of("first")),
            cost_estimate=estimate(0.1),
            name="first",
        )(ids, *[in_hbm(p) for p in given], tokens)


    small_move = Move(along, small_mine[None])
    coming = generations(seq_count)
    bits = [1 << b for b in reversed(range(seq_count.bit_length() - 1))]
    large, large_masks = large_mine[None], [0]
    large_move = Move(along, large, bits[:1])
    route_columns, bounds, unit, ids, large = phase(
        [small_move, large_move], first_work, held=[large]
    )
    for group in (along, plane, core):
        group.ids = ids
    small = merge([small_mine[None]] + [small_move.got[m] for m in range(1, seq_count)], along)
    for bit, later in zip(bits, bits[1:]):
        large_masks = large_masks + [m | bit for m in large_masks]
        large = call(
            join_kernel, "join", shape_of((2 * large.shape[0],) + large.shape[1:], LOW), 0.1
        )(large, large_move.got[bit])
        large, small = together(large, small)
        large_move = Move(along, large, [later])
        if later != bits[-1]:
            phase([large_move])
    small_move = Move(plane, small)
    phase([small_move, large_move])
    large_parts = [large, large_move.got[bits[-1]]]
    large_masks = [large_masks, [m | bits[-1] for m in large_masks]]
    small = merge([small] + [small_move.got[m] for m in range(1, plane_count)], plane)[0]
    small_move = Move(core, small)
    phase([small_move])
    small_shape = (plane_count, seq_count * rows, width + side_width)
    smalls = [small.reshape(small_shape), small_move.got[1].reshape(small_shape)]
    hidden, kv_mine, gates, small = call(
        functools.partial(hidden_kernel, experts=experts),
        "hidden",
        [
            shape_of((token_count, width), LOW),
            shape_of((token_count, LANES), LOW),
            shape_of((2, token_count, LANES), FULL),
            shape_of((width, width + side_width), LOW),
        ],
        0.5,
        scalars=1,
    )(ids, unit, *smalls, route_columns)

    def attend(state, masks, queries, last=False):
        return call(
            functools.partial(
                forward_kernel, head=head, first=not state, last=last, masks=masks, part=part
            ),
            "attention_forward",
            [shape_of((row_count, LANES), t) for t in ((FULL, LOW) if last else (FULL,))],
            FORWARD_COST * len(masks),
            scalars=1,
            more=3 * (len(masks) - 1),
        )(ids, queries, bounds, *[shards[m] for m in masks], *state)

    def keys_of(masks):
        return [Move(along, shards[m & (m - 1)], [m & -m]) for m in masks]

    def come(masks, moves):
        for mask, move in zip(masks, moves):
            shards[mask] = move.got[mask & -mask]

    shards = {0: kv_mine}
    keys = keys_of(coming[0])

    for move in keys:
        move.begin()
    queries = call(
        functools.partial(query_kernel, head=head),
        "queries",
        shape_of((row_count, LANES), LOW),
        QUERY_COST,
        scalars=1,
    )(ids, hidden, small, route_columns, bounds)
    queries, *large_parts = together(queries, *large_parts)
    if rows % 16:
        blocks = {m: x[i] for x, masks in zip(large_parts, large_masks) for i, m in enumerate(masks)}
        lines = jnp.stack(by_place([blocks[m] for m in range(seq_count)], my_index))
        pair = lines[:, : slots * rows].reshape(seq_count, slots, rows, width)
        pair = pair.transpose(1, 0, 2, 3).reshape(slots, seq_count * rows, width)
        half = lines[:, slots * rows :].reshape(1, seq_count * contract_rows, width)
    else:
        pair, half = call(
            functools.partial(spread_kernel, masks=large_masks, slots=slots, rows=rows),
            "spread",
            [
                shape_of((slots, seq_count * rows, width), LOW),
                shape_of((seq_count * contract_rows, width), LOW),
            ],
            0.1,
            scalars=1,
        )(ids, *large_parts)
        half = half[None]
    pair_move = Move(plane, pair).begin()
    state, half = phase(keys, lambda: attend([], [0], queries), held=[half])
    come(coming[0], keys)
    for before, masks in zip(coming, coming[1:]):
        keys = keys_of(masks)
        moves = keys + [pair_move] if masks is coming[-1] else keys
        [state] = phase(moves, lambda: attend([state], before, queries))
        come(masks, keys)
    pair = merge([pair] + [pair_move.got[m] for m in range(1, plane_count)], plane)
    pair = pair.reshape(slots, plane_count, -1, width)
    pair_move = Move(core, pair)
    half_move = Move(plane, half).begin()
    own_core = Move(core, half)
    attn, wide_queries = phase([pair_move, own_core], lambda: attend([state], coming[-1], queries, True))
    attn = attn.reshape(2, token_count, LANES)
    pairs = [pair, pair_move.got[1]]
    vectors, bias = call(
        functools.partial(vectors_kernel, experts=experts, rows=rows),
        "vectors",
        [shape_of((8, width), FULL), shape_of((1, inner_width), FULL)],
        0.1,
    )(small)

    plain = (plane_count, seq_count * contract_rows, width)
    mixed, hidden_two, active, steep, keep_half, send_half = phase(
        [half_move],
        lambda: feed_up(
            ids, tokens, cotangent, attn, gates, route_columns, vectors, bias, pairs, plain, head
        ),
    )
    masks = list(range(1, plane_count))
    rest = call(
        stack_kernel, "join", shape_of((len(masks),) + half.shape[1:], LOW), 0.1
    )(*[half_move.got[m] for m in masks])
    rest_move, half_core = Move(core, rest), Move(core, send_half)
    out_held, grad_held, keep_own, send_own, bias_own = phase(
        [rest_move, half_core],
        lambda: feed_down(
            ids, hidden_two, cotangent, active, steep, pairs, (half, own_core.got[1]), [0], head
        ),
    )
    flat = lambda lead, *terms: [t.reshape(lead, -1, width) for t in terms]
    half_fold = Fold([(flat(1, keep_half, half_core.got[1]), 0, 1)], [plane, along])
    (
        out, branch, grad_attn, grad_logits, grad_rows, keep_pair, send_pair, grad_bias
    ) = phase(
        fold([half_fold]),
        lambda: feed_down(
            ids, hidden_two, cotangent, active, steep, pairs, (rest, rest_move.got[1]), masks, head,
            (
                out_held, grad_held, keep_own, send_own, bias_own, tokens, mixed, attn, gates,
                route_columns, vectors
            ),
        ),
    )
    folded([half_fold])

    grad_rows_in = grad_attn.reshape(row_count, LANES)
    masks = list(range(seq_count - 1, 0, -1))
    if seq_count > 2:
        masks = [2] + [m for m in masks if m != 2]
    third = max(1, len(masks) // 3)
    groups = [masks[:third], masks[third:], [0]]

    def backward(masks, before):
        return call(
            functools.partial(
                backward_kernel, head=head, first=before is None, masks=masks, part=part
            ),
            "attention_backward",
            [shape_of((head, row_count), FULL)]
            + [shape_of((token_count, LANES), LOW)] * len(masks),
            BACKWARD_COST * len(masks),
            scalars=1,
            more=3 * (len(masks) - 1),
        )(
            ids, wide_queries, grad_rows_in, bounds, *[shards[m] for m in masks],
            *([] if before is None else [before])
        )

    pair_move = Move(core, send_pair)
    first_query, *leaving = phase([pair_move], lambda: backward(groups[0], None))
    pair_terms = flat(slots, keep_pair, pair_move.got[1])
    part_way = (slots + 1) // 2
    pair_folds = [
        Fold([(pair_terms, 0, part_way)], [plane, along]),
        Fold([(pair_terms, part_way, slots)], [plane, along], upward=True),
    ]
    both = [half_fold] + pair_folds
    keys_first = Move(along, dict(zip(groups[0], leaving)), groups[0])
    second_query, *leaving = phase(
        [keys_first] + fold(both), lambda: backward(groups[1], first_query)
    )
    folded(both)
    keys_second = Move(along, dict(zip(groups[1], leaving)), groups[1])

    def work():
        grad_query, own = backward(groups[2], second_query)
        shape = (plane_count, seq_count * rows, width)
        return own, *call(
            functools.partial(placed_kernel, head=head),
            "query_gradient",
            [
                shape_of((token_count, width), FULL),
                shape_of(shape, LOW),
                shape_of(shape, LOW),
                shape_of((width, LANES), FULL),
                shape_of((token_count, width), FULL),
                shape_of((token_count, LANES), FULL),
            ],
            1.0,
            scalars=1,
        )(ids, grad_query, hidden, route_columns, grad_logits, small, tokens)

    grad_kv, grad_before, keep_query, send_query, grad_router, unit, factor = phase(
        [keys_second] + fold(both), work
    )
    folded(both)
    if not any(group is plane for f in pair_folds for group, _ in f.stages):
        pair_folds[0].sets += pair_folds.pop().sets
        both = [half_fold] + pair_folds
    query_move = Move(core, send_query)
    others = list(keys_first.got.values()) + list(keys_second.got.values())
    shape = (plane_count, seq_count * rows, side_width)
    grad_hidden, keep_side, send_side = phase(
        [query_move],
        lambda: call(
            functools.partial(side_kernel, experts=experts, others=len(others), rows=rows),
            "key_gradient",
            [shape_of((token_count, width), FULL), shape_of(shape, LOW), shape_of(shape, LOW)],
            1.0,
            scalars=1,
        )(
            ids, hidden, grad_before, unit, small, grad_rows, grad_bias, grad_router,
            grad_kv, *others
        ),
    )

    side_move = Move(core, send_side)
    phase([side_move])
    moves = fold(both)
    keep_query, *_ = together(keep_query, *[f.keep for f in both if f.move is not None])
    line = lambda *terms: [t.reshape(1, -1, t.shape[-1]) for t in terms]
    small_sent = cut(
        [line(keep_query, query_move.got[1]), line(keep_side, side_move.got[1])],
        plane,
        width + side_width,
    )
    small_move = Move(plane, dict(enumerate(small_sent)))
    phase([small_move] + moves)
    folded(both)
    last_sent = cut([line(small_sent[0], *small_move.got.values())], along, width)
    last_move = Move(along, dict(enumerate(last_sent)))
    moves = fold(both)
    [grad_tokens] = phase(
        [last_move] + moves,
        lambda: [
            call(
                functools.partial(tokens_kernel, experts=experts),
                "token_gradient",
                shape_of((token_count, width), LOW),
                1.0,
            )(grad_hidden, unit, factor, branch, small)
        ],
    )
    folded(both)
    while any(f.stages for f in both):
        phase(fold(both))
        folded(both)
    terms = [t for f in pair_folds for t in f.sets[0][0]] + half_fold.sets[0][0]
    parts = len(pair_folds)
    terms += [last_sent[0]] + list(last_move.got.values())
    vector_shape = shape_of((1, rows), FULL)
    (
        grad_expand, grad_output, grad_contract, grad_query_map, grad_router, grad_keyval,
        *vector_sums, grad_spread
    ) = call(
        functools.partial(finish_kernel, terms=len(terms), slots=chunks, parts=parts),
        "finish",
        [
            shape_of(expand.shape, FULL),
            shape_of(output_map.shape, FULL),
            shape_of(contract.shape, FULL),
            shape_of(query_map.shape, FULL),
            shape_of((experts, rows), FULL),
            shape_of(keyval.shape, FULL),
        ]
        + [vector_shape] * 5
        + [shape_of((1, expand_bias.shape[0]), FULL)],
        0.1,
    )(*terms)
    grad_gain, grad_shift, grad_gain_two, grad_shift_two, grad_contract_bias = (
        v.reshape(rows) for v in vector_sums
    )
    return (
        out, grad_tokens, grad_gain, grad_shift, grad_router.T, grad_query_map, grad_keyval,
        grad_output, grad_gain_two, grad_shift_two, grad_expand, grad_spread.reshape(-1),
        grad_contract, grad_contract_bias
    )


def solution(mesh):
    both = ("dp", "seq")
    rows, vector = P(both, None), P(both)
    return jax.shard_map(
        per_device,
        mesh=mesh,
        in_specs=(
            rows, rows, P("dp", None), rows, vector, vector, rows, rows, rows, rows, vector, vector,
            rows, vector, rows, vector
        ),
        out_specs=(
            rows, rows, vector, vector, rows, rows, rows, rows, vector, vector, rows, vector, rows,
            vector
        ),
        check_vma=False,
    )
```

```python
import functools

import jax
import jax.numpy as jnp
from jax import lax
from jax.experimental import pallas as pl
from jax.experimental.pallas import tpu as pltpu
from jax.sharding import PartitionSpec as P

LOW = jnp.bfloat16
FULL = jnp.float32
FAR = 1e30
EPS = 1e-05
DOC_LANE = 64
LSE_LANE = 96
SUM_LANE = 64
MAX_LANE = 67
BIAS_LANE = 64
SEQ_SLOT, PLANE_SLOT, CORE_SLOT = range(3)
LANES = 128
MEGA = 1 << 20
FORWARD_COST = 0.1
QUERY_COST = 0.05
BACKWARD_COST = 3.0
FEED_COST = 8.0
LIMITS = {
    "pack": 4, "first": 8, "hidden": 6, "vectors": 2, "queries": 6, "attention_forward": 8,
    "attention_backward": 8, "query_gradient": 8, "key_gradient": 12, "token_gradient": 12, "merge": 2, "join": 2, "spread": 2,
    "cut": 3, "fold": 4, "finish": 2, "feed_up": 8,
    "feed_down": 6, "feed_down_last": 17,
}


def to_low(matrix):
    return matrix.astype(LOW)


def dot_plain(left, right):
    return lax.dot_general(left, right, (((1,), (0,)), ((), ())), preferred_element_type=FULL)


def dot_last(left, right):
    return lax.dot_general(left, right, (((1,), (1,)), ((), ())), preferred_element_type=FULL)


def dot_first(left, right):
    return lax.dot_general(left, right, (((0,), (0,)), ((), ())), preferred_element_type=FULL)


class Group:
    def __init__(self, axis, shift, size, slot):
        self.axis, self.shift, self.size, self.slot = axis, shift, size, slot
        self.ids = None

    def index(self):
        return (lax.axis_index(self.axis) >> self.shift) & (self.size - 1)

    def exchange(self, block, mask):
        step = mask << self.shift
        pairs = [(i, i ^ step) for i in range(lax.axis_size(self.axis))]
        return lax.ppermute(block, self.axis, pairs)


def by_place(blocks, index):
    blocks = list(blocks)
    for bit in range(len(blocks).bit_length() - 1):
        swap = (index >> bit) & 1 == 1
        blocks = [jnp.where(swap, blocks[i ^ (1 << bit)], blocks[i]) for i in range(len(blocks))]
    return blocks


def merge_kernel(ids_ref, *refs, count, slot):
    out_ref = refs[count]
    rows = refs[0].shape[1]
    for mask in range(count):
        start = pl.multiple_of((ids_ref[slot] ^ mask) * rows, rows)
        out_ref[:, pl.ds(start, rows), :] = refs[mask][...]


def merge(blocks, group):
    lead, rows, columns = blocks[0].shape
    if rows % 16:
        return jnp.concatenate(by_place(blocks, group.index()), axis=1)
    return call(
        functools.partial(merge_kernel, count=len(blocks), slot=group.slot),
        "merge",
        shape_of((lead, rows * len(blocks), columns), blocks[0].dtype),
        0.1,
        scalars=1,
    )(group.ids, *blocks)


def columns_of(columns, width):
    return [slice(i, min(i + width, columns)) for i in range(0, columns, width)]


def cut_kernel(ids_ref, *refs, sizes, count, slot):
    outs = refs[len(refs) - count :]
    refs = list(refs[: len(refs) - count])
    sets = [[refs.pop(0) for _ in range(size)] for size in sizes]
    width = outs[0].shape[1]
    for mask in range(count):
        row = column = 0
        for terms in sets:
            lead, total, columns = terms[0].shape
            rows = total // count
            start = pl.multiple_of((ids_ref[slot] ^ mask) * rows, rows)
            for at in range(lead):
                for piece in columns_of(columns, width):
                    value = sum(term[at, pl.ds(start, rows), piece].astype(FULL) for term in terms)
                    end = column + value.shape[1]
                    outs[mask][row : row + rows, column:end] = to_low(value)
                    column = end % width
                    row += 0 if column else rows
        if column:
            rest = outs[mask].shape[0] - row
            outs[mask][row:, column:] = jnp.zeros((rest, width - column), LOW)


def cut(sets, group, width):
    count = group.size
    sets = [[t.reshape((-1,) + t.shape[-2:]) for t in terms] for terms in sets]
    rows = [terms[0].shape[1] // count for terms in sets]
    total = sum(t[0].shape[0] * r * t[0].shape[2] for t, r in zip(sets, rows))
    total = -(-total // (width * rows[-1])) * rows[-1]
    if any(r % 16 for r in rows):
        index = group.index()
        results = []
        for mask in range(count):
            bands, band = [], []
            for terms, r in zip(sets, rows):
                value = sum(t.astype(FULL) for t in terms)
                value = lax.dynamic_slice_in_dim(value, (index ^ mask) * r, r, 1)
                for at in range(value.shape[0]):
                    for piece in columns_of(value.shape[2], width):
                        band.append(value[at, :, piece])
                        if sum(b.shape[1] for b in band) == width:
                            bands.append(jnp.concatenate(band, axis=1))
                            band = []
            if band:
                band = jnp.concatenate(band, axis=1)
                bands.append(jnp.pad(band, ((0, 0), (0, width - band.shape[1]))))
            results.append(to_low(jnp.concatenate(bands, axis=0)))
        return results
    return call(
        functools.partial(
            cut_kernel, sizes=[len(t) for t in sets], count=count, slot=group.slot
        ),
        "cut",
        [shape_of((total, width), LOW)] * count,
        0.1,
        scalars=1,
    )(group.ids, *[t for terms in sets for t in terms])


def together(*values):
    return lax.optimization_barrier(values)


class Move:
    def __init__(self, group, blocks, masks=None):
        self.group = group
        self.masks = list(range(1, group.size)) if masks is None else masks
        self.blocks = blocks if isinstance(blocks, dict) else {m: blocks for m in self.masks}

    def begin(self):
        self.moved = [self.group.exchange(self.blocks[m], m) for m in self.masks]
        return self

    def end(self, got):
        self.got = dict(zip(self.masks, got))
        self.moved = None


def phase(moves, work=lambda: (), held=()):
    for move in moves:
        if getattr(move, "moved", None) is None:
            move.begin()
    done = work()
    ended = list(together(*[x for m in moves for x in m.moved], *done, *held))
    for move in moves:
        move.end([ended.pop(0) for _ in move.masks])
    return ended


def fold_kernel(ids_ref, *refs, plan):
    refs = list(refs)
    folds = [(*step, [refs.pop(0) for _ in step[1]]) for step in plan]
    keeps = [refs.pop(0) for _ in plan]
    for keep_ref, ((slot, shift), lows, half, count, out, place, terms) in zip(keeps, folds):
        bit = (ids_ref[slot] >> shift) & 1
        for pair in range(count):
            mine, other = (
                sum(
                    t[pl.ds(low + (2 * pair + b) * half, half)].astype(FULL)
                    for t, low in zip(terms, lows)
                )
                for b in (bit, 1 - bit)
            )
            keep_ref[pair * half : (pair + 1) * half] = mine
            refs[out][place + pair * half : place + (pair + 1) * half] = to_low(other)


class Fold:
    def __init__(self, terms, lead, rows, groups, upward=False):
        self.terms, self.lead, self.rows = terms, lead, rows
        self.left = [(g, b) for g in groups for b in reversed(range(g.size.bit_length() - 1))]
        over = [x for x in self.left if x[0].axis == "dp"]
        self.stages = over[::-1] if upward else over
        self.stages += [x for x in self.left if x[0].axis == "seq"][::-1]
        self.move = None

    def part(self):
        ahead = 1 << self.left.index(self.stages[0])
        return (self.rows << len(self.left)) // (2 * ahead), self.lead * ahead


def fold(folds, unit):
    folds = [f for f in folds if f.stages]
    if not folds:
        return []
    ways, filled, plan, operands, keeps = [], [], [], [], []
    for f in folds:
        if f.stages[0] not in ways:
            ways.append(f.stages[0])
            filled.append(0)
        group, bit = f.stages[0]
        half, count = f.part()
        at = ways.index(f.stages[0])
        columns = f.terms[0][0].shape[-1]
        lows = [low // unit for _, low in f.terms]
        f.start = filled[at]
        plan.append(((group.slot, bit), lows, half // unit, count, at, f.start // unit))
        operands += [a.reshape(-1, unit, columns) for a, _ in f.terms]
        keeps.append(shape_of((half * count // unit, unit, columns), FULL))
        filled[at] += half * count
    sends = [shape_of((rows // unit, unit, columns), LOW) for rows in filled]
    results = call(
        functools.partial(fold_kernel, plan=plan), "fold", keeps + sends, 0.1, scalars=1
    )(ways[0][0].ids, *operands)
    moves = [
        Move(group, sent, [1 << bit]) for (group, bit), sent in zip(ways, results[len(folds) :])
    ]
    for f, keep in zip(folds, results):
        f.keep, f.move = keep, moves[ways.index(f.stages[0])]
        f.left.remove(f.stages.pop(0))
    return moves


def folded(folds):
    for f in folds:
        if f.move is not None:
            [got] = f.move.got.values()
            f.terms = [(f.keep, 0), (got, f.start)]
            f.move = None


def lane_ids(shape):
    return lax.broadcasted_iota(jnp.int32, shape, len(shape) - 1)


def row_positions(offset, rows):
    return offset + lax.broadcasted_iota(jnp.int32, (rows, 1), 0)


def in_document(bounds_ref, positions):
    return (positions >= bounds_ref[0:1, :]) & (positions < bounds_ref[1:2, :])


def put_parts(base, lanes, lane, rows, count):
    for step in range(count):
        part = to_low(rows).astype(FULL)
        base = jnp.where(lanes == lane + step, part, base)
        rows = rows - part
    return base


def lane_sum(matrix):
    total = sum(matrix[:, i : i + LANES] for i in range(0, matrix.shape[1], LANES))
    high = to_low(total)
    low = to_low(total - high.astype(FULL))
    ones = jnp.ones((LANES, LANES), LOW)
    return dot_plain(high, ones) + dot_plain(low, ones)


def over(rows, width):
    return jnp.concatenate([rows] * (width // LANES), axis=1)


def normalize(matrix):
    width = matrix.shape[1]
    center = matrix - over(lane_sum(matrix) * (1.0 / width), width)
    factor = lax.rsqrt(lane_sum(center * center) * (1.0 / width) + EPS)
    return center * over(factor, width), factor


def norm_backward(grad, unit, factor, gain):
    width = grad.shape[1]
    scaled = grad * gain
    mean = over(lane_sum(scaled) * (1.0 / width), width)
    along = over(lane_sum(scaled * unit) * (1.0 / width), width)
    return over(factor, width) * (scaled - mean - unit * along)


def choose(wide, route, head):
    shift = (LANES // head).bit_length() - 1
    tile = lax.shift_right_logical(route, shift)
    picked = wide[:, :LANES]
    for index in range(1, wide.shape[1] // LANES):
        picked = jnp.where(tile == index, wide[:, index * LANES : (index + 1) * LANES], picked)
    turned = pltpu.roll(picked, head, 1)
    lanes = lane_ids((1, LANES))
    mine = (lanes // head) == (route & ((1 << shift) - 1))
    return jnp.where(mine, picked, turned)


def place(doubled, routes, head, width):
    lanes = lane_ids((1, LANES))
    per_tile = LANES // head
    tiles = []
    for index in range(width // LANES):
        expert = lanes // head + index * per_tile
        tile = jnp.zeros_like(doubled[0])
        for rows, route in zip(doubled, routes):
            tile = jnp.where(route == expert, rows, tile)
        tiles.append(tile)
    return jnp.concatenate(tiles, axis=1)


def doubled_head(rows, head):
    lanes = lane_ids((1, LANES))
    return jnp.where(lanes < head, rows, pltpu.roll(rows, head, 1))


def key_rows_of(kv, hot, head):
    lanes = lane_ids((1, LANES))
    kv = kv.astype(FULL)
    marks = jnp.where((lanes >= LSE_LANE) & (lanes < LSE_LANE + 3), 1.0, 0.0)
    keys = jnp.where(lanes < head, kv, jnp.where(hot, 1.0, marks))
    ones = jnp.where((lanes >= SUM_LANE) & (lanes < SUM_LANE + 3), 1.0, 0.0)
    values = jnp.where(lanes < head, pltpu.roll(kv, head, 1), ones)
    return to_low(keys), to_low(values)


def as_column(row):
    rows = row.shape[1]
    lanes = lax.broadcasted_iota(jnp.int32, (rows, rows), 1)
    here = lax.broadcasted_iota(jnp.int32, (rows, rows), 0)
    return jnp.sum(jnp.where(lanes == here, row, 0.0), axis=1, keepdims=True)


def as_row(column):
    rows = column.shape[0]
    lanes = lax.broadcasted_iota(jnp.int32, (rows, rows), 1)
    here = lax.broadcasted_iota(jnp.int32, (rows, rows), 0)
    return jnp.sum(jnp.where(lanes == here, column, 0.0), axis=0, keepdims=True)


def fetch(refs, held, semaphores):
    copies = [
        pltpu.make_async_copy(ref, into, semaphores.at[i])
        for i, (ref, into) in enumerate(zip(refs, held))
    ]
    for copy in copies:
        copy.start()
    for copy in copies:
        copy.wait()


def pack_kernel(*refs, count):
    small_ref, large_ref = refs[count : count + 2]
    held = refs[count + 2 : -1]
    fetch(refs[:count], held, refs[-1])
    (
        query_ref, keyval_ref, router_ref, gain_ref, shift_ref, gain_two_ref, shift_two_ref,
        contract_bias_ref, expand_bias_ref, output_ref, expand_ref, contract_ref
    ) = held
    rows, width = query_ref.shape
    experts = router_ref.shape[0]
    keyval_width = keyval_ref.shape[1]
    small_ref[:, :width] = to_low(query_ref[...])
    small_ref[:, width : width + keyval_width] = to_low(keyval_ref[...])
    lanes = lane_ids((1, LANES))
    turned = router_ref[...]
    side = jnp.zeros((rows, LANES), FULL)
    for expert in range(experts):
        side = jnp.where(lanes == expert, as_column(turned[expert : expert + 1]), side)
    vectors = [gain_ref, shift_ref, gain_two_ref, shift_two_ref, contract_bias_ref]
    for index, ref in enumerate(vectors):
        side = jnp.where(lanes == experts + index, as_column(ref[...]), side)
    extra = expand_bias_ref.shape[1]
    bias = jnp.pad(expand_bias_ref[...], ((0, 0), (BIAS_LANE, LANES - BIAS_LANE - extra)))
    first = lax.broadcasted_iota(jnp.int32, (rows, 1), 0) == 0
    side = side + jnp.where(first, bias, 0.0)
    small_ref[:, width + keyval_width :] = to_low(side)
    large = [output_ref[...]]
    large += [
        expand_ref[:, c * width : (c + 1) * width] for c in range(expand_ref.shape[1] // width)
    ]
    large_ref[...] = to_low(jnp.concatenate(large + [contract_ref[...]], axis=0))


def first_kernel(
    ids_ref, routes_hbm, lengths_hbm, tokens_ref, columns_ref, bounds_ref, unit_ref, ids_out, *held
):
    unit_ref[...] = normalize(tokens_ref[...].astype(FULL))[0]
    for slot in range(ids_ref.shape[0]):
        ids_out[slot] = ids_ref[slot]
    routes_ref, lengths_ref, semaphores = held
    fetch((routes_hbm, lengths_hbm), (routes_ref, lengths_ref), semaphores)
    routes = routes_ref[...].astype(FULL)
    choices = routes.shape[0]
    routes = jnp.concatenate([routes, jnp.zeros((8 - routes.shape[0], routes.shape[1]), FULL)], axis=0)
    turned = routes.T
    for j in range(choices):
        wide = jnp.broadcast_to(turned[:, j : j + 1], columns_ref.shape[1:])
        columns_ref[j] = wide.astype(jnp.int32)
    count = lengths_ref.shape[1]
    lanes = lane_ids((1, LANES))
    rest = jnp.zeros((1, LANES - DOC_LANE - count), jnp.int32)
    lengths = jnp.concatenate(
        [jnp.zeros((1, DOC_LANE), jnp.int32), lengths_ref[...], rest], axis=1
    )
    ends = lengths
    step = 1
    while step < count:
        ends = ends + jnp.where(lanes >= DOC_LANE + step, pltpu.roll(ends, step, 1), 0)
        step *= 2
    here = (lanes >= DOC_LANE) & (lanes < DOC_LANE + count)
    starts = jnp.where(here, ends - lengths, 1 << 30)
    ends = jnp.where(here, ends, 0)
    index = lax.broadcasted_iota(jnp.int32, (8, 1), 0)
    bounds_ref[...] = jnp.where(index == 0, starts, jnp.where(index == 1, ends, 0))


def vectors_kernel(small_ref, vectors_ref, bias_ref, *, experts, rows):
    misc = small_ref[:, small_ref.shape[1] - LANES :].astype(FULL)
    turned = misc.T
    vectors_ref[...] = turned[experts + 2 : experts + 10]
    count = misc.shape[0] // rows
    each = bias_ref.shape[1] // count
    per_tile = LANES // each
    firsts = misc.reshape(count, rows, LANES)[:, 0, :].reshape(count // per_tile, per_tile, LANES)
    lanes = lane_ids((1, LANES))
    tiles = jnp.zeros((count // per_tile, LANES), FULL)
    for k in range(per_tile):
        moved = pltpu.roll(firsts[:, k, :], (k * each - BIAS_LANE) % LANES, 1)
        tiles = jnp.where(lanes // each == k, moved, tiles)
    for index in range(count // per_tile):
        bias_ref[:, index * LANES : (index + 1) * LANES] = tiles[index : index + 1]


def bias_rows(bias, count, rows):
    each = bias.shape[1] // count
    per_tile = LANES // each
    tiles = jnp.concatenate(
        [bias[:, i : i + LANES] for i in range(0, bias.shape[1], LANES)], axis=0
    )
    lanes = lane_ids((1, LANES))
    mine = (lanes >= BIAS_LANE) & (lanes < BIAS_LANE + each)
    parts = [
        jnp.where(mine, pltpu.roll(tiles, (BIAS_LANE - k * each) % LANES, 1), 0.0)
        for k in range(per_tile)
    ]
    firsts = jnp.stack(parts, axis=1).reshape(count, 1, LANES)
    here = lax.broadcasted_iota(jnp.int32, (1, rows, 1), 1) == 0
    return jnp.where(here, firsts, 0.0).reshape(count * rows, LANES)


def stack_kernel(*refs):
    for at, ref in enumerate(refs[:-1]):
        refs[-1][at] = ref[0]


def join_kernel(first_ref, second_ref, out_ref):
    count = first_ref.shape[0]
    out_ref[:count] = first_ref[...]
    out_ref[count:] = second_ref[...]


def spread_kernel(ids_ref, *refs, masks, slots, rows):
    pair_ref, half_ref = refs[len(masks) :]
    more = refs[0].shape[1] - slots * rows
    for ref, masks_of in zip(refs, masks):
        for at, mask in enumerate(masks_of):
            place = ids_ref[SEQ_SLOT] ^ mask
            start = pl.multiple_of(place * rows, rows)
            for slot in range(slots):
                here = slice(slot * rows, (slot + 1) * rows)
                pair_ref[slot, pl.ds(start, rows), :] = ref[at, here, :]
            half_ref[pl.ds(pl.multiple_of(place * more, more), more), :] = ref[at, slots * rows :, :]


def hidden_kernel(
    ids_ref, unit_ref, mine_ref, other_ref, routes_ref, hidden_ref, kv_ref, gates_ref, small_ref, *, experts
):
    small = merged(mine_ref[...], other_ref[...], ids_ref[CORE_SLOT])
    small_ref[...] = small
    side = small[:, small.shape[1] - 2 * LANES :]
    vectors = side[:, LANES:].astype(FULL).T
    hidden = to_low(
        unit_ref[...] * vectors[experts : experts + 1] + vectors[experts + 1 : experts + 2]
    )
    hidden_ref[...] = hidden
    both = dot_plain(hidden, side)
    kv_ref[...] = to_low(both[:, :LANES])
    logits = both[:, LANES:]
    lanes = lane_ids((1, LANES))
    picked = [lane_sum(jnp.where(lanes == routes_ref[j], logits, 0.0)) for j in range(2)]
    top = jnp.maximum(picked[0], picked[1])
    raised = [jnp.exp(p - top) for p in picked]
    total = raised[0] + raised[1]
    for j in range(2):
        gates_ref[j] = raised[j] / total


def query_kernel(ids_ref, hidden_ref, small_ref, routes_ref, bounds_ref, query_ref, *, head):
    rows, width = hidden_ref.shape
    wide = dot_plain(hidden_ref[...], small_ref[:, :width])
    lanes = lane_ids((1, LANES))
    hot = in_document(bounds_ref, row_positions(ids_ref[SEQ_SLOT] * rows, rows))
    documents = (bounds_ref[1:2, :] > 0) & (lanes >= head)
    marks = jnp.where(documents & jnp.logical_not(hot), -FAR, 0.0)
    for j in range(2):
        rows_of = choose(wide, routes_ref[j], head) * head**-0.5
        query_ref[j * rows : (j + 1) * rows, :] = to_low(jnp.where(lanes < head, rows_of, marks))


def forward_kernel(ids_ref, query_ref, bounds_ref, *rest, head, first, last, masks, part):
    count = len(masks)
    kv_refs, rest = rest[:count], list(rest[count:])
    state_ref = None if first else rest.pop(0)
    lanes = lane_ids((1, LANES))
    blocks = []
    for index, ref in enumerate(kv_refs):
        start = (ids_ref[SEQ_SLOT] ^ masks[index]) * ref.shape[0]
        hot = in_document(bounds_ref, row_positions(start, ref.shape[0]))
        blocks.append(key_rows_of(ref[...], hot, head))
    for start in range(0, query_ref.shape[0], part):
        rows = slice(start, start + part)
        query = query_ref[rows, :]
        state = None if first else state_ref[rows, :]
        for keys, values in blocks:
            scores = dot_last(query, keys)
            top = jnp.max(scores, axis=1, keepdims=True)
            if state is None:
                new = top
                state = dot_plain(to_low(jnp.exp(scores - new)), values)
            else:
                old = state[:, MAX_LANE : MAX_LANE + 1]
                new = jnp.maximum(old, top)
                weights = to_low(jnp.exp(scores - new))
                state = state * jnp.exp(old - new) + dot_plain(weights, values)
            state = jnp.where(lanes == MAX_LANE, new, state)
        if last:
            attn_ref, wide_ref = rest
            total = state[:, SUM_LANE : SUM_LANE + 1]
            attn_ref[rows, :] = jnp.where(lanes < head, state / total, 0.0)
            log_total = state[:, MAX_LANE : MAX_LANE + 1] + jnp.log(total)
            wide_ref[rows, :] = to_low(
                put_parts(query.astype(FULL), lanes, LSE_LANE, -log_total, 3)
            )
        else:
            rest[0][rows, :] = state


def merged(mine, other, bit):
    low = bit == 0
    both = jnp.stack([jnp.where(low, mine, other), jnp.where(low, other, mine)], axis=1)
    return both.reshape(-1, mine.shape[-1])


def parted(whole, bit, shape):
    both = whole.reshape(shape[0], 2, shape[1], shape[2])
    low = bit == 0
    first, second = both[:, 0], both[:, 1]
    return jnp.where(low, first, second), jnp.where(low, second, first)


def weights(refs, bit):
    mine, other = refs[0][...], refs[1][...]
    shape = mine.shape[-3:]
    return merged(mine.reshape(shape), other.reshape(shape), bit)


def weights(mine, other, ids_ref):
    return merged(mine, other, ids_ref[CORE_SLOT])


def unit_of(ids_ref, mask, inner, size):
    unit = ids_ref[PLANE_SLOT] ^ mask
    shift = (inner // size).bit_length() - 1
    everywhere = pl.ds(pl.multiple_of(unit * size, size), size)
    if not shift:
        return unit, slice(0, size), everywhere
    start = pl.multiple_of((unit & ((1 << shift) - 1)) * size, size)
    return lax.shift_right_logical(unit, shift), pl.ds(start, size), everywhere


def up_kernel(
    ids_ref, tokens_ref, cotangent_ref, attn_ref, gates_ref, routes_ref, vectors_ref, bias_ref,
    pair_mine, pair_other, mixed_ref, hidden_ref, active_ref, steep_ref, keep_ref, send_ref, *, head
):
    width = tokens_ref.shape[1]
    wide = [doubled_head(attn_ref[j], head) * gates_ref[j] for j in range(2)]
    mixed = to_low(place(wide, [routes_ref[j] for j in range(2)], head, width))
    mixed_ref[...] = mixed
    output_weight = weights(pair_mine[0], pair_other[0], ids_ref)
    middle = tokens_ref[...].astype(FULL) + dot_plain(mixed, output_weight)
    unit, _ = normalize(middle)
    hidden = to_low(unit * vectors_ref[0:1, :] + vectors_ref[1:2, :])
    hidden_ref[...] = hidden
    slope = 0.7978845608028654
    cube = 0.044715
    chunks, _, inner_width = active_ref.shape
    part = min(256, tokens_ref.shape[0])
    groups = keep_ref.shape[0] // chunks
    for chunk in range(chunks):
        expand = weights(pair_mine[chunk + 1], pair_other[chunk + 1], ids_ref)
        columns = slice(chunk * inner_width, (chunk + 1) * inner_width)
        for start in range(0, hidden.shape[0], part):
            here = slice(start, start + part)
            inner = dot_plain(hidden[here], expand) + bias_ref[:, columns]
            square = inner * inner
            half = 0.5 + 0.5 * jnp.tanh(inner * (slope + slope * cube * square))
            whole = inner * half
            active_ref[chunk, here] = to_low(whole)
            steep = half + whole * (1.0 - half) * (2.0 * slope + 6.0 * slope * cube * square)
            steep_ref[chunk, here] = to_low(steep)
        shape = (groups,) + keep_ref.shape[1:]
        grad = to_low(dot_first(active_ref[chunk], cotangent_ref[...]))
        here = slice(chunk * groups, (chunk + 1) * groups)
        keep_ref[here], send_ref[here] = parted(grad, ids_ref[CORE_SLOT], shape)


def down_kernel(
    ids_ref, hidden_ref, cotangent_ref, active_ref, steep_ref, pair_mine, pair_other, contract_mine,
    contract_other, *rest, head, masks, last
):
    rest = list(rest)
    take = lambda n: [rest.pop(0) for _ in range(n)]
    _, _, inner = active_ref.shape
    size = 2 * contract_mine.shape[1]
    if last:
        out_before, grad_before, keep_before, send_before, bias_before = take(5)
        tokens_ref, mixed_ref, attn_ref, gates_ref, routes_ref, vectors_ref = take(6)
        out_ref, branch_ref, grad_attn_ref, grad_logits_ref, grad_rows_ref = take(5)
        keep_ref, send_ref, grad_bias_ref = take(3)
        out, grad_hidden = out_before[...], grad_before[...]
        chunk, columns, everywhere = unit_of(ids_ref, 0, inner, size)
        keep_ref[chunk, :, :, columns] = keep_before[...]
        send_ref[chunk, :, :, columns] = send_before[...]
        grad_bias_ref[:, everywhere] = bias_before[...]
    else:
        out_held, grad_held, keep_ref, send_ref, grad_bias_ref = take(5)
        out = grad_hidden = None
    add = lambda total, term: term if total is None else total + term
    for at, mask in enumerate(masks):
        chunk, columns, everywhere = unit_of(ids_ref, mask, inner, size)
        expand = weights(
            pair_mine[chunk + 1, :, :, columns], pair_other[chunk + 1, :, :, columns], ids_ref
        )
        contract = weights(contract_mine[at : at + 1], contract_other[at : at + 1], ids_ref)
        out = add(out, dot_plain(active_ref[chunk, :, columns], contract))
        grad_active = dot_last(cotangent_ref[...], contract)
        grad_inner = to_low(steep_ref[chunk, :, columns].astype(FULL) * grad_active)
        grad_bias = jnp.sum(grad_inner.astype(FULL), axis=0, keepdims=True)
        grad_hidden = add(grad_hidden, dot_last(grad_inner, expand))
        grad = to_low(dot_first(hidden_ref[...], grad_inner))
        keep, send = parted(grad, ids_ref[CORE_SLOT], pair_mine.shape[1:3] + (size,))
        if last:
            grad_bias_ref[:, everywhere] = grad_bias
            keep_ref[chunk, :, :, columns] = keep
            send_ref[chunk, :, :, columns] = send
        else:
            grad_bias_ref[...] = grad_bias
            keep_ref[...] = keep
            send_ref[...] = send
    if not last:
        out_held[...] = out
        grad_held[...] = grad_hidden
        return
    lanes = lane_ids((1, LANES))
    gain, contract_bias = vectors_ref[0:1, :], vectors_ref[2:3, :]
    output_weight = weights(pair_mine[0], pair_other[0], ids_ref)
    mixed = mixed_ref[...]
    middle = tokens_ref[...].astype(FULL) + dot_plain(mixed, output_weight)
    out_ref[...] = to_low(out + middle + contract_bias)
    unit, factor = normalize(middle)
    cotangent = cotangent_ref[...].astype(FULL)
    branch = to_low(cotangent + norm_backward(grad_hidden, unit, factor, gain))
    branch_ref[...] = branch
    grad_rows_ref[...] = jnp.zeros_like(grad_rows_ref)
    grad_rows_ref[0:1, :] = jnp.sum(grad_hidden * unit, axis=0, keepdims=True)
    grad_rows_ref[1:2, :] = jnp.sum(grad_hidden, axis=0, keepdims=True)
    grad_rows_ref[2:3, :] = jnp.sum(cotangent, axis=0, keepdims=True)
    grad = to_low(dot_first(mixed, branch))
    end = keep_ref.shape[0] - 1
    keep_ref[end], send_ref[end] = parted(grad, ids_ref[CORE_SLOT], keep_ref.shape[1:])
    grad_mixed = dot_last(branch, output_weight)
    scaled = []
    for j in range(2):
        weighted = jnp.where(lanes < head, choose(grad_mixed, routes_ref[j], head), 0.0)
        scaled.append(gates_ref[j] * lane_sum(weighted * attn_ref[j]))
        grad_attn = weighted * gates_ref[j]
        grad_attn_ref[j] = to_low(put_parts(grad_attn, lanes, SUM_LANE, -scaled[j], 3))
    mean = scaled[0] + scaled[1]
    grad_logits = jnp.zeros(gates_ref.shape[1:], FULL)
    for j in range(2):
        grad_picked = scaled[j] - gates_ref[j] * mean
        grad_logits = jnp.where(lanes == routes_ref[j], grad_picked, grad_logits)
    grad_logits_ref[...] = to_low(grad_logits)


def backward_kernel(ids_ref, query_ref, grad_ref, bounds_ref, *rest, head, first, masks, part):
    count = len(masks)
    kv_refs, rest = rest[:count], list(rest[count:])
    before_ref = None if first else rest.pop(0)
    grad_query_ref, grad_kv_refs = rest[0], rest[1:]
    lanes = lane_ids((1, LANES))
    key_count = kv_refs[0].shape[0]
    blocks = []
    for index, ref in enumerate(kv_refs):
        start = (ids_ref[SEQ_SLOT] ^ masks[index]) * key_count
        hot = in_document(bounds_ref, row_positions(start, key_count))
        keys, values = key_rows_of(ref[...], hot, head)
        blocks.append((keys, values, to_low(keys.astype(FULL).T[:head])))
    totals = [None] * count
    for start in range(0, query_ref.shape[0], part):
        rows = slice(start, start + part)
        query = query_ref[rows, :]
        grad = grad_ref[rows, :]
        only_query = to_low(jnp.where(lanes < head, query.astype(FULL), 0.0))
        turned = pltpu.roll(grad.astype(FULL), head, 1)
        only_grad = to_low(jnp.where(lanes < head, 0.0, turned))
        grad_query = None if first else before_ref[:, rows]
        for index, (keys, values, turned_keys) in enumerate(blocks):
            probs = jnp.exp(dot_last(keys, query))
            grad_scores = to_low(probs * dot_last(values, grad))
            update = dot_plain(grad_scores, only_query) + dot_plain(to_low(probs), only_grad)
            totals[index] = update if totals[index] is None else totals[index] + update
            step = dot_plain(turned_keys, grad_scores)
            grad_query = step if grad_query is None else grad_query + step
        grad_query_ref[:, rows] = grad_query
    for index in range(count):
        grad_kv_refs[index][...] = to_low(totals[index])


def placed_kernel(
    ids_ref, grad_query_ref, hidden_ref, routes_ref, grad_logits_ref, small_ref, tokens_ref,
    grad_hidden_ref, keep_ref, send_ref, grad_router_ref, unit_ref, factor_ref, *, head
):
    unit_ref[...], factor_ref[...] = normalize(tokens_ref[...].astype(FULL))
    count, width = hidden_ref.shape
    turned = (grad_query_ref[...] * head**-0.5).T
    rows = []
    for j in range(2):
        half = to_low(turned[j * count : (j + 1) * count]).astype(FULL)
        rows.append(jnp.concatenate([half] * (LANES // head), axis=1))
    placed = to_low(place(rows, [routes_ref[j] for j in range(2)], head, width))
    hidden = hidden_ref[...]
    grad_logits = grad_logits_ref[...]
    keep, send = parted(to_low(dot_first(hidden, placed)), ids_ref[CORE_SLOT], keep_ref.shape)
    keep_ref[...] = keep
    send_ref[...] = send
    grad_router_ref[...] = dot_first(hidden, grad_logits)
    grad_hidden_ref[...] = dot_last(placed, small_ref[:, :width]) + dot_last(
        grad_logits, small_ref[:, small_ref.shape[1] - LANES :]
    )


def side_kernel(
    ids_ref, hidden_ref, grad_before_ref, unit_ref, small_ref, rows_ref, bias_ref,
    grad_router_ref, own_ref, *rest, experts, others, rows
):
    other_refs = rest[:others]
    grad_hidden_ref, keep_ref, send_ref = rest[others:]
    side = small_ref[:, small_ref.shape[1] - 2 * LANES :]
    grad_kv = own_ref[...].astype(FULL)
    for ref in other_refs:
        grad_kv += ref[...].astype(FULL)
    grad_kv = to_low(grad_kv)
    grad_keyval = dot_first(hidden_ref[...], grad_kv)
    grad_hidden = grad_before_ref[...] + dot_last(grad_kv, side[:, :LANES])
    grad_hidden_ref[...] = grad_hidden
    gain_grad = jnp.sum(grad_hidden * unit_ref[...], axis=0, keepdims=True)
    shift_grad = jnp.sum(grad_hidden, axis=0, keepdims=True)
    width = hidden_ref.shape[1]
    index = lax.broadcasted_iota(jnp.int32, (8, 1), 0)
    later = pltpu.roll(rows_ref[...], 2, 0)
    vectors = jnp.where(index == 0, gain_grad, jnp.where(index == 1, shift_grad, later))
    ahead = jnp.zeros((experts, width), FULL)
    behind = jnp.zeros((LANES - experts - 8, width), FULL)
    columns = jnp.concatenate([ahead, vectors, behind], axis=0).T
    spread = bias_rows(bias_ref[...], width // rows, rows)
    grad_side = jnp.concatenate([grad_keyval, columns + grad_router_ref[...] + spread], axis=1)
    keep_ref[...], send_ref[...] = parted(to_low(grad_side), ids_ref[CORE_SLOT], keep_ref.shape)


def tokens_kernel(
    grad_hidden_ref, unit_ref, factor_ref, grad_middle_ref, small_ref, grad_tokens_ref, *, experts
):
    misc = small_ref[:, small_ref.shape[1] - LANES :]
    gain = misc.astype(FULL).T[experts : experts + 1]
    grad = norm_backward(grad_hidden_ref[...], unit_ref[...], factor_ref[...], gain)
    grad_tokens_ref[...] = to_low(grad_middle_ref[...].astype(FULL) + grad)


def finish_kernel(*refs, terms, slots, plan):
    sums = []
    for at, (lows, count) in enumerate(plan):
        pair = refs[2 * at : 2 * at + 2]
        sums.append(sum(t[low : low + count, :].astype(FULL) for t, low in zip(pair, lows)))
    rest = sums.pop()
    total = jnp.concatenate(sums, axis=0)
    last = sum(ref[...].astype(FULL) for ref in refs[2 * len(plan) : terms])
    expand_ref, output_ref, contract_ref, query_ref, router_ref, keyval_ref = refs[terms : terms + 6]
    *vector_refs, bias_ref = refs[terms + 6 :]
    rows, width = output_ref.shape
    for slot in range(slots):
        expand_ref[:, slot * width : (slot + 1) * width] = total[slot * rows : (slot + 1) * rows]
    output_ref[...] = total[slots * rows :]
    query_ref[...] = last[:rows]
    side = last[rows:]
    contract_ref[...] = rest
    experts = router_ref.shape[0]
    keyval_ref[...] = side[:, :LANES]
    for expert in range(experts):
        lane = LANES + expert
        router_ref[expert : expert + 1, :] = as_row(side[:, lane : lane + 1])
    for index, ref in enumerate(vector_refs):
        lane = LANES + experts + index
        ref[...] = as_row(side[:, lane : lane + 1])
    start = LANES + BIAS_LANE
    bias_ref[...] = side[0:1, start : start + bias_ref.shape[1]]


def in_hbm(array):
    return pltpu.with_memory_space_constraint(array, pltpu.HBM)


def smem_spec():
    return pl.BlockSpec(memory_space=pltpu.SMEM)


def vmem_spec():
    return pl.BlockSpec(memory_space=pltpu.VMEM)


def shape_of(shape, dtype):
    return jax.ShapeDtypeStruct(tuple(shape), dtype)


def limit_of(name):
    return LIMITS[name] * MEGA


def estimate(cost):
    return pl.CostEstimate(flops=int(cost * 1e9), bytes_accessed=0, transcendentals=0)


def call(kernel, name, outs, cost, scalars=0, more=0):
    def run(*operands):
        return pl.pallas_call(
            kernel,
            in_specs=[smem_spec()] * scalars + [vmem_spec()] * (len(operands) - scalars),
            out_specs=[vmem_spec()] * len(outs) if isinstance(outs, list) else vmem_spec(),
            out_shape=outs,
            compiler_params=pltpu.CompilerParams(vmem_limit_bytes=limit_of(name) + more * MEGA),
            cost_estimate=estimate(cost),
            name=name,
        )(*operands)

    return run


def generations(seq_count):
    masks = range(1, seq_count)
    most = seq_count.bit_length() - 1
    return [[m for m in masks if bin(m).count("1") == n] for n in range(1, most + 1)]


def feed_up(ids, tokens, cotangent, attn, gates, routes, vectors, bias, pairs, plain, head):
    token_count, width = tokens.shape
    chunks = pairs[0].shape[0] - 1
    rows = shape_of((token_count, width), LOW)
    held = shape_of((chunks, token_count, bias.shape[1] // chunks), LOW)
    return call(
        functools.partial(up_kernel, head=head), "feed_up", [rows, rows, held, held]
        + [shape_of(plain, LOW)] * 2, FEED_COST / 2, scalars=1
    )(ids, tokens, cotangent, attn, gates, routes, vectors, bias, *pairs)


def feed_down(ids, hidden, cotangent, active, steep, pairs, contracts, masks, head, end=()):
    token_count, width = hidden.shape
    last = bool(end)
    rows = (token_count, width)
    size = 2 * contracts[0].shape[1]
    if last:
        grads = shape_of(pairs[0].shape, LOW)
        outs = [
            shape_of(rows, LOW),
            shape_of(rows, LOW),
            shape_of((2, token_count, LANES), LOW),
            shape_of((token_count, LANES), LOW),
            shape_of((8, width), FULL),
            grads,
            grads,
            shape_of((1, active.shape[0] * active.shape[2]), FULL),
        ]
    else:
        grads = shape_of(pairs[0].shape[1:3] + (size,), LOW)
        outs = [shape_of(rows, FULL)] * 2 + [grads, grads, shape_of((1, size), FULL)]
    return call(
        functools.partial(down_kernel, head=head, masks=masks, last=last),
        "feed_down_last" if last else "feed_down",
        outs,
        FEED_COST / 2,
        scalars=1,
    )(ids, hidden, cotangent, active, steep, *pairs, *contracts, *end)


def per_device(
    tokens, routes, lengths, cotangent, first_gain, first_shift, router, query_map, keyval,
    output_map, second_gain, second_shift, expand, expand_bias, contract, contract_bias
):
    seq_count, plane_count = lax.axis_size("seq"), lax.axis_size("dp") // 2
    along = Group("seq", 0, seq_count, SEQ_SLOT)
    plane = Group("dp", 1, plane_count, PLANE_SLOT)
    core = Group("dp", 0, 2, CORE_SLOT)
    token_count, width = tokens.shape
    rows = first_gain.shape[0]
    contract_rows = contract.shape[0]
    experts = router.shape[1]
    head = keyval.shape[1] // 2
    inner_width = expand.shape[1]
    chunks = inner_width // width
    slots = 1 + chunks
    my_index = along.index()
    ids = jnp.stack([g.index() for g in (along, plane, core)]).astype(jnp.int32)
    side_width = 2 * LANES
    row_count = 2 * token_count
    part = min(1024, row_count)

    params = [
        query_map, keyval, router.T, first_gain[None], first_shift[None], second_gain[None],
        second_shift[None], contract_bias[None], expand_bias[None], output_map, expand, contract
    ]
    small_mine, large_mine = pl.pallas_call(
        functools.partial(pack_kernel, count=len(params)),
        in_specs=[pl.BlockSpec(memory_space=pltpu.HBM)] * len(params),
        out_specs=[vmem_spec()] * 2,
        out_shape=[
            shape_of((rows, width + side_width), LOW),
            shape_of((slots * rows + contract_rows, width), LOW),
        ],
        scratch_shapes=[pltpu.VMEM(p.shape, p.dtype) for p in params]
        + [pltpu.SemaphoreType.DMA((len(params),))],
        compiler_params=pltpu.CompilerParams(vmem_limit_bytes=limit_of("pack")),
        cost_estimate=estimate(0.1),
        name="pack",
    )(*[in_hbm(p) for p in params])

    def first_work():
        given = [routes.T, lengths]
        return pl.pallas_call(
            first_kernel,
            in_specs=[smem_spec()] + [pl.BlockSpec(memory_space=pltpu.HBM)] * 2 + [vmem_spec()],
            out_specs=[vmem_spec()] * 3 + [smem_spec()],
            out_shape=[
                shape_of((2, token_count, LANES), jnp.int32),
                shape_of((8, LANES), jnp.int32),
                shape_of(tokens.shape, FULL),
                shape_of(ids.shape, jnp.int32),
            ],
            scratch_shapes=[pltpu.VMEM(p.shape, p.dtype) for p in given]
            + [pltpu.SemaphoreType.DMA((2,))],
            compiler_params=pltpu.CompilerParams(vmem_limit_bytes=limit_of("first")),
            cost_estimate=estimate(0.1),
            name="first",
        )(ids, *[in_hbm(p) for p in given], tokens)


    small_move = Move(along, small_mine[None])
    coming = generations(seq_count)
    bits = [1 << b for b in reversed(range(seq_count.bit_length() - 1))]
    large, large_masks = large_mine[None], [0]
    large_move = Move(along, large, bits[:1])
    route_columns, bounds, unit, ids, large = phase(
        [small_move, large_move], first_work, held=[large]
    )
    for group in (along, plane, core):
        group.ids = ids
    small = merge([small_mine[None]] + [small_move.got[m] for m in range(1, seq_count)], along)
    for bit, later in zip(bits, bits[1:]):
        large_masks = large_masks + [m | bit for m in large_masks]
        large = call(
            join_kernel, "join", shape_of((2 * large.shape[0],) + large.shape[1:], LOW), 0.1
        )(large, large_move.got[bit])
        large, small = together(large, small)
        large_move = Move(along, large, [later])
        if later != bits[-1]:
            phase([large_move])
    small_move = Move(plane, small)
    phase([small_move, large_move])
    large_parts = [large, large_move.got[bits[-1]]]
    large_masks = [large_masks, [m | bits[-1] for m in large_masks]]
    small = merge([small] + [small_move.got[m] for m in range(1, plane_count)], plane)[0]
    small_move = Move(core, small)
    phase([small_move])
    small_shape = (plane_count, seq_count * rows, width + side_width)
    smalls = [small.reshape(small_shape), small_move.got[1].reshape(small_shape)]
    hidden, kv_mine, gates, small = call(
        functools.partial(hidden_kernel, experts=experts),
        "hidden",
        [
            shape_of((token_count, width), LOW),
            shape_of((token_count, LANES), LOW),
            shape_of((2, token_count, LANES), FULL),
            shape_of((width, width + side_width), LOW),
        ],
        0.5,
        scalars=1,
    )(ids, unit, *smalls, route_columns)

    def attend(state, masks, queries, last=False):
        return call(
            functools.partial(
                forward_kernel, head=head, first=not state, last=last, masks=masks, part=part
            ),
            "attention_forward",
            [shape_of((row_count, LANES), t) for t in ((FULL, LOW) if last else (FULL,))],
            FORWARD_COST * len(masks),
            scalars=1,
            more=3 * (len(masks) - 1),
        )(ids, queries, bounds, *[shards[m] for m in masks], *state)

    def keys_of(masks):
        return [Move(along, shards[m & (m - 1)], [m & -m]) for m in masks]

    def come(masks, moves):
        for mask, move in zip(masks, moves):
            shards[mask] = move.got[mask & -mask]

    shards = {0: kv_mine}
    keys = keys_of(coming[0])

    for move in keys:
        move.begin()
    queries = call(
        functools.partial(query_kernel, head=head),
        "queries",
        shape_of((row_count, LANES), LOW),
        QUERY_COST,
        scalars=1,
    )(ids, hidden, small, route_columns, bounds)
    queries, *large_parts = together(queries, *large_parts)
    if rows % 16:
        blocks = {m: x[i] for x, masks in zip(large_parts, large_masks) for i, m in enumerate(masks)}
        lines = jnp.stack(by_place([blocks[m] for m in range(seq_count)], my_index))
        pair = lines[:, : slots * rows].reshape(seq_count, slots, rows, width)
        pair = pair.transpose(1, 0, 2, 3).reshape(slots, seq_count * rows, width)
        half = lines[:, slots * rows :].reshape(1, seq_count * contract_rows, width)
    else:
        pair, half = call(
            functools.partial(spread_kernel, masks=large_masks, slots=slots, rows=rows),
            "spread",
            [
                shape_of((slots, seq_count * rows, width), LOW),
                shape_of((seq_count * contract_rows, width), LOW),
            ],
            0.1,
            scalars=1,
        )(ids, *large_parts)
        half = half[None]
    pair_move = Move(plane, pair).begin()
    state, half = phase(keys, lambda: attend([], [0], queries), held=[half])
    come(coming[0], keys)
    for before, masks in zip(coming, coming[1:]):
        keys = keys_of(masks)
        moves = keys + [pair_move] if masks is coming[-1] else keys
        [state] = phase(moves, lambda: attend([state], before, queries))
        come(masks, keys)
    pair = merge([pair] + [pair_move.got[m] for m in range(1, plane_count)], plane)
    pair = pair.reshape(slots, plane_count, -1, width)
    pair_move = Move(core, pair)
    half_move = Move(plane, half).begin()
    own_core = Move(core, half)
    attn, wide_queries = phase([pair_move, own_core], lambda: attend([state], coming[-1], queries, True))
    attn = attn.reshape(2, token_count, LANES)
    pairs = [pair, pair_move.got[1]]
    vectors, bias = call(
        functools.partial(vectors_kernel, experts=experts, rows=rows),
        "vectors",
        [shape_of((8, width), FULL), shape_of((1, inner_width), FULL)],
        0.1,
    )(small)

    plain = (plane_count, seq_count * contract_rows, width)
    mixed, hidden_two, active, steep, keep_half, send_half = phase(
        [half_move],
        lambda: feed_up(
            ids, tokens, cotangent, attn, gates, route_columns, vectors, bias, pairs, plain, head
        ),
    )
    masks = list(range(1, plane_count))
    rest = call(
        stack_kernel, "join", shape_of((len(masks),) + half.shape[1:], LOW), 0.1
    )(*[half_move.got[m] for m in masks])
    rest_move, half_core = Move(core, rest), Move(core, send_half)
    out_held, grad_held, keep_own, send_own, bias_own = phase(
        [rest_move, half_core],
        lambda: feed_down(
            ids, hidden_two, cotangent, active, steep, pairs, (half, own_core.got[1]), [0], head
        ),
    )
    half_terms = [(keep_half, 0), (half_core.got[1], 0)]
    half_fold = Fold(half_terms, 1, contract_rows, [plane, along])
    (
        out, branch, grad_attn, grad_logits, grad_rows, keep_pair, send_pair, grad_bias
    ) = phase(
        fold([half_fold], rows),
        lambda: feed_down(
            ids, hidden_two, cotangent, active, steep, pairs, (rest, rest_move.got[1]), masks, head,
            (
                out_held, grad_held, keep_own, send_own, bias_own, tokens, mixed, attn, gates,
                route_columns, vectors
            ),
        ),
    )
    folded([half_fold])

    grad_rows_in = grad_attn.reshape(row_count, LANES)
    masks = list(range(seq_count - 1, 0, -1))
    if seq_count > 2:
        masks = [2] + [m for m in masks if m != 2]
    third = max(1, len(masks) // 3)
    groups = [masks[:third], masks[third:], [0]]

    def backward(masks, before):
        return call(
            functools.partial(
                backward_kernel, head=head, first=before is None, masks=masks, part=part
            ),
            "attention_backward",
            [shape_of((head, row_count), FULL)]
            + [shape_of((token_count, LANES), LOW)] * len(masks),
            BACKWARD_COST * len(masks),
            scalars=1,
            more=3 * (len(masks) - 1),
        )(
            ids, wide_queries, grad_rows_in, bounds, *[shards[m] for m in masks],
            *([] if before is None else [before])
        )

    pair_move = Move(core, send_pair)
    first_query, *leaving = phase([pair_move], lambda: backward(groups[0], None))
    part_way = (slots + 1) // 2
    begin = part_way * width
    pair_got = pair_move.got[1]
    pair_folds = [
        Fold([(keep_pair, 0), (pair_got, 0)], part_way, rows, [plane, along]),
        Fold(
            [(keep_pair, begin // 2), (pair_got, begin // 2)], slots - part_way, rows, [plane, along],
            upward=True,
        ),
    ]
    both = [half_fold] + pair_folds
    keys_first = Move(along, dict(zip(groups[0], leaving)), groups[0])
    second_query, *leaving = phase(
        [keys_first] + fold(both, rows), lambda: backward(groups[1], first_query)
    )
    folded(both)
    keys_second = Move(along, dict(zip(groups[1], leaving)), groups[1])

    def work():
        grad_query, own = backward(groups[2], second_query)
        shape = (plane_count, seq_count * rows, width)
        return own, *call(
            functools.partial(placed_kernel, head=head),
            "query_gradient",
            [
                shape_of((token_count, width), FULL),
                shape_of(shape, LOW),
                shape_of(shape, LOW),
                shape_of((width, LANES), FULL),
                shape_of((token_count, width), FULL),
                shape_of((token_count, LANES), FULL),
            ],
            1.0,
            scalars=1,
        )(ids, grad_query, hidden, route_columns, grad_logits, small, tokens)

    grad_kv, grad_before, keep_query, send_query, grad_router, unit, factor = phase(
        [keys_second] + fold(pair_folds, rows), work
    )
    folded(pair_folds)
    query_move = Move(core, send_query)
    others = list(keys_first.got.values()) + list(keys_second.got.values())
    shape = (plane_count, seq_count * rows, side_width)
    grad_hidden, keep_side, send_side = phase(
        [query_move],
        lambda: call(
            functools.partial(side_kernel, experts=experts, others=len(others), rows=rows),
            "key_gradient",
            [shape_of((token_count, width), FULL), shape_of(shape, LOW), shape_of(shape, LOW)],
            1.0,
            scalars=1,
        )(
            ids, hidden, grad_before, unit, small, grad_rows, grad_bias, grad_router,
            grad_kv, *others
        ),
    )

    side_move = Move(core, send_side)
    phase([side_move])
    moves = fold(both, rows)
    keep_query, *_ = together(keep_query, *[f.keep for f in both if f.move is not None])
    line = lambda *terms: [t.reshape(1, -1, t.shape[-1]) for t in terms]
    small_sent = cut(
        [line(keep_query, query_move.got[1]), line(keep_side, side_move.got[1])],
        plane,
        width + side_width,
    )
    small_move = Move(plane, dict(enumerate(small_sent)))
    phase([small_move] + moves)
    folded(both)
    last_sent = cut([line(small_sent[0], *small_move.got.values())], along, width)
    last_move = Move(along, dict(enumerate(last_sent)))
    moves = fold(both, rows)
    [grad_tokens] = phase(
        [last_move] + moves,
        lambda: [
            call(
                functools.partial(tokens_kernel, experts=experts),
                "token_gradient",
                shape_of((token_count, width), LOW),
                1.0,
            )(grad_hidden, unit, factor, branch, small)
        ],
    )
    folded(both)
    while any(f.stages for f in both):
        phase(fold(both, rows))
        folded(both)
    ends = pair_folds + [half_fold]
    plan = [([low for _, low in f.terms], f.lead * f.rows) for f in ends]
    terms = [a.reshape(-1, width) for f in ends for a, _ in f.terms]
    terms += [last_sent[0]] + list(last_move.got.values())
    vector_shape = shape_of((1, rows), FULL)
    (
        grad_expand, grad_output, grad_contract, grad_query_map, grad_router, grad_keyval,
        *vector_sums, grad_spread
    ) = call(
        functools.partial(finish_kernel, terms=len(terms), slots=chunks, plan=plan),
        "finish",
        [
            shape_of(expand.shape, FULL),
            shape_of(output_map.shape, FULL),
            shape_of(contract.shape, FULL),
            shape_of(query_map.shape, FULL),
            shape_of((experts, rows), FULL),
            shape_of(keyval.shape, FULL),
        ]
        + [vector_shape] * 5
        + [shape_of((1, expand_bias.shape[0]), FULL)],
        0.1,
    )(*terms)
    grad_gain, grad_shift, grad_gain_two, grad_shift_two, grad_contract_bias = (
        v.reshape(rows) for v in vector_sums
    )
    return (
        out, grad_tokens, grad_gain, grad_shift, grad_router.T, grad_query_map, grad_keyval,
        grad_output, grad_gain_two, grad_shift_two, grad_expand, grad_spread.reshape(-1),
        grad_contract, grad_contract_bias
    )


def solution(mesh):
    both = ("dp", "seq")
    rows, vector = P(both, None), P(both)
    return jax.shard_map(
        per_device,
        mesh=mesh,
        in_specs=(
            rows, rows, P("dp", None), rows, vector, vector, rows, rows, rows, rows, vector, vector,
            rows, vector, rows, vector
        ),
        out_specs=(
            rows, rows, vector, vector, rows, rows, rows, rows, vector, vector, rows, vector, rows,
            vector
        ),
        check_vma=False,
    )
```

```python
import functools

import jax
import jax.numpy as jnp
from jax import lax
from jax.experimental import pallas as pl
from jax.experimental.pallas import tpu as pltpu
from jax.sharding import PartitionSpec as P

LOW = jnp.bfloat16
FULL = jnp.float32
FAR = 1e30
EPS = 1e-05
DOC_LANE = 64
LSE_LANE = 96
SUM_LANE = 64
MAX_LANE = 67
BIAS_LANE = 64
SEQ_SLOT, PLANE_SLOT, CORE_SLOT = range(3)
LANES = 128
MEGA = 1 << 20
FORWARD_COST = 0.1
QUERY_COST = 0.05
BACKWARD_COST = 3.0
FEED_COST = 8.0
LIMITS = {
    "pack": 4, "first": 4, "unit": 6, "hidden": 6, "vectors": 2, "queries": 6, "attention_forward": 8,
    "attention_backward": 8, "query_gradient": 8, "key_gradient": 12, "token_gradient": 12, "merge": 2, "join": 2, "spread": 2,
    "cut": 3, "fold": 4, "finish": 2, "feed_up": 8,
    "feed_down": 6, "feed_down_last": 17,
}


def to_low(matrix):
    return matrix.astype(LOW)


def dot_plain(left, right):
    return lax.dot_general(left, right, (((1,), (0,)), ((), ())), preferred_element_type=FULL)


def dot_last(left, right):
    return lax.dot_general(left, right, (((1,), (1,)), ((), ())), preferred_element_type=FULL)


def dot_first(left, right):
    return lax.dot_general(left, right, (((0,), (0,)), ((), ())), preferred_element_type=FULL)


class Group:
    def __init__(self, axis, shift, size, slot):
        self.axis, self.shift, self.size, self.slot = axis, shift, size, slot
        self.ids = None

    def index(self):
        return (lax.axis_index(self.axis) >> self.shift) & (self.size - 1)

    def exchange(self, block, mask):
        step = mask << self.shift
        pairs = [(i, i ^ step) for i in range(lax.axis_size(self.axis))]
        return lax.ppermute(block, self.axis, pairs)


def by_place(blocks, index):
    blocks = list(blocks)
    for bit in range(len(blocks).bit_length() - 1):
        swap = (index >> bit) & 1 == 1
        blocks = [jnp.where(swap, blocks[i ^ (1 << bit)], blocks[i]) for i in range(len(blocks))]
    return blocks


def merge_kernel(ids_ref, *refs, count, slot):
    out_ref = refs[count]
    rows = refs[0].shape[1]
    for mask in range(count):
        start = pl.multiple_of((ids_ref[slot] ^ mask) * rows, rows)
        out_ref[:, pl.ds(start, rows), :] = refs[mask][...]


def merge(blocks, group):
    lead, rows, columns = blocks[0].shape
    if rows % 16:
        return jnp.concatenate(by_place(blocks, group.index()), axis=1)
    return call(
        functools.partial(merge_kernel, count=len(blocks), slot=group.slot),
        "merge",
        shape_of((lead, rows * len(blocks), columns), blocks[0].dtype),
        0.1,
        scalars=1,
    )(group.ids, *blocks)


def columns_of(columns, width):
    return [slice(i, min(i + width, columns)) for i in range(0, columns, width)]


def cut_kernel(ids_ref, *refs, sizes, count, slot):
    outs = refs[len(refs) - count :]
    refs = list(refs[: len(refs) - count])
    sets = [[refs.pop(0) for _ in range(size)] for size in sizes]
    width = outs[0].shape[1]
    for mask in range(count):
        row = column = 0
        for terms in sets:
            lead, total, columns = terms[0].shape
            rows = total // count
            start = pl.multiple_of((ids_ref[slot] ^ mask) * rows, rows)
            for at in range(lead):
                for piece in columns_of(columns, width):
                    value = sum(term[at, pl.ds(start, rows), piece].astype(FULL) for term in terms)
                    end = column + value.shape[1]
                    outs[mask][row : row + rows, column:end] = to_low(value)
                    column = end % width
                    row += 0 if column else rows
        if column:
            rest = outs[mask].shape[0] - row
            outs[mask][row:, column:] = jnp.zeros((rest, width - column), LOW)


def cut(sets, group, width):
    count = group.size
    sets = [[t.reshape((-1,) + t.shape[-2:]) for t in terms] for terms in sets]
    rows = [terms[0].shape[1] // count for terms in sets]
    total = sum(t[0].shape[0] * r * t[0].shape[2] for t, r in zip(sets, rows))
    total = -(-total // (width * rows[-1])) * rows[-1]
    if any(r % 16 for r in rows):
        index = group.index()
        results = []
        for mask in range(count):
            bands, band = [], []
            for terms, r in zip(sets, rows):
                value = sum(t.astype(FULL) for t in terms)
                value = lax.dynamic_slice_in_dim(value, (index ^ mask) * r, r, 1)
                for at in range(value.shape[0]):
                    for piece in columns_of(value.shape[2], width):
                        band.append(value[at, :, piece])
                        if sum(b.shape[1] for b in band) == width:
                            bands.append(jnp.concatenate(band, axis=1))
                            band = []
            if band:
                band = jnp.concatenate(band, axis=1)
                bands.append(jnp.pad(band, ((0, 0), (0, width - band.shape[1]))))
            results.append(to_low(jnp.concatenate(bands, axis=0)))
        return results
    return call(
        functools.partial(
            cut_kernel, sizes=[len(t) for t in sets], count=count, slot=group.slot
        ),
        "cut",
        [shape_of((total, width), LOW)] * count,
        0.1,
        scalars=1,
    )(group.ids, *[t for terms in sets for t in terms])


def together(*values):
    return lax.optimization_barrier(values)


class Move:
    def __init__(self, group, blocks, masks=None):
        self.group = group
        self.masks = list(range(1, group.size)) if masks is None else masks
        self.blocks = blocks if isinstance(blocks, dict) else {m: blocks for m in self.masks}

    def begin(self):
        self.moved = [self.group.exchange(self.blocks[m], m) for m in self.masks]
        return self

    def end(self, got):
        self.got = dict(zip(self.masks, got))
        self.moved = None


def phase(moves, work=lambda: (), held=()):
    for move in moves:
        if getattr(move, "moved", None) is None:
            move.begin()
    done = work()
    ended = list(together(*[x for m in moves for x in m.moved], *done, *held))
    for move in moves:
        move.end([ended.pop(0) for _ in move.masks])
    return ended


def fold_kernel(ids_ref, *refs, plan):
    refs = list(refs)
    folds = [(*step, [refs.pop(0) for _ in step[1]]) for step in plan]
    keeps = [refs.pop(0) for _ in plan]
    for keep_ref, ((slot, shift), lows, half, count, out, place, terms) in zip(keeps, folds):
        bit = (ids_ref[slot] >> shift) & 1
        for pair in range(count):
            mine, other = (
                sum(
                    t[pl.ds(low + (2 * pair + b) * half, half)].astype(FULL)
                    for t, low in zip(terms, lows)
                )
                for b in (bit, 1 - bit)
            )
            keep_ref[pair * half : (pair + 1) * half] = mine
            refs[out][place + pair * half : place + (pair + 1) * half] = to_low(other)


class Fold:
    def __init__(self, terms, lead, rows, groups, upward=False):
        self.terms, self.lead, self.rows = terms, lead, rows
        self.left = [(g, b) for g in groups for b in reversed(range(g.size.bit_length() - 1))]
        over = [x for x in self.left if x[0].axis == "dp"]
        self.stages = over[::-1] if upward else over
        self.stages += [x for x in self.left if x[0].axis == "seq"][::-1]
        self.move = None

    def part(self):
        ahead = 1 << self.left.index(self.stages[0])
        return (self.rows << len(self.left)) // (2 * ahead), self.lead * ahead


def fold(folds, unit):
    folds = [f for f in folds if f.stages]
    if not folds:
        return []
    ways, filled, plan, operands, keeps = [], [], [], [], []
    for f in folds:
        if f.stages[0] not in ways:
            ways.append(f.stages[0])
            filled.append(0)
        group, bit = f.stages[0]
        half, count = f.part()
        at = ways.index(f.stages[0])
        columns = f.terms[0][0].shape[-1]
        lows = [low // unit for _, low in f.terms]
        f.start = filled[at]
        plan.append(((group.slot, bit), lows, half // unit, count, at, f.start // unit))
        operands += [a.reshape(-1, unit, columns) for a, _ in f.terms]
        keeps.append(shape_of((half * count // unit, unit, columns), FULL))
        filled[at] += half * count
    sends = [shape_of((rows // unit, unit, columns), LOW) for rows in filled]
    results = call(
        functools.partial(fold_kernel, plan=plan), "fold", keeps + sends, 0.1, scalars=1
    )(ways[0][0].ids, *operands)
    moves = [
        Move(group, sent, [1 << bit]) for (group, bit), sent in zip(ways, results[len(folds) :])
    ]
    for f, keep in zip(folds, results):
        f.keep, f.move = keep, moves[ways.index(f.stages[0])]
        f.left.remove(f.stages.pop(0))
    return moves


def folded(folds):
    for f in folds:
        if f.move is not None:
            [got] = f.move.got.values()
            f.terms = [(f.keep, 0), (got, f.start)]
            f.move = None


def lane_ids(shape):
    return lax.broadcasted_iota(jnp.int32, shape, len(shape) - 1)


def row_positions(offset, rows):
    return offset + lax.broadcasted_iota(jnp.int32, (rows, 1), 0)


def in_document(bounds_ref, positions):
    return (positions >= bounds_ref[0:1, :]) & (positions < bounds_ref[1:2, :])


def put_parts(base, lanes, lane, rows, count):
    for step in range(count):
        part = to_low(rows).astype(FULL)
        base = jnp.where(lanes == lane + step, part, base)
        rows = rows - part
    return base


def lane_sum(matrix, parts=2):
    rest = sum(matrix[:, i : i + LANES] for i in range(0, matrix.shape[1], LANES))
    ones = jnp.ones((LANES, LANES), LOW)
    total = None
    for _ in range(parts):
        part = to_low(rest)
        rest = rest - part.astype(FULL)
        term = dot_plain(part, ones)
        total = term if total is None else total + term
    return total


def over(rows, width):
    return jnp.concatenate([rows] * (width // LANES), axis=1)


def normalize(matrix):
    width = matrix.shape[1]
    center = matrix - over(lane_sum(matrix, 3) * (1.0 / width), width)
    factor = lax.rsqrt(lane_sum(center * center) * (1.0 / width) + EPS)
    return center * over(factor, width), factor


def norm_backward(grad, unit, factor, gain):
    width = grad.shape[1]
    scaled = grad * gain
    mean = over(lane_sum(scaled) * (1.0 / width), width)
    along = over(lane_sum(scaled * unit) * (1.0 / width), width)
    return over(factor, width) * (scaled - mean - unit * along)


def choose(wide, route, head):
    shift = (LANES // head).bit_length() - 1
    tile = lax.shift_right_logical(route, shift)
    picked = wide[:, :LANES]
    for index in range(1, wide.shape[1] // LANES):
        picked = jnp.where(tile == index, wide[:, index * LANES : (index + 1) * LANES], picked)
    turned = pltpu.roll(picked, head, 1)
    lanes = lane_ids((1, LANES))
    mine = (lanes // head) == (route & ((1 << shift) - 1))
    return jnp.where(mine, picked, turned)


def place(doubled, routes, head, width):
    lanes = lane_ids((1, LANES))
    per_tile = LANES // head
    tiles = []
    for index in range(width // LANES):
        expert = lanes // head + index * per_tile
        tile = jnp.zeros_like(doubled[0])
        for rows, route in zip(doubled, routes):
            tile = jnp.where(route == expert, rows, tile)
        tiles.append(tile)
    return jnp.concatenate(tiles, axis=1)


def doubled_head(rows, head):
    lanes = lane_ids((1, LANES))
    return jnp.where(lanes < head, rows, pltpu.roll(rows, head, 1))


def key_rows_of(kv, hot, head):
    lanes = lane_ids((1, LANES))
    kv = kv.astype(FULL)
    marks = jnp.where((lanes >= LSE_LANE) & (lanes < LSE_LANE + 3), 1.0, 0.0)
    keys = jnp.where(lanes < head, kv, jnp.where(hot, 1.0, marks))
    ones = jnp.where((lanes >= SUM_LANE) & (lanes < SUM_LANE + 3), 1.0, 0.0)
    values = jnp.where(lanes < head, pltpu.roll(kv, head, 1), ones)
    return to_low(keys), to_low(values)


def as_column(row):
    rows = row.shape[1]
    lanes = lax.broadcasted_iota(jnp.int32, (rows, rows), 1)
    here = lax.broadcasted_iota(jnp.int32, (rows, rows), 0)
    return jnp.sum(jnp.where(lanes == here, row, 0.0), axis=1, keepdims=True)


def as_row(column):
    rows = column.shape[0]
    lanes = lax.broadcasted_iota(jnp.int32, (rows, rows), 1)
    here = lax.broadcasted_iota(jnp.int32, (rows, rows), 0)
    return jnp.sum(jnp.where(lanes == here, column, 0.0), axis=0, keepdims=True)


def fetch(refs, held, semaphores):
    copies = [
        pltpu.make_async_copy(ref, into, semaphores.at[i])
        for i, (ref, into) in enumerate(zip(refs, held))
    ]
    for copy in copies:
        copy.start()
    for copy in copies:
        copy.wait()


def pack_kernel(*refs, count):
    small_ref, large_ref = refs[count : count + 2]
    held = refs[count + 2 : -1]
    fetch(refs[:count], held, refs[-1])
    (
        query_ref, keyval_ref, router_ref, gain_ref, shift_ref, gain_two_ref, shift_two_ref,
        contract_bias_ref, expand_bias_ref, output_ref, expand_ref, contract_ref
    ) = held
    rows, width = query_ref.shape
    experts = router_ref.shape[0]
    keyval_width = keyval_ref.shape[1]
    small_ref[:, :width] = to_low(query_ref[...])
    small_ref[:, width : width + keyval_width] = to_low(keyval_ref[...])
    lanes = lane_ids((1, LANES))
    turned = router_ref[...]
    side = jnp.zeros((rows, LANES), FULL)
    for expert in range(experts):
        side = jnp.where(lanes == expert, as_column(turned[expert : expert + 1]), side)
    vectors = [gain_ref, shift_ref, gain_two_ref, shift_two_ref, contract_bias_ref]
    for index, ref in enumerate(vectors):
        side = jnp.where(lanes == experts + index, as_column(ref[...]), side)
    extra = expand_bias_ref.shape[1]
    bias = jnp.pad(expand_bias_ref[...], ((0, 0), (BIAS_LANE, LANES - BIAS_LANE - extra)))
    first = lax.broadcasted_iota(jnp.int32, (rows, 1), 0) == 0
    side = side + jnp.where(first, bias, 0.0)
    small_ref[:, width + keyval_width :] = to_low(side)
    large = [output_ref[...]]
    large += [
        expand_ref[:, c * width : (c + 1) * width] for c in range(expand_ref.shape[1] // width)
    ]
    large_ref[...] = to_low(jnp.concatenate(large + [contract_ref[...]], axis=0))


def unit_kernel(tokens_ref, unit_ref, factor_ref):
    unit_ref[...], factor_ref[...] = normalize(tokens_ref[...].astype(FULL))


def first_kernel(ids_ref, routes_hbm, lengths_hbm, columns_ref, bounds_ref, ids_out, *held):
    for slot in range(ids_ref.shape[0]):
        ids_out[slot] = ids_ref[slot]
    routes_ref, lengths_ref, semaphores = held
    fetch((routes_hbm, lengths_hbm), (routes_ref, lengths_ref), semaphores)
    routes = routes_ref[...].astype(FULL)
    choices = routes.shape[0]
    routes = jnp.concatenate([routes, jnp.zeros((8 - routes.shape[0], routes.shape[1]), FULL)], axis=0)
    turned = routes.T
    for j in range(choices):
        wide = jnp.broadcast_to(turned[:, j : j + 1], columns_ref.shape[1:])
        columns_ref[j] = wide.astype(jnp.int32)
    count = lengths_ref.shape[1]
    lanes = lane_ids((1, LANES))
    rest = jnp.zeros((1, LANES - DOC_LANE - count), jnp.int32)
    lengths = jnp.concatenate(
        [jnp.zeros((1, DOC_LANE), jnp.int32), lengths_ref[...], rest], axis=1
    )
    ends = lengths
    step = 1
    while step < count:
        ends = ends + jnp.where(lanes >= DOC_LANE + step, pltpu.roll(ends, step, 1), 0)
        step *= 2
    here = (lanes >= DOC_LANE) & (lanes < DOC_LANE + count)
    starts = jnp.where(here, ends - lengths, 1 << 30)
    ends = jnp.where(here, ends, 0)
    index = lax.broadcasted_iota(jnp.int32, (8, 1), 0)
    bounds_ref[...] = jnp.where(index == 0, starts, jnp.where(index == 1, ends, 0))


def vectors_kernel(small_ref, vectors_ref, bias_ref, *, experts, rows):
    misc = small_ref[:, small_ref.shape[1] - LANES :].astype(FULL)
    turned = misc.T
    vectors_ref[...] = turned[experts + 2 : experts + 10]
    count = misc.shape[0] // rows
    each = bias_ref.shape[1] // count
    per_tile = LANES // each
    firsts = misc.reshape(count, rows, LANES)[:, 0, :].reshape(count // per_tile, per_tile, LANES)
    lanes = lane_ids((1, LANES))
    tiles = jnp.zeros((count // per_tile, LANES), FULL)
    for k in range(per_tile):
        moved = pltpu.roll(firsts[:, k, :], (k * each - BIAS_LANE) % LANES, 1)
        tiles = jnp.where(lanes // each == k, moved, tiles)
    for index in range(count // per_tile):
        bias_ref[:, index * LANES : (index + 1) * LANES] = tiles[index : index + 1]


def bias_rows(bias, count, rows):
    each = bias.shape[1] // count
    per_tile = LANES // each
    tiles = jnp.concatenate(
        [bias[:, i : i + LANES] for i in range(0, bias.shape[1], LANES)], axis=0
    )
    lanes = lane_ids((1, LANES))
    mine = (lanes >= BIAS_LANE) & (lanes < BIAS_LANE + each)
    parts = [
        jnp.where(mine, pltpu.roll(tiles, (BIAS_LANE - k * each) % LANES, 1), 0.0)
        for k in range(per_tile)
    ]
    firsts = jnp.stack(parts, axis=1).reshape(count, 1, LANES)
    here = lax.broadcasted_iota(jnp.int32, (1, rows, 1), 1) == 0
    return jnp.where(here, firsts, 0.0).reshape(count * rows, LANES)


def stack_kernel(*refs):
    for at, ref in enumerate(refs[:-1]):
        refs[-1][at] = ref[0]


def join_kernel(first_ref, second_ref, out_ref):
    count = first_ref.shape[0]
    out_ref[:count] = first_ref[...]
    out_ref[count:] = second_ref[...]


def spread_kernel(ids_ref, *refs, masks, slots, rows):
    pair_ref, half_ref = refs[len(masks) :]
    more = refs[0].shape[1] - slots * rows
    for ref, masks_of in zip(refs, masks):
        for at, mask in enumerate(masks_of):
            place = ids_ref[SEQ_SLOT] ^ mask
            start = pl.multiple_of(place * rows, rows)
            for slot in range(slots):
                here = slice(slot * rows, (slot + 1) * rows)
                pair_ref[slot, pl.ds(start, rows), :] = ref[at, here, :]
            half_ref[pl.ds(pl.multiple_of(place * more, more), more), :] = ref[at, slots * rows :, :]


def hidden_kernel(
    ids_ref, unit_ref, mine_ref, other_ref, routes_ref, hidden_ref, kv_ref, gates_ref, small_ref, *, experts
):
    small = merged(mine_ref[...], other_ref[...], ids_ref[CORE_SLOT])
    small_ref[...] = small
    side = small[:, small.shape[1] - 2 * LANES :]
    vectors = side[:, LANES:].astype(FULL).T
    hidden = to_low(
        unit_ref[...] * vectors[experts : experts + 1] + vectors[experts + 1 : experts + 2]
    )
    hidden_ref[...] = hidden
    both = dot_plain(hidden, side)
    kv_ref[...] = to_low(both[:, :LANES])
    logits = both[:, LANES:]
    lanes = lane_ids((1, LANES))
    picked = [lane_sum(jnp.where(lanes == routes_ref[j], logits, 0.0), 3) for j in range(2)]
    top = jnp.maximum(picked[0], picked[1])
    raised = [jnp.exp(p - top) for p in picked]
    total = raised[0] + raised[1]
    for j in range(2):
        gates_ref[j] = raised[j] / total


def query_kernel(ids_ref, hidden_ref, small_ref, routes_ref, bounds_ref, query_ref, *, head):
    rows, width = hidden_ref.shape
    wide = dot_plain(hidden_ref[...], small_ref[:, :width])
    lanes = lane_ids((1, LANES))
    hot = in_document(bounds_ref, row_positions(ids_ref[SEQ_SLOT] * rows, rows))
    documents = (bounds_ref[1:2, :] > 0) & (lanes >= head)
    marks = jnp.where(documents & jnp.logical_not(hot), -FAR, 0.0)
    for j in range(2):
        rows_of = choose(wide, routes_ref[j], head) * head**-0.5
        query_ref[j * rows : (j + 1) * rows, :] = to_low(jnp.where(lanes < head, rows_of, marks))


def forward_kernel(ids_ref, query_ref, bounds_ref, *rest, head, first, last, masks, part):
    count = len(masks)
    kv_refs, rest = rest[:count], list(rest[count:])
    state_ref = None if first else rest.pop(0)
    lanes = lane_ids((1, LANES))
    blocks = []
    for index, ref in enumerate(kv_refs):
        start = (ids_ref[SEQ_SLOT] ^ masks[index]) * ref.shape[0]
        hot = in_document(bounds_ref, row_positions(start, ref.shape[0]))
        blocks.append(key_rows_of(ref[...], hot, head))
    for start in range(0, query_ref.shape[0], part):
        rows = slice(start, start + part)
        query = query_ref[rows, :]
        state = None if first else state_ref[rows, :]
        for keys, values in blocks:
            scores = dot_last(query, keys)
            top = jnp.max(scores, axis=1, keepdims=True)
            if state is None:
                new = top
                state = dot_plain(to_low(jnp.exp(scores - new)), values)
            else:
                old = state[:, MAX_LANE : MAX_LANE + 1]
                new = jnp.maximum(old, top)
                weights = to_low(jnp.exp(scores - new))
                state = state * jnp.exp(old - new) + dot_plain(weights, values)
            state = jnp.where(lanes == MAX_LANE, new, state)
        if last:
            attn_ref, wide_ref = rest
            total = state[:, SUM_LANE : SUM_LANE + 1]
            attn_ref[rows, :] = jnp.where(lanes < head, state / total, 0.0)
            log_total = state[:, MAX_LANE : MAX_LANE + 1] + jnp.log(total)
            wide_ref[rows, :] = to_low(
                put_parts(query.astype(FULL), lanes, LSE_LANE, -log_total, 3)
            )
        else:
            rest[0][rows, :] = state


def merged(mine, other, bit):
    low = bit == 0
    both = jnp.stack([jnp.where(low, mine, other), jnp.where(low, other, mine)], axis=1)
    return both.reshape(-1, mine.shape[-1])


def parted(whole, bit, shape):
    both = whole.reshape(shape[0], 2, shape[1], shape[2])
    low = bit == 0
    first, second = both[:, 0], both[:, 1]
    return jnp.where(low, first, second), jnp.where(low, second, first)


def weights(refs, bit):
    mine, other = refs[0][...], refs[1][...]
    shape = mine.shape[-3:]
    return merged(mine.reshape(shape), other.reshape(shape), bit)


def weights(mine, other, ids_ref):
    return merged(mine, other, ids_ref[CORE_SLOT])


def unit_of(ids_ref, mask, inner, size):
    unit = ids_ref[PLANE_SLOT] ^ mask
    shift = (inner // size).bit_length() - 1
    everywhere = pl.ds(pl.multiple_of(unit * size, size), size)
    if not shift:
        return unit, slice(0, size), everywhere
    start = pl.multiple_of((unit & ((1 << shift) - 1)) * size, size)
    return lax.shift_right_logical(unit, shift), pl.ds(start, size), everywhere


def up_kernel(
    ids_ref, tokens_ref, cotangent_ref, attn_ref, gates_ref, routes_ref, vectors_ref, bias_ref,
    pair_mine, pair_other, mixed_ref, hidden_ref, active_ref, steep_ref, keep_ref, send_ref, *, head
):
    width = tokens_ref.shape[1]
    wide = [doubled_head(attn_ref[j], head) * gates_ref[j] for j in range(2)]
    mixed = to_low(place(wide, [routes_ref[j] for j in range(2)], head, width))
    mixed_ref[...] = mixed
    output_weight = weights(pair_mine[0], pair_other[0], ids_ref)
    middle = tokens_ref[...].astype(FULL) + dot_plain(mixed, output_weight)
    unit, _ = normalize(middle)
    hidden = to_low(unit * vectors_ref[0:1, :] + vectors_ref[1:2, :])
    hidden_ref[...] = hidden
    slope = 0.7978845608028654
    cube = 0.044715
    chunks, _, inner_width = active_ref.shape
    part = min(256, tokens_ref.shape[0])
    groups = keep_ref.shape[0] // chunks
    for chunk in range(chunks):
        expand = weights(pair_mine[chunk + 1], pair_other[chunk + 1], ids_ref)
        columns = slice(chunk * inner_width, (chunk + 1) * inner_width)
        for start in range(0, hidden.shape[0], part):
            here = slice(start, start + part)
            inner = dot_plain(hidden[here], expand) + bias_ref[:, columns]
            square = inner * inner
            half = 0.5 + 0.5 * jnp.tanh(inner * (slope + slope * cube * square))
            whole = inner * half
            active_ref[chunk, here] = to_low(whole)
            steep = half + whole * (1.0 - half) * (2.0 * slope + 6.0 * slope * cube * square)
            steep_ref[chunk, here] = to_low(steep)
        shape = (groups,) + keep_ref.shape[1:]
        grad = to_low(dot_first(active_ref[chunk], cotangent_ref[...]))
        here = slice(chunk * groups, (chunk + 1) * groups)
        keep_ref[here], send_ref[here] = parted(grad, ids_ref[CORE_SLOT], shape)


def down_kernel(
    ids_ref, hidden_ref, cotangent_ref, active_ref, steep_ref, pair_mine, pair_other, contract_mine,
    contract_other, *rest, head, masks, last
):
    rest = list(rest)
    take = lambda n: [rest.pop(0) for _ in range(n)]
    _, _, inner = active_ref.shape
    size = 2 * contract_mine.shape[1]
    if last:
        out_before, grad_before, keep_before, send_before, bias_before = take(5)
        tokens_ref, mixed_ref, attn_ref, gates_ref, routes_ref, vectors_ref = take(6)
        out_ref, branch_ref, grad_attn_ref, grad_logits_ref, grad_rows_ref = take(5)
        keep_ref, send_ref, grad_bias_ref = take(3)
        out, grad_hidden = out_before[...], grad_before[...]
        chunk, columns, everywhere = unit_of(ids_ref, 0, inner, size)
        keep_ref[chunk, :, :, columns] = keep_before[...]
        send_ref[chunk, :, :, columns] = send_before[...]
        grad_bias_ref[:, everywhere] = bias_before[...]
    else:
        out_held, grad_held, keep_ref, send_ref, grad_bias_ref = take(5)
        out = grad_hidden = None
    add = lambda total, term: term if total is None else total + term
    for at, mask in enumerate(masks):
        chunk, columns, everywhere = unit_of(ids_ref, mask, inner, size)
        expand = weights(
            pair_mine[chunk + 1, :, :, columns], pair_other[chunk + 1, :, :, columns], ids_ref
        )
        contract = weights(contract_mine[at : at + 1], contract_other[at : at + 1], ids_ref)
        out = add(out, dot_plain(active_ref[chunk, :, columns], contract))
        grad_active = dot_last(cotangent_ref[...], contract)
        grad_inner = to_low(steep_ref[chunk, :, columns].astype(FULL) * grad_active)
        grad_bias = jnp.sum(grad_inner.astype(FULL), axis=0, keepdims=True)
        grad_hidden = add(grad_hidden, dot_last(grad_inner, expand))
        grad = to_low(dot_first(hidden_ref[...], grad_inner))
        keep, send = parted(grad, ids_ref[CORE_SLOT], pair_mine.shape[1:3] + (size,))
        if last:
            grad_bias_ref[:, everywhere] = grad_bias
            keep_ref[chunk, :, :, columns] = keep
            send_ref[chunk, :, :, columns] = send
        else:
            grad_bias_ref[...] = grad_bias
            keep_ref[...] = keep
            send_ref[...] = send
    if not last:
        out_held[...] = out
        grad_held[...] = grad_hidden
        return
    lanes = lane_ids((1, LANES))
    gain, contract_bias = vectors_ref[0:1, :], vectors_ref[2:3, :]
    output_weight = weights(pair_mine[0], pair_other[0], ids_ref)
    mixed = mixed_ref[...]
    middle = tokens_ref[...].astype(FULL) + dot_plain(mixed, output_weight)
    out_ref[...] = to_low(out + middle + contract_bias)
    unit, factor = normalize(middle)
    cotangent = cotangent_ref[...].astype(FULL)
    branch = to_low(cotangent + norm_backward(grad_hidden, unit, factor, gain))
    branch_ref[...] = branch
    grad_rows_ref[...] = jnp.zeros_like(grad_rows_ref)
    grad_rows_ref[0:1, :] = jnp.sum(grad_hidden * unit, axis=0, keepdims=True)
    grad_rows_ref[1:2, :] = jnp.sum(grad_hidden, axis=0, keepdims=True)
    grad_rows_ref[2:3, :] = jnp.sum(cotangent, axis=0, keepdims=True)
    grad = to_low(dot_first(mixed, branch))
    end = keep_ref.shape[0] - 1
    keep_ref[end], send_ref[end] = parted(grad, ids_ref[CORE_SLOT], keep_ref.shape[1:])
    grad_mixed = dot_last(branch, output_weight)
    scaled = []
    for j in range(2):
        weighted = jnp.where(lanes < head, choose(grad_mixed, routes_ref[j], head), 0.0)
        scaled.append(gates_ref[j] * lane_sum(weighted * attn_ref[j]))
        grad_attn = weighted * gates_ref[j]
        grad_attn_ref[j] = to_low(put_parts(grad_attn, lanes, SUM_LANE, -scaled[j], 3))
    mean = scaled[0] + scaled[1]
    grad_logits = jnp.zeros(gates_ref.shape[1:], FULL)
    for j in range(2):
        grad_picked = scaled[j] - gates_ref[j] * mean
        grad_logits = jnp.where(lanes == routes_ref[j], grad_picked, grad_logits)
    grad_logits_ref[...] = to_low(grad_logits)


def backward_kernel(ids_ref, query_ref, grad_ref, bounds_ref, *rest, head, first, masks, part):
    count = len(masks)
    kv_refs, rest = rest[:count], list(rest[count:])
    before_ref = None if first else rest.pop(0)
    grad_query_ref, grad_kv_refs = rest[0], rest[1:]
    lanes = lane_ids((1, LANES))
    key_count = kv_refs[0].shape[0]
    blocks = []
    for index, ref in enumerate(kv_refs):
        start = (ids_ref[SEQ_SLOT] ^ masks[index]) * key_count
        hot = in_document(bounds_ref, row_positions(start, key_count))
        keys, values = key_rows_of(ref[...], hot, head)
        blocks.append((keys, values, to_low(keys.astype(FULL).T[:head])))
    totals = [None] * count
    for start in range(0, query_ref.shape[0], part):
        rows = slice(start, start + part)
        query = query_ref[rows, :]
        grad = grad_ref[rows, :]
        only_query = to_low(jnp.where(lanes < head, query.astype(FULL), 0.0))
        turned = pltpu.roll(grad.astype(FULL), head, 1)
        only_grad = to_low(jnp.where(lanes < head, 0.0, turned))
        grad_query = None if first else before_ref[:, rows]
        for index, (keys, values, turned_keys) in enumerate(blocks):
            probs = jnp.exp(dot_last(keys, query))
            grad_scores = to_low(probs * dot_last(values, grad))
            update = dot_plain(grad_scores, only_query) + dot_plain(to_low(probs), only_grad)
            totals[index] = update if totals[index] is None else totals[index] + update
            step = dot_plain(turned_keys, grad_scores)
            grad_query = step if grad_query is None else grad_query + step
        grad_query_ref[:, rows] = grad_query
    for index in range(count):
        grad_kv_refs[index][...] = to_low(totals[index])


def placed_kernel(
    ids_ref, grad_query_ref, hidden_ref, routes_ref, grad_logits_ref, small_ref, grad_hidden_ref,
    keep_ref, send_ref, grad_router_ref, *, head
):
    count, width = hidden_ref.shape
    turned = (grad_query_ref[...] * head**-0.5).T
    rows = []
    for j in range(2):
        half = to_low(turned[j * count : (j + 1) * count]).astype(FULL)
        rows.append(jnp.concatenate([half] * (LANES // head), axis=1))
    placed = to_low(place(rows, [routes_ref[j] for j in range(2)], head, width))
    hidden = hidden_ref[...]
    grad_logits = grad_logits_ref[...]
    keep, send = parted(to_low(dot_first(hidden, placed)), ids_ref[CORE_SLOT], keep_ref.shape)
    keep_ref[...] = keep
    send_ref[...] = send
    grad_router_ref[...] = dot_first(hidden, grad_logits)
    grad_hidden_ref[...] = dot_last(placed, small_ref[:, :width]) + dot_last(
        grad_logits, small_ref[:, small_ref.shape[1] - LANES :]
    )


def side_kernel(
    ids_ref, hidden_ref, grad_before_ref, unit_ref, small_ref, rows_ref, bias_ref,
    grad_router_ref, own_ref, *rest, experts, others, rows
):
    other_refs = rest[:others]
    grad_hidden_ref, keep_ref, send_ref = rest[others:]
    side = small_ref[:, small_ref.shape[1] - 2 * LANES :]
    grad_kv = own_ref[...].astype(FULL)
    for ref in other_refs:
        grad_kv += ref[...].astype(FULL)
    grad_kv = to_low(grad_kv)
    grad_keyval = dot_first(hidden_ref[...], grad_kv)
    grad_hidden = grad_before_ref[...] + dot_last(grad_kv, side[:, :LANES])
    grad_hidden_ref[...] = grad_hidden
    gain_grad = jnp.sum(grad_hidden * unit_ref[...], axis=0, keepdims=True)
    shift_grad = jnp.sum(grad_hidden, axis=0, keepdims=True)
    width = hidden_ref.shape[1]
    index = lax.broadcasted_iota(jnp.int32, (8, 1), 0)
    later = pltpu.roll(rows_ref[...], 2, 0)
    vectors = jnp.where(index == 0, gain_grad, jnp.where(index == 1, shift_grad, later))
    ahead = jnp.zeros((experts, width), FULL)
    behind = jnp.zeros((LANES - experts - 8, width), FULL)
    columns = jnp.concatenate([ahead, vectors, behind], axis=0).T
    spread = bias_rows(bias_ref[...], width // rows, rows)
    grad_side = jnp.concatenate([grad_keyval, columns + grad_router_ref[...] + spread], axis=1)
    keep_ref[...], send_ref[...] = parted(to_low(grad_side), ids_ref[CORE_SLOT], keep_ref.shape)


def tokens_kernel(
    grad_hidden_ref, unit_ref, factor_ref, grad_middle_ref, small_ref, grad_tokens_ref, *, experts
):
    misc = small_ref[:, small_ref.shape[1] - LANES :]
    gain = misc.astype(FULL).T[experts : experts + 1]
    grad = norm_backward(grad_hidden_ref[...], unit_ref[...], factor_ref[...], gain)
    grad_tokens_ref[...] = to_low(grad_middle_ref[...].astype(FULL) + grad)


def finish_kernel(*refs, terms, slots, plan):
    sums = []
    for at, (lows, count) in enumerate(plan):
        pair = refs[2 * at : 2 * at + 2]
        sums.append(sum(t[low : low + count, :].astype(FULL) for t, low in zip(pair, lows)))
    rest = sums.pop()
    total = jnp.concatenate(sums, axis=0)
    last = sum(ref[...].astype(FULL) for ref in refs[2 * len(plan) : terms])
    expand_ref, output_ref, contract_ref, query_ref, router_ref, keyval_ref = refs[terms : terms + 6]
    *vector_refs, bias_ref = refs[terms + 6 :]
    rows, width = output_ref.shape
    for slot in range(slots):
        expand_ref[:, slot * width : (slot + 1) * width] = total[slot * rows : (slot + 1) * rows]
    output_ref[...] = total[slots * rows :]
    query_ref[...] = last[:rows]
    side = last[rows:]
    contract_ref[...] = rest
    experts = router_ref.shape[0]
    keyval_ref[...] = side[:, :LANES]
    for expert in range(experts):
        lane = LANES + expert
        router_ref[expert : expert + 1, :] = as_row(side[:, lane : lane + 1])
    for index, ref in enumerate(vector_refs):
        lane = LANES + experts + index
        ref[...] = as_row(side[:, lane : lane + 1])
    start = LANES + BIAS_LANE
    bias_ref[...] = side[0:1, start : start + bias_ref.shape[1]]


def in_hbm(array):
    return pltpu.with_memory_space_constraint(array, pltpu.HBM)


def smem_spec():
    return pl.BlockSpec(memory_space=pltpu.SMEM)


def vmem_spec():
    return pl.BlockSpec(memory_space=pltpu.VMEM)


def shape_of(shape, dtype):
    return jax.ShapeDtypeStruct(tuple(shape), dtype)


def limit_of(name):
    return LIMITS[name] * MEGA


def estimate(cost):
    return pl.CostEstimate(flops=int(cost * 1e9), bytes_accessed=0, transcendentals=0)


def call(kernel, name, outs, cost, scalars=0, more=0):
    def run(*operands):
        return pl.pallas_call(
            kernel,
            in_specs=[smem_spec()] * scalars + [vmem_spec()] * (len(operands) - scalars),
            out_specs=[vmem_spec()] * len(outs) if isinstance(outs, list) else vmem_spec(),
            out_shape=outs,
            compiler_params=pltpu.CompilerParams(vmem_limit_bytes=limit_of(name) + more * MEGA),
            cost_estimate=estimate(cost),
            name=name,
        )(*operands)

    return run


def generations(seq_count):
    masks = range(1, seq_count)
    most = seq_count.bit_length() - 1
    return [[m for m in masks if bin(m).count("1") == n] for n in range(1, most + 1)]


def feed_up(ids, tokens, cotangent, attn, gates, routes, vectors, bias, pairs, plain, head):
    token_count, width = tokens.shape
    chunks = pairs[0].shape[0] - 1
    rows = shape_of((token_count, width), LOW)
    held = shape_of((chunks, token_count, bias.shape[1] // chunks), LOW)
    return call(
        functools.partial(up_kernel, head=head), "feed_up", [rows, rows, held, held]
        + [shape_of(plain, LOW)] * 2, FEED_COST / 2, scalars=1
    )(ids, tokens, cotangent, attn, gates, routes, vectors, bias, *pairs)


def feed_down(ids, hidden, cotangent, active, steep, pairs, contracts, masks, head, end=()):
    token_count, width = hidden.shape
    last = bool(end)
    rows = (token_count, width)
    size = 2 * contracts[0].shape[1]
    if last:
        grads = shape_of(pairs[0].shape, LOW)
        outs = [
            shape_of(rows, LOW),
            shape_of(rows, LOW),
            shape_of((2, token_count, LANES), LOW),
            shape_of((token_count, LANES), LOW),
            shape_of((8, width), FULL),
            grads,
            grads,
            shape_of((1, active.shape[0] * active.shape[2]), FULL),
        ]
    else:
        grads = shape_of(pairs[0].shape[1:3] + (size,), LOW)
        outs = [shape_of(rows, FULL)] * 2 + [grads, grads, shape_of((1, size), FULL)]
    return call(
        functools.partial(down_kernel, head=head, masks=masks, last=last),
        "feed_down_last" if last else "feed_down",
        outs,
        FEED_COST / 2,
        scalars=1,
    )(ids, hidden, cotangent, active, steep, *pairs, *contracts, *end)


def per_device(
    tokens, routes, lengths, cotangent, first_gain, first_shift, router, query_map, keyval,
    output_map, second_gain, second_shift, expand, expand_bias, contract, contract_bias
):
    seq_count, plane_count = lax.axis_size("seq"), lax.axis_size("dp") // 2
    along = Group("seq", 0, seq_count, SEQ_SLOT)
    plane = Group("dp", 1, plane_count, PLANE_SLOT)
    core = Group("dp", 0, 2, CORE_SLOT)
    token_count, width = tokens.shape
    rows = first_gain.shape[0]
    contract_rows = contract.shape[0]
    experts = router.shape[1]
    head = keyval.shape[1] // 2
    inner_width = expand.shape[1]
    chunks = inner_width // width
    slots = 1 + chunks
    my_index = along.index()
    ids = jnp.stack([g.index() for g in (along, plane, core)]).astype(jnp.int32)
    side_width = 2 * LANES
    row_count = 2 * token_count
    part = min(1024, row_count)

    params = [
        query_map, keyval, router.T, first_gain[None], first_shift[None], second_gain[None],
        second_shift[None], contract_bias[None], expand_bias[None], output_map, expand, contract
    ]
    small_mine, large_mine = pl.pallas_call(
        functools.partial(pack_kernel, count=len(params)),
        in_specs=[pl.BlockSpec(memory_space=pltpu.HBM)] * len(params),
        out_specs=[vmem_spec()] * 2,
        out_shape=[
            shape_of((rows, width + side_width), LOW),
            shape_of((slots * rows + contract_rows, width), LOW),
        ],
        scratch_shapes=[pltpu.VMEM(p.shape, p.dtype) for p in params]
        + [pltpu.SemaphoreType.DMA((len(params),))],
        compiler_params=pltpu.CompilerParams(vmem_limit_bytes=limit_of("pack")),
        cost_estimate=estimate(0.1),
        name="pack",
    )(*[in_hbm(p) for p in params])

    def first_work():
        given = [routes.T, lengths]
        return pl.pallas_call(
            first_kernel,
            in_specs=[smem_spec()] + [pl.BlockSpec(memory_space=pltpu.HBM)] * 2,
            out_specs=[vmem_spec()] * 2 + [smem_spec()],
            out_shape=[
                shape_of((2, token_count, LANES), jnp.int32),
                shape_of((8, LANES), jnp.int32),
                shape_of(ids.shape, jnp.int32),
            ],
            scratch_shapes=[pltpu.VMEM(p.shape, p.dtype) for p in given]
            + [pltpu.SemaphoreType.DMA((2,))],
            compiler_params=pltpu.CompilerParams(vmem_limit_bytes=limit_of("first")),
            cost_estimate=estimate(0.1),
            name="first",
        )(ids, *[in_hbm(p) for p in given])


    small_move = Move(along, small_mine[None])
    coming = generations(seq_count)
    bits = [1 << b for b in reversed(range(seq_count.bit_length() - 1))]
    large, large_masks = large_mine[None], [0]
    large_move = Move(along, large, bits[:1])
    route_columns, bounds, ids, large = phase(
        [small_move, large_move], first_work, held=[large]
    )
    for group in (along, plane, core):
        group.ids = ids
    small = merge([small_mine[None]] + [small_move.got[m] for m in range(1, seq_count)], along)
    for bit, later in zip(bits, bits[1:]):
        large_masks = large_masks + [m | bit for m in large_masks]
        large = call(
            join_kernel, "join", shape_of((2 * large.shape[0],) + large.shape[1:], LOW), 0.1
        )(large, large_move.got[bit])
        large, small = together(large, small)
        large_move = Move(along, large, [later])
        if later != bits[-1]:
            phase([large_move])
    small_move = Move(plane, small)
    unit_shapes = [shape_of(tokens.shape, FULL), shape_of((token_count, LANES), FULL)]
    unit, factor = phase(
        [small_move, large_move], lambda: call(unit_kernel, "unit", unit_shapes, 0.1)(tokens)
    )
    large_parts = [large, large_move.got[bits[-1]]]
    large_masks = [large_masks, [m | bits[-1] for m in large_masks]]
    small = merge([small] + [small_move.got[m] for m in range(1, plane_count)], plane)[0]
    small_move = Move(core, small)
    phase([small_move])
    small_shape = (plane_count, seq_count * rows, width + side_width)
    smalls = [small.reshape(small_shape), small_move.got[1].reshape(small_shape)]
    hidden, kv_mine, gates, small = call(
        functools.partial(hidden_kernel, experts=experts),
        "hidden",
        [
            shape_of((token_count, width), LOW),
            shape_of((token_count, LANES), LOW),
            shape_of((2, token_count, LANES), FULL),
            shape_of((width, width + side_width), LOW),
        ],
        0.5,
        scalars=1,
    )(ids, unit, *smalls, route_columns)

    def attend(state, masks, queries, last=False):
        return call(
            functools.partial(
                forward_kernel, head=head, first=not state, last=last, masks=masks, part=part
            ),
            "attention_forward",
            [shape_of((row_count, LANES), t) for t in ((FULL, LOW) if last else (FULL,))],
            FORWARD_COST * len(masks),
            scalars=1,
            more=3 * (len(masks) - 1),
        )(ids, queries, bounds, *[shards[m] for m in masks], *state)

    def keys_of(masks):
        return [Move(along, shards[m & (m - 1)], [m & -m]) for m in masks]

    def come(masks, moves):
        for mask, move in zip(masks, moves):
            shards[mask] = move.got[mask & -mask]

    shards = {0: kv_mine}
    keys = keys_of(coming[0])

    for move in keys:
        move.begin()
    queries = call(
        functools.partial(query_kernel, head=head),
        "queries",
        shape_of((row_count, LANES), LOW),
        QUERY_COST,
        scalars=1,
    )(ids, hidden, small, route_columns, bounds)
    queries, *large_parts = together(queries, *large_parts)
    if rows % 16:
        blocks = {m: x[i] for x, masks in zip(large_parts, large_masks) for i, m in enumerate(masks)}
        lines = jnp.stack(by_place([blocks[m] for m in range(seq_count)], my_index))
        pair = lines[:, : slots * rows].reshape(seq_count, slots, rows, width)
        pair = pair.transpose(1, 0, 2, 3).reshape(slots, seq_count * rows, width)
        half = lines[:, slots * rows :].reshape(1, seq_count * contract_rows, width)
    else:
        pair, half = call(
            functools.partial(spread_kernel, masks=large_masks, slots=slots, rows=rows),
            "spread",
            [
                shape_of((slots, seq_count * rows, width), LOW),
                shape_of((seq_count * contract_rows, width), LOW),
            ],
            0.1,
            scalars=1,
        )(ids, *large_parts)
        half = half[None]
    pair_move = Move(plane, pair).begin()
    state, half = phase(keys, lambda: attend([], [0], queries), held=[half])
    come(coming[0], keys)
    for before, masks in zip(coming, coming[1:]):
        keys = keys_of(masks)
        moves = keys + [pair_move] if masks is coming[-1] else keys
        [state] = phase(moves, lambda: attend([state], before, queries))
        come(masks, keys)
    pair = merge([pair] + [pair_move.got[m] for m in range(1, plane_count)], plane)
    pair = pair.reshape(slots, plane_count, -1, width)
    pair_move = Move(core, pair)
    half_move = Move(plane, half).begin()
    own_core = Move(core, half)
    attn, wide_queries = phase([pair_move, own_core], lambda: attend([state], coming[-1], queries, True))
    attn = attn.reshape(2, token_count, LANES)
    pairs = [pair, pair_move.got[1]]
    vectors, bias = call(
        functools.partial(vectors_kernel, experts=experts, rows=rows),
        "vectors",
        [shape_of((8, width), FULL), shape_of((1, inner_width), FULL)],
        0.1,
    )(small)

    plain = (plane_count, seq_count * contract_rows, width)
    mixed, hidden_two, active, steep, keep_half, send_half = phase(
        [half_move],
        lambda: feed_up(
            ids, tokens, cotangent, attn, gates, route_columns, vectors, bias, pairs, plain, head
        ),
    )
    masks = list(range(1, plane_count))
    rest = call(
        stack_kernel, "join", shape_of((len(masks),) + half.shape[1:], LOW), 0.1
    )(*[half_move.got[m] for m in masks])
    rest_move, half_core = Move(core, rest), Move(core, send_half)
    out_held, grad_held, keep_own, send_own, bias_own = phase(
        [rest_move, half_core],
        lambda: feed_down(
            ids, hidden_two, cotangent, active, steep, pairs, (half, own_core.got[1]), [0], head
        ),
    )
    half_terms = [(keep_half, 0), (half_core.got[1], 0)]
    half_fold = Fold(half_terms, 1, contract_rows, [plane, along])
    (
        out, branch, grad_attn, grad_logits, grad_rows, keep_pair, send_pair, grad_bias
    ) = phase(
        fold([half_fold], rows),
        lambda: feed_down(
            ids, hidden_two, cotangent, active, steep, pairs, (rest, rest_move.got[1]), masks, head,
            (
                out_held, grad_held, keep_own, send_own, bias_own, tokens, mixed, attn, gates,
                route_columns, vectors
            ),
        ),
    )
    folded([half_fold])

    grad_rows_in = grad_attn.reshape(row_count, LANES)
    masks = list(range(seq_count - 1, 0, -1))
    if seq_count > 2:
        masks = [2] + [m for m in masks if m != 2]
    third = max(1, len(masks) // 3)
    groups = [masks[:third], masks[third:], [0]]

    def backward(masks, before):
        return call(
            functools.partial(
                backward_kernel, head=head, first=before is None, masks=masks, part=part
            ),
            "attention_backward",
            [shape_of((head, row_count), FULL)]
            + [shape_of((token_count, LANES), LOW)] * len(masks),
            BACKWARD_COST * len(masks),
            scalars=1,
            more=3 * (len(masks) - 1),
        )(
            ids, wide_queries, grad_rows_in, bounds, *[shards[m] for m in masks],
            *([] if before is None else [before])
        )

    pair_move = Move(core, send_pair)
    first_query, *leaving = phase([pair_move], lambda: backward(groups[0], None))
    part_way = (slots + 1) // 2
    begin = part_way * width
    pair_got = pair_move.got[1]
    pair_folds = [
        Fold([(keep_pair, 0), (pair_got, 0)], part_way, rows, [plane, along]),
        Fold(
            [(keep_pair, begin // 2), (pair_got, begin // 2)], slots - part_way, rows, [plane, along],
            upward=True,
        ),
    ]
    both = [half_fold] + pair_folds
    keys_first = Move(along, dict(zip(groups[0], leaving)), groups[0])
    second_query, *leaving = phase(
        [keys_first] + fold(both, rows), lambda: backward(groups[1], first_query)
    )
    folded(both)
    keys_second = Move(along, dict(zip(groups[1], leaving)), groups[1])

    def work():
        grad_query, own = backward(groups[2], second_query)
        shape = (plane_count, seq_count * rows, width)
        return own, *call(
            functools.partial(placed_kernel, head=head),
            "query_gradient",
            [
                shape_of((token_count, width), FULL),
                shape_of(shape, LOW),
                shape_of(shape, LOW),
                shape_of((width, LANES), FULL),
            ],
            1.0,
            scalars=1,
        )(ids, grad_query, hidden, route_columns, grad_logits, small)

    grad_kv, grad_before, keep_query, send_query, grad_router = phase(
        [keys_second] + fold(pair_folds, rows), work
    )
    folded(pair_folds)
    query_move = Move(core, send_query)
    others = list(keys_first.got.values()) + list(keys_second.got.values())
    shape = (plane_count, seq_count * rows, side_width)
    grad_hidden, keep_side, send_side = phase(
        [query_move],
        lambda: call(
            functools.partial(side_kernel, experts=experts, others=len(others), rows=rows),
            "key_gradient",
            [shape_of((token_count, width), FULL), shape_of(shape, LOW), shape_of(shape, LOW)],
            1.0,
            scalars=1,
        )(
            ids, hidden, grad_before, unit, small, grad_rows, grad_bias, grad_router,
            grad_kv, *others
        ),
    )

    side_move = Move(core, send_side)
    phase([side_move])
    moves = fold(both, rows)
    keep_query, *_ = together(keep_query, *[f.keep for f in both if f.move is not None])
    line = lambda *terms: [t.reshape(1, -1, t.shape[-1]) for t in terms]
    small_sent = cut(
        [line(keep_query, query_move.got[1]), line(keep_side, side_move.got[1])],
        plane,
        width + side_width,
    )
    small_move = Move(plane, dict(enumerate(small_sent)))
    phase([small_move] + moves)
    folded(both)
    last_sent = cut([line(small_sent[0], *small_move.got.values())], along, width)
    last_move = Move(along, dict(enumerate(last_sent)))
    moves = fold(both, rows)
    [grad_tokens] = phase(
        [last_move] + moves,
        lambda: [
            call(
                functools.partial(tokens_kernel, experts=experts),
                "token_gradient",
                shape_of((token_count, width), LOW),
                1.0,
            )(grad_hidden, unit, factor, branch, small)
        ],
    )
    folded(both)
    while any(f.stages for f in both):
        phase(fold(both, rows))
        folded(both)
    ends = pair_folds + [half_fold]
    plan = [([low for _, low in f.terms], f.lead * f.rows) for f in ends]
    terms = [a.reshape(-1, width) for f in ends for a, _ in f.terms]
    terms += [last_sent[0]] + list(last_move.got.values())
    vector_shape = shape_of((1, rows), FULL)
    (
        grad_expand, grad_output, grad_contract, grad_query_map, grad_router, grad_keyval,
        *vector_sums, grad_spread
    ) = call(
        functools.partial(finish_kernel, terms=len(terms), slots=chunks, plan=plan),
        "finish",
        [
            shape_of(expand.shape, FULL),
            shape_of(output_map.shape, FULL),
            shape_of(contract.shape, FULL),
            shape_of(query_map.shape, FULL),
            shape_of((experts, rows), FULL),
            shape_of(keyval.shape, FULL),
        ]
        + [vector_shape] * 5
        + [shape_of((1, expand_bias.shape[0]), FULL)],
        0.1,
    )(*terms)
    grad_gain, grad_shift, grad_gain_two, grad_shift_two, grad_contract_bias = (
        v.reshape(rows) for v in vector_sums
    )
    return (
        out, grad_tokens, grad_gain, grad_shift, grad_router.T, grad_query_map, grad_keyval,
        grad_output, grad_gain_two, grad_shift_two, grad_expand, grad_spread.reshape(-1),
        grad_contract, grad_contract_bias
    )


def solution(mesh):
    both = ("dp", "seq")
    rows, vector = P(both, None), P(both)
    return jax.shard_map(
        per_device,
        mesh=mesh,
        in_specs=(
            rows, rows, P("dp", None), rows, vector, vector, rows, rows, rows, rows, vector, vector,
            rows, vector, rows, vector
        ),
        out_specs=(
            rows, rows, vector, vector, rows, rows, rows, rows, vector, vector, rows, vector, rows,
            vector
        ),
        check_vma=False,
    )
```

```python
import functools

import jax
import jax.numpy as jnp
from jax import lax
from jax.experimental import pallas as pl
from jax.experimental.pallas import tpu as pltpu
from jax.sharding import PartitionSpec as P

LOW = jnp.bfloat16
FULL = jnp.float32
FAR = 1e30
EPS = 1e-05
DOC_LANE = 64
LSE_LANE = 96
SUM_LANE = 64
MAX_LANE = 67
BIAS_LANE = 64
SEQ_SLOT, PLANE_SLOT, CORE_SLOT = range(3)
LANES = 128
MEGA = 1 << 20
FORWARD_COST = 0.1
QUERY_COST = 0.05
BACKWARD_COST = 3.0
FEED_COST = 8.0
LIMITS = {
    "pack": 4, "first": 4, "unit": 6, "hidden": 6, "vectors": 2, "queries": 6, "attention_forward": 16,
    "attention_backward": 8, "query_gradient": 8, "key_gradient": 12, "token_gradient": 12, "merge": 2, "join": 2, "spread": 2,
    "cut": 3, "fold": 4, "finish": 2, "feed_up": 8,
    "feed_down": 6, "feed_down_last": 17,
}


def to_low(matrix):
    return matrix.astype(LOW)


def dot_plain(left, right):
    return lax.dot_general(left, right, (((1,), (0,)), ((), ())), preferred_element_type=FULL)


def dot_last(left, right):
    return lax.dot_general(left, right, (((1,), (1,)), ((), ())), preferred_element_type=FULL)


def dot_first(left, right):
    return lax.dot_general(left, right, (((0,), (0,)), ((), ())), preferred_element_type=FULL)


class Group:
    def __init__(self, axis, shift, size, slot):
        self.axis, self.shift, self.size, self.slot = axis, shift, size, slot
        self.ids = None

    def index(self):
        return (lax.axis_index(self.axis) >> self.shift) & (self.size - 1)

    def exchange(self, block, mask):
        step = mask << self.shift
        pairs = [(i, i ^ step) for i in range(lax.axis_size(self.axis))]
        return lax.ppermute(block, self.axis, pairs)


def by_place(blocks, index):
    blocks = list(blocks)
    for bit in range(len(blocks).bit_length() - 1):
        swap = (index >> bit) & 1 == 1
        blocks = [jnp.where(swap, blocks[i ^ (1 << bit)], blocks[i]) for i in range(len(blocks))]
    return blocks


def merge_kernel(ids_ref, *refs, count, slot):
    out_ref = refs[count]
    rows = refs[0].shape[1]
    for mask in range(count):
        start = pl.multiple_of((ids_ref[slot] ^ mask) * rows, rows)
        out_ref[:, pl.ds(start, rows), :] = refs[mask][...]


def merge(blocks, group):
    lead, rows, columns = blocks[0].shape
    if rows % 16:
        return jnp.concatenate(by_place(blocks, group.index()), axis=1)
    return call(
        functools.partial(merge_kernel, count=len(blocks), slot=group.slot),
        "merge",
        shape_of((lead, rows * len(blocks), columns), blocks[0].dtype),
        0.1,
        scalars=1,
    )(group.ids, *blocks)


def columns_of(columns, width):
    return [slice(i, min(i + width, columns)) for i in range(0, columns, width)]


def cut_kernel(ids_ref, *refs, sizes, count, slot):
    outs = refs[len(refs) - count :]
    refs = list(refs[: len(refs) - count])
    sets = [[refs.pop(0) for _ in range(size)] for size in sizes]
    width = outs[0].shape[1]
    for mask in range(count):
        row = column = 0
        for terms in sets:
            lead, total, columns = terms[0].shape
            rows = total // count
            start = pl.multiple_of((ids_ref[slot] ^ mask) * rows, rows)
            for at in range(lead):
                for piece in columns_of(columns, width):
                    value = sum(term[at, pl.ds(start, rows), piece].astype(FULL) for term in terms)
                    end = column + value.shape[1]
                    outs[mask][row : row + rows, column:end] = to_low(value)
                    column = end % width
                    row += 0 if column else rows
        if column:
            rest = outs[mask].shape[0] - row
            outs[mask][row:, column:] = jnp.zeros((rest, width - column), LOW)


def cut(sets, group, width):
    count = group.size
    sets = [[t.reshape((-1,) + t.shape[-2:]) for t in terms] for terms in sets]
    rows = [terms[0].shape[1] // count for terms in sets]
    total = sum(t[0].shape[0] * r * t[0].shape[2] for t, r in zip(sets, rows))
    total = -(-total // (width * rows[-1])) * rows[-1]
    if any(r % 16 for r in rows):
        index = group.index()
        results = []
        for mask in range(count):
            bands, band = [], []
            for terms, r in zip(sets, rows):
                value = sum(t.astype(FULL) for t in terms)
                value = lax.dynamic_slice_in_dim(value, (index ^ mask) * r, r, 1)
                for at in range(value.shape[0]):
                    for piece in columns_of(value.shape[2], width):
                        band.append(value[at, :, piece])
                        if sum(b.shape[1] for b in band) == width:
                            bands.append(jnp.concatenate(band, axis=1))
                            band = []
            if band:
                band = jnp.concatenate(band, axis=1)
                bands.append(jnp.pad(band, ((0, 0), (0, width - band.shape[1]))))
            results.append(to_low(jnp.concatenate(bands, axis=0)))
        return results
    return call(
        functools.partial(
            cut_kernel, sizes=[len(t) for t in sets], count=count, slot=group.slot
        ),
        "cut",
        [shape_of((total, width), LOW)] * count,
        0.1,
        scalars=1,
    )(group.ids, *[t for terms in sets for t in terms])


def together(*values):
    return lax.optimization_barrier(values)


class Move:
    def __init__(self, group, blocks, masks=None):
        self.group = group
        self.masks = list(range(1, group.size)) if masks is None else masks
        self.blocks = blocks if isinstance(blocks, dict) else {m: blocks for m in self.masks}

    def begin(self):
        self.moved = [self.group.exchange(self.blocks[m], m) for m in self.masks]
        return self

    def end(self, got):
        self.got = dict(zip(self.masks, got))
        self.moved = None


def phase(moves, work=lambda: (), held=()):
    for move in moves:
        if getattr(move, "moved", None) is None:
            move.begin()
    done = work()
    ended = list(together(*[x for m in moves for x in m.moved], *done, *held))
    for move in moves:
        move.end([ended.pop(0) for _ in move.masks])
    return ended


def fold_kernel(ids_ref, *refs, plan):
    refs = list(refs)
    folds = [(*step, [refs.pop(0) for _ in step[1]]) for step in plan]
    keeps = [refs.pop(0) for _ in plan]
    for keep_ref, ((slot, shift), lows, half, count, out, place, terms) in zip(keeps, folds):
        bit = (ids_ref[slot] >> shift) & 1
        for pair in range(count):
            mine, other = (
                sum(
                    t[pl.ds(low + (2 * pair + b) * half, half)].astype(FULL)
                    for t, low in zip(terms, lows)
                )
                for b in (bit, 1 - bit)
            )
            keep_ref[pair * half : (pair + 1) * half] = mine
            refs[out][place + pair * half : place + (pair + 1) * half] = to_low(other)


class Fold:
    def __init__(self, terms, lead, rows, groups, upward=False):
        self.terms, self.lead, self.rows = terms, lead, rows
        self.left = [(g, b) for g in groups for b in reversed(range(g.size.bit_length() - 1))]
        over = [x for x in self.left if x[0].axis == "dp"]
        self.stages = over[::-1] if upward else over
        self.stages += [x for x in self.left if x[0].axis == "seq"][::-1]
        self.move = None

    def part(self):
        ahead = 1 << self.left.index(self.stages[0])
        return (self.rows << len(self.left)) // (2 * ahead), self.lead * ahead


def fold(folds, unit):
    folds = [f for f in folds if f.stages]
    if not folds:
        return []
    ways, filled, plan, operands, keeps = [], [], [], [], []
    for f in folds:
        if f.stages[0] not in ways:
            ways.append(f.stages[0])
            filled.append(0)
        group, bit = f.stages[0]
        half, count = f.part()
        at = ways.index(f.stages[0])
        columns = f.terms[0][0].shape[-1]
        lows = [low // unit for _, low in f.terms]
        f.start = filled[at]
        plan.append(((group.slot, bit), lows, half // unit, count, at, f.start // unit))
        operands += [a.reshape(-1, unit, columns) for a, _ in f.terms]
        keeps.append(shape_of((half * count // unit, unit, columns), FULL))
        filled[at] += half * count
    sends = [shape_of((rows // unit, unit, columns), LOW) for rows in filled]
    results = call(
        functools.partial(fold_kernel, plan=plan), "fold", keeps + sends, 0.1, scalars=1
    )(ways[0][0].ids, *operands)
    moves = [
        Move(group, sent, [1 << bit]) for (group, bit), sent in zip(ways, results[len(folds) :])
    ]
    for f, keep in zip(folds, results):
        f.keep, f.move = keep, moves[ways.index(f.stages[0])]
        f.left.remove(f.stages.pop(0))
    return moves


def folded(folds):
    for f in folds:
        if f.move is not None:
            [got] = f.move.got.values()
            f.terms = [(f.keep, 0), (got, f.start)]
            f.move = None


def lane_ids(shape):
    return lax.broadcasted_iota(jnp.int32, shape, len(shape) - 1)


def row_positions(offset, rows):
    return offset + lax.broadcasted_iota(jnp.int32, (rows, 1), 0)


def in_document(bounds_ref, positions):
    return (positions >= bounds_ref[0:1, :]) & (positions < bounds_ref[1:2, :])


def put_parts(base, lanes, lane, rows, count):
    for step in range(count):
        part = to_low(rows).astype(FULL)
        base = jnp.where(lanes == lane + step, part, base)
        rows = rows - part
    return base


def lane_sum(matrix, parts=2):
    rest = sum(matrix[:, i : i + LANES] for i in range(0, matrix.shape[1], LANES))
    ones = jnp.ones((LANES, LANES), LOW)
    total = None
    for _ in range(parts):
        part = to_low(rest)
        rest = rest - part.astype(FULL)
        term = dot_plain(part, ones)
        total = term if total is None else total + term
    return total


def over(rows, width):
    return jnp.concatenate([rows] * (width // LANES), axis=1)


def normalize(matrix):
    width = matrix.shape[1]
    center = matrix - over(lane_sum(matrix, 3) * (1.0 / width), width)
    factor = lax.rsqrt(lane_sum(center * center) * (1.0 / width) + EPS)
    return center * over(factor, width), factor


def norm_backward(grad, unit, factor, gain):
    width = grad.shape[1]
    scaled = grad * gain
    mean = over(lane_sum(scaled) * (1.0 / width), width)
    along = over(lane_sum(scaled * unit) * (1.0 / width), width)
    return over(factor, width) * (scaled - mean - unit * along)


def choose(wide, route, head):
    shift = (LANES // head).bit_length() - 1
    tile = lax.shift_right_logical(route, shift)
    picked = wide[:, :LANES]
    for index in range(1, wide.shape[1] // LANES):
        picked = jnp.where(tile == index, wide[:, index * LANES : (index + 1) * LANES], picked)
    turned = pltpu.roll(picked, head, 1)
    lanes = lane_ids((1, LANES))
    mine = (lanes // head) == (route & ((1 << shift) - 1))
    return jnp.where(mine, picked, turned)


def place(doubled, routes, head, width):
    lanes = lane_ids((1, LANES))
    per_tile = LANES // head
    tiles = []
    for index in range(width // LANES):
        expert = lanes // head + index * per_tile
        tile = jnp.zeros_like(doubled[0])
        for rows, route in zip(doubled, routes):
            tile = jnp.where(route == expert, rows, tile)
        tiles.append(tile)
    return jnp.concatenate(tiles, axis=1)


def doubled_head(rows, head):
    lanes = lane_ids((1, LANES))
    return jnp.where(lanes < head, rows, pltpu.roll(rows, head, 1))


def key_rows_of(kv, hot, head):
    lanes = lane_ids((1, LANES))
    kv = kv.astype(FULL)
    marks = jnp.where((lanes >= LSE_LANE) & (lanes < LSE_LANE + 3), 1.0, 0.0)
    keys = jnp.where(lanes < head, kv, jnp.where(hot, 1.0, marks))
    ones = jnp.where((lanes >= SUM_LANE) & (lanes < SUM_LANE + 3), 1.0, 0.0)
    values = jnp.where(lanes < head, pltpu.roll(kv, head, 1), ones)
    return to_low(keys), to_low(values)


def as_column(row):
    rows = row.shape[1]
    lanes = lax.broadcasted_iota(jnp.int32, (rows, rows), 1)
    here = lax.broadcasted_iota(jnp.int32, (rows, rows), 0)
    return jnp.sum(jnp.where(lanes == here, row, 0.0), axis=1, keepdims=True)


def as_row(column):
    rows = column.shape[0]
    lanes = lax.broadcasted_iota(jnp.int32, (rows, rows), 1)
    here = lax.broadcasted_iota(jnp.int32, (rows, rows), 0)
    return jnp.sum(jnp.where(lanes == here, column, 0.0), axis=0, keepdims=True)


def fetch(refs, held, semaphores):
    copies = [
        pltpu.make_async_copy(ref, into, semaphores.at[i])
        for i, (ref, into) in enumerate(zip(refs, held))
    ]
    for copy in copies:
        copy.start()
    for copy in copies:
        copy.wait()


def pack_kernel(*refs, count):
    small_ref, large_ref = refs[count : count + 2]
    held = refs[count + 2 : -1]
    fetch(refs[:count], held, refs[-1])
    (
        query_ref, keyval_ref, router_ref, gain_ref, shift_ref, gain_two_ref, shift_two_ref,
        contract_bias_ref, expand_bias_ref, output_ref, expand_ref, contract_ref
    ) = held
    rows, width = query_ref.shape
    experts = router_ref.shape[0]
    keyval_width = keyval_ref.shape[1]
    small_ref[:, :width] = to_low(query_ref[...])
    small_ref[:, width : width + keyval_width] = to_low(keyval_ref[...])
    lanes = lane_ids((1, LANES))
    turned = router_ref[...]
    side = jnp.zeros((rows, LANES), FULL)
    for expert in range(experts):
        side = jnp.where(lanes == expert, as_column(turned[expert : expert + 1]), side)
    vectors = [gain_ref, shift_ref, gain_two_ref, shift_two_ref, contract_bias_ref]
    for index, ref in enumerate(vectors):
        side = jnp.where(lanes == experts + index, as_column(ref[...]), side)
    extra = expand_bias_ref.shape[1]
    bias = jnp.pad(expand_bias_ref[...], ((0, 0), (BIAS_LANE, LANES - BIAS_LANE - extra)))
    first = lax.broadcasted_iota(jnp.int32, (rows, 1), 0) == 0
    side = side + jnp.where(first, bias, 0.0)
    small_ref[:, width + keyval_width :] = to_low(side)
    large = [output_ref[...]]
    large += [
        expand_ref[:, c * width : (c + 1) * width] for c in range(expand_ref.shape[1] // width)
    ]
    large_ref[...] = to_low(jnp.concatenate(large + [contract_ref[...]], axis=0))


def unit_kernel(tokens_ref, unit_ref, factor_ref):
    unit_ref[...], factor_ref[...] = normalize(tokens_ref[...].astype(FULL))


def first_kernel(ids_ref, routes_hbm, lengths_hbm, columns_ref, bounds_ref, ids_out, *held):
    for slot in range(ids_ref.shape[0]):
        ids_out[slot] = ids_ref[slot]
    routes_ref, lengths_ref, semaphores = held
    fetch((routes_hbm, lengths_hbm), (routes_ref, lengths_ref), semaphores)
    routes = routes_ref[...].astype(FULL)
    choices = routes.shape[0]
    routes = jnp.concatenate([routes, jnp.zeros((8 - routes.shape[0], routes.shape[1]), FULL)], axis=0)
    turned = routes.T
    for j in range(choices):
        wide = jnp.broadcast_to(turned[:, j : j + 1], columns_ref.shape[1:])
        columns_ref[j] = wide.astype(jnp.int32)
    count = lengths_ref.shape[1]
    lanes = lane_ids((1, LANES))
    rest = jnp.zeros((1, LANES - DOC_LANE - count), jnp.int32)
    lengths = jnp.concatenate(
        [jnp.zeros((1, DOC_LANE), jnp.int32), lengths_ref[...], rest], axis=1
    )
    ends = lengths
    step = 1
    while step < count:
        ends = ends + jnp.where(lanes >= DOC_LANE + step, pltpu.roll(ends, step, 1), 0)
        step *= 2
    here = (lanes >= DOC_LANE) & (lanes < DOC_LANE + count)
    starts = jnp.where(here, ends - lengths, 1 << 30)
    ends = jnp.where(here, ends, 0)
    index = lax.broadcasted_iota(jnp.int32, (8, 1), 0)
    bounds_ref[...] = jnp.where(index == 0, starts, jnp.where(index == 1, ends, 0))


def vectors_kernel(small_ref, vectors_ref, bias_ref, *, experts, rows):
    misc = small_ref[:, small_ref.shape[1] - LANES :].astype(FULL)
    turned = misc.T
    vectors_ref[...] = turned[experts + 2 : experts + 10]
    count = misc.shape[0] // rows
    each = bias_ref.shape[1] // count
    per_tile = LANES // each
    firsts = misc.reshape(count, rows, LANES)[:, 0, :].reshape(count // per_tile, per_tile, LANES)
    lanes = lane_ids((1, LANES))
    tiles = jnp.zeros((count // per_tile, LANES), FULL)
    for k in range(per_tile):
        moved = pltpu.roll(firsts[:, k, :], (k * each - BIAS_LANE) % LANES, 1)
        tiles = jnp.where(lanes // each == k, moved, tiles)
    for index in range(count // per_tile):
        bias_ref[:, index * LANES : (index + 1) * LANES] = tiles[index : index + 1]


def bias_rows(bias, count, rows):
    each = bias.shape[1] // count
    per_tile = LANES // each
    tiles = jnp.concatenate(
        [bias[:, i : i + LANES] for i in range(0, bias.shape[1], LANES)], axis=0
    )
    lanes = lane_ids((1, LANES))
    mine = (lanes >= BIAS_LANE) & (lanes < BIAS_LANE + each)
    parts = [
        jnp.where(mine, pltpu.roll(tiles, (BIAS_LANE - k * each) % LANES, 1), 0.0)
        for k in range(per_tile)
    ]
    firsts = jnp.stack(parts, axis=1).reshape(count, 1, LANES)
    here = lax.broadcasted_iota(jnp.int32, (1, rows, 1), 1) == 0
    return jnp.where(here, firsts, 0.0).reshape(count * rows, LANES)


def stack_kernel(*refs):
    for at, ref in enumerate(refs[:-1]):
        refs[-1][at] = ref[0]


def join_kernel(first_ref, second_ref, out_ref):
    count = first_ref.shape[0]
    out_ref[:count] = first_ref[...]
    out_ref[count:] = second_ref[...]


def spread_kernel(ids_ref, *refs, masks, slots, rows):
    pair_ref, half_ref = refs[len(masks) :]
    more = refs[0].shape[1] - slots * rows
    for ref, masks_of in zip(refs, masks):
        for at, mask in enumerate(masks_of):
            place = ids_ref[SEQ_SLOT] ^ mask
            start = pl.multiple_of(place * rows, rows)
            for slot in range(slots):
                here = slice(slot * rows, (slot + 1) * rows)
                pair_ref[slot, pl.ds(start, rows), :] = ref[at, here, :]
            half_ref[pl.ds(pl.multiple_of(place * more, more), more), :] = ref[at, slots * rows :, :]


def hidden_kernel(
    ids_ref, unit_ref, mine_ref, other_ref, routes_ref, hidden_ref, kv_ref, gates_ref, small_ref, *, experts
):
    small = merged(mine_ref[...], other_ref[...], ids_ref[CORE_SLOT])
    small_ref[...] = small
    side = small[:, small.shape[1] - 2 * LANES :]
    vectors = side[:, LANES:].astype(FULL).T
    hidden = to_low(
        unit_ref[...] * vectors[experts : experts + 1] + vectors[experts + 1 : experts + 2]
    )
    hidden_ref[...] = hidden
    both = dot_plain(hidden, side)
    kv_ref[...] = to_low(both[:, :LANES])
    logits = both[:, LANES:]
    lanes = lane_ids((1, LANES))
    picked = [lane_sum(jnp.where(lanes == routes_ref[j], logits, 0.0), 3) for j in range(2)]
    top = jnp.maximum(picked[0], picked[1])
    raised = [jnp.exp(p - top) for p in picked]
    total = raised[0] + raised[1]
    for j in range(2):
        gates_ref[j] = raised[j] / total


def query_kernel(ids_ref, hidden_ref, small_ref, routes_ref, bounds_ref, query_ref, *, head):
    rows, width = hidden_ref.shape
    wide = dot_plain(hidden_ref[...], small_ref[:, :width])
    lanes = lane_ids((1, LANES))
    hot = in_document(bounds_ref, row_positions(ids_ref[SEQ_SLOT] * rows, rows))
    documents = (bounds_ref[1:2, :] > 0) & (lanes >= head)
    marks = jnp.where(documents & jnp.logical_not(hot), -FAR, 0.0)
    for j in range(2):
        rows_of = choose(wide, routes_ref[j], head) * head**-0.5
        query_ref[j * rows : (j + 1) * rows, :] = to_low(jnp.where(lanes < head, rows_of, marks))


def forward_kernel(ids_ref, query_ref, bounds_ref, *rest, head, first, last, masks, part):
    count = len(masks)
    kv_refs, rest = rest[:count], list(rest[count:])
    state_ref = None if first else rest.pop(0)
    lanes = lane_ids((1, LANES))
    blocks = []
    for index, ref in enumerate(kv_refs):
        start = (ids_ref[SEQ_SLOT] ^ masks[index]) * ref.shape[0]
        hot = in_document(bounds_ref, row_positions(start, ref.shape[0]))
        blocks.append(key_rows_of(ref[...], hot, head))
    for start in range(0, query_ref.shape[0], part):
        rows = slice(start, start + part)
        query = query_ref[rows, :]
        state = None if first else state_ref[rows, :]
        for keys, values in blocks:
            scores = dot_last(query, keys)
            top = jnp.max(scores, axis=1, keepdims=True)
            if state is None:
                new = top
                state = dot_plain(to_low(jnp.exp(scores - new)), values)
            else:
                old = state[:, MAX_LANE : MAX_LANE + 1]
                new = jnp.maximum(old, top)
                weights = to_low(jnp.exp(scores - new))
                state = state * jnp.exp(old - new) + dot_plain(weights, values)
            state = jnp.where(lanes == MAX_LANE, new, state)
        if last:
            attn_ref, wide_ref = rest
            total = state[:, SUM_LANE : SUM_LANE + 1]
            attn_ref[rows, :] = jnp.where(lanes < head, state / total, 0.0)
            log_total = state[:, MAX_LANE : MAX_LANE + 1] + jnp.log(total)
            wide_ref[rows, :] = to_low(
                put_parts(query.astype(FULL), lanes, LSE_LANE, -log_total, 3)
            )
        else:
            rest[0][rows, :] = state


def merged(mine, other, bit):
    low = bit == 0
    both = jnp.stack([jnp.where(low, mine, other), jnp.where(low, other, mine)], axis=1)
    return both.reshape(-1, mine.shape[-1])


def parted(whole, bit, shape):
    both = whole.reshape(shape[0], 2, shape[1], shape[2])
    low = bit == 0
    first, second = both[:, 0], both[:, 1]
    return jnp.where(low, first, second), jnp.where(low, second, first)


def weights(refs, bit):
    mine, other = refs[0][...], refs[1][...]
    shape = mine.shape[-3:]
    return merged(mine.reshape(shape), other.reshape(shape), bit)


def weights(mine, other, ids_ref):
    return merged(mine, other, ids_ref[CORE_SLOT])


def unit_of(ids_ref, mask, inner, size):
    unit = ids_ref[PLANE_SLOT] ^ mask
    shift = (inner // size).bit_length() - 1
    everywhere = pl.ds(pl.multiple_of(unit * size, size), size)
    if not shift:
        return unit, slice(0, size), everywhere
    start = pl.multiple_of((unit & ((1 << shift) - 1)) * size, size)
    return lax.shift_right_logical(unit, shift), pl.ds(start, size), everywhere


def up_kernel(
    ids_ref, tokens_ref, cotangent_ref, attn_ref, gates_ref, routes_ref, vectors_ref, bias_ref,
    pair_mine, pair_other, mixed_ref, hidden_ref, active_ref, steep_ref, keep_ref, send_ref, *, head
):
    width = tokens_ref.shape[1]
    wide = [doubled_head(attn_ref[j], head) * gates_ref[j] for j in range(2)]
    mixed = to_low(place(wide, [routes_ref[j] for j in range(2)], head, width))
    mixed_ref[...] = mixed
    output_weight = weights(pair_mine[0], pair_other[0], ids_ref)
    middle = tokens_ref[...].astype(FULL) + dot_plain(mixed, output_weight)
    unit, _ = normalize(middle)
    hidden = to_low(unit * vectors_ref[0:1, :] + vectors_ref[1:2, :])
    hidden_ref[...] = hidden
    slope = 0.7978845608028654
    cube = 0.044715
    chunks, _, inner_width = active_ref.shape
    part = min(256, tokens_ref.shape[0])
    groups = keep_ref.shape[0] // chunks
    for chunk in range(chunks):
        expand = weights(pair_mine[chunk + 1], pair_other[chunk + 1], ids_ref)
        columns = slice(chunk * inner_width, (chunk + 1) * inner_width)
        for start in range(0, hidden.shape[0], part):
            here = slice(start, start + part)
            inner = dot_plain(hidden[here], expand) + bias_ref[:, columns]
            square = inner * inner
            half = 0.5 + 0.5 * jnp.tanh(inner * (slope + slope * cube * square))
            whole = inner * half
            active_ref[chunk, here] = to_low(whole)
            steep = half + whole * (1.0 - half) * (2.0 * slope + 6.0 * slope * cube * square)
            steep_ref[chunk, here] = to_low(steep)
        shape = (groups,) + keep_ref.shape[1:]
        grad = to_low(dot_first(active_ref[chunk], cotangent_ref[...]))
        here = slice(chunk * groups, (chunk + 1) * groups)
        keep_ref[here], send_ref[here] = parted(grad, ids_ref[CORE_SLOT], shape)


def down_kernel(
    ids_ref, hidden_ref, cotangent_ref, active_ref, steep_ref, pair_mine, pair_other, contract_mine,
    contract_other, *rest, head, masks, last
):
    rest = list(rest)
    take = lambda n: [rest.pop(0) for _ in range(n)]
    _, _, inner = active_ref.shape
    size = 2 * contract_mine.shape[1]
    if last:
        out_before, grad_before, keep_before, send_before, bias_before = take(5)
        tokens_ref, mixed_ref, attn_ref, gates_ref, routes_ref, vectors_ref = take(6)
        out_ref, branch_ref, grad_attn_ref, grad_logits_ref, grad_rows_ref = take(5)
        keep_ref, send_ref, grad_bias_ref = take(3)
        out, grad_hidden = out_before[...], grad_before[...]
        chunk, columns, everywhere = unit_of(ids_ref, 0, inner, size)
        keep_ref[chunk, :, :, columns] = keep_before[...]
        send_ref[chunk, :, :, columns] = send_before[...]
        grad_bias_ref[:, everywhere] = bias_before[...]
    else:
        out_held, grad_held, keep_ref, send_ref, grad_bias_ref = take(5)
        out = grad_hidden = None
    add = lambda total, term: term if total is None else total + term
    for at, mask in enumerate(masks):
        chunk, columns, everywhere = unit_of(ids_ref, mask, inner, size)
        expand = weights(
            pair_mine[chunk + 1, :, :, columns], pair_other[chunk + 1, :, :, columns], ids_ref
        )
        contract = weights(contract_mine[at : at + 1], contract_other[at : at + 1], ids_ref)
        out = add(out, dot_plain(active_ref[chunk, :, columns], contract))
        grad_active = dot_last(cotangent_ref[...], contract)
        grad_inner = to_low(steep_ref[chunk, :, columns].astype(FULL) * grad_active)
        grad_bias = jnp.sum(grad_inner.astype(FULL), axis=0, keepdims=True)
        grad_hidden = add(grad_hidden, dot_last(grad_inner, expand))
        grad = to_low(dot_first(hidden_ref[...], grad_inner))
        keep, send = parted(grad, ids_ref[CORE_SLOT], pair_mine.shape[1:3] + (size,))
        if last:
            grad_bias_ref[:, everywhere] = grad_bias
            keep_ref[chunk, :, :, columns] = keep
            send_ref[chunk, :, :, columns] = send
        else:
            grad_bias_ref[...] = grad_bias
            keep_ref[...] = keep
            send_ref[...] = send
    if not last:
        out_held[...] = out
        grad_held[...] = grad_hidden
        return
    lanes = lane_ids((1, LANES))
    gain, contract_bias = vectors_ref[0:1, :], vectors_ref[2:3, :]
    output_weight = weights(pair_mine[0], pair_other[0], ids_ref)
    mixed = mixed_ref[...]
    middle = tokens_ref[...].astype(FULL) + dot_plain(mixed, output_weight)
    out_ref[...] = to_low(out + middle + contract_bias)
    unit, factor = normalize(middle)
    cotangent = cotangent_ref[...].astype(FULL)
    branch = to_low(cotangent + norm_backward(grad_hidden, unit, factor, gain))
    branch_ref[...] = branch
    grad_rows_ref[...] = jnp.zeros_like(grad_rows_ref)
    grad_rows_ref[0:1, :] = jnp.sum(grad_hidden * unit, axis=0, keepdims=True)
    grad_rows_ref[1:2, :] = jnp.sum(grad_hidden, axis=0, keepdims=True)
    grad_rows_ref[2:3, :] = jnp.sum(cotangent, axis=0, keepdims=True)
    grad = to_low(dot_first(mixed, branch))
    end = keep_ref.shape[0] - 1
    keep_ref[end], send_ref[end] = parted(grad, ids_ref[CORE_SLOT], keep_ref.shape[1:])
    grad_mixed = dot_last(branch, output_weight)
    scaled = []
    for j in range(2):
        weighted = jnp.where(lanes < head, choose(grad_mixed, routes_ref[j], head), 0.0)
        scaled.append(gates_ref[j] * lane_sum(weighted * attn_ref[j]))
        grad_attn = weighted * gates_ref[j]
        grad_attn_ref[j] = to_low(put_parts(grad_attn, lanes, SUM_LANE, -scaled[j], 3))
    mean = scaled[0] + scaled[1]
    grad_logits = jnp.zeros(gates_ref.shape[1:], FULL)
    for j in range(2):
        grad_picked = scaled[j] - gates_ref[j] * mean
        grad_logits = jnp.where(lanes == routes_ref[j], grad_picked, grad_logits)
    grad_logits_ref[...] = to_low(grad_logits)


def backward_kernel(ids_ref, query_ref, grad_ref, bounds_ref, *rest, head, first, masks, part):
    count = len(masks)
    kv_refs, rest = rest[:count], list(rest[count:])
    before_ref = None if first else rest.pop(0)
    grad_query_ref, grad_kv_refs = rest[0], rest[1:]
    lanes = lane_ids((1, LANES))
    key_count = kv_refs[0].shape[0]
    blocks = []
    for index, ref in enumerate(kv_refs):
        start = (ids_ref[SEQ_SLOT] ^ masks[index]) * key_count
        hot = in_document(bounds_ref, row_positions(start, key_count))
        keys, values = key_rows_of(ref[...], hot, head)
        blocks.append((keys, values, to_low(keys.astype(FULL).T[:head])))
    totals = [None] * count
    for start in range(0, query_ref.shape[0], part):
        rows = slice(start, start + part)
        query = query_ref[rows, :]
        grad = grad_ref[rows, :]
        only_query = to_low(jnp.where(lanes < head, query.astype(FULL), 0.0))
        turned = pltpu.roll(grad.astype(FULL), head, 1)
        only_grad = to_low(jnp.where(lanes < head, 0.0, turned))
        grad_query = None if first else before_ref[:, rows]
        for index, (keys, values, turned_keys) in enumerate(blocks):
            probs = jnp.exp(dot_last(keys, query))
            grad_scores = to_low(probs * dot_last(values, grad))
            update = dot_plain(grad_scores, only_query) + dot_plain(to_low(probs), only_grad)
            totals[index] = update if totals[index] is None else totals[index] + update
            step = dot_plain(turned_keys, grad_scores)
            grad_query = step if grad_query is None else grad_query + step
        grad_query_ref[:, rows] = grad_query
    for index in range(count):
        grad_kv_refs[index][...] = to_low(totals[index])


def placed_kernel(
    ids_ref, grad_query_ref, hidden_ref, routes_ref, grad_logits_ref, small_ref, grad_hidden_ref,
    keep_ref, send_ref, grad_router_ref, *, head
):
    count, width = hidden_ref.shape
    turned = (grad_query_ref[...] * head**-0.5).T
    rows = []
    for j in range(2):
        half = to_low(turned[j * count : (j + 1) * count]).astype(FULL)
        rows.append(jnp.concatenate([half] * (LANES // head), axis=1))
    placed = to_low(place(rows, [routes_ref[j] for j in range(2)], head, width))
    hidden = hidden_ref[...]
    grad_logits = grad_logits_ref[...]
    keep, send = parted(to_low(dot_first(hidden, placed)), ids_ref[CORE_SLOT], keep_ref.shape)
    keep_ref[...] = keep
    send_ref[...] = send
    grad_router_ref[...] = dot_first(hidden, grad_logits)
    grad_hidden_ref[...] = dot_last(placed, small_ref[:, :width]) + dot_last(
        grad_logits, small_ref[:, small_ref.shape[1] - LANES :]
    )


def side_kernel(
    ids_ref, hidden_ref, grad_before_ref, unit_ref, small_ref, rows_ref, bias_ref,
    grad_router_ref, own_ref, *rest, experts, others, rows
):
    other_refs = rest[:others]
    grad_hidden_ref, keep_ref, send_ref = rest[others:]
    side = small_ref[:, small_ref.shape[1] - 2 * LANES :]
    grad_kv = own_ref[...].astype(FULL)
    for ref in other_refs:
        grad_kv += ref[...].astype(FULL)
    grad_kv = to_low(grad_kv)
    grad_keyval = dot_first(hidden_ref[...], grad_kv)
    grad_hidden = grad_before_ref[...] + dot_last(grad_kv, side[:, :LANES])
    grad_hidden_ref[...] = grad_hidden
    gain_grad = jnp.sum(grad_hidden * unit_ref[...], axis=0, keepdims=True)
    shift_grad = jnp.sum(grad_hidden, axis=0, keepdims=True)
    width = hidden_ref.shape[1]
    index = lax.broadcasted_iota(jnp.int32, (8, 1), 0)
    later = pltpu.roll(rows_ref[...], 2, 0)
    vectors = jnp.where(index == 0, gain_grad, jnp.where(index == 1, shift_grad, later))
    ahead = jnp.zeros((experts, width), FULL)
    behind = jnp.zeros((LANES - experts - 8, width), FULL)
    columns = jnp.concatenate([ahead, vectors, behind], axis=0).T
    spread = bias_rows(bias_ref[...], width // rows, rows)
    grad_side = jnp.concatenate([grad_keyval, columns + grad_router_ref[...] + spread], axis=1)
    keep_ref[...], send_ref[...] = parted(to_low(grad_side), ids_ref[CORE_SLOT], keep_ref.shape)


def tokens_kernel(
    grad_hidden_ref, unit_ref, factor_ref, grad_middle_ref, small_ref, grad_tokens_ref, *, experts
):
    misc = small_ref[:, small_ref.shape[1] - LANES :]
    gain = misc.astype(FULL).T[experts : experts + 1]
    grad = norm_backward(grad_hidden_ref[...], unit_ref[...], factor_ref[...], gain)
    grad_tokens_ref[...] = to_low(grad_middle_ref[...].astype(FULL) + grad)


def finish_kernel(*refs, terms, slots, plan):
    sums = []
    for at, (lows, count) in enumerate(plan):
        pair = refs[2 * at : 2 * at + 2]
        sums.append(sum(t[low : low + count, :].astype(FULL) for t, low in zip(pair, lows)))
    rest = sums.pop()
    total = jnp.concatenate(sums, axis=0)
    last = sum(ref[...].astype(FULL) for ref in refs[2 * len(plan) : terms])
    expand_ref, output_ref, contract_ref, query_ref, router_ref, keyval_ref = refs[terms : terms + 6]
    *vector_refs, bias_ref = refs[terms + 6 :]
    rows, width = output_ref.shape
    for slot in range(slots):
        expand_ref[:, slot * width : (slot + 1) * width] = total[slot * rows : (slot + 1) * rows]
    output_ref[...] = total[slots * rows :]
    query_ref[...] = last[:rows]
    side = last[rows:]
    contract_ref[...] = rest
    experts = router_ref.shape[0]
    keyval_ref[...] = side[:, :LANES]
    for expert in range(experts):
        lane = LANES + expert
        router_ref[expert : expert + 1, :] = as_row(side[:, lane : lane + 1])
    for index, ref in enumerate(vector_refs):
        lane = LANES + experts + index
        ref[...] = as_row(side[:, lane : lane + 1])
    start = LANES + BIAS_LANE
    bias_ref[...] = side[0:1, start : start + bias_ref.shape[1]]


def in_hbm(array):
    return pltpu.with_memory_space_constraint(array, pltpu.HBM)


def smem_spec():
    return pl.BlockSpec(memory_space=pltpu.SMEM)


def vmem_spec():
    return pl.BlockSpec(memory_space=pltpu.VMEM)


def shape_of(shape, dtype):
    return jax.ShapeDtypeStruct(tuple(shape), dtype)


def limit_of(name):
    return LIMITS[name] * MEGA


def estimate(cost):
    return pl.CostEstimate(flops=int(cost * 1e9), bytes_accessed=0, transcendentals=0)


def call(kernel, name, outs, cost, scalars=0, more=0):
    def run(*operands):
        return pl.pallas_call(
            kernel,
            in_specs=[smem_spec()] * scalars + [vmem_spec()] * (len(operands) - scalars),
            out_specs=[vmem_spec()] * len(outs) if isinstance(outs, list) else vmem_spec(),
            out_shape=outs,
            compiler_params=pltpu.CompilerParams(vmem_limit_bytes=limit_of(name) + more * MEGA),
            cost_estimate=estimate(cost),
            name=name,
        )(*operands)

    return run


def generations(seq_count):
    masks = range(1, seq_count)
    most = seq_count.bit_length() - 1
    return [[m for m in masks if bin(m).count("1") == n] for n in range(1, most + 1)]


def feed_up(ids, tokens, cotangent, attn, gates, routes, vectors, bias, pairs, plain, head):
    token_count, width = tokens.shape
    chunks = pairs[0].shape[0] - 1
    rows = shape_of((token_count, width), LOW)
    held = shape_of((chunks, token_count, bias.shape[1] // chunks), LOW)
    return call(
        functools.partial(up_kernel, head=head), "feed_up", [rows, rows, held, held]
        + [shape_of(plain, LOW)] * 2, FEED_COST / 2, scalars=1
    )(ids, tokens, cotangent, attn, gates, routes, vectors, bias, *pairs)


def feed_down(ids, hidden, cotangent, active, steep, pairs, contracts, masks, head, end=()):
    token_count, width = hidden.shape
    last = bool(end)
    rows = (token_count, width)
    size = 2 * contracts[0].shape[1]
    if last:
        grads = shape_of(pairs[0].shape, LOW)
        outs = [
            shape_of(rows, LOW),
            shape_of(rows, LOW),
            shape_of((2, token_count, LANES), LOW),
            shape_of((token_count, LANES), LOW),
            shape_of((8, width), FULL),
            grads,
            grads,
            shape_of((1, active.shape[0] * active.shape[2]), FULL),
        ]
    else:
        grads = shape_of(pairs[0].shape[1:3] + (size,), LOW)
        outs = [shape_of(rows, FULL)] * 2 + [grads, grads, shape_of((1, size), FULL)]
    return call(
        functools.partial(down_kernel, head=head, masks=masks, last=last),
        "feed_down_last" if last else "feed_down",
        outs,
        FEED_COST / 2,
        scalars=1,
    )(ids, hidden, cotangent, active, steep, *pairs, *contracts, *end)


def per_device(
    tokens, routes, lengths, cotangent, first_gain, first_shift, router, query_map, keyval,
    output_map, second_gain, second_shift, expand, expand_bias, contract, contract_bias
):
    seq_count, plane_count = lax.axis_size("seq"), lax.axis_size("dp") // 2
    along = Group("seq", 0, seq_count, SEQ_SLOT)
    plane = Group("dp", 1, plane_count, PLANE_SLOT)
    core = Group("dp", 0, 2, CORE_SLOT)
    token_count, width = tokens.shape
    rows = first_gain.shape[0]
    contract_rows = contract.shape[0]
    experts = router.shape[1]
    head = keyval.shape[1] // 2
    inner_width = expand.shape[1]
    chunks = inner_width // width
    slots = 1 + chunks
    my_index = along.index()
    ids = jnp.stack([g.index() for g in (along, plane, core)]).astype(jnp.int32)
    side_width = 2 * LANES
    row_count = 2 * token_count
    part = min(1024, row_count)

    params = [
        query_map, keyval, router.T, first_gain[None], first_shift[None], second_gain[None],
        second_shift[None], contract_bias[None], expand_bias[None], output_map, expand, contract
    ]
    small_mine, large_mine = pl.pallas_call(
        functools.partial(pack_kernel, count=len(params)),
        in_specs=[pl.BlockSpec(memory_space=pltpu.HBM)] * len(params),
        out_specs=[vmem_spec()] * 2,
        out_shape=[
            shape_of((rows, width + side_width), LOW),
            shape_of((slots * rows + contract_rows, width), LOW),
        ],
        scratch_shapes=[pltpu.VMEM(p.shape, p.dtype) for p in params]
        + [pltpu.SemaphoreType.DMA((len(params),))],
        compiler_params=pltpu.CompilerParams(vmem_limit_bytes=limit_of("pack")),
        cost_estimate=estimate(0.1),
        name="pack",
    )(*[in_hbm(p) for p in params])

    def first_work():
        given = [routes.T, lengths]
        return pl.pallas_call(
            first_kernel,
            in_specs=[smem_spec()] + [pl.BlockSpec(memory_space=pltpu.HBM)] * 2,
            out_specs=[vmem_spec()] * 2 + [smem_spec()],
            out_shape=[
                shape_of((2, token_count, LANES), jnp.int32),
                shape_of((8, LANES), jnp.int32),
                shape_of(ids.shape, jnp.int32),
            ],
            scratch_shapes=[pltpu.VMEM(p.shape, p.dtype) for p in given]
            + [pltpu.SemaphoreType.DMA((2,))],
            compiler_params=pltpu.CompilerParams(vmem_limit_bytes=limit_of("first")),
            cost_estimate=estimate(0.1),
            name="first",
        )(ids, *[in_hbm(p) for p in given])


    small_move = Move(along, small_mine[None])
    coming = generations(seq_count)
    bits = [1 << b for b in reversed(range(seq_count.bit_length() - 1))]
    large, large_masks = large_mine[None], [0]
    large_move = Move(along, large, bits[:1])
    route_columns, bounds, ids, large = phase(
        [small_move, large_move], first_work, held=[large]
    )
    for group in (along, plane, core):
        group.ids = ids
    small = merge([small_mine[None]] + [small_move.got[m] for m in range(1, seq_count)], along)
    for bit, later in zip(bits, bits[1:]):
        large_masks = large_masks + [m | bit for m in large_masks]
        large = call(
            join_kernel, "join", shape_of((2 * large.shape[0],) + large.shape[1:], LOW), 0.1
        )(large, large_move.got[bit])
        large, small = together(large, small)
        large_move = Move(along, large, [later])
        if later != bits[-1]:
            phase([large_move])
    small_move = Move(plane, small)
    unit_shapes = [shape_of(tokens.shape, FULL), shape_of((token_count, LANES), FULL)]
    unit, factor = phase(
        [small_move, large_move], lambda: call(unit_kernel, "unit", unit_shapes, 0.1)(tokens)
    )
    large_parts = [large, large_move.got[bits[-1]]]
    large_masks = [large_masks, [m | bits[-1] for m in large_masks]]
    small = merge([small] + [small_move.got[m] for m in range(1, plane_count)], plane)[0]
    small_move = Move(core, small)
    phase([small_move])
    small_shape = (plane_count, seq_count * rows, width + side_width)
    smalls = [small.reshape(small_shape), small_move.got[1].reshape(small_shape)]
    hidden, kv_mine, gates, small = call(
        functools.partial(hidden_kernel, experts=experts),
        "hidden",
        [
            shape_of((token_count, width), LOW),
            shape_of((token_count, LANES), LOW),
            shape_of((2, token_count, LANES), FULL),
            shape_of((width, width + side_width), LOW),
        ],
        0.5,
        scalars=1,
    )(ids, unit, *smalls, route_columns)

    def attend(state, masks, queries, last=False):
        return call(
            functools.partial(
                forward_kernel, head=head, first=not state, last=last, masks=masks, part=row_count
            ),
            "attention_forward",
            [shape_of((row_count, LANES), t) for t in ((FULL, LOW) if last else (FULL,))],
            FORWARD_COST * len(masks),
            scalars=1,
            more=3 * (len(masks) - 1),
        )(ids, queries, bounds, *[shards[m] for m in masks], *state)

    def keys_of(masks):
        return [Move(along, shards[m & (m - 1)], [m & -m]) for m in masks]

    def come(masks, moves):
        for mask, move in zip(masks, moves):
            shards[mask] = move.got[mask & -mask]

    shards = {0: kv_mine}
    keys = keys_of(coming[0])

    for move in keys:
        move.begin()
    queries = call(
        functools.partial(query_kernel, head=head),
        "queries",
        shape_of((row_count, LANES), LOW),
        QUERY_COST,
        scalars=1,
    )(ids, hidden, small, route_columns, bounds)
    queries, *large_parts = together(queries, *large_parts)
    if rows % 16:
        blocks = {m: x[i] for x, masks in zip(large_parts, large_masks) for i, m in enumerate(masks)}
        lines = jnp.stack(by_place([blocks[m] for m in range(seq_count)], my_index))
        pair = lines[:, : slots * rows].reshape(seq_count, slots, rows, width)
        pair = pair.transpose(1, 0, 2, 3).reshape(slots, seq_count * rows, width)
        half = lines[:, slots * rows :].reshape(1, seq_count * contract_rows, width)
    else:
        pair, half = call(
            functools.partial(spread_kernel, masks=large_masks, slots=slots, rows=rows),
            "spread",
            [
                shape_of((slots, seq_count * rows, width), LOW),
                shape_of((seq_count * contract_rows, width), LOW),
            ],
            0.1,
            scalars=1,
        )(ids, *large_parts)
        half = half[None]
    pair_move = Move(plane, pair).begin()
    state, half = phase(keys, lambda: attend([], [0], queries), held=[half])
    come(coming[0], keys)
    for before, masks in zip(coming, coming[1:]):
        keys = keys_of(masks)
        moves = keys + [pair_move] if masks is coming[-1] else keys
        [state] = phase(moves, lambda: attend([state], before, queries))
        come(masks, keys)
    pair = merge([pair] + [pair_move.got[m] for m in range(1, plane_count)], plane)
    pair = pair.reshape(slots, plane_count, -1, width)
    pair_move = Move(core, pair)
    half_move = Move(plane, half).begin()
    own_core = Move(core, half)
    attn, wide_queries = phase([pair_move, own_core], lambda: attend([state], coming[-1], queries, True))
    attn = attn.reshape(2, token_count, LANES)
    pairs = [pair, pair_move.got[1]]
    vectors, bias = call(
        functools.partial(vectors_kernel, experts=experts, rows=rows),
        "vectors",
        [shape_of((8, width), FULL), shape_of((1, inner_width), FULL)],
        0.1,
    )(small)

    plain = (plane_count, seq_count * contract_rows, width)
    mixed, hidden_two, active, steep, keep_half, send_half = phase(
        [half_move],
        lambda: feed_up(
            ids, tokens, cotangent, attn, gates, route_columns, vectors, bias, pairs, plain, head
        ),
    )
    masks = list(range(1, plane_count))
    rest = call(
        stack_kernel, "join", shape_of((len(masks),) + half.shape[1:], LOW), 0.1
    )(*[half_move.got[m] for m in masks])
    rest_move, half_core = Move(core, rest), Move(core, send_half)
    out_held, grad_held, keep_own, send_own, bias_own = phase(
        [rest_move, half_core],
        lambda: feed_down(
            ids, hidden_two, cotangent, active, steep, pairs, (half, own_core.got[1]), [0], head
        ),
    )
    half_terms = [(keep_half, 0), (half_core.got[1], 0)]
    half_fold = Fold(half_terms, 1, contract_rows, [plane, along])
    (
        out, branch, grad_attn, grad_logits, grad_rows, keep_pair, send_pair, grad_bias
    ) = phase(
        fold([half_fold], rows),
        lambda: feed_down(
            ids, hidden_two, cotangent, active, steep, pairs, (rest, rest_move.got[1]), masks, head,
            (
                out_held, grad_held, keep_own, send_own, bias_own, tokens, mixed, attn, gates,
                route_columns, vectors
            ),
        ),
    )
    folded([half_fold])

    grad_rows_in = grad_attn.reshape(row_count, LANES)
    masks = list(range(seq_count - 1, 0, -1))
    if seq_count > 2:
        masks = [2] + [m for m in masks if m != 2]
    third = max(1, len(masks) // 3)
    groups = [masks[:third], masks[third:], [0]]

    def backward(masks, before):
        return call(
            functools.partial(
                backward_kernel, head=head, first=before is None, masks=masks, part=part
            ),
            "attention_backward",
            [shape_of((head, row_count), FULL)]
            + [shape_of((token_count, LANES), LOW)] * len(masks),
            BACKWARD_COST * len(masks),
            scalars=1,
            more=3 * (len(masks) - 1),
        )(
            ids, wide_queries, grad_rows_in, bounds, *[shards[m] for m in masks],
            *([] if before is None else [before])
        )

    pair_move = Move(core, send_pair)
    first_query, *leaving = phase([pair_move], lambda: backward(groups[0], None))
    part_way = (slots + 1) // 2
    begin = part_way * width
    pair_got = pair_move.got[1]
    pair_folds = [
        Fold([(keep_pair, 0), (pair_got, 0)], part_way, rows, [plane, along]),
        Fold(
            [(keep_pair, begin // 2), (pair_got, begin // 2)], slots - part_way, rows, [plane, along],
            upward=True,
        ),
    ]
    both = [half_fold] + pair_folds
    keys_first = Move(along, dict(zip(groups[0], leaving)), groups[0])
    second_query, *leaving = phase(
        [keys_first] + fold(both, rows), lambda: backward(groups[1], first_query)
    )
    folded(both)
    keys_second = Move(along, dict(zip(groups[1], leaving)), groups[1])

    def work():
        grad_query, own = backward(groups[2], second_query)
        shape = (plane_count, seq_count * rows, width)
        return own, *call(
            functools.partial(placed_kernel, head=head),
            "query_gradient",
            [
                shape_of((token_count, width), FULL),
                shape_of(shape, LOW),
                shape_of(shape, LOW),
                shape_of((width, LANES), FULL),
            ],
            1.0,
            scalars=1,
        )(ids, grad_query, hidden, route_columns, grad_logits, small)

    grad_kv, grad_before, keep_query, send_query, grad_router = phase(
        [keys_second] + fold(pair_folds, rows), work
    )
    folded(pair_folds)
    query_move = Move(core, send_query)
    others = list(keys_first.got.values()) + list(keys_second.got.values())
    shape = (plane_count, seq_count * rows, side_width)
    grad_hidden, keep_side, send_side = phase(
        [query_move],
        lambda: call(
            functools.partial(side_kernel, experts=experts, others=len(others), rows=rows),
            "key_gradient",
            [shape_of((token_count, width), FULL), shape_of(shape, LOW), shape_of(shape, LOW)],
            1.0,
            scalars=1,
        )(
            ids, hidden, grad_before, unit, small, grad_rows, grad_bias, grad_router,
            grad_kv, *others
        ),
    )

    side_move = Move(core, send_side)
    phase([side_move])
    moves = fold(both, rows)
    keep_query, *_ = together(keep_query, *[f.keep for f in both if f.move is not None])
    line = lambda *terms: [t.reshape(1, -1, t.shape[-1]) for t in terms]
    small_sent = cut(
        [line(keep_query, query_move.got[1]), line(keep_side, side_move.got[1])],
        plane,
        width + side_width,
    )
    small_move = Move(plane, dict(enumerate(small_sent)))
    phase([small_move] + moves)
    folded(both)
    last_sent = cut([line(small_sent[0], *small_move.got.values())], along, width)
    last_move = Move(along, dict(enumerate(last_sent)))
    moves = fold(both, rows)
    [grad_tokens] = phase(
        [last_move] + moves,
        lambda: [
            call(
                functools.partial(tokens_kernel, experts=experts),
                "token_gradient",
                shape_of((token_count, width), LOW),
                1.0,
            )(grad_hidden, unit, factor, branch, small)
        ],
    )
    folded(both)
    while any(f.stages for f in both):
        phase(fold(both, rows))
        folded(both)
    ends = pair_folds + [half_fold]
    plan = [([low for _, low in f.terms], f.lead * f.rows) for f in ends]
    terms = [a.reshape(-1, width) for f in ends for a, _ in f.terms]
    terms += [last_sent[0]] + list(last_move.got.values())
    vector_shape = shape_of((1, rows), FULL)
    (
        grad_expand, grad_output, grad_contract, grad_query_map, grad_router, grad_keyval,
        *vector_sums, grad_spread
    ) = call(
        functools.partial(finish_kernel, terms=len(terms), slots=chunks, plan=plan),
        "finish",
        [
            shape_of(expand.shape, FULL),
            shape_of(output_map.shape, FULL),
            shape_of(contract.shape, FULL),
            shape_of(query_map.shape, FULL),
            shape_of((experts, rows), FULL),
            shape_of(keyval.shape, FULL),
        ]
        + [vector_shape] * 5
        + [shape_of((1, expand_bias.shape[0]), FULL)],
        0.1,
    )(*terms)
    grad_gain, grad_shift, grad_gain_two, grad_shift_two, grad_contract_bias = (
        v.reshape(rows) for v in vector_sums
    )
    return (
        out, grad_tokens, grad_gain, grad_shift, grad_router.T, grad_query_map, grad_keyval,
        grad_output, grad_gain_two, grad_shift_two, grad_expand, grad_spread.reshape(-1),
        grad_contract, grad_contract_bias
    )


def solution(mesh):
    both = ("dp", "seq")
    rows, vector = P(both, None), P(both)
    return jax.shard_map(
        per_device,
        mesh=mesh,
        in_specs=(
            rows, rows, P("dp", None), rows, vector, vector, rows, rows, rows, rows, vector, vector,
            rows, vector, rows, vector
        ),
        out_specs=(
            rows, rows, vector, vector, rows, rows, rows, rows, vector, vector, rows, vector, rows,
            vector
        ),
        check_vma=False,
    )
```
